32 devices in a mesh: row: 4 (over y, core), seq: 8 (over z, x).
Axes of the slice: x: 2, y: 2, z: 4, core: 2. Of those that a mesh axis runs over, the one named last changes fastest.
Arguments:
- layer_in: bfloat16 [4, 1024, 2048], P('row', 'seq'), may hold values from -6 to 6
- segments: int32 [4, 1024], P('row', 'seq'), may hold values from 0 to 2, as said below
- positions: int32 [4, 1024], P('row', 'seq'), may hold values from 0 to 1023, as said below
- attn_norm_gain: bfloat16 [2048], P(('row', 'seq')), may hold values from 0.099609375 to 1.8984375
- attn_norm_bias: bfloat16 [2048], P(('row', 'seq')), may hold values from -3 to 3
- qkv_weight: bfloat16 [2048, 6144], P(('row', 'seq')), may hold values from -0.125 to 0.125
- qkv_bias: bfloat16 [6144], P(('row', 'seq')), may hold values from -0.5 to 0.5
- out_weight: bfloat16 [2048, 2048], P(('row', 'seq')), may hold values from -3 to 3
- mlp_norm_gain: bfloat16 [2048], P(('row', 'seq')), may hold values from 0.099609375 to 1.8984375
- mlp_norm_bias: bfloat16 [2048], P(('row', 'seq')), may hold values from -3 to 3
- gate_weight: bfloat16 [2048, 5632], P(('row', 'seq')), may hold values from -0.125 to 0.125
- up_weight: bfloat16 [2048, 5632], P(('row', 'seq')), may hold values from -0.125 to 0.125
- down_weight: bfloat16 [5632, 2048], P(('row', 'seq')), may hold values from -0.078125 to 0.078125
- out_grad: bfloat16 [4, 1024, 2048], P('row', 'seq'), may hold values from -6 to 6
Outputs:
- layer_out: bfloat16 [4, 1024, 2048], P('row', 'seq')
- input_grad: float32 [4, 1024, 2048], P('row', 'seq')
- attn_norm_gain_grad: float32 [2048], P(('row', 'seq'))
- attn_norm_bias_grad: float32 [2048], P(('row', 'seq'))
- qkv_weight_grad: float32 [2048, 6144], P(('row', 'seq'))
- qkv_bias_grad: float32 [6144], P(('row', 'seq'))
- out_weight_grad: float32 [2048, 2048], P(('row', 'seq'))
- mlp_norm_gain_grad: float32 [2048], P(('row', 'seq'))
- mlp_norm_bias_grad: float32 [2048], P(('row', 'seq'))
- gate_weight_grad: float32 [2048, 5632], P(('row', 'seq'))
- up_weight_grad: float32 [2048, 5632], P(('row', 'seq'))
- down_weight_grad: float32 [5632, 2048], P(('row', 'seq'))
The draws below stay inside these ranges and needn't reach their ends.
Inputs may be any that keep to these rules, and one draw needn't show every extreme that they name: `segments`: along each row the numbers are 0, then 1, then 2; document 1 begins within the row's first 128 tokens and ends within its last 128. `positions`: within a document they rise by one from token to token; document 1 of every row starts at 0; document 0 of every row ends at 1023.
All inputs are finite; a program needn't handle non-finite values.
Results may differ from the reference program's by a relative error of at most 0.012.
Values may be sent and summed in bfloat16 or wider, within the bound.
A program may use at most 448 MiB of HBM per device.

```python
import math
import jax
import jax.numpy as jnp
from jax import lax

D = 2048
H = 32
HD = 64
FF = 5632
ROT = 16
KBLOCK = 512
TOK_DEV = 128
ROWS = 4
LENGTH = 1024


def document_bounds(key):
    first_key, last_key = jax.random.split(jax.random.fold_in(key, 11))
    leading = jax.random.randint(first_key, (ROWS,), 1, TOK_DEV)
    trailing = jax.random.randint(last_key, (ROWS,), 1, TOK_DEV)
    return (leading, trailing)


def draw_segments(key, part):
    leading, trailing = document_bounds(key)
    index = jnp.arange(LENGTH, dtype=jnp.int32)[None, :]
    second_doc = (index >= leading[:, None]).astype(jnp.int32)
    third_doc = (index >= LENGTH - trailing[:, None]).astype(jnp.int32)
    return second_doc + third_doc


def draw_positions(key, part):
    leading, trailing = document_bounds(key)
    key = jax.random.fold_in(key, 5)
    shifts = jax.random.randint(key, (ROWS, 1), 0, LENGTH - TOK_DEV)
    index = jnp.arange(LENGTH, dtype=jnp.int32)[None, :]
    second_doc = index >= leading[:, None]
    third_doc = index >= LENGTH - trailing[:, None]
    doc_start = jnp.where(third_doc, LENGTH - trailing[:, None], jnp.where(second_doc, leading[:, None], leading[:, None] - LENGTH))
    doc_shift = jnp.where(third_doc, shifts, 0)
    return (index - doc_start + doc_shift).astype(jnp.int32)


def levels(key, shape, cuts, least, top_value):
    factor_of = 1.0
    for axis_at, parts in cuts:
        draws = jax.random.uniform(jax.random.fold_in(jax.random.fold_in(key, 6), axis_at), (parts,), jnp.float32, least / len(cuts), top_value / len(cuts))
        factor_of = factor_of * jnp.repeat(jnp.exp(draws), shape[axis_at] // parts).reshape((-1,) + (1,) * (len(shape) - 1 - axis_at))
    return factor_of


def noise(stream_key, shape, width, limit, pieces=(), kind=jnp.bfloat16):
    result = width * jax.random.normal(stream_key, shape, jnp.float32)
    if pieces:
        result = result * levels(stream_key, shape, pieces, -0.22, 0.18)
    return jnp.clip(result, -limit, limit).astype(kind)


def setup_inputs(seed: int = 0) -> dict:
    key_list = jax.random.split(jax.random.key(seed), 15)
    layer_in = noise(key_list[0], (ROWS, LENGTH, D), 1.0, 6.0, ((0, 4), (1, 8)))
    segments = draw_segments(jax.random.fold_in(key_list[14], 71), 0)
    positions = draw_positions(jax.random.fold_in(key_list[14], 71), 0)
    attn_norm_gain = jnp.clip(1.0 + 0.18 * jax.random.normal(key_list[3], (D,), jnp.float32), 0.099609375, 1.8984375).astype(jnp.bfloat16)
    attn_norm_bias = noise(key_list[4], (D,), 0.3, 3.0, ((0, 32),))
    qkv_weight = noise(key_list[5], (D, 3 * D), D ** -0.5, 0.125, ((0, 32),))
    qkv_bias = noise(key_list[6], (3 * D,), 0.05, 0.5, ((0, 32),))
    out_weight = noise(key_list[7], (D, D), (max(D // 512, 1)) ** -0.5, 3.0, ((0, 32),))
    mlp_norm_gain = jnp.clip(1.0 + 0.18 * jax.random.normal(key_list[8], (D,), jnp.float32), 0.099609375, 1.8984375).astype(jnp.bfloat16)
    mlp_norm_bias = noise(key_list[9], (D,), 0.3, 3.0, ((0, 32),))
    gate_weight = noise(key_list[10], (D, FF), D ** -0.5, 0.125, ((0, 32),))
    up_weight = noise(key_list[11], (D, FF), D ** -0.5, 0.125, ((0, 32),))
    down_weight = noise(key_list[12], (FF, D), FF ** -0.5, 0.078125, ((0, 32),))
    out_grad = noise(key_list[13], (ROWS, LENGTH, D), 1.0, 6.0, ((0, 4), (1, 8)))
    return dict(layer_in=layer_in, segments=segments, positions=positions, attn_norm_gain=attn_norm_gain, attn_norm_bias=attn_norm_bias, qkv_weight=qkv_weight, qkv_bias=qkv_bias, out_weight=out_weight, mlp_norm_gain=mlp_norm_gain, mlp_norm_bias=mlp_norm_bias, gate_weight=gate_weight, up_weight=up_weight, down_weight=down_weight, out_grad=out_grad)


EPSILON = 1e-05
HIGHEST = lax.Precision.HIGHEST

@jax.custom_vjp
def low(v):
    return lax.optimization_barrier(v.astype(jnp.bfloat16)).astype(jnp.float32)

@jax.custom_vjp
def low_back(v):
    return v

def low_keep(v):
    return (low(v), None)

def low_pass(kept, grad):
    return (grad,)

def back_keep(v):
    return (v, None)

def back_low(kept, grad):
    return (low(grad),)
low.defvjp(low_keep, low_pass)
low_back.defvjp(back_keep, back_low)

def layer_norm(values_in, gain_vector, bias_vector):
    average = lax.optimization_barrier(jnp.mean(values_in, axis=-1, keepdims=True))
    centered = values_in - average
    inv_std = lax.rsqrt(lax.optimization_barrier(jnp.mean(centered * centered, axis=-1, keepdims=True)) + EPSILON)
    return centered * inv_std * gain_vector + bias_vector

def rotate(head_values, positions):
    half_rot = ROT // 2
    frequency = 10000.0 ** (-2.0 * jnp.arange(half_rot, dtype=jnp.float32) / ROT)
    angles = positions.astype(jnp.float32)[:, None] * frequency[None, :]
    cosine = jnp.cos(angles)[:, None, :]
    sine_part = jnp.sin(angles)[:, None, :]
    first_half = head_values[..., :half_rot]
    second = head_values[..., half_rot:ROT]
    return jnp.concatenate([first_half * cosine - second * sine_part, second * cosine + first_half * sine_part, head_values[..., ROT:]], axis=-1)

def attend(queries, keys_all, values_all, segments):
    key_rows = jnp.arange(LENGTH, dtype=jnp.int32)

    def one_block(block_start):
        query_block = lax.dynamic_slice_in_dim(queries, block_start, KBLOCK, 0)
        seg_block = lax.dynamic_slice_in_dim(segments, block_start, KBLOCK, 0)
        query_rows = block_start + jnp.arange(KBLOCK, dtype=jnp.int32)
        scores = low_back(jnp.einsum('qhd,khd->hqk', query_block, keys_all, precision=HIGHEST))
        allowed = (seg_block[:, None] == segments[None, :]) & (key_rows[None, :] <= query_rows[:, None])
        exp_weights = jnp.where(allowed[None], jnp.exp(scores), 0.0)
        denominator = lax.optimization_barrier(jnp.sum(exp_weights, axis=-1))
        numerator = low_back(jnp.einsum('hqk,khd->qhd', low(exp_weights), values_all, precision=HIGHEST))
        return numerator / jnp.transpose(denominator)[:, :, None]
    block_starts = (jnp.arange(LENGTH // KBLOCK, dtype=jnp.int32) * KBLOCK).astype(jnp.int32)
    context = lax.map(jax.checkpoint(one_block), block_starts)
    return context.reshape(LENGTH, D)

def forward(layer_rows, segments, positions, params):
    attn_gain, attn_bias, qkv_all, qkv_shift, out_all, mlp_gain, mlp_bias, gate_all, up_all, down_all = params
    inputs_low = low(layer_norm(layer_rows, attn_gain, attn_bias))
    projected = low_back(jnp.dot(inputs_low, qkv_all, precision=HIGHEST) + qkv_shift)
    head_split = projected.reshape(LENGTH, 3, H, HD)
    queries = low(rotate(head_split[:, 0], positions) / math.sqrt(HD))
    keys_all = low(rotate(head_split[:, 1], positions))
    values_all = low(head_split[:, 2])
    context = attend(queries, keys_all, values_all, segments)
    attn_branch = low_back(jnp.dot(low(context), out_all, precision=HIGHEST))
    hidden_mid = layer_rows + attn_branch
    middle_low = low(layer_norm(hidden_mid, mlp_gain, mlp_bias))
    gate_pre = low_back(jnp.dot(middle_low, gate_all, precision=HIGHEST))
    up_pre = low_back(jnp.dot(middle_low, up_all, precision=HIGHEST))
    inner_act = low(jax.nn.silu(gate_pre) * up_pre)
    mlp_branch = low_back(jnp.dot(inner_act, down_all, precision=HIGHEST))
    return hidden_mid + mlp_branch

def reference(layer_in, segments, positions, attn_norm_gain, attn_norm_bias, qkv_weight, qkv_bias, out_weight, mlp_norm_gain, mlp_norm_bias, gate_weight, up_weight, down_weight, out_grad):
    params = tuple((weight.astype(jnp.float32) for weight in (attn_norm_gain, attn_norm_bias, qkv_weight, qkv_bias, out_weight, mlp_norm_gain, mlp_norm_bias, gate_weight, up_weight, down_weight)))
    start_grads = tuple((jnp.zeros_like(weight) for weight in params))

    def one_row(summed, row_data):
        row_in, row_segments, row_positions, row_grad = row_data

        def row_forward(row_float, weights):
            return forward(row_float, row_segments, row_positions, weights)
        outputs, pullback = jax.vjp(row_forward, row_in.astype(jnp.float32), params)
        row_input_grad, weight_grads = pullback(row_grad.astype(jnp.float32))
        summed = tuple((total + extra for total, extra in zip(summed, weight_grads)))
        return (summed, (outputs.astype(jnp.bfloat16), row_input_grad))
    grads, (layer_out, input_grad) = lax.scan(one_row, start_grads, (layer_in, segments, positions, out_grad))
    return (layer_out, input_grad, grads[0], grads[1], grads[2], grads[3], grads[4], grads[5], grads[6], grads[7], grads[8], grads[9])
```

```python
import math

import jax
import jax.numpy as jnp
from jax import lax
from jax.sharding import PartitionSpec as P

D = 2048
H = 32
HD = 64
ROT = 16
EPSILON = 1e-05
BF = jnp.bfloat16
F32 = jnp.float32


def dot(a, b, ca, cb):
    return lax.dot_general(a, b, (((ca,), (cb,)), ((), ())), preferred_element_type=F32)


def norm_stats(values_in):
    average = jnp.mean(values_in, axis=-1, keepdims=True)
    centered = values_in - average
    inv_std = lax.rsqrt(jnp.mean(centered * centered, axis=-1, keepdims=True) + EPSILON)
    return (centered * inv_std, inv_std)


def norm_back(grad_in, normed, inv_std, gain_vector):
    scaled = grad_in * gain_vector
    return inv_std * (
        scaled
        - jnp.mean(scaled, axis=-1, keepdims=True)
        - normed * jnp.mean(scaled * normed, axis=-1, keepdims=True)
    )


def rotary_tables(positions):
    half_rot = ROT // 2
    frequency = 10000.0 ** (-2.0 * jnp.arange(half_rot, dtype=F32) / ROT)
    angles = positions.astype(F32)[:, None] * frequency[None, :]
    return (jnp.cos(angles)[:, None, :], jnp.sin(angles)[:, None, :])


def rotate(head_values, cosine, sine_part, direction):
    half_rot = ROT // 2
    first_half = head_values[..., :half_rot]
    second = head_values[..., half_rot:ROT]
    return jnp.concatenate(
        [
            first_half * cosine - direction * second * sine_part,
            second * cosine + direction * first_half * sine_part,
            head_values[..., ROT:],
        ],
        axis=-1,
    )


def gather_seq(v):
    return lax.all_gather(v, "seq", axis=0, tiled=True)


def scatter_seq(v):
    return lax.psum_scatter(v, "seq", scatter_dimension=0, tiled=True)


def columns_in(blocks):
    n, k, c = blocks.shape
    moved = lax.all_to_all(blocks, "seq", 0, 0)
    return lax.all_gather(moved.reshape(n * k, c), "row", axis=0, tiled=True)


def columns_out(grad, n, k):
    c = grad.shape[1]
    own = lax.psum_scatter(grad, "row", scatter_dimension=0, tiled=True)
    return lax.all_to_all(own.reshape(n, k, c), "seq", 0, 0)


def rows_in(shard):
    return lax.all_gather(shard, "row", axis=0, tiled=True)


def rows_out(grad):
    return lax.psum_scatter(grad, "row", scatter_dimension=0, tiled=True)


def attention(queries, keys, values, allowed):
    scores = jnp.einsum("qhd,khd->hqk", queries, keys, preferred_element_type=F32)
    exp_weights = jnp.where(allowed[None], jnp.exp(scores), 0.0)
    denominator = jnp.sum(exp_weights, axis=-1)
    numerator = jnp.einsum(
        "hqk,khd->qhd", exp_weights.astype(BF), values, preferred_element_type=F32
    )
    return numerator / jnp.transpose(denominator)[:, :, None], denominator


def attention_back(queries, keys, values, allowed, denominator, context, g_context):
    den = jnp.transpose(denominator)
    g_numer = (g_context / den[:, :, None]).astype(BF)
    g_den = jnp.transpose(-jnp.sum(g_context * context, axis=-1) / den)
    scores = jnp.einsum("qhd,khd->hqk", queries, keys, preferred_element_type=F32)
    exp_weights = jnp.where(allowed[None], jnp.exp(scores), 0.0)
    g_values = jnp.einsum(
        "hqk,qhd->khd", exp_weights.astype(BF), g_numer, preferred_element_type=F32
    )
    g_weights = jnp.einsum("qhd,khd->hqk", g_numer, values, preferred_element_type=F32)
    g_scores = (exp_weights * (g_weights + g_den[:, :, None])).astype(BF)
    g_queries = jnp.einsum("hqk,khd->qhd", g_scores, keys, preferred_element_type=F32)
    g_keys = jnp.einsum("hqk,qhd->khd", g_scores, queries, preferred_element_type=F32)
    return g_queries, g_keys, g_values


def body(nrow, n, *args):
    (
        layer_in,
        segments,
        positions,
        attn_norm_gain,
        attn_norm_bias,
        qkv_weight,
        qkv_bias,
        out_weight,
        mlp_norm_gain,
        mlp_norm_bias,
        gate_weight,
        up_weight,
        down_weight,
        out_grad,
    ) = args
    j = lax.axis_index("seq")
    tok = layer_in.shape[1]
    length = n * tok
    k = qkv_weight.shape[0]
    f = down_weight.shape[0]
    hp = H // n
    whole_heads = out_weight.shape[0] == HD

    def split_heads(w):
        lead = w.shape[0]
        if whole_heads:
            w = w.reshape(lead, 3, nrow, n, HD).transpose(3, 0, 1, 2, 4)
        else:
            w = w.reshape(lead, 3, n, hp, HD).transpose(2, 0, 1, 3, 4)
        return w.reshape(n, lead, 3 * hp * HD)

    def join_heads(blocks):
        lead = blocks.shape[1]
        if whole_heads:
            w = blocks.reshape(n, lead, 3, nrow, HD).transpose(1, 2, 3, 0, 4)
        else:
            w = blocks.reshape(n, lead, 3, hp, HD).transpose(1, 2, 0, 3, 4)
        return w.reshape(lead, 3 * D)

    def split_ff(w):
        return w.reshape(k, nrow, n, f).transpose(2, 0, 1, 3).reshape(n, k, nrow * f)

    def join_ff(blocks):
        return blocks.reshape(n, k, nrow, f).transpose(1, 2, 0, 3).reshape(k, nrow * n * f)

    small = jnp.concatenate(
        [attn_norm_gain, attn_norm_bias, mlp_norm_gain, mlp_norm_bias, qkv_bias]
    )
    small_all = lax.all_gather(small, ("row", "seq"), axis=0)
    cuts = [0, k, 2 * k, 3 * k, 4 * k]
    attn_gain, attn_bias, mlp_gain, mlp_bias = (
        small_all[:, c : c + k].reshape(1, D).astype(F32) for c in cuts[:4]
    )
    qkv_shift = small_all[:, 4 * k :].reshape(1, 3 * D)
    shift_own = lax.dynamic_index_in_dim(split_heads(qkv_shift), j, 0, keepdims=False).astype(F32)

    ints = lax.all_gather(jnp.concatenate([segments, positions], 0), "seq", axis=1, tiled=True)
    seg_all, pos_all = ints[0], ints[1]

    qkv_own = columns_in(split_heads(qkv_weight))
    gate_own = columns_in(split_ff(gate_weight))
    up_own = columns_in(split_ff(up_weight))
    down_own = rows_in(down_weight)
    if whole_heads:
        out_own = rows_in(out_weight)
    else:
        out_full = lax.all_gather(out_weight, ("row", "seq"), axis=0, tiled=True)
        out_own = lax.dynamic_slice_in_dim(out_full, j * hp * HD, hp * HD, 0)

    x_all = gather_seq(layer_in[0])
    inputs_all = (norm_stats(x_all.astype(F32))[0] * attn_gain + attn_bias).astype(BF)
    projected = dot(inputs_all, qkv_own, 1, 0) + shift_own
    head_split = projected.reshape(length, 3, hp, HD)
    cosine, sine_part = rotary_tables(pos_all)
    queries = (rotate(head_split[:, 0], cosine, sine_part, 1.0) / math.sqrt(HD)).astype(BF)
    keys = rotate(head_split[:, 1], cosine, sine_part, 1.0).astype(BF)
    values = head_split[:, 2].astype(BF)
    index = jnp.arange(length, dtype=jnp.int32)
    allowed = (seg_all[:, None] == seg_all[None, :]) & (index[None, :] <= index[:, None])
    context, denominator = attention(queries, keys, values, allowed)
    context_low = context.reshape(length, hp * HD).astype(BF)
    attn_branch = scatter_seq(dot(context_low, out_own, 1, 0).astype(BF)).astype(F32)

    x_float = layer_in[0].astype(F32)
    normed1, inv_std1 = norm_stats(x_float)
    hidden_mid = x_float + attn_branch
    normed2, inv_std2 = norm_stats(hidden_mid)
    middle_all = gather_seq((normed2 * mlp_gain + mlp_bias).astype(BF))
    gate_pre = dot(middle_all, gate_own, 1, 0)
    up_pre = dot(middle_all, up_own, 1, 0)
    sig = jax.nn.sigmoid(gate_pre)
    silu = gate_pre * sig
    inner_act = (silu * up_pre).astype(BF)
    mlp_branch = scatter_seq(dot(inner_act, down_own, 1, 0).astype(BF)).astype(F32)
    layer_out = (hidden_mid + mlp_branch).astype(BF)

    grad_all = gather_seq(out_grad[0])
    grad_float = out_grad[0].astype(F32)
    g_inner = dot(grad_all, down_own, 1, 1)
    g_gate = (g_inner * up_pre * sig * (1.0 + gate_pre * (1.0 - sig))).astype(BF)
    g_up = (g_inner * silu).astype(BF)
    g_middle = scatter_seq(
        (dot(g_gate, gate_own, 1, 1) + dot(g_up, up_own, 1, 1)).astype(BF)
    ).astype(F32)
    g_hidden = grad_float + norm_back(g_middle, normed2, inv_std2, mlp_gain)
    g_attn_all = gather_seq(g_hidden.astype(BF))
    down_grad = rows_out(dot(inner_act, grad_all, 0, 0).astype(BF)).astype(F32)
    gate_grad = join_ff(columns_out(dot(middle_all, g_gate, 0, 0).astype(BF), n, k)).astype(F32)
    up_grad = join_ff(columns_out(dot(middle_all, g_up, 0, 0).astype(BF), n, k)).astype(F32)

    out_part = dot(context_low, g_attn_all, 0, 0)
    if whole_heads:
        out_w_grad = rows_out(out_part.astype(BF)).astype(F32)
    else:
        placed = lax.dynamic_update_slice_in_dim(
            jnp.zeros((D, D), BF), out_part.astype(BF), j * hp * HD, 0
        )
        out_w_grad = lax.psum_scatter(
            placed, ("row", "seq"), scatter_dimension=0, tiled=True
        ).astype(F32)
    g_context = dot(g_attn_all, out_own, 1, 1).reshape(length, hp, HD)
    g_queries, g_keys, g_values = attention_back(
        queries, keys, values, allowed, denominator, context, g_context
    )
    query_part = rotate(g_queries, cosine, sine_part, -1.0) / math.sqrt(HD)
    key_part = rotate(g_keys, cosine, sine_part, -1.0)
    g_projected = (
        jnp.stack([query_part, key_part, g_values], 1).reshape(length, 3 * hp * HD).astype(BF)
    )
    g_inputs = scatter_seq(dot(g_projected, qkv_own, 1, 1).astype(BF)).astype(F32)
    qkv_grad = join_heads(
        columns_out(dot(inputs_all, g_projected, 0, 0).astype(BF), n, k)
    ).astype(F32)
    shift_sum = jnp.sum(g_projected.astype(F32), axis=0)
    shift_blocks = lax.dynamic_update_slice_in_dim(
        jnp.zeros((n, 1, 3 * hp * HD), F32), shift_sum[None, None], j, 0
    )
    shift_full = join_heads(shift_blocks)[0]
    input_grad = g_hidden + norm_back(g_inputs, normed1, inv_std1, attn_gain)

    sums = [
        jnp.sum(g_inputs * normed1, axis=0),
        jnp.sum(g_inputs, axis=0),
        jnp.sum(g_middle * normed2, axis=0),
        jnp.sum(g_middle, axis=0),
        shift_full,
    ]
    packed = jnp.concatenate([s.reshape(nrow * n, -1) for s in sums], axis=1)
    own = lax.psum_scatter(packed, ("row", "seq"), scatter_dimension=0, tiled=True)[0]
    return (
        layer_out[None],
        input_grad[None],
        own[0:k],
        own[k : 2 * k],
        qkv_grad,
        own[4 * k :],
        out_w_grad,
        own[2 * k : 3 * k],
        own[3 * k : 4 * k],
        gate_grad,
        up_grad,
        down_grad,
    )


def solution(mesh):
    nrow, n = mesh.shape["row"], mesh.shape["seq"]

    def local(*args):
        return body(nrow, n, *args)

    tokens, ints = P("row", "seq", None), P("row", "seq")
    vec, mat = P(("row", "seq")), P(("row", "seq"), None)
    return jax.shard_map(
        local,
        mesh=mesh,
        in_specs=(
            tokens, ints, ints, vec, vec, mat, vec, mat, vec, vec, mat, mat, mat, tokens,
        ),
        out_specs=(tokens, tokens, vec, vec, mat, vec, mat, vec, vec, mat, mat, mat),
        check_vma=False,
    )
```

```python
import math

import jax
import jax.numpy as jnp
from jax import lax
from jax.experimental import pallas as pl
from jax.experimental.pallas import tpu as pltpu
from jax.sharding import PartitionSpec as P

D = 2048
H = 32
HD = 64
ROT = 16
EPSILON = 1e-05
BF = jnp.bfloat16
F32 = jnp.float32


def dot(a, b, ca, cb):
    return lax.dot_general(a, b, (((ca,), (cb,)), ((), ())), preferred_element_type=F32)


def norm_stats(values_in):
    average = jnp.mean(values_in, axis=-1, keepdims=True)
    centered = values_in - average
    inv_std = lax.rsqrt(jnp.mean(centered * centered, axis=-1, keepdims=True) + EPSILON)
    return (centered * inv_std, inv_std)


def norm_back(grad_in, normed, inv_std, gain_vector):
    scaled = grad_in * gain_vector
    return inv_std * (
        scaled
        - jnp.mean(scaled, axis=-1, keepdims=True)
        - normed * jnp.mean(scaled * normed, axis=-1, keepdims=True)
    )


def rotary_tables(positions):
    half_rot = ROT // 2
    frequency = 10000.0 ** (-2.0 * jnp.arange(half_rot, dtype=F32) / ROT)
    angles = positions.astype(F32)[:, None] * frequency[None, :]
    return (jnp.cos(angles)[:, None, :], jnp.sin(angles)[:, None, :])


def rotate(head_values, cosine, sine_part, direction):
    half_rot = ROT // 2
    first_half = head_values[..., :half_rot]
    second = head_values[..., half_rot:ROT]
    return jnp.concatenate(
        [
            first_half * cosine - direction * second * sine_part,
            second * cosine + direction * first_half * sine_part,
            head_values[..., ROT:],
        ],
        axis=-1,
    )


MESH = pl.DeviceIdType.MESH
LINE = 4


class Place:
    def __init__(self, n):
        self.n = n
        self.depth = LINE
        self.width = n // LINE
        self.r = lax.axis_index("row")
        self.j = lax.axis_index("seq")
        self.z = self.j // self.width
        self.x = lax.rem(self.j, self.width)
        y, c = self.r // 2, lax.rem(self.r, 2)
        self.y, self.c = y, c
        self.r_y = (1 - y) * 2 + c
        self.r_c = y * 2 + (1 - c)
        self.r_yc = (1 - y) * 2 + (1 - c)

    def seq(self, j):
        return (self.r, j)

    def row(self, r):
        return (r, self.j)

    def other(self, i):
        return lax.rem(self.j + i, self.n)

    def meet(self):
        barrier = pltpu.get_barrier_semaphore()
        for r in (self.r_y, self.r_c, self.r_yc):
            pl.semaphore_signal(barrier, inc=1, device_id=self.row(r), device_id_type=MESH)
        for i in range(1, self.n):
            pl.semaphore_signal(
                barrier, inc=1, device_id=self.seq(self.other(i)), device_id_type=MESH
            )
        pl.semaphore_wait(barrier, self.n + 2)


def remote(src, dst, ssem, rsem, device):
    return pltpu.make_async_remote_copy(
        src_ref=src, dst_ref=dst, send_sem=ssem, recv_sem=rsem, device_id=device,
        device_id_type=MESH,
    )


class Gather:
    @staticmethod
    def sems(n):
        w = n // LINE
        return [
            pltpu.SemaphoreType.DMA((2, LINE)),
            pltpu.SemaphoreType.DMA((LINE, max(w - 1, 1))),
            pltpu.SemaphoreType.DMA((n,)),
        ]

    def __init__(self, at, buf, sems):
        self.at, self.buf = at, buf
        self.line, self.side, self.got = sems

    def up(self, zz):
        at = self.at
        b = zz * at.width + at.x
        return remote(
            self.buf.at[b], self.buf.at[b], self.line.at[0, zz], self.got.at[b],
            at.seq(at.j + at.width),
        )

    def down(self, zz):
        at = self.at
        b = zz * at.width + at.x
        return remote(
            self.buf.at[b], self.buf.at[b], self.line.at[1, zz], self.got.at[b],
            at.seq(at.j - at.width),
        )

    def across(self, zz, i):
        at = self.at
        b = zz * at.width + at.x
        there = at.z * at.width + lax.rem(at.x + i, at.width)
        return remote(
            self.buf.at[b], self.buf.at[b], self.side.at[zz, i - 1], self.got.at[b], at.seq(there)
        )

    def take(self, b):
        at = self.at
        remote(
            self.buf.at[b], self.buf.at[b], self.line.at[0, 0], self.got.at[b], at.seq(at.other(1))
        ).wait_recv()

    def start(self):
        at = self.at

        @pl.when(at.z < at.depth - 1)
        def _():
            self.up(at.z).start()

        @pl.when(at.z > 0)
        def _():
            self.down(at.z).start()

        for i in range(1, at.width):
            self.across(at.z, i).start()

    def step(self, s):
        at = self.at

        @pl.when(at.z - s >= 0)
        def _():
            zz = at.z - s
            self.take(zz * at.width + at.x)

            @pl.when(at.z < at.depth - 1)
            def _():
                self.up(zz).start()

            for i in range(1, at.width):
                self.across(zz, i).start()

        @pl.when(at.z + s < at.depth)
        def _():
            zz = at.z + s
            self.take(zz * at.width + at.x)

            @pl.when(at.z > 0)
            def _():
                self.down(zz).start()

            for i in range(1, at.width):
                self.across(zz, i).start()

    def take_side(self, zz):
        at = self.at
        for i in range(1, at.width):
            self.take(zz * at.width + lax.rem(at.x + i, at.width))

    def finish(self):
        at = self.at
        for zz in range(at.depth):
            for i in range(1, at.width):
                self.across(zz, i).wait_send()

            @pl.when(jnp.logical_and(at.z >= zz, at.z < at.depth - 1))
            def _():
                self.up(zz).wait_send()

            @pl.when(jnp.logical_and(at.z <= zz, at.z > 0))
            def _():
                self.down(zz).wait_send()


class Reduce:
    @staticmethod
    def scratch(n, t, w):
        width = n // LINE
        return [
            pltpu.VMEM((LINE, max(width - 1, 1), t, w), BF),
            pltpu.VMEM((2, LINE, t, w), BF),
            pltpu.VMEM((2, LINE, t, w), BF),
            pltpu.SemaphoreType.DMA((LINE, max(width - 1, 1))),
            pltpu.SemaphoreType.DMA((LINE, max(width - 1, 1))),
            pltpu.SemaphoreType.DMA((2, LINE)),
            pltpu.SemaphoreType.DMA((2, LINE)),
        ]

    def __init__(self, at, part, refs):
        self.at, self.part = at, part
        self.xr, self.lr, self.ls, self.xs_sem, self.xr_sem, self.ls_sem, self.lr_sem = refs

    def across(self, t, i):
        at = self.at
        xx = lax.rem(at.x + i, at.width)
        return remote(
            self.part.at[t * at.width + xx], self.xr.at[t, i - 1], self.xs_sem.at[t, i - 1],
            self.xr_sem.at[t, i - 1], at.seq(at.z * at.width + xx),
        )

    def along(self, way, t):
        at = self.at
        there = at.j + at.width if way == 0 else at.j - at.width
        return remote(
            self.ls.at[way, t], self.lr.at[way, t], self.ls_sem.at[way, t],
            self.lr_sem.at[way, t], at.seq(there),
        )

    def emit(self, t):
        for i in range(1, self.at.width):
            self.across(t, i).start()

    def summed(self, t):
        at = self.at
        total = self.part[t * at.width + at.x].astype(F32)
        for i in range(1, at.width):
            self.across(t, i).wait_recv()
            total = total + self.xr[t, i - 1].astype(F32)
        return total

    def reduce(self, s):
        at = self.at

        @pl.when(at.z + s < at.depth)
        def _():
            t = at.z + s

            @pl.when(at.z > 0)
            def _():
                self.along(0, t).wait_recv()
                self.ls[0, t] = (self.summed(t) + self.lr[0, t].astype(F32)).astype(BF)

            @pl.when(at.z == 0)
            def _():
                self.ls[0, t] = self.summed(t).astype(BF)

            self.along(0, t).start()

        @pl.when(at.z - s >= 0)
        def _():
            t = at.z - s

            @pl.when(at.z < at.depth - 1)
            def _():
                self.along(1, t).wait_recv()
                self.ls[1, t] = (self.summed(t) + self.lr[1, t].astype(F32)).astype(BF)

            @pl.when(at.z == at.depth - 1)
            def _():
                self.ls[1, t] = self.summed(t).astype(BF)

            self.along(1, t).start()

    def last(self, out):
        at = self.at
        out[...] = self.summed(at.z)

        @pl.when(at.z > 0)
        def _():
            self.along(0, at.z).wait_recv()
            out[...] += self.lr[0, at.z].astype(F32)

        @pl.when(at.z < at.depth - 1)
        def _():
            self.along(1, at.z).wait_recv()
            out[...] += self.lr[1, at.z].astype(F32)

    def finish(self):
        at = self.at
        for t in range(at.depth):
            for i in range(1, at.width):
                self.across(t, i).wait_send()

            @pl.when(at.z < t)
            def _():
                self.along(0, t).wait_send()

            @pl.when(at.z > t)
            def _():
                self.along(1, t).wait_send()


class Columns:
    @staticmethod
    def sems(n):
        return [pltpu.SemaphoreType.DMA((4, n)), pltpu.SemaphoreType.DMA((4, n))]

    def __init__(self, at, pieces, full, sems):
        self.at, self.pieces, self.full = at, pieces, full
        self.ssem, self.rsem = sems

    def first(self, i):
        at = self.at
        to = at.other(i)
        return remote(
            self.pieces.at[to], self.full.at[at.r, at.j], self.ssem.at[0, to],
            self.rsem.at[at.r, at.j], at.seq(to),
        )

    def own(self):
        at = self.at
        return pltpu.make_async_copy(
            self.pieces.at[at.j], self.full.at[at.r, at.j], self.ssem.at[0, at.j]
        )

    def pass_on(self, r, js, to, k):
        return remote(
            self.full.at[r, js], self.full.at[r, js], self.ssem.at[k, js], self.rsem.at[r, js],
            self.at.row(to),
        )

    def take(self, r, js):
        self.pass_on(r, js, self.at.r_c, 0).wait_recv()

    def start(self):
        at = self.at
        self.own().start()

        @pl.loop(1, at.n)
        def _(i):
            self.first(i).start()

    def step(self, lo, hi):
        at = self.at

        @pl.loop(lo, hi)
        def _(i):
            js = lax.rem(at.j + at.n - i, at.n)

            @pl.when(i == 0)
            def _():
                self.own().wait()

            @pl.when(i > 0)
            def _():
                self.take(at.r, js)

            self.pass_on(at.r, js, at.r_y, 1).start()
            self.pass_on(at.r, js, at.r_c, 2).start()

    def relay(self, lo, hi):
        at = self.at

        @pl.loop(lo, hi)
        def _(i):
            js = lax.rem(at.j + at.n - i, at.n)
            self.take(at.r_y, js)
            self.pass_on(at.r_y, js, at.r_c, 3).start()

    def finish(self):
        at = self.at

        @pl.loop(0, at.n)
        def _(js):
            self.take(at.r_c, js)
            self.take(at.r_yc, js)
            self.pass_on(at.r, js, at.r_y, 1).wait_send()
            self.pass_on(at.r, js, at.r_c, 2).wait_send()
            self.pass_on(at.r_y, js, at.r_c, 3).wait_send()

        @pl.loop(1, at.n)
        def _(i):
            self.first(i).wait_send()


class Rows:
    @staticmethod
    def sems():
        return [pltpu.SemaphoreType.DMA((4,)), pltpu.SemaphoreType.DMA((4,))]

    def __init__(self, at, shard, full, sems):
        self.at, self.shard, self.full = at, shard, full
        self.ssem, self.rsem = sems

    def own(self):
        return pltpu.make_async_copy(self.shard, self.full.at[self.at.r], self.ssem.at[0])

    def direct(self, to, k):
        r = self.at.r
        return remote(
            self.shard, self.full.at[r], self.ssem.at[k], self.rsem.at[r], self.at.row(to)
        )

    def onward(self):
        at = self.at
        r = at.r_y
        return remote(
            self.full.at[r], self.full.at[r], self.ssem.at[3], self.rsem.at[r], at.row(at.r_c)
        )

    def take(self, r):
        at = self.at
        remote(
            self.full.at[r], self.full.at[r], self.ssem.at[0], self.rsem.at[r], at.row(at.r_c)
        ).wait_recv()

    def start(self):
        at = self.at
        self.own().start()
        self.direct(at.r_y, 1).start()
        self.direct(at.r_c, 2).start()

    def relay(self):
        self.take(self.at.r_y)
        self.onward().start()

    def finish(self):
        at = self.at
        self.own().wait()
        self.take(at.r_c)
        self.take(at.r_yc)
        self.direct(at.r_y, 1).wait_send()
        self.direct(at.r_c, 2).wait_send()
        self.onward().wait_send()


class RowSum:
    @staticmethod
    def scratch(m, c):
        return [
            pltpu.VMEM((2, m, c), BF),
            pltpu.VMEM((m, c), BF),
            pltpu.VMEM((m, c), BF),
            pltpu.SemaphoreType.DMA((3,)),
            pltpu.SemaphoreType.DMA((3,)),
        ]

    def __init__(self, at, grad, refs):
        self.at, self.grad = at, grad
        self.core_in, self.y_out, self.y_in, self.ssem, self.rsem = refs

    def to_core(self, far):
        at = self.at
        yy = 1 - at.y if far else at.y
        k = 1 if far else 0
        return remote(
            self.grad.at[yy * 2 + 1 - at.c], self.core_in.at[k], self.ssem.at[k], self.rsem.at[k],
            at.row(at.r_c),
        )

    def over_y(self):
        at = self.at
        return remote(
            self.y_out, self.y_in, self.ssem.at[2], self.rsem.at[2], at.row(at.r_y)
        )

    def start(self):
        self.to_core(1).start()
        self.to_core(0).start()

    def cross(self):
        at = self.at
        self.to_core(1).wait_recv()
        self.y_out[...] = (
            self.grad[at.r_y].astype(F32) + self.core_in[1].astype(F32)
        ).astype(BF)
        self.over_y().start()

    def total(self):
        at = self.at
        self.to_core(0).wait_recv()
        self.over_y().wait_recv()
        return (
            self.grad[at.r].astype(F32) + self.core_in[0].astype(F32) + self.y_in[...].astype(F32)
        )

    def finish(self):
        self.to_core(1).wait_send()
        self.to_core(0).wait_send()
        self.over_y().wait_send()


class Exchange:
    @staticmethod
    def sems(n):
        return [pltpu.SemaphoreType.DMA((n,)), pltpu.SemaphoreType.DMA((n,))]

    def __init__(self, at, mine, got, sems):
        self.at, self.mine, self.got = at, mine, got
        self.ssem, self.rsem = sems

    def send(self, i):
        at = self.at
        to = at.other(i)
        return remote(
            self.mine.at[to], self.got.at[at.j], self.ssem.at[to], self.rsem.at[at.j], at.seq(to)
        )

    def own(self):
        at = self.at
        return pltpu.make_async_copy(
            self.mine.at[at.j], self.got.at[at.j], self.ssem.at[at.j]
        )

    def start(self):
        self.own().start()

        @pl.loop(1, self.at.n)
        def _(i):
            self.send(i).start()

    def finish(self):
        at = self.at
        self.own().wait()

        @pl.loop(1, at.n)
        def _(i):
            src = at.other(i)
            remote(
                self.mine.at[src], self.got.at[src], self.ssem.at[src], self.rsem.at[src],
                at.seq(src),
            ).wait()


class SmallGather:
    @staticmethod
    def sems(n):
        return [pltpu.SemaphoreType.DMA((4,))] * 2 + [pltpu.SemaphoreType.DMA((n,))] * 2

    def __init__(self, at, mine, full, sems):
        self.at, self.mine, self.full = at, mine, full
        self.rs, self.rr, self.ss, self.sr = sems

    def beside(self, r):
        at = self.at
        return remote(
            self.mine, self.full.at[at.j, at.r], self.rs.at[r], self.rr.at[at.r], at.row(r)
        )

    def own(self):
        at = self.at
        return pltpu.make_async_copy(self.mine, self.full.at[at.j, at.r], self.rs.at[at.r])

    def onward(self, to):
        at = self.at
        return remote(
            self.full.at[at.j], self.full.at[at.j], self.ss.at[to], self.sr.at[at.j], at.seq(to)
        )

    def start(self):
        at = self.at
        self.own().start()
        for r in (at.r_y, at.r_c, at.r_yc):
            self.beside(r).start()

    def step(self):
        at = self.at
        self.own().wait()
        for r in (at.r_y, at.r_c, at.r_yc):
            remote(
                self.mine, self.full.at[at.j, r], self.rs.at[r], self.rr.at[r], at.row(r)
            ).wait()

        @pl.loop(1, at.n)
        def _(i):
            self.onward(at.other(i)).start()

    def finish(self):
        at = self.at

        @pl.loop(1, at.n)
        def _(i):
            src = at.other(i)
            remote(
                self.full.at[src], self.full.at[src], self.ss.at[src], self.sr.at[src],
                at.seq(src),
            ).wait()


class SmallSum:
    @staticmethod
    def scratch(n, w):
        q = w // 4
        return (
            [pltpu.VMEM((8, w), F32), pltpu.VMEM((4, 8, q), F32), pltpu.VMEM((8, q), F32)]
            + [pltpu.VMEM((n, 8, q), F32)]
            + [pltpu.SemaphoreType.DMA((4,))] * 2
            + [pltpu.SemaphoreType.DMA((n,))] * 2
        )

    def __init__(self, at, refs):
        self.at = at
        self.terms, self.beside_in, self.acc, self.seq_in = refs[:4]
        self.rs, self.rr, self.ss, self.sr = refs[4:]
        self.q = self.terms.shape[1] // 4

    def part(self, r):
        return self.terms.at[:, pl.ds(pl.multiple_of(r * self.q, self.q), self.q)]

    def beside(self, r):
        at = self.at
        return remote(
            self.part(r), self.beside_in.at[at.r], self.rs.at[r], self.rr.at[at.r], at.row(r)
        )

    def run(self, out):
        at = self.at
        near = (at.r_y, at.r_c, at.r_yc)
        for r in near:
            self.beside(r).start()
        self.acc[...] = self.part(at.r)[...]
        for r in near:
            remote(
                self.part(r), self.beside_in.at[r], self.rs.at[r], self.rr.at[r], at.row(r)
            ).wait()
            self.acc[...] += self.beside_in[r]

        @pl.loop(1, at.n)
        def _(i):
            to = at.other(i)
            remote(
                self.acc, self.seq_in.at[at.j], self.ss.at[to], self.sr.at[at.j], at.seq(to)
            ).start()

        out[...] = self.acc[...]

        @pl.loop(1, at.n)
        def _(i):
            src = at.other(i)
            remote(
                self.acc, self.seq_in.at[src], self.ss.at[src], self.sr.at[src], at.seq(src)
            ).wait()
            out[...] += self.seq_in[src]


class Call:
    def __init__(self, n, cid, name):
        self.n, self.cid, self.name = n, cid, name
        self.args, self.ins, self.outs, self.out_specs, self.scr = [], [], [], [], []

    def give(self, array, space=pltpu.VMEM):
        self.args.append(array)
        self.ins.append(pl.BlockSpec(memory_space=space))
        return ("i", len(self.args) - 1)

    def make(self, shape, dtype, space=pltpu.VMEM):
        self.outs.append(jax.ShapeDtypeStruct(shape, dtype))
        self.out_specs.append(pl.BlockSpec(memory_space=space))
        return ("o", len(self.outs) - 1)

    def scratch(self, items):
        at = len(self.scr)
        self.scr.extend(items)
        return [("s", at + i) for i in range(len(items))]

    def run(self, body, flops=0):
        ni, no = len(self.ins), len(self.outs)

        def kernel(*refs):
            def of(key):
                if isinstance(key, list):
                    return [of(k) for k in key]
                kind, i = key
                return refs[i + {"i": 0, "o": ni, "s": ni + no}[kind]]

            at = Place(self.n)
            at.meet()
            body(at, of)

        return pl.pallas_call(
            kernel,
            out_shape=self.outs,
            in_specs=self.ins,
            out_specs=self.out_specs,
            scratch_shapes=self.scr,
            name=self.name,
            cost_estimate=pl.CostEstimate(
                flops=flops, bytes_accessed=1 << 24, transcendentals=0
            ),
            compiler_params=pltpu.CompilerParams(
                collective_id=self.cid, has_side_effects=True, vmem_limit_bytes=VMEM_LIMIT
            ),
        )(*self.args)


VMEM_LIMIT = 58 << 20
ANY = pl.ANY
CHUNK = 512


def product(at, of, part, pairs, t):
    width, tok = at.width, part.shape[1]

    @pl.loop(0, part.shape[2] // CHUNK)
    def _(i):
        cols = pl.ds(pl.multiple_of(i * CHUNK, CHUNK), CHUNK)
        total = None
        for lhs, rhs, flip in pairs:
            if flip:
                term = dot(of(lhs)[t], of(rhs)[cols, :], 1, 1)
            else:
                term = dot(of(lhs)[t], of(rhs)[:, cols], 1, 0)
            total = term if total is None else total + term
        part[pl.ds(t * width, width), :, cols] = total.reshape(width, tok, CHUNK).astype(BF)


def products(at, of, part, pairs, red):
    for s in range(at.depth - 1, -1, -1):
        for t in [at.z + s, at.z - s] if s else [at.z]:

            @pl.when(jnp.logical_and(t >= 0, t < at.depth))
            def _(t=t):
                product(at, of, part, pairs, t)
                red.emit(t)


def gather_all(g, between=None):
    at = g.at
    for s in range(1, at.depth):
        g.step(s)
        if between is not None:
            between(s)
    for s in range(at.depth):
        for zz in [at.z - s, at.z + s] if s else [at.z]:

            @pl.when(jnp.logical_and(zz >= 0, zz < at.depth))
            def _(zz=zz):
                g.take_side(zz)


def place_own(at, src, buf, sem):
    copy = pltpu.make_async_copy(src, buf.at[at.j], sem)
    copy.start()
    copy.wait()


def front_call(n, x, small, ints, pieces, out_w):
    tok, d = x.shape
    _, k, c = pieces.shape
    call = Call(n, 1, "front")
    ix = call.give(x, ANY)
    ism, iin = call.give(small), call.give(ints)
    iw = call.give(pieces, ANY)
    ox = call.make((n, tok, d), BF, ANY)
    osm = call.make((n, 4) + small.shape, BF)
    oin = call.make((n,) + ints.shape, jnp.int32)
    ow = call.make((4, n, k, c), BF, ANY)
    sx = call.scratch(Gather.sems(n))
    sl = call.scratch([pltpu.SemaphoreType.DMA])
    ssm = call.scratch(SmallGather.sems(n))
    sin = call.scratch(Exchange.sems(n))
    sw = call.scratch(Columns.sems(n))
    if out_w is not None:
        io = call.give(out_w, ANY)
        oo = call.make((4,) + out_w.shape, BF, ANY)
        so = call.scratch(Rows.sems())

    def body(at, of):
        sm = SmallGather(at, of(ism), of(osm), of(ssm))
        g = Gather(at, of(ox), of(sx))
        cols = Columns(at, of(iw), of(ow), of(sw))
        spread = Spread(at, of(iin), of(oin), of(sin))
        sm.start()
        place_own(at, of(ix), of(ox), of(sl)[0])
        g.start()
        cols.start()
        spread.start()
        sm.step()
        if out_w is not None:
            rows = Rows(at, of(io), of(oo), of(so))
            rows.start()
        cuts = [0, n // 4, n // 2, n]

        def between(s):
            cols.step(cuts[s - 1], cuts[s])

        gather_all(g, between)
        cols.relay(0, n)
        if out_w is not None:
            rows.relay()
            rows.finish()
        cols.finish()
        g.finish()
        sm.finish()
        spread.finish()

    return call.run(body)


class Spread:
    def __init__(self, at, mine, got, sems):
        self.at, self.mine, self.got = at, mine, got
        self.ssem, self.rsem = sems

    def copy(self, to, src):
        at = self.at
        return remote(
            self.mine, self.got.at[src], self.ssem.at[to], self.rsem.at[src], at.seq(to)
        )

    def own(self):
        return pltpu.make_async_copy(self.mine, self.got.at[self.at.j], self.ssem.at[self.at.j])

    def start(self):
        self.own().start()

        @pl.loop(1, self.at.n)
        def _(i):
            self.copy(self.at.other(i), self.at.j).start()

    def finish(self):
        self.own().wait()

        @pl.loop(1, self.at.n)
        def _(i):
            p = self.at.other(i)
            self.copy(p, p).wait()


def sum_call(n, cid, name, pairs, tok, columns=(), rows=(), gathers=(), row_sums=(), col_sums=()):
    call = Call(n, cid, name)
    d = pairs[0][1].shape[0 if pairs[0][2] else 1]
    keys = []
    for lhs, rhs, flip in pairs:
        lhs = lhs.reshape(LINE, lhs.shape[0] // LINE, lhs.shape[1])
        keys.append((call.give(lhs), call.give(rhs), flip))
    out = call.make((tok, d), F32)
    part = call.scratch([pltpu.VMEM((n, tok, d), BF)])
    red_s = call.scratch(Reduce.scratch(n, tok, d))
    extra = Extras(call, n, columns, rows, gathers, row_sums, col_sums)

    def body(at, of):
        part_ref = of(part)[0]
        red = Reduce(at, part_ref, of(red_s))
        extra.bind(at, of)
        extra.start()
        products(at, of, part_ref, keys, red)
        for s in range(at.depth - 1, 0, -1):
            red.reduce(s)
            extra.between(at.depth - s)
        red.last(of(out))
        extra.finish()
        red.finish()

    flops = sum(2 * l.shape[0] * l.shape[1] * d for l, _, _ in pairs)
    return call.run(body, flops)


class Extras:
    def __init__(self, call, n, columns=(), rows=(), gathers=(), row_sums=(), col_sums=()):
        self.n = n
        self.columns = [
            (call.give(p, ANY), call.make((4,) + p.shape, BF, ANY), call.scratch(Columns.sems(n)))
            for p in columns
        ]
        self.rows = [
            (call.give(p, ANY), call.make((4,) + p.shape, BF, ANY), call.scratch(Rows.sems()))
            for p in rows
        ]
        self.gathers = [
            (
                call.give(p, ANY),
                call.make((n,) + p.shape, BF, ANY),
                call.scratch(Gather.sems(n)),
                call.scratch([pltpu.SemaphoreType.DMA]),
            )
            for p in gathers
        ]
        self.row_sums = [
            (
                call.give(p),
                call.make(p.shape[1:], F32),
                call.scratch(RowSum.scratch(*p.shape[1:])),
            )
            for p in row_sums
        ]
        self.col_sums = [
            (
                call.give(p.reshape(4, n * p.shape[2], p.shape[3])),
                call.make(p.shape[1:], BF),
                call.scratch(RowSum.scratch(n * p.shape[2], p.shape[3])),
                call.scratch([pltpu.VMEM(p.shape[1:], BF)]),
                call.scratch(Exchange.sems(n)),
            )
            for p in col_sums
        ]

    def bind(self, at, of):
        self.at, self.of = at, of
        self.b_columns = [Columns(at, of(i), of(o), of(s)) for i, o, s in self.columns]
        self.b_rows = [Rows(at, of(i), of(o), of(s)) for i, o, s in self.rows]
        self.b_gathers = [
            (Gather(at, of(o), of(s)), of(i), of(o), of(l)[0]) for i, o, s, l in self.gathers
        ]
        self.b_sums = [
            (RowSum(at, of(i), of(s)), of(o)) for i, o, s in self.row_sums
        ]
        self.b_cols = [
            (RowSum(at, of(i), of(s)), of(v)[0], Exchange(at, of(v)[0], of(o), of(e)))
            for i, o, s, v, e in self.col_sums
        ]

    def start(self):
        for rs, _ in self.b_sums:
            rs.start()
        for rs, _, _ in self.b_cols:
            rs.start()
        for g, src, buf, sem in self.b_gathers:
            place_own(self.at, src, buf, sem)
            g.start()
        for c in self.b_columns:
            c.start()
        for r in self.b_rows:
            r.start()
        for rs, _ in self.b_sums:
            rs.cross()
        for rs, _, _ in self.b_cols:
            rs.cross()

    def between(self, s):
        n = self.n
        cuts = [0, n // 4, n // 2, n]
        for g, _, _, _ in self.b_gathers:
            g.step(s)
        for c in self.b_columns:
            c.step(cuts[s - 1], cuts[s])
        if s == 2:
            for rs, mid, ex in self.b_cols:
                mid[...] = rs.total().reshape(mid.shape).astype(BF)
                ex.start()

    def finish(self):
        at = self.at
        for g, _, _, _ in self.b_gathers:
            for zz in range(at.depth):
                g.take_side(zz)
            g.finish()
        for r in self.b_rows:
            r.relay()
        for c in self.b_columns:
            c.relay(0, self.n)
        for r in self.b_rows:
            r.finish()
        for c in self.b_columns:
            c.finish()
        for rs, out in self.b_sums:
            out[...] = rs.total()
            rs.finish()
        for rs, _, ex in self.b_cols:
            ex.finish()
            rs.finish()


def gather_call(n, cid, name, x, columns=(), rows=(), row_sums=(), col_sums=()):
    call = Call(n, cid, name)
    extra = Extras(call, n, columns, rows, [x], row_sums, col_sums)

    def body(at, of):
        extra.bind(at, of)
        extra.start()
        for s in range(1, at.depth):
            extra.between(s)
        extra.finish()

    return call.run(body)


def last_call(n, cid, pairs, tok, normed, known, row_sums, col_sums):
    call = Call(n, cid, "last")
    d = pairs[0][1].shape[0]
    keys = []
    for lhs, rhs, flip in pairs:
        lhs = lhs.reshape(LINE, lhs.shape[0] // LINE, lhs.shape[1])
        keys.append((call.give(lhs), call.give(rhs), flip))
    i_norm, i_known = call.give(normed), call.give(known)
    out = call.make((tok, d), F32)
    o_small = call.make((8, d // 4), F32)
    part = call.scratch([pltpu.VMEM((n, tok, d), BF)])
    red_s = call.scratch(Reduce.scratch(n, tok, d))
    s_small = call.scratch(SmallSum.scratch(n, d))
    extra = Extras(call, n, row_sums=row_sums, col_sums=col_sums)

    def body(at, of):
        part_ref = of(part)[0]
        red = Reduce(at, part_ref, of(red_s))
        extra.bind(at, of)
        extra.start()
        products(at, of, part_ref, keys, red)
        for s in range(at.depth - 1, 0, -1):
            red.reduce(s)
            extra.between(at.depth - s)
        red.last(of(out))
        small = SmallSum(at, of(s_small))
        small.terms[...] = of(i_known)[...]
        grad = of(out)[...]
        small.terms[0:1, :] = jnp.sum(grad * of(i_norm)[...], axis=0, keepdims=True)
        small.terms[1:2, :] = jnp.sum(grad, axis=0, keepdims=True)
        small.run(of(o_small))
        extra.finish()
        red.finish()

    return call.run(body)


def attention(queries, keys, values, allowed):
    scores = jnp.einsum("qhd,khd->hqk", queries, keys, preferred_element_type=F32)
    exp_weights = jnp.where(allowed[None], jnp.exp(scores), 0.0)
    denominator = jnp.sum(exp_weights, axis=-1)
    numerator = jnp.einsum(
        "hqk,khd->qhd", exp_weights.astype(BF), values, preferred_element_type=F32
    )
    return numerator / jnp.transpose(denominator)[:, :, None], denominator


def attention_back(queries, keys, values, allowed, denominator, context, g_context):
    den = jnp.transpose(denominator)
    g_numer = (g_context / den[:, :, None]).astype(BF)
    g_den = jnp.transpose(-jnp.sum(g_context * context, axis=-1) / den)
    scores = jnp.einsum("qhd,khd->hqk", queries, keys, preferred_element_type=F32)
    exp_weights = jnp.where(allowed[None], jnp.exp(scores), 0.0)
    g_values = jnp.einsum(
        "hqk,qhd->khd", exp_weights.astype(BF), g_numer, preferred_element_type=F32
    )
    g_weights = jnp.einsum("qhd,khd->hqk", g_numer, values, preferred_element_type=F32)
    g_scores = (exp_weights * (g_weights + g_den[:, :, None])).astype(BF)
    g_queries = jnp.einsum("hqk,khd->qhd", g_scores, keys, preferred_element_type=F32)
    g_keys = jnp.einsum("hqk,qhd->khd", g_scores, queries, preferred_element_type=F32)
    return g_queries, g_keys, g_values


def body(nrow, n, *args):
    (
        layer_in,
        segments,
        positions,
        attn_norm_gain,
        attn_norm_bias,
        qkv_weight,
        qkv_bias,
        out_weight,
        mlp_norm_gain,
        mlp_norm_bias,
        gate_weight,
        up_weight,
        down_weight,
        out_grad,
    ) = args
    j = lax.axis_index("seq")
    tok = layer_in.shape[1]
    length = n * tok
    k = qkv_weight.shape[0]
    f = down_weight.shape[0]
    hp = H // n
    whole_heads = out_weight.shape[0] == HD

    def split_heads(w):
        lead = w.shape[0]
        if whole_heads:
            w = w.reshape(lead, 3, nrow, n, HD).transpose(3, 0, 1, 2, 4)
        else:
            w = w.reshape(lead, 3, n, hp, HD).transpose(2, 0, 1, 3, 4)
        return w.reshape(n, lead, 3 * hp * HD)

    def join_heads(blocks):
        lead = blocks.shape[1]
        if whole_heads:
            w = blocks.reshape(n, lead, 3, nrow, HD).transpose(1, 2, 3, 0, 4)
        else:
            w = blocks.reshape(n, lead, 3, hp, HD).transpose(1, 2, 0, 3, 4)
        return w.reshape(lead, 3 * D)

    def split_ff(w):
        return w.reshape(k, nrow, n, f).transpose(2, 0, 1, 3).reshape(n, k, nrow * f)

    def join_ff(blocks):
        return blocks.reshape(n, k, nrow, f).transpose(1, 2, 0, 3).reshape(k, nrow * n * f)

    small = jnp.concatenate(
        [attn_norm_gain, attn_norm_bias, mlp_norm_gain, mlp_norm_bias, qkv_bias]
    )
    small = jnp.pad(small, (0, 2048 - small.shape[0])).reshape(16, 128)
    ints = jnp.concatenate([segments, positions, jnp.zeros((6, tok), jnp.int32)], 0)
    front = front_call(
        n, layer_in[0], small, ints, split_heads(qkv_weight), out_weight if whole_heads else None
    )
    x_all, small_all, ints_all, qkv_own = front[:4]
    x_all = x_all.reshape(length, D)
    qkv_own = qkv_own.reshape(D, 3 * hp * HD)
    if whole_heads:
        out_own = front[4].reshape(hp * HD, D)
    else:
        out_full = lax.all_gather(out_weight, ("row", "seq"), axis=0, tiled=True)
        out_own = lax.dynamic_slice_in_dim(out_full, j * hp * HD, hp * HD, 0)
    small_all = small_all.transpose(1, 0, 2, 3).reshape(nrow * n, 2048)
    attn_gain, attn_bias, mlp_gain, mlp_bias = (
        small_all[:, c : c + k].reshape(1, D).astype(F32) for c in (0, k, 2 * k, 3 * k)
    )
    qkv_shift = small_all[:, 4 * k : 4 * k + 3 * k].reshape(1, 3 * D)
    shift_own = lax.dynamic_index_in_dim(split_heads(qkv_shift), j, 0, keepdims=False).astype(F32)
    seg_all, pos_all = ints_all[:, 0].reshape(length), ints_all[:, 1].reshape(length)

    inputs_all = (norm_stats(x_all.astype(F32))[0] * attn_gain + attn_bias).astype(BF)
    projected = dot(inputs_all, qkv_own, 1, 0) + shift_own
    head_split = projected.reshape(length, 3, hp, HD)
    cosine, sine_part = rotary_tables(pos_all)
    queries = (rotate(head_split[:, 0], cosine, sine_part, 1.0) / math.sqrt(HD)).astype(BF)
    keys = rotate(head_split[:, 1], cosine, sine_part, 1.0).astype(BF)
    values = head_split[:, 2].astype(BF)
    index = jnp.arange(length, dtype=jnp.int32)
    allowed = (seg_all[:, None] == seg_all[None, :]) & (index[None, :] <= index[:, None])
    context, denominator = attention(queries, keys, values, allowed)
    context_low = context.reshape(length, hp * HD).astype(BF)
    attn_branch, gate_own, up_own = sum_call(
        n, 2, "mix_sum", [(context_low, out_own, False)], tok,
        columns=[split_ff(gate_weight), split_ff(up_weight)],
    )
    gate_own, up_own = gate_own.reshape(D, nrow * f), up_own.reshape(D, nrow * f)

    x_float = layer_in[0].astype(F32)
    normed1, inv_std1 = norm_stats(x_float)
    hidden_mid = x_float + attn_branch
    normed2, inv_std2 = norm_stats(hidden_mid)
    middle = (normed2 * mlp_gain + mlp_bias).astype(BF)
    down_own, middle_all = gather_call(n, 3, "middle", middle, rows=[down_weight])
    down_own, middle_all = down_own.reshape(nrow * f, D), middle_all.reshape(length, D)
    gate_pre = dot(middle_all, gate_own, 1, 0)
    up_pre = dot(middle_all, up_own, 1, 0)
    sig = jax.nn.sigmoid(gate_pre)
    silu = gate_pre * sig
    inner_act = (silu * up_pre).astype(BF)
    mlp_branch, grad_all = sum_call(
        n, 4, "mlp_sum", [(inner_act, down_own, False)], tok, gathers=[out_grad[0]]
    )
    grad_all = grad_all.reshape(length, D)
    layer_out = (hidden_mid + mlp_branch).astype(BF)

    grad_float = out_grad[0].astype(F32)
    g_inner = dot(grad_all, down_own, 1, 1)
    g_gate = (g_inner * up_pre * sig * (1.0 + gate_pre * (1.0 - sig))).astype(BF)
    g_up = (g_inner * silu).astype(BF)
    down_part = dot(inner_act, grad_all, 0, 0).astype(BF).reshape(nrow, f, D)
    gate_part = dot(middle_all, g_gate, 0, 0).astype(BF).reshape(nrow, n, k, nrow * f)
    up_part = dot(middle_all, g_up, 0, 0).astype(BF).reshape(nrow, n, k, nrow * f)
    g_middle, down_grad, gate_blocks = sum_call(
        n, 5, "mlp_back", [(g_gate, gate_own, True), (g_up, up_own, True)], tok,
        row_sums=[down_part], col_sums=[gate_part],
    )
    gate_grad = join_ff(gate_blocks).astype(F32)
    g_hidden = grad_float + norm_back(g_middle, normed2, inv_std2, mlp_gain)
    g_attn_all, up_blocks = gather_call(
        n, 6, "hidden_back", g_hidden.astype(BF), col_sums=[up_part]
    )
    g_attn_all = g_attn_all.reshape(length, D)
    up_grad = join_ff(up_blocks).astype(F32)

    out_part = dot(context_low, g_attn_all, 0, 0)
    g_context = dot(g_attn_all, out_own, 1, 1).reshape(length, hp, HD)
    g_queries, g_keys, g_values = attention_back(
        queries, keys, values, allowed, denominator, context, g_context
    )
    query_part = rotate(g_queries, cosine, sine_part, -1.0) / math.sqrt(HD)
    key_part = rotate(g_keys, cosine, sine_part, -1.0)
    g_projected = (
        jnp.stack([query_part, key_part, g_values], 1).reshape(length, 3 * hp * HD).astype(BF)
    )
    qkv_part = dot(inputs_all, g_projected, 0, 0).astype(BF).reshape(nrow, n, k, 3 * hp * HD)
    shift_sum = jnp.sum(g_projected.astype(F32), axis=0)
    shift_blocks = lax.dynamic_update_slice_in_dim(
        jnp.zeros((n, 1, 3 * hp * HD), F32), shift_sum[None, None], j, 0
    )
    shift_full = join_heads(shift_blocks)[0]
    known = jnp.concatenate(
        [
            jnp.zeros((2, D), F32),
            jnp.sum(g_middle * normed2, axis=0)[None],
            jnp.sum(g_middle, axis=0)[None],
            shift_full.reshape(nrow, 3, D // nrow).transpose(1, 0, 2).reshape(3, D),
            jnp.zeros((1, D), F32),
        ]
    )
    last = last_call(
        n, 7, [(g_projected, qkv_own, True)], tok, normed1, known,
        [out_part.astype(BF).reshape((nrow,) + out_weight.shape)] if whole_heads else [],
        [qkv_part],
    )
    if whole_heads:
        g_inputs, small_grads, out_w_grad, qkv_blocks = last
    else:
        g_inputs, small_grads, qkv_blocks = last
        placed = lax.dynamic_update_slice_in_dim(
            jnp.zeros((D, D), BF), out_part.astype(BF), j * hp * HD, 0
        )
        out_w_grad = lax.psum_scatter(
            placed, ("row", "seq"), scatter_dimension=0, tiled=True
        ).astype(F32)
    qkv_grad = join_heads(qkv_blocks).astype(F32)
    input_grad = g_hidden + norm_back(g_inputs, normed1, inv_std1, attn_gain)
    own = lax.dynamic_slice_in_dim(small_grads, j * k, k, 1)
    shift_own_grad = lax.dynamic_slice_in_dim(small_grads[4:7].reshape(-1), j * 3 * k, 3 * k, 0)
    return (
        layer_out[None],
        input_grad[None],
        own[0],
        own[1],
        qkv_grad,
        shift_own_grad,
        out_w_grad,
        own[2],
        own[3],
        gate_grad,
        up_grad,
        down_grad,
    )


def solution(mesh):
    nrow, n = mesh.shape["row"], mesh.shape["seq"]

    def local(*args):
        return body(nrow, n, *args)

    tokens, ints = P("row", "seq", None), P("row", "seq")
    vec, mat = P(("row", "seq")), P(("row", "seq"), None)
    return jax.shard_map(
        local,
        mesh=mesh,
        in_specs=(
            tokens, ints, ints, vec, vec, mat, vec, mat, vec, vec, mat, mat, mat, tokens,
        ),
        out_specs=(tokens, tokens, vec, vec, mat, vec, mat, vec, vec, mat, mat, mat),
        check_vma=False,
    )
```

```python
import math

import jax
import jax.numpy as jnp
from jax import lax
from jax.experimental import pallas as pl
from jax.experimental.pallas import tpu as pltpu
from jax.sharding import PartitionSpec as P

D = 2048
H = 32
HD = 64
ROT = 16
EPSILON = 1e-05
BF = jnp.bfloat16
F32 = jnp.float32


def dot(a, b, ca, cb):
    return lax.dot_general(a, b, (((ca,), (cb,)), ((), ())), preferred_element_type=F32)


def norm_stats(values_in):
    average = jnp.mean(values_in, axis=-1, keepdims=True)
    centered = values_in - average
    inv_std = lax.rsqrt(jnp.mean(centered * centered, axis=-1, keepdims=True) + EPSILON)
    return (centered * inv_std, inv_std)


def norm_back(grad_in, normed, inv_std, gain_vector):
    scaled = grad_in * gain_vector
    return inv_std * (
        scaled
        - jnp.mean(scaled, axis=-1, keepdims=True)
        - normed * jnp.mean(scaled * normed, axis=-1, keepdims=True)
    )


def rotary_tables(positions):
    half_rot = ROT // 2
    frequency = 10000.0 ** (-2.0 * jnp.arange(half_rot, dtype=F32) / ROT)
    angles = positions.astype(F32)[:, None] * frequency[None, :]
    return (jnp.cos(angles)[:, None, :], jnp.sin(angles)[:, None, :])


def rotate(head_values, cosine, sine_part, direction):
    half_rot = ROT // 2
    first_half = head_values[..., :half_rot]
    second = head_values[..., half_rot:ROT]
    return jnp.concatenate(
        [
            first_half * cosine - direction * second * sine_part,
            second * cosine + direction * first_half * sine_part,
            head_values[..., ROT:],
        ],
        axis=-1,
    )


MESH = pl.DeviceIdType.MESH
LINE = 4


class Place:
    def __init__(self, n):
        self.n = n
        self.depth = LINE
        self.width = n // LINE
        self.r = lax.axis_index("row")
        self.j = lax.axis_index("seq")
        self.z = self.j // self.width
        self.x = lax.rem(self.j, self.width)
        y, c = self.r // 2, lax.rem(self.r, 2)
        self.y, self.c = y, c
        self.r_y = (1 - y) * 2 + c
        self.r_c = y * 2 + (1 - c)
        self.r_yc = (1 - y) * 2 + (1 - c)

    def seq(self, j):
        return (self.r, j)

    def row(self, r):
        return (r, self.j)

    def other(self, i):
        return lax.rem(self.j + i, self.n)

    def meet(self):
        barrier = pltpu.get_barrier_semaphore()
        for r in (self.r_y, self.r_c, self.r_yc):
            pl.semaphore_signal(barrier, inc=1, device_id=self.row(r), device_id_type=MESH)
        for i in range(1, self.n):
            pl.semaphore_signal(
                barrier, inc=1, device_id=self.seq(self.other(i)), device_id_type=MESH
            )
        pl.semaphore_wait(barrier, self.n + 2)


def remote(src, dst, ssem, rsem, device):
    return pltpu.make_async_remote_copy(
        src_ref=src, dst_ref=dst, send_sem=ssem, recv_sem=rsem, device_id=device,
        device_id_type=MESH,
    )


ALONE = ((1, True), (3, False), (4, False))
PAIRED = ((2, True), (3, False), (3, False))
PIECES = 2
MLP_CUTS = ((2, True), (3, False), (3, False))
MLP_PIECES = 2


class Gather:
    @staticmethod
    def sems(n, cuts):
        w = n // LINE
        out = []
        for _ in cuts:
            out += [
                pltpu.SemaphoreType.DMA((2, n)),
                pltpu.SemaphoreType.DMA((LINE, max(w - 1, 1))),
                pltpu.SemaphoreType.DMA((n,)),
            ]
        return out

    def __init__(self, at, buf, sems, cuts):
        self.at, self.buf = at, buf
        tok = buf.shape[1]
        self.cuts = []
        first = 0
        for i, (share, wide) in enumerate(cuts):
            rows = tok * share // 8
            self.cuts.append((pl.ds(first, rows), wide, sems[3 * i : 3 * i + 3]))
            first += rows

    def copy(self, cut, b, to, sem):
        here = self.buf.at[b, cut[0]]
        return remote(here, here, sem, cut[2][2].at[b], self.at.seq(to))

    def along(self, cut, way, b):
        at = self.at
        to = at.j + at.width if way == 0 else at.j - at.width
        return self.copy(cut, b, to, cut[2][0].at[way, b])

    def across(self, cut, zz, i):
        at = self.at
        to = at.z * at.width + lax.rem(at.x + i, at.width)
        return self.copy(cut, zz * at.width + at.x, to, cut[2][1].at[zz, i - 1])

    def take(self, cut, b):
        self.copy(cut, b, self.at.other(1), cut[2][0].at[0, 0]).wait_recv()

    def onward(self, cut, way, b):
        at = self.at

        @pl.when(at.z < at.depth - 1 if way == 0 else at.z > 0)
        def _():
            self.along(cut, way, b).start()

    def start(self):
        at = self.at
        for cut in self.cuts:
            if cut[1]:
                for i in range(1, at.width):
                    self.across(cut, at.z, i).start()
        for cut in self.cuts:
            for way in range(2):
                self.onward(cut, way, at.j)
            if not cut[1]:
                for i in range(1, at.width):
                    self.across(cut, at.z, i).start()

    def step(self, s):
        at = self.at
        for cut in self.cuts:
            if s == 1 and cut[1]:
                for i in range(1, at.width):
                    b = at.z * at.width + lax.rem(at.x + i, at.width)
                    self.take(cut, b)
                    for way in range(2):
                        self.onward(cut, way, b)
        for cut in self.cuts:
            for way in range(2):
                zz = at.z - s if way == 0 else at.z + s

                @pl.when(zz >= 0 if way == 0 else zz < at.depth)
                def _(zz=zz, way=way, cut=cut):
                    if cut[1]:
                        for i in range(at.width):
                            b = zz * at.width + lax.rem(at.x + i, at.width)
                            self.take(cut, b)
                            self.onward(cut, way, b)
                    else:
                        b = zz * at.width + at.x
                        self.take(cut, b)
                        self.onward(cut, way, b)
                        for i in range(1, at.width):
                            self.across(cut, zz, i).start()

    def fetch(self, zz):
        at = self.at
        for way in range(2):

            @pl.when(zz < at.z if way == 0 else zz > at.z)
            def _(way=way):
                for cut in self.cuts:
                    for i in range(at.width if cut[1] else 1):
                        b = zz * at.width + lax.rem(at.x + i, at.width)
                        self.take(cut, b)
                        self.onward(cut, way, b)
                    if not cut[1]:
                        for i in range(1, at.width):
                            self.across(cut, zz, i).start()

    def open_wide(self):
        at = self.at
        for cut in self.cuts:
            if cut[1]:
                for i in range(1, at.width):
                    b = at.z * at.width + lax.rem(at.x + i, at.width)
                    self.take(cut, b)
                    for way in range(2):
                        self.onward(cut, way, b)

    def take_side(self, zz):
        at = self.at
        for cut in self.cuts:
            if not cut[1]:
                for i in range(1, at.width):
                    self.take(cut, zz * at.width + lax.rem(at.x + i, at.width))

    def finish(self):
        at = self.at
        for cut in self.cuts:
            for zz in range(at.depth):
                for i in range(1, at.width):
                    if cut[1]:
                        @pl.when(at.z == zz)
                        def _(zz=zz, i=i, cut=cut):
                            self.across(cut, zz, i).wait_send()
                    else:
                        self.across(cut, zz, i).wait_send()
                for way in range(2):
                    ok = jnp.logical_and(at.z >= zz, at.z < at.depth - 1) if way == 0 else jnp.logical_and(at.z <= zz, at.z > 0)

                    @pl.when(ok)
                    def _(zz=zz, way=way, cut=cut):
                        for i in range(at.width if cut[1] else 1):
                            b = zz * at.width + lax.rem(at.x + i, at.width)
                            self.along(cut, way, b).wait_send()


class Reduce:
    @staticmethod
    def scratch(n, tok, d, cuts):
        side = max(n // LINE - 1, 1)
        return (
            [pltpu.VMEM((LINE, side, tok, d), BF), pltpu.VMEM((LINE + 1, tok, d), BF)]
            + [pltpu.SemaphoreType.DMA((LINE, side * cuts))] * 2
            + [pltpu.SemaphoreType.DMA((LINE, cuts)), pltpu.SemaphoreType.DMA((LINE + 1, cuts))]
        )

    def __init__(self, at, part, refs, cuts):
        self.at, self.part, self.cuts = at, part, cuts
        self.xr, self.lr, self.xs_sem, self.xr_sem, self.ls_sem, self.lr_sem = refs
        self.size = part.shape[1] // cuts

    def rows(self, h):
        return pl.ds(h * self.size, self.size)

    def across(self, t, i, h):
        at = self.at
        xx = lax.rem(at.x + i, at.width)
        k = (i - 1) * self.cuts + h
        return remote(
            self.part.at[t * at.width + xx, self.rows(h)], self.xr.at[t, i - 1, self.rows(h)],
            self.xs_sem.at[t, k], self.xr_sem.at[t, k], at.seq(at.z * at.width + xx),
        )

    def along(self, t, h):
        at = self.at
        there = jnp.where(t > at.z, at.j + at.width, at.j - at.width)
        slot = jnp.where(t == at.z - 1, at.depth, t)
        return remote(
            self.part.at[t * at.width + at.x, self.rows(h)], self.lr.at[slot, self.rows(h)],
            self.ls_sem.at[t, h], self.lr_sem.at[slot, h], at.seq(there),
        )

    def landed(self, slot, h):
        at = self.at
        remote(
            self.lr.at[slot, self.rows(h)], self.lr.at[slot, self.rows(h)], self.ls_sem.at[0, h],
            self.lr_sem.at[slot, h], at.seq(at.other(1)),
        ).wait_recv()

    def emit(self, t):
        for h in range(self.cuts):
            for i in range(1, self.at.width):
                self.across(t, i, h).start()

    def summed(self, t, h):
        at = self.at
        total = self.part[t * at.width + at.x, self.rows(h)].astype(F32)
        for i in range(1, at.width):
            self.across(t, i, h).wait_recv()
            total = total + self.xr[t, i - 1, self.rows(h)].astype(F32)
        return total

    def pass_on(self, t):
        at = self.at
        inner = jnp.logical_or(
            jnp.logical_and(t > at.z, at.z > 0), jnp.logical_and(t < at.z, at.z < at.depth - 1)
        )
        for h in range(self.cuts):
            block = (t * at.width + at.x, self.rows(h))
            total = self.summed(t, h)

            @pl.when(inner)
            def _(block=block, total=total, h=h):
                self.landed(t, h)
                self.part[block] = (total + self.lr[t, self.rows(h)].astype(F32)).astype(BF)

            @pl.when(jnp.logical_not(inner))
            def _(block=block, total=total):
                self.part[block] = total.astype(BF)

            self.along(t, h).start()

    def reduce(self, s):
        at = self.at
        for t in (at.z + s, at.z - s):

            @pl.when(jnp.logical_and(t >= 0, t < at.depth))
            def _(t=t):
                self.pass_on(t)

    def last(self, out):
        at = self.at
        for h in range(self.cuts):
            out[self.rows(h)] = self.summed(at.z, h)

        for h in range(self.cuts):

            @pl.when(at.z > 0)
            def _(h=h):
                self.landed(at.z, h)
                out[self.rows(h)] += self.lr[at.z, self.rows(h)].astype(F32)

            @pl.when(at.z < at.depth - 1)
            def _(h=h):
                self.landed(at.depth, h)
                out[self.rows(h)] += self.lr[at.depth, self.rows(h)].astype(F32)

    def finish(self):
        at = self.at
        for t in range(at.depth):
            for h in range(self.cuts):
                for i in range(1, at.width):
                    self.across(t, i, h).wait_send()

                @pl.when(at.z != t)
                def _(t=t, h=h):
                    self.along(t, h).wait_send()


class Columns:
    @staticmethod
    def sems(n):
        return [pltpu.SemaphoreType.DMA((4, n)), pltpu.SemaphoreType.DMA((4, n))]

    def __init__(self, at, pieces, full, sems):
        self.at, self.pieces, self.full = at, pieces, full
        self.ssem, self.rsem = sems

    def first(self, i):
        at = self.at
        to = at.other(i)
        return remote(
            self.pieces.at[to], self.full.at[at.r, at.j], self.ssem.at[0, to],
            self.rsem.at[at.r, at.j], at.seq(to),
        )

    def own(self):
        at = self.at
        return pltpu.make_async_copy(
            self.pieces.at[at.j], self.full.at[at.r, at.j], self.ssem.at[0, at.j]
        )

    def pass_on(self, r, js, to, k):
        return remote(
            self.full.at[r, js], self.full.at[r, js], self.ssem.at[k, js], self.rsem.at[r, js],
            self.at.row(to),
        )

    def take(self, r, js):
        self.pass_on(r, js, self.at.r_c, 0).wait_recv()

    def start(self):
        at = self.at
        self.own().start()

        @pl.loop(1, at.n)
        def _(i):
            self.first(i).start()

    def step(self, lo, hi):
        at = self.at

        @pl.loop(lo, hi)
        def _(i):
            js = lax.rem(at.j + at.n - i, at.n)

            @pl.when(i == 0)
            def _():
                self.own().wait()

            @pl.when(i > 0)
            def _():
                self.take(at.r, js)

            self.pass_on(at.r, js, at.r_y, 1).start()
            self.pass_on(at.r, js, at.r_c, 2).start()

    def relay(self, lo, hi):
        at = self.at

        @pl.loop(lo, hi)
        def _(i):
            js = lax.rem(at.j + at.n - i, at.n)
            self.take(at.r_y, js)
            self.pass_on(at.r_y, js, at.r_c, 3).start()

    def finish(self):
        at = self.at

        @pl.loop(0, at.n)
        def _(js):
            self.take(at.r_c, js)
            self.take(at.r_yc, js)
            self.pass_on(at.r, js, at.r_y, 1).wait_send()
            self.pass_on(at.r, js, at.r_c, 2).wait_send()
            self.pass_on(at.r_y, js, at.r_c, 3).wait_send()

        @pl.loop(1, at.n)
        def _(i):
            self.first(i).wait_send()


class Rows:
    @staticmethod
    def sems():
        return [pltpu.SemaphoreType.DMA((4,)), pltpu.SemaphoreType.DMA((4,))]

    def __init__(self, at, shard, full, sems):
        self.at, self.shard, self.full = at, shard, full
        self.ssem, self.rsem = sems

    def own(self):
        return pltpu.make_async_copy(self.shard, self.full.at[self.at.r], self.ssem.at[0])

    def direct(self, to, k):
        r = self.at.r
        return remote(
            self.shard, self.full.at[r], self.ssem.at[k], self.rsem.at[r], self.at.row(to)
        )

    def onward(self):
        at = self.at
        r = at.r_y
        return remote(
            self.full.at[r], self.full.at[r], self.ssem.at[3], self.rsem.at[r], at.row(at.r_c)
        )

    def take(self, r):
        at = self.at
        remote(
            self.full.at[r], self.full.at[r], self.ssem.at[0], self.rsem.at[r], at.row(at.r_c)
        ).wait_recv()

    def start(self):
        at = self.at
        self.own().start()
        self.direct(at.r_y, 1).start()
        self.direct(at.r_c, 2).start()

    def relay(self):
        self.take(self.at.r_y)
        self.onward().start()

    def finish(self):
        at = self.at
        self.own().wait()
        self.take(at.r_c)
        self.take(at.r_yc)
        self.direct(at.r_y, 1).wait_send()
        self.direct(at.r_c, 2).wait_send()
        self.onward().wait_send()


class RowSum:
    @staticmethod
    def scratch(m, c):
        return [
            pltpu.VMEM((2, m, c), BF),
            pltpu.VMEM((m, c), BF),
            pltpu.VMEM((m, c), BF),
            pltpu.SemaphoreType.DMA((3,)),
            pltpu.SemaphoreType.DMA((3,)),
        ]

    def __init__(self, at, grad, refs):
        self.at, self.grad = at, grad
        self.core_in, self.y_out, self.y_in, self.ssem, self.rsem = refs

    def to_core(self, far):
        at = self.at
        yy = 1 - at.y if far else at.y
        k = 1 if far else 0
        return remote(
            self.grad.at[yy * 2 + 1 - at.c], self.core_in.at[k], self.ssem.at[k], self.rsem.at[k],
            at.row(at.r_c),
        )

    def over_y(self):
        at = self.at
        return remote(
            self.y_out, self.y_in, self.ssem.at[2], self.rsem.at[2], at.row(at.r_y)
        )

    def start(self):
        self.to_core(1).start()
        self.to_core(0).start()

    def cross(self):
        at = self.at
        self.to_core(1).wait_recv()
        self.y_out[...] = (
            self.grad[at.r_y].astype(F32) + self.core_in[1].astype(F32)
        ).astype(BF)
        self.over_y().start()

    def total(self):
        at = self.at
        self.to_core(0).wait_recv()
        self.over_y().wait_recv()
        return (
            self.grad[at.r].astype(F32) + self.core_in[0].astype(F32) + self.y_in[...].astype(F32)
        )

    def finish(self):
        self.to_core(1).wait_send()
        self.to_core(0).wait_send()
        self.over_y().wait_send()


class Exchange:
    @staticmethod
    def sems(n):
        return [pltpu.SemaphoreType.DMA((n,)), pltpu.SemaphoreType.DMA((n,))]

    def __init__(self, at, mine, got, sems):
        self.at, self.mine, self.got = at, mine, got
        self.ssem, self.rsem = sems

    def send(self, i):
        at = self.at
        to = at.other(i)
        return remote(
            self.mine.at[to], self.got.at[at.j], self.ssem.at[to], self.rsem.at[at.j], at.seq(to)
        )

    def own(self):
        at = self.at
        return pltpu.make_async_copy(
            self.mine.at[at.j], self.got.at[at.j], self.ssem.at[at.j]
        )

    def start(self):
        self.own().start()

        @pl.loop(1, self.at.n)
        def _(i):
            self.send(i).start()

    def finish(self):
        at = self.at
        self.own().wait()

        @pl.loop(1, at.n)
        def _(i):
            src = at.other(i)
            remote(
                self.mine.at[src], self.got.at[src], self.ssem.at[src], self.rsem.at[src],
                at.seq(src),
            ).wait()


class SmallGather:
    @staticmethod
    def sems(n):
        return [pltpu.SemaphoreType.DMA((4,))] * 2 + [pltpu.SemaphoreType.DMA((n,))] * 2

    def __init__(self, at, mine, full, sems):
        self.at, self.mine, self.full = at, mine, full
        self.rs, self.rr, self.ss, self.sr = sems

    def beside(self, r):
        at = self.at
        return remote(
            self.mine, self.full.at[at.j, at.r], self.rs.at[r], self.rr.at[at.r], at.row(r)
        )

    def own(self):
        at = self.at
        return pltpu.make_async_copy(self.mine, self.full.at[at.j, at.r], self.rs.at[at.r])

    def onward(self, to):
        at = self.at
        return remote(
            self.full.at[at.j], self.full.at[at.j], self.ss.at[to], self.sr.at[at.j], at.seq(to)
        )

    def start(self):
        at = self.at
        self.own().start()
        for r in (at.r_y, at.r_c, at.r_yc):
            self.beside(r).start()

    def step(self):
        at = self.at
        self.own().wait()
        for r in (at.r_y, at.r_c, at.r_yc):
            remote(
                self.mine, self.full.at[at.j, r], self.rs.at[r], self.rr.at[r], at.row(r)
            ).wait()

        @pl.loop(1, at.n)
        def _(i):
            self.onward(at.other(i)).start()

    def finish(self):
        at = self.at

        @pl.loop(1, at.n)
        def _(i):
            src = at.other(i)
            remote(
                self.full.at[src], self.full.at[src], self.ss.at[src], self.sr.at[src],
                at.seq(src),
            ).wait()


class SmallSum:
    @staticmethod
    def scratch(n, w):
        q = w // 4
        return (
            [pltpu.VMEM((8, w), F32), pltpu.VMEM((4, 8, q), F32), pltpu.VMEM((8, q), F32)]
            + [pltpu.VMEM((n, 8, q), F32)]
            + [pltpu.SemaphoreType.DMA((4,))] * 2
            + [pltpu.SemaphoreType.DMA((n,))] * 2
        )

    def __init__(self, at, refs):
        self.at = at
        self.terms, self.beside_in, self.acc, self.seq_in = refs[:4]
        self.rs, self.rr, self.ss, self.sr = refs[4:]
        self.q = self.terms.shape[1] // 4

    def part(self, r):
        return self.terms.at[:, pl.ds(pl.multiple_of(r * self.q, self.q), self.q)]

    def beside(self, r):
        at = self.at
        return remote(
            self.part(r), self.beside_in.at[at.r], self.rs.at[r], self.rr.at[at.r], at.row(r)
        )

    def run(self, out):
        at = self.at
        near = (at.r_y, at.r_c, at.r_yc)
        for r in near:
            self.beside(r).start()
        self.acc[...] = self.part(at.r)[...]
        for r in near:
            remote(
                self.part(r), self.beside_in.at[r], self.rs.at[r], self.rr.at[r], at.row(r)
            ).wait()
            self.acc[...] += self.beside_in[r]

        @pl.loop(1, at.n)
        def _(i):
            to = at.other(i)
            remote(
                self.acc, self.seq_in.at[at.j], self.ss.at[to], self.sr.at[at.j], at.seq(to)
            ).start()

        out[...] = self.acc[...]

        @pl.loop(1, at.n)
        def _(i):
            src = at.other(i)
            remote(
                self.acc, self.seq_in.at[src], self.ss.at[src], self.sr.at[src], at.seq(src)
            ).wait()
            out[...] += self.seq_in[src]


class Call:
    def __init__(self, n, cid, name):
        self.n, self.cid, self.name = n, cid, name
        self.args, self.ins, self.outs, self.out_specs, self.scr = [], [], [], [], []

    def give(self, array, space=pltpu.VMEM):
        self.args.append(array)
        self.ins.append(pl.BlockSpec(memory_space=space))
        return ("i", len(self.args) - 1)

    def make(self, shape, dtype, space=pltpu.VMEM):
        self.outs.append(jax.ShapeDtypeStruct(shape, dtype))
        self.out_specs.append(pl.BlockSpec(memory_space=space))
        return ("o", len(self.outs) - 1)

    def scratch(self, items):
        at = len(self.scr)
        self.scr.extend(items)
        return [("s", at + i) for i in range(len(items))]

    def run(self, body, flops=0):
        ni, no = len(self.ins), len(self.outs)

        def kernel(*refs):
            def of(key):
                if isinstance(key, list):
                    return [of(k) for k in key]
                kind, i = key
                return refs[i + {"i": 0, "o": ni, "s": ni + no}[kind]]

            at = Place(self.n)
            at.meet()
            body(at, of)

        return pl.pallas_call(
            kernel,
            out_shape=self.outs,
            in_specs=self.ins,
            out_specs=self.out_specs,
            scratch_shapes=self.scr,
            name=self.name,
            cost_estimate=pl.CostEstimate(
                flops=flops, bytes_accessed=1 << 24, transcendentals=0
            ),
            compiler_params=pltpu.CompilerParams(
                collective_id=self.cid, has_side_effects=True, vmem_limit_bytes=VMEM_LIMIT
            ),
        )(*self.args)


VMEM_LIMIT = 58 << 20
ANY = pltpu.VMEM
CHUNK = 512


def product(at, of, part, pairs, t):
    width, tok = at.width, part.shape[1]

    @pl.loop(0, part.shape[2] // CHUNK)
    def _(i):
        cols = pl.ds(pl.multiple_of(i * CHUNK, CHUNK), CHUNK)
        total = None
        for lhs, rhs, flip in pairs:
            if flip:
                term = dot(of(lhs)[t], of(rhs)[cols, :], 1, 1)
            else:
                term = dot(of(lhs)[t], of(rhs)[:, cols], 1, 0)
            total = term if total is None else total + term
        part[pl.ds(t * width, width), :, cols] = total.reshape(width, tok, CHUNK).astype(BF)


def products(at, of, part, pairs, red):
    for s in range(at.depth - 1, -1, -1):
        for t in [at.z + s, at.z - s] if s else [at.z]:

            @pl.when(jnp.logical_and(t >= 0, t < at.depth))
            def _(t=t):
                product(at, of, part, pairs, t)
                red.emit(t)


def gather_all(g, between=None):
    at = g.at
    for s in range(1, at.depth):
        g.step(s)
        if between is not None:
            between(s)
    for s in range(at.depth):
        for zz in [at.z - s, at.z + s] if s else [at.z]:

            @pl.when(jnp.logical_and(zz >= 0, zz < at.depth))
            def _(zz=zz):
                g.take_side(zz)


def split_columns(src, dst, runs):
    for b, to, at, size in runs:
        dst[b, :, to : to + size] = src[:, at : at + size]


def join_columns(src, dst, runs):
    for b, to, at, size in runs:
        dst[:, at : at + size] = src[b, :, to : to + size].astype(dst.dtype)


def front_call(n, x, small, ints, weight, runs, out_w):
    tok, d = x.shape
    k, c = weight.shape[0], weight.shape[1] // n
    call = Call(n, 1, "front")
    ix = call.give(x, ANY)
    ism, iin = call.give(small), call.give(ints)
    iw = call.give(weight, ANY)
    ox = call.make((n, tok, d), BF, ANY)
    osm = call.make((n, 4) + small.shape, BF)
    oin = call.make((n,) + ints.shape, jnp.int32)
    ow = call.make((4, n, k, c), BF, ANY)
    sx = call.scratch(Gather.sems(n, ALONE))
    sp = call.scratch([pltpu.VMEM((n, k, c), BF)])
    ssm = call.scratch(SmallGather.sems(n))
    sin = call.scratch(Exchange.sems(n))
    sw = call.scratch(Columns.sems(n))
    if out_w is not None:
        io = call.give(out_w, ANY)
        oo = call.make((4,) + out_w.shape, BF, ANY)
        so = call.scratch(Rows.sems())

    def body(at, of):
        sm = SmallGather(at, of(ism), of(osm), of(ssm))
        g = Gather(at, of(ox), of(sx), ALONE)
        cols = Columns(at, of(sp)[0], of(ow), of(sw))
        spread = Spread(at, of(iin), of(oin), of(sin))
        sm.start()
        of(ox)[at.j] = of(ix)[...]
        g.start()
        spread.start()
        split_columns(of(iw), of(sp)[0], runs)
        cols.start()
        sm.step()
        if out_w is not None:
            rows = Rows(at, of(io), of(oo), of(so))
            rows.start()
        cuts = [0, n // 4, n // 2, n]

        def between(s):
            cols.step(cuts[s - 1], cuts[s])

        gather_all(g, between)
        cols.relay(0, n)
        if out_w is not None:
            rows.relay()
            rows.finish()
        cols.finish()
        g.finish()
        sm.finish()
        spread.finish()

    return call.run(body)


class Spread:
    def __init__(self, at, mine, got, sems):
        self.at, self.mine, self.got = at, mine, got
        self.ssem, self.rsem = sems

    def copy(self, to, src):
        at = self.at
        return remote(
            self.mine, self.got.at[src], self.ssem.at[to], self.rsem.at[src], at.seq(to)
        )

    def own(self):
        return pltpu.make_async_copy(self.mine, self.got.at[self.at.j], self.ssem.at[self.at.j])

    def start(self):
        self.own().start()

        @pl.loop(1, self.at.n)
        def _(i):
            self.copy(self.at.other(i), self.at.j).start()

    def finish(self):
        self.own().wait()

        @pl.loop(1, self.at.n)
        def _(i):
            p = self.at.other(i)
            self.copy(p, p).wait()


def sum_call(n, cid, name, pairs, tok, columns=(), rows=(), gathers=(), row_sums=(), col_sums=()):
    call = Call(n, cid, name)
    d = pairs[0][1].shape[0 if pairs[0][2] else 1]
    keys = []
    for lhs, rhs, flip in pairs:
        lhs = lhs.reshape(LINE, lhs.shape[0] // LINE, lhs.shape[1])
        keys.append((call.give(lhs), call.give(rhs), flip))
    out = call.make((tok, d), F32)
    part = call.scratch([pltpu.VMEM((n, tok, d), BF)])
    red_s = call.scratch(Reduce.scratch(n, tok, d, PIECES))
    extra = Extras(call, n, columns, rows, gathers, row_sums, col_sums, PAIRED)

    def body(at, of):
        part_ref = of(part)[0]
        red = Reduce(at, part_ref, of(red_s), PIECES)
        extra.bind(at, of)
        extra.start()
        products(at, of, part_ref, keys, red)
        extra.cross()
        for s in range(at.depth - 1, 0, -1):
            red.reduce(s)
            extra.between(at.depth - s)
        red.last(of(out))
        extra.finish()
        red.finish()

    flops = sum(2 * l.shape[0] * l.shape[1] * d for l, _, _ in pairs)
    return call.run(body, flops)


class Extras:
    def __init__(
        self, call, n, columns=(), rows=(), gathers=(), row_sums=(), col_sums=(), cuts=None
    ):
        self.n, self.cuts = n, cuts
        self.columns, self.rows, self.gathers, self.row_sums, self.col_sums = [], [], [], [], []
        for w, runs in columns:
            shape = (n, w.shape[0], w.shape[1] // n)
            self.columns.append(
                (
                    call.give(w),
                    call.make((4,) + shape, BF, ANY),
                    call.scratch([pltpu.VMEM(shape, BF)]),
                    call.scratch(Columns.sems(n)),
                    runs,
                )
            )
        for p in rows:
            self.rows.append(
                (call.give(p, ANY), call.make((4,) + p.shape, BF, ANY), call.scratch(Rows.sems()))
            )
        for p in gathers:
            self.gathers.append(
                (
                    call.give(p, ANY),
                    call.make((n,) + p.shape, BF, ANY),
                    call.scratch(Gather.sems(n, cuts)),
                )
            )
        for p in row_sums:
            self.row_sums.append(
                (
                    call.give(p),
                    call.make(p.shape[1:], F32),
                    call.scratch(RowSum.scratch(*p.shape[1:])),
                )
            )
        for p, runs in col_sums:
            k, c = p.shape[2:]
            self.col_sums.append(
                (
                    call.give(p.reshape(4, n * k, c)),
                    call.make((k, n * c), F32),
                    call.scratch(RowSum.scratch(n * k, c)),
                    call.scratch([pltpu.VMEM((n, k, c), BF)] * 2),
                    call.scratch(Exchange.sems(n)),
                    runs,
                )
            )

    def bind(self, at, of):
        self.at, self.of = at, of
        self.b_columns = [
            (Columns(at, of(p)[0], of(o), of(s)), of(i), of(p)[0], runs)
            for i, o, p, s, runs in self.columns
        ]
        self.b_rows = [Rows(at, of(i), of(o), of(s)) for i, o, s in self.rows]
        self.b_gathers = [
            (Gather(at, of(o), of(s), self.cuts), of(i), of(o)) for i, o, s in self.gathers
        ]
        self.b_sums = [(RowSum(at, of(i), of(s)), of(o)) for i, o, s in self.row_sums]
        self.b_cols = []
        for i, o, s, v, e, runs in self.col_sums:
            mine, got = of(v)
            self.b_cols.append(
                (
                    RowSum(at, of(i), of(s)),
                    mine,
                    Exchange(at, mine, got, of(e)),
                    (got, of(o), runs),
                )
            )

    def start(self):
        at = self.at
        for rs, _ in self.b_sums:
            rs.start()
        for rs, *_ in self.b_cols:
            rs.start()
        for g, src, buf in self.b_gathers:
            buf[at.j] = src[...]
            g.start()
        for r in self.b_rows:
            r.start()
        for c, src, pieces, runs in self.b_columns:
            split_columns(src, pieces, runs)
            c.start()

    def cross(self):
        for rs, _ in self.b_sums:
            rs.cross()
        for rs, *_ in self.b_cols:
            rs.cross()

    def between(self, s):
        n = self.n
        cuts = [0, n // 4, n // 2, n]
        for g, _, _ in self.b_gathers:
            g.step(s)
        for c, *_ in self.b_columns:
            c.step(cuts[s - 1], cuts[s])
        if s == 2:
            for rs, mine, ex, _ in self.b_cols:
                mine[...] = rs.total().reshape(mine.shape).astype(BF)
                ex.start()

    def finish(self):
        at = self.at
        for g, _, _ in self.b_gathers:
            for zz in range(at.depth):
                g.take_side(zz)
            g.finish()
        for r in self.b_rows:
            r.relay()
        for c, *_ in self.b_columns:
            c.relay(0, self.n)
        for r in self.b_rows:
            r.finish()
        for c, *_ in self.b_columns:
            c.finish()
        for rs, out in self.b_sums:
            out[...] = rs.total()
            rs.finish()
        for rs, _, ex, (got, out, runs) in self.b_cols:
            ex.finish()
            rs.finish()
            join_columns(got, out, runs)


def gather_call(n, cid, name, x, columns=(), rows=(), row_sums=(), col_sums=()):
    call = Call(n, cid, name)
    extra = Extras(call, n, columns, rows, [x], row_sums, col_sums, ALONE)

    def body(at, of):
        extra.bind(at, of)
        extra.start()
        extra.cross()
        for s in range(1, at.depth):
            extra.between(s)
        extra.finish()

    return call.run(body)


def digit(code, i):
    return lax.rem(code // jnp.where(i == 0, 1, jnp.where(i == 1, 10, jnp.where(i == 2, 100, 1000))), 10)


def by_place(z, codes):
    return jnp.where(z == 0, codes[0], jnp.where(z == 1, codes[1], jnp.where(z == 2, codes[2], codes[3])))


def mlp_call(n, middle, gate, up, down, grads):
    call = Call(n, 9, "mlp")
    tok, d = middle.shape
    c = gate.shape[1]
    wide = n // LINE * tok
    i_mid, i_gate, i_up = call.give(middle), call.give(gate), call.give(up)
    i_down, i_grads = call.give(down), call.give(grads)
    out = call.make((tok, d), F32)
    o_mid = call.make((n, tok, d), BF)
    o_acts = [call.make((LINE, wide, c), BF) for _ in range(3)]
    part = call.scratch([pltpu.VMEM((n, tok, d), BF)])
    gat_s = call.scratch(Gather.sems(n, MLP_CUTS))
    red_s = call.scratch(Reduce.scratch(n, tok, d, MLP_PIECES))

    def body(at, of):
        part_ref = of(part)[0]
        mid, grad = of(o_mid), of(i_grads)
        inner_ref, gg_ref, gu_ref = of(o_acts)
        gat = Gather(at, mid, of(gat_s), MLP_CUTS)
        red = Reduce(at, part_ref, of(red_s), MLP_PIECES)
        mid[at.j] = of(i_mid)[...]
        gat.start()
        gat.open_wide()
        order = by_place(at.z, (3210, 3201, 132, 123))
        edge = jnp.logical_or(at.z == 0, at.z == at.depth - 1)

        @pl.loop(0, LINE)
        def _(i):
            t = digit(order, i)
            lo = jnp.where(edge, i + 1, jnp.where(i == 0, 1, jnp.where(i == 1, 3, 4)))
            hi = jnp.where(edge, jnp.minimum(i + 2, 4), jnp.where(i == 0, 3, 4))

            @pl.loop(lo, hi)
            def _(m):
                gat.fetch(digit(order, m))

            gat.take_side(t)
            here = pl.ds(t * at.width, at.width)
            rows = mid[here].reshape(wide, d)
            gate_pre = dot(rows, of(i_gate)[...], 1, 0)
            sig = 1.0 / (1.0 + jnp.exp(-gate_pre))
            silu = gate_pre * sig
            up_pre = dot(rows, of(i_up)[...], 1, 0)
            inner_ref[t] = (silu * up_pre).astype(BF)
            g_inner = dot(grad[here].reshape(wide, d), of(i_down)[...], 1, 1)
            gu_ref[t] = (g_inner * silu).astype(BF)
            gg_ref[t] = (g_inner * up_pre * sig * (1.0 + gate_pre * (1.0 - sig))).astype(BF)
            product(
                at, lambda k: k, part_ref,
                [(gg_ref, of(i_gate), True), (gu_ref, of(i_up), True)], t,
            )
            red.emit(t)

            @pl.when(jnp.logical_and(edge, i >= 2))
            def _():
                red.pass_on(digit(order, i - 1))

        rest = by_place(at.z, (3, 32, 301, 0))

        @pl.loop(0, jnp.where(edge, 1, 3))
        def _(i):
            red.pass_on(digit(rest, i))

        red.last(of(out))
        gat.finish()
        red.finish()

    return call.run(body)


def last_call(n, cid, pairs, tok, normed, known, row_sums, col_sums):
    call = Call(n, cid, "last")
    d = pairs[0][1].shape[0]
    keys = []
    for lhs, rhs, flip in pairs:
        lhs = lhs.reshape(LINE, lhs.shape[0] // LINE, lhs.shape[1])
        keys.append((call.give(lhs), call.give(rhs), flip))
    i_norm, i_known = call.give(normed), call.give(known)
    out = call.make((tok, d), F32)
    o_small = call.make((8, d // 4), F32)
    part = call.scratch([pltpu.VMEM((n, tok, d), BF)])
    red_s = call.scratch(Reduce.scratch(n, tok, d, PIECES))
    s_small = call.scratch(SmallSum.scratch(n, d))
    extra = Extras(call, n, row_sums=row_sums, col_sums=col_sums)

    def body(at, of):
        part_ref = of(part)[0]
        red = Reduce(at, part_ref, of(red_s), PIECES)
        extra.bind(at, of)
        extra.start()
        products(at, of, part_ref, keys, red)
        extra.cross()
        for s in range(at.depth - 1, 0, -1):
            red.reduce(s)
            extra.between(at.depth - s)
        red.last(of(out))
        small = SmallSum(at, of(s_small))
        small.terms[...] = of(i_known)[...]
        grad = of(out)[...]
        small.terms[0:1, :] = jnp.sum(grad * of(i_norm)[...], axis=0, keepdims=True)
        small.terms[1:2, :] = jnp.sum(grad, axis=0, keepdims=True)
        small.run(of(o_small))
        extra.finish()
        red.finish()

    return call.run(body)


def attention(queries, keys, values, allowed):
    scores = jnp.einsum("qhd,khd->hqk", queries, keys, preferred_element_type=F32)
    exp_weights = jnp.where(allowed[None], jnp.exp(scores), 0.0)
    denominator = jnp.sum(exp_weights, axis=-1)
    numerator = jnp.einsum(
        "hqk,khd->qhd", exp_weights.astype(BF), values, preferred_element_type=F32
    )
    return numerator / jnp.transpose(denominator)[:, :, None], denominator


def attention_back(queries, keys, values, allowed, denominator, context, g_context):
    den = jnp.transpose(denominator)
    g_numer = (g_context / den[:, :, None]).astype(BF)
    g_den = jnp.transpose(-jnp.sum(g_context * context, axis=-1) / den)
    scores = jnp.einsum("qhd,khd->hqk", queries, keys, preferred_element_type=F32)
    exp_weights = jnp.where(allowed[None], jnp.exp(scores), 0.0)
    g_values = jnp.einsum(
        "hqk,qhd->khd", exp_weights.astype(BF), g_numer, preferred_element_type=F32
    )
    g_weights = jnp.einsum("qhd,khd->hqk", g_numer, values, preferred_element_type=F32)
    g_scores = (exp_weights * (g_weights + g_den[:, :, None])).astype(BF)
    g_queries = jnp.einsum("hqk,khd->qhd", g_scores, keys, preferred_element_type=F32)
    g_keys = jnp.einsum("hqk,qhd->khd", g_scores, queries, preferred_element_type=F32)
    return g_queries, g_keys, g_values


def body(nrow, n, *args):
    (
        layer_in,
        segments,
        positions,
        attn_norm_gain,
        attn_norm_bias,
        qkv_weight,
        qkv_bias,
        out_weight,
        mlp_norm_gain,
        mlp_norm_bias,
        gate_weight,
        up_weight,
        down_weight,
        out_grad,
    ) = args
    j = lax.axis_index("seq")
    tok = layer_in.shape[1]
    length = n * tok
    k = qkv_weight.shape[0]
    f = down_weight.shape[0]
    hp = H // n
    whole_heads = out_weight.shape[0] == HD
    roomy = length * D <= 1 << 22

    if whole_heads:
        head_runs = [
            (b, (m * nrow + r) * HD, m * D + (r * n + b) * HD, HD)
            for b in range(n) for m in range(3) for r in range(nrow)
        ]
    else:
        size = hp * HD
        head_runs = [
            (b, m * size, m * D + b * size, size) for b in range(n) for m in range(3)
        ]
    ff_runs = [(b, r * f, (r * n + b) * f, f) for b in range(n) for r in range(nrow)]

    def split_heads(w):
        lead = w.shape[0]
        if whole_heads:
            w = w.reshape(lead, 3, nrow, n, HD).transpose(3, 0, 1, 2, 4)
        else:
            w = w.reshape(lead, 3, n, hp, HD).transpose(2, 0, 1, 3, 4)
        return w.reshape(n, lead, 3 * hp * HD)

    def join_heads(blocks):
        lead = blocks.shape[1]
        if whole_heads:
            w = blocks.reshape(n, lead, 3, nrow, HD).transpose(1, 2, 3, 0, 4)
        else:
            w = blocks.reshape(n, lead, 3, hp, HD).transpose(1, 2, 0, 3, 4)
        return w.reshape(lead, 3 * D)

    small = jnp.concatenate(
        [attn_norm_gain, attn_norm_bias, mlp_norm_gain, mlp_norm_bias, qkv_bias]
    )
    small = jnp.pad(small, (0, 2048 - small.shape[0])).reshape(16, 128)
    ints = jnp.concatenate([segments, positions, jnp.zeros((6, tok), jnp.int32)], 0)
    front = front_call(
        n, layer_in[0], small, ints, qkv_weight, head_runs, out_weight if whole_heads else None
    )
    x_all, small_all, ints_all, qkv_own = front[:4]
    x_all = x_all.reshape(length, D)
    qkv_own = qkv_own.reshape(D, 3 * hp * HD)
    if whole_heads:
        out_own = front[4].reshape(hp * HD, D)
    else:
        out_full = lax.all_gather(out_weight, ("row", "seq"), axis=0, tiled=True)
        out_own = lax.dynamic_slice_in_dim(out_full, j * hp * HD, hp * HD, 0)
    small_all = small_all.transpose(1, 0, 2, 3).reshape(nrow * n, 2048)
    attn_gain, attn_bias, mlp_gain, mlp_bias = (
        small_all[:, c : c + k].reshape(1, D).astype(F32) for c in (0, k, 2 * k, 3 * k)
    )
    qkv_shift = small_all[:, 4 * k : 4 * k + 3 * k].reshape(1, 3 * D)
    shift_own = lax.dynamic_index_in_dim(split_heads(qkv_shift), j, 0, keepdims=False).astype(F32)
    seg_all, pos_all = ints_all[:, 0].reshape(length), ints_all[:, 1].reshape(length)

    inputs_all = (norm_stats(x_all.astype(F32))[0] * attn_gain + attn_bias).astype(BF)
    projected = dot(inputs_all, qkv_own, 1, 0) + shift_own
    head_split = projected.reshape(length, 3, hp, HD)
    cosine, sine_part = rotary_tables(pos_all)
    queries = (rotate(head_split[:, 0], cosine, sine_part, 1.0) / math.sqrt(HD)).astype(BF)
    keys = rotate(head_split[:, 1], cosine, sine_part, 1.0).astype(BF)
    values = head_split[:, 2].astype(BF)
    index = jnp.arange(length, dtype=jnp.int32)
    allowed = (seg_all[:, None] == seg_all[None, :]) & (index[None, :] <= index[:, None])
    context, denominator = attention(queries, keys, values, allowed)
    context_low = context.reshape(length, hp * HD).astype(BF)
    attn_branch, *weights = sum_call(
        n, 2, "mix_sum", [(context_low, out_own, False)], tok,
        columns=[(gate_weight, ff_runs), (up_weight, ff_runs)], rows=[down_weight],
        gathers=[out_grad[0]] if roomy else [],
    )
    gate_own, up_own = weights[0].reshape(D, nrow * f), weights[1].reshape(D, nrow * f)
    down_own = weights[2].reshape(nrow * f, D)

    x_float = layer_in[0].astype(F32)
    normed1, inv_std1 = norm_stats(x_float)
    hidden_mid = x_float + attn_branch
    normed2, inv_std2 = norm_stats(hidden_mid)
    middle = (normed2 * mlp_gain + mlp_bias).astype(BF)
    grad_float = out_grad[0].astype(F32)
    if roomy:
        grad_all = weights[3]
        g_middle, middle_all, inner_act, g_gate, g_up = mlp_call(
            n, middle, gate_own, up_own, down_own, grad_all
        )
        middle_all, grad_all = middle_all.reshape(length, D), grad_all.reshape(length, D)
        inner_act, g_gate, g_up = (a.reshape(length, nrow * f) for a in (inner_act, g_gate, g_up))
    else:
        (middle_all,) = gather_call(n, 3, "middle", middle)
        middle_all = middle_all.reshape(length, D)
        gate_pre = dot(middle_all, gate_own, 1, 0)
        up_pre = dot(middle_all, up_own, 1, 0)
        sig = jax.nn.sigmoid(gate_pre)
        silu = gate_pre * sig
        inner_act = (silu * up_pre).astype(BF)
        (grad_all,) = gather_call(n, 8, "grads", out_grad[0])
        grad_all = grad_all.reshape(length, D)
        g_inner = dot(grad_all, down_own, 1, 1)
        g_gate = (g_inner * up_pre * sig * (1.0 + gate_pre * (1.0 - sig))).astype(BF)
        g_up = (g_inner * silu).astype(BF)
        (g_middle,) = sum_call(
            n, 5, "mlp_back", [(g_gate, gate_own, True), (g_up, up_own, True)], tok
        )
    down_part = dot(inner_act, grad_all, 0, 0).astype(BF).reshape(nrow, f, D)
    gate_part = dot(middle_all, g_gate, 0, 0).astype(BF).reshape(nrow, n, k, nrow * f)
    up_part = dot(middle_all, g_up, 0, 0).astype(BF).reshape(nrow, n, k, nrow * f)
    g_hidden = grad_float + norm_back(g_middle, normed2, inv_std2, mlp_gain)
    g_attn = g_hidden.astype(BF)
    if roomy:
        mlp_branch, g_attn_all, down_grad, gate_grad, up_grad = sum_call(
            n, 6, "mlp_sum", [(inner_act, down_own, False)], tok, gathers=[g_attn],
            row_sums=[down_part], col_sums=[(gate_part, ff_runs), (up_part, ff_runs)],
        )
    else:
        mlp_branch, down_grad = sum_call(
            n, 4, "mlp_sum", [(inner_act, down_own, False)], tok, row_sums=[down_part]
        )
        g_attn_all, gate_grad, up_grad = gather_call(
            n, 6, "hidden_back", g_attn, col_sums=[(gate_part, ff_runs), (up_part, ff_runs)]
        )
    g_attn_all = g_attn_all.reshape(length, D)
    layer_out = (hidden_mid + mlp_branch).astype(BF)

    out_part = dot(context_low, g_attn_all, 0, 0)
    g_context = dot(g_attn_all, out_own, 1, 1).reshape(length, hp, HD)
    g_queries, g_keys, g_values = attention_back(
        queries, keys, values, allowed, denominator, context, g_context
    )
    query_part = rotate(g_queries, cosine, sine_part, -1.0) / math.sqrt(HD)
    key_part = rotate(g_keys, cosine, sine_part, -1.0)
    g_projected = (
        jnp.stack([query_part, key_part, g_values], 1).reshape(length, 3 * hp * HD).astype(BF)
    )
    qkv_part = dot(inputs_all, g_projected, 0, 0).astype(BF).reshape(nrow, n, k, 3 * hp * HD)
    shift_sum = jnp.sum(g_projected.astype(F32), axis=0)
    shift_blocks = lax.dynamic_update_slice_in_dim(
        jnp.zeros((n, 1, 3 * hp * HD), F32), shift_sum[None, None], j, 0
    )
    shift_full = join_heads(shift_blocks)[0]
    known = jnp.concatenate(
        [
            jnp.zeros((2, D), F32),
            jnp.sum(g_middle * normed2, axis=0)[None],
            jnp.sum(g_middle, axis=0)[None],
            shift_full.reshape(nrow, 3, D // nrow).transpose(1, 0, 2).reshape(3, D),
            jnp.zeros((1, D), F32),
        ]
    )
    last = last_call(
        n, 7, [(g_projected, qkv_own, True)], tok, normed1, known,
        [out_part.astype(BF).reshape((nrow,) + out_weight.shape)] if whole_heads else [],
        [(qkv_part, head_runs)],
    )
    if whole_heads:
        g_inputs, small_grads, out_w_grad, qkv_grad = last
    else:
        g_inputs, small_grads, qkv_grad = last
        placed = lax.dynamic_update_slice_in_dim(
            jnp.zeros((D, D), BF), out_part.astype(BF), j * hp * HD, 0
        )
        out_w_grad = lax.psum_scatter(
            placed, ("row", "seq"), scatter_dimension=0, tiled=True
        ).astype(F32)
    input_grad = g_hidden + norm_back(g_inputs, normed1, inv_std1, attn_gain)
    own = lax.dynamic_slice_in_dim(small_grads, j * k, k, 1)
    shift_own_grad = lax.dynamic_slice_in_dim(small_grads[4:7].reshape(-1), j * 3 * k, 3 * k, 0)
    return (
        layer_out[None],
        input_grad[None],
        own[0],
        own[1],
        qkv_grad,
        shift_own_grad,
        out_w_grad,
        own[2],
        own[3],
        gate_grad,
        up_grad,
        down_grad,
    )


def solution(mesh):
    nrow, n = mesh.shape["row"], mesh.shape["seq"]

    def local(*args):
        return body(nrow, n, *args)

    tokens, ints = P("row", "seq", None), P("row", "seq")
    vec, mat = P(("row", "seq")), P(("row", "seq"), None)
    return jax.shard_map(
        local,
        mesh=mesh,
        in_specs=(
            tokens, ints, ints, vec, vec, mat, vec, mat, vec, vec, mat, mat, mat, tokens,
        ),
        out_specs=(tokens, tokens, vec, vec, mat, vec, mat, vec, vec, mat, mat, mat),
        check_vma=False,
    )
```

```python
import functools
import math

import jax
import jax.numpy as jnp
from jax import lax
from jax.experimental import pallas as pl
from jax.experimental.pallas import tpu as pltpu
from jax.sharding import PartitionSpec as P

D = 2048
H = 32
HD = 64
ROT = 16
EPSILON = 1e-05
BF = jnp.bfloat16
F32 = jnp.float32


def dot(a, b, ca, cb):
    return lax.dot_general(a, b, (((ca,), (cb,)), ((), ())), preferred_element_type=F32)


def norm_stats(values_in):
    average = jnp.mean(values_in, axis=-1, keepdims=True)
    centered = values_in - average
    inv_std = lax.rsqrt(jnp.mean(centered * centered, axis=-1, keepdims=True) + EPSILON)
    return (centered * inv_std, inv_std)


def norm_back(grad_in, normed, inv_std, gain_vector):
    scaled = grad_in * gain_vector
    return inv_std * (
        scaled
        - jnp.mean(scaled, axis=-1, keepdims=True)
        - normed * jnp.mean(scaled * normed, axis=-1, keepdims=True)
    )


def rotary_tables(positions):
    half_rot = ROT // 2
    frequency = 10000.0 ** (-2.0 * jnp.arange(half_rot, dtype=F32) / ROT)
    angles = positions.astype(F32)[:, None] * frequency[None, :]
    return (jnp.cos(angles)[:, None, :], jnp.sin(angles)[:, None, :])


def rotate(head_values, cosine, sine_part, direction):
    half_rot = ROT // 2
    first_half = head_values[..., :half_rot]
    second = head_values[..., half_rot:ROT]
    return jnp.concatenate(
        [
            first_half * cosine - direction * second * sine_part,
            second * cosine + direction * first_half * sine_part,
            head_values[..., ROT:],
        ],
        axis=-1,
    )


MESH = pl.DeviceIdType.MESH
LINE = 4


class Place:
    def __init__(self, n):
        self.n = n
        self.depth = LINE
        self.width = n // LINE
        self.r = lax.axis_index("row")
        self.j = lax.axis_index("seq")
        self.z = self.j // self.width
        self.x = lax.rem(self.j, self.width)
        y, c = self.r // 2, lax.rem(self.r, 2)
        self.y, self.c = y, c
        self.r_y = (1 - y) * 2 + c
        self.r_c = y * 2 + (1 - c)
        self.r_yc = (1 - y) * 2 + (1 - c)

    def inner(self, t):
        return jnp.logical_or(
            jnp.logical_and(t > self.z, self.z > 0),
            jnp.logical_and(t < self.z, self.z < self.depth - 1),
        )

    def seq(self, j):
        return (self.r, j)

    def row(self, r):
        return (r, self.j)

    def other(self, i):
        return lax.rem(self.j + i, self.n)

    def meet(self):
        barrier = pltpu.get_barrier_semaphore()
        for r in (self.r_y, self.r_c, self.r_yc):
            pl.semaphore_signal(barrier, inc=1, device_id=self.row(r), device_id_type=MESH)
        for i in range(1, self.n):
            pl.semaphore_signal(
                barrier, inc=1, device_id=self.seq(self.other(i)), device_id_type=MESH
            )
        pl.semaphore_wait(barrier, self.n + 2)


def remote(src, dst, ssem, rsem, device):
    return pltpu.make_async_remote_copy(
        src_ref=src, dst_ref=dst, send_sem=ssem, recv_sem=rsem, device_id=device,
        device_id_type=MESH,
    )


ALONE = ((1, True), (3, False), (4, False))
PAIRED = ((2, True), (6, False))
SUM_CUTS = ((2, True), (6, False))
MLP_CUTS = ((2, True), (3, False), (3, False))
MLP_SUMS = ((2, True), (3, False), (3, False))


class Gather:
    @staticmethod
    def sems(n, cuts):
        w = n // LINE
        out = []
        for _ in cuts:
            out += [
                pltpu.SemaphoreType.DMA((2, n)),
                pltpu.SemaphoreType.DMA((LINE, max(w - 1, 1))),
                pltpu.SemaphoreType.DMA((n,)),
            ]
        return out

    def __init__(self, at, buf, sems, cuts):
        self.at, self.buf = at, buf
        tok = buf.shape[1]
        self.cuts = []
        first = 0
        for i, (share, wide) in enumerate(cuts):
            rows = tok * share // 8
            self.cuts.append((pl.ds(first, rows), wide, sems[3 * i : 3 * i + 3]))
            first += rows

    def copy(self, cut, b, to, sem):
        here = self.buf.at[b, cut[0]]
        return remote(here, here, sem, cut[2][2].at[b], self.at.seq(to))

    def along(self, cut, way, b):
        at = self.at
        to = at.j + at.width if way == 0 else at.j - at.width
        return self.copy(cut, b, to, cut[2][0].at[way, b])

    def across(self, cut, zz, i):
        at = self.at
        to = at.z * at.width + lax.rem(at.x + i, at.width)
        return self.copy(cut, zz * at.width + at.x, to, cut[2][1].at[zz, i - 1])

    def take(self, cut, b):
        self.copy(cut, b, self.at.other(1), cut[2][0].at[0, 0]).wait_recv()

    def onward(self, cut, way, b):
        at = self.at

        @pl.when(at.z < at.depth - 1 if way == 0 else at.z > 0)
        def _():
            self.along(cut, way, b).start()

    def start(self):
        at = self.at
        for cut in self.cuts:
            if cut[1]:
                for i in range(1, at.width):
                    self.across(cut, at.z, i).start()
        for cut in self.cuts:
            for way in range(2):
                self.onward(cut, way, at.j)
            if not cut[1]:
                for i in range(1, at.width):
                    self.across(cut, at.z, i).start()

    def step(self, s):
        at = self.at
        for cut in self.cuts:
            if s == 1 and cut[1]:
                for i in range(1, at.width):
                    b = at.z * at.width + lax.rem(at.x + i, at.width)
                    self.take(cut, b)
                    for way in range(2):
                        self.onward(cut, way, b)
        for cut in self.cuts:
            for way in range(2):
                zz = at.z - s if way == 0 else at.z + s

                @pl.when(zz >= 0 if way == 0 else zz < at.depth)
                def _(zz=zz, way=way, cut=cut):
                    if cut[1]:
                        for i in range(at.width):
                            b = zz * at.width + lax.rem(at.x + i, at.width)
                            self.take(cut, b)
                            self.onward(cut, way, b)
                    else:
                        b = zz * at.width + at.x
                        self.take(cut, b)
                        self.onward(cut, way, b)
                        for i in range(1, at.width):
                            self.across(cut, zz, i).start()

    def fetch(self, zz):
        at = self.at
        for way in range(2):

            @pl.when(zz < at.z if way == 0 else zz > at.z)
            def _(way=way):
                for cut in self.cuts:
                    for i in range(at.width if cut[1] else 1):
                        b = zz * at.width + lax.rem(at.x + i, at.width)
                        self.take(cut, b)
                        self.onward(cut, way, b)
                    if not cut[1]:
                        for i in range(1, at.width):
                            self.across(cut, zz, i).start()

    def open_wide(self):
        at = self.at
        for cut in self.cuts:
            if cut[1]:
                for i in range(1, at.width):
                    b = at.z * at.width + lax.rem(at.x + i, at.width)
                    self.take(cut, b)
                    for way in range(2):
                        self.onward(cut, way, b)

    def take_side(self, zz):
        at = self.at
        for cut in self.cuts:
            if not cut[1]:
                for i in range(1, at.width):
                    self.take(cut, zz * at.width + lax.rem(at.x + i, at.width))

    def finish(self):
        at = self.at
        for cut in self.cuts:
            for zz in range(at.depth):
                for i in range(1, at.width):
                    if cut[1]:
                        @pl.when(at.z == zz)
                        def _(zz=zz, i=i, cut=cut):
                            self.across(cut, zz, i).wait_send()
                    else:
                        self.across(cut, zz, i).wait_send()
                for way in range(2):
                    ok = jnp.logical_and(at.z >= zz, at.z < at.depth - 1) if way == 0 else jnp.logical_and(at.z <= zz, at.z > 0)

                    @pl.when(ok)
                    def _(zz=zz, way=way, cut=cut):
                        for i in range(at.width if cut[1] else 1):
                            b = zz * at.width + lax.rem(at.x + i, at.width)
                            self.along(cut, way, b).wait_send()


class NarrowSum:
    @staticmethod
    def scratch(n, size, d):
        side = max(n // LINE - 1, 1)
        return (
            [pltpu.VMEM((LINE, side, size, d), BF), pltpu.VMEM((LINE + 1, size, d), BF)]
            + [pltpu.SemaphoreType.DMA((LINE, side))] * 2
            + [pltpu.SemaphoreType.DMA((LINE,)), pltpu.SemaphoreType.DMA((LINE + 1,))]
        )

    def __init__(self, at, part, rows, refs):
        self.at, self.part, self.rows = at, part, rows
        self.xr, self.lr, self.xs_sem, self.xr_sem, self.ls_sem, self.lr_sem = refs

    def across(self, t, i):
        at = self.at
        xx = lax.rem(at.x + i, at.width)
        return remote(
            self.part.at[t * at.width + xx, self.rows], self.xr.at[t, i - 1],
            self.xs_sem.at[t, i - 1], self.xr_sem.at[t, i - 1], at.seq(at.z * at.width + xx),
        )

    def along(self, t):
        at = self.at
        there = jnp.where(t > at.z, at.j + at.width, at.j - at.width)
        slot = jnp.where(t == at.z - 1, at.depth, t)
        return remote(
            self.part.at[t * at.width + at.x, self.rows], self.lr.at[slot],
            self.ls_sem.at[t], self.lr_sem.at[slot], at.seq(there),
        )

    def landed(self, slot):
        remote(
            self.lr.at[slot], self.lr.at[slot], self.ls_sem.at[0], self.lr_sem.at[slot],
            self.at.seq(self.at.other(1)),
        ).wait_recv()

    def emit(self, t):
        for i in range(1, self.at.width):
            self.across(t, i).start()

    def summed(self, t):
        at = self.at
        total = self.part[t * at.width + at.x, self.rows].astype(F32)
        for i in range(1, at.width):
            self.across(t, i).wait_recv()
            total = total + self.xr[t, i - 1].astype(F32)
        return total

    def pass_on(self, t):
        at = self.at
        block = (t * at.width + at.x, self.rows)
        total = self.summed(t)
        inner = at.inner(t)

        @pl.when(inner)
        def _():
            self.landed(t)
            self.part[block] = (total + self.lr[t].astype(F32)).astype(BF)

        @pl.when(jnp.logical_not(inner))
        def _():
            self.part[block] = total.astype(BF)

        self.along(t).start()

    def close(self):
        pass

    def last(self, out):
        at = self.at
        out[self.rows] = self.summed(at.z)

        @pl.when(at.z > 0)
        def _():
            self.landed(at.z)
            out[self.rows] += self.lr[at.z].astype(F32)

        @pl.when(at.z < at.depth - 1)
        def _():
            self.landed(at.depth)
            out[self.rows] += self.lr[at.depth].astype(F32)

    def finish(self):
        at = self.at
        for t in range(at.depth):
            for i in range(1, at.width):
                self.across(t, i).wait_send()

            @pl.when(at.z != t)
            def _(t=t):
                self.along(t).wait_send()


class WideSum:
    @staticmethod
    def scratch(n, size, d):
        w = n // LINE
        side = max(w - 1, 1)
        return (
            [pltpu.VMEM((side, size, d), BF), pltpu.VMEM((LINE + 1, w, size, d), BF)]
            + [pltpu.SemaphoreType.DMA((side,))] * 2
            + [pltpu.SemaphoreType.DMA((LINE, w)), pltpu.SemaphoreType.DMA((LINE + 1, w))]
        )

    def __init__(self, at, part, rows, refs):
        self.at, self.part, self.rows = at, part, rows
        self.xr, self.lr, self.xs_sem, self.xr_sem, self.ls_sem, self.lr_sem = refs

    def across(self, i):
        at = self.at
        xx = lax.rem(at.x + i, at.width)
        return remote(
            self.part.at[at.z * at.width + xx, self.rows], self.xr.at[i - 1],
            self.xs_sem.at[i - 1], self.xr_sem.at[i - 1], at.seq(at.z * at.width + xx),
        )

    def along(self, t, xx):
        at = self.at
        there = jnp.where(t > at.z, at.j + at.width, at.j - at.width)
        slot = jnp.where(t == at.z - 1, at.depth, t)
        return remote(
            self.part.at[t * at.width + xx, self.rows], self.lr.at[slot, xx],
            self.ls_sem.at[t, xx], self.lr_sem.at[slot, xx], at.seq(there),
        )

    def landed(self, slot, xx):
        remote(
            self.lr.at[slot, xx], self.lr.at[slot, xx], self.ls_sem.at[0, xx],
            self.lr_sem.at[slot, xx], self.at.seq(self.at.other(1)),
        ).wait_recv()

    def emit(self, t):
        at = self.at

        @pl.when(jnp.logical_and(t != at.z, jnp.logical_not(at.inner(t))))
        def _():
            for xx in range(at.width):
                self.along(t, xx).start()

    def pass_on(self, t):
        at = self.at

        @pl.when(at.inner(t))
        def _():
            for xx in range(at.width):
                self.landed(t, xx)
                block = (t * at.width + xx, self.rows)
                total = self.part[block].astype(F32) + self.lr[t, xx].astype(F32)
                self.part[block] = total.astype(BF)
                self.along(t, xx).start()

    def line_sum(self, xx, put):
        at = self.at
        own = self.part[at.z * at.width + xx, self.rows].astype(F32)

        @pl.when(at.z == 0)
        def _():
            self.landed(at.depth, xx)
            put(own + self.lr[at.depth, xx].astype(F32))

        @pl.when(at.z == at.depth - 1)
        def _():
            self.landed(at.z, xx)
            put(own + self.lr[at.z, xx].astype(F32))

        @pl.when(jnp.logical_and(at.z > 0, at.z < at.depth - 1))
        def _():
            self.landed(at.depth, xx)
            self.landed(at.z, xx)
            put(own + self.lr[at.depth, xx].astype(F32) + self.lr[at.z, xx].astype(F32))

    def close(self):
        at = self.at
        for i in range(1, at.width):
            xx = lax.rem(at.x + i, at.width)

            def put(total, xx=xx):
                self.part[at.z * at.width + xx, self.rows] = total.astype(BF)

            self.line_sum(xx, put)
            self.across(i).start()

    def last(self, out):
        at = self.at

        def put(total):
            out[self.rows] = total

        self.line_sum(at.x, put)
        for i in range(1, at.width):
            self.across(i).wait_recv()
            out[self.rows] += self.xr[i - 1].astype(F32)

    def finish(self):
        at = self.at
        for i in range(1, at.width):
            self.across(i).wait_send()
        for t in range(at.depth):

            @pl.when(at.z != t)
            def _(t=t):
                for xx in range(at.width):
                    self.along(t, xx).wait_send()


class Reduce:
    @staticmethod
    def scratch(n, tok, d, cuts):
        out = []
        for share, wide in cuts:
            out += (WideSum if wide else NarrowSum).scratch(n, tok * share // 8, d)
        return out

    def __init__(self, at, part, refs, cuts):
        self.at, self.cuts = at, []
        tok = part.shape[1]
        first = 0
        for i, (share, wide) in enumerate(cuts):
            rows = pl.ds(first, tok * share // 8)
            first += tok * share // 8
            self.cuts.append((WideSum if wide else NarrowSum)(at, part, rows, refs[6 * i : 6 * i + 6]))

    def emit(self, t):
        for c in self.cuts:
            c.emit(t)

    def pass_on(self, t):
        for c in self.cuts:
            c.pass_on(t)

    def reduce(self, s):
        at = self.at
        for t in (at.z + s, at.z - s):

            @pl.when(jnp.logical_and(t >= 0, t < at.depth))
            def _(t=t):
                self.pass_on(t)

    def last(self, out):
        for c in self.cuts:
            c.close()
        for c in self.cuts[::-1]:
            c.last(out)

    def finish(self):
        for c in self.cuts:
            c.finish()


class Columns:
    @staticmethod
    def sems(n):
        return [pltpu.SemaphoreType.DMA((4, n)), pltpu.SemaphoreType.DMA((4, n))]

    def __init__(self, at, pieces, full, sems):
        self.at, self.pieces, self.full = at, pieces, full
        self.ssem, self.rsem = sems

    def first(self, i):
        at = self.at
        to = at.other(i)
        return remote(
            self.pieces.at[to], self.full.at[at.r, at.j], self.ssem.at[0, to],
            self.rsem.at[at.r, at.j], at.seq(to),
        )

    def own(self):
        at = self.at
        return pltpu.make_async_copy(
            self.pieces.at[at.j], self.full.at[at.r, at.j], self.ssem.at[0, at.j]
        )

    def pass_on(self, r, js, to, k):
        return remote(
            self.full.at[r, js], self.full.at[r, js], self.ssem.at[k, js], self.rsem.at[r, js],
            self.at.row(to),
        )

    def take(self, r, js):
        self.pass_on(r, js, self.at.r_c, 0).wait_recv()

    def start(self):
        at = self.at
        self.own().start()

        @pl.loop(1, at.n)
        def _(i):
            self.first(i).start()

    def step(self, lo, hi):
        at = self.at

        @pl.loop(lo, hi)
        def _(i):
            js = lax.rem(at.j + at.n - i, at.n)

            @pl.when(i == 0)
            def _():
                self.own().wait()

            @pl.when(i > 0)
            def _():
                self.take(at.r, js)

            self.pass_on(at.r, js, at.r_y, 1).start()
            self.pass_on(at.r, js, at.r_c, 2).start()

    def relay(self, lo, hi):
        at = self.at

        @pl.loop(lo, hi)
        def _(i):
            js = lax.rem(at.j + at.n - i, at.n)
            self.take(at.r_y, js)
            self.pass_on(at.r_y, js, at.r_c, 3).start()

    def finish(self):
        at = self.at

        @pl.loop(0, at.n)
        def _(js):
            self.take(at.r_c, js)
            self.take(at.r_yc, js)
            self.pass_on(at.r, js, at.r_y, 1).wait_send()
            self.pass_on(at.r, js, at.r_c, 2).wait_send()
            self.pass_on(at.r_y, js, at.r_c, 3).wait_send()

        @pl.loop(1, at.n)
        def _(i):
            self.first(i).wait_send()


class Rows:
    @staticmethod
    def sems():
        return [pltpu.SemaphoreType.DMA((4,)), pltpu.SemaphoreType.DMA((4,))]

    def __init__(self, at, shard, full, sems):
        self.at, self.shard, self.full = at, shard, full
        self.ssem, self.rsem = sems

    def own(self):
        return pltpu.make_async_copy(self.shard, self.full.at[self.at.r], self.ssem.at[0])

    def direct(self, to, k):
        r = self.at.r
        return remote(
            self.shard, self.full.at[r], self.ssem.at[k], self.rsem.at[r], self.at.row(to)
        )

    def onward(self):
        at = self.at
        r = at.r_y
        return remote(
            self.full.at[r], self.full.at[r], self.ssem.at[3], self.rsem.at[r], at.row(at.r_c)
        )

    def take(self, r):
        at = self.at
        remote(
            self.full.at[r], self.full.at[r], self.ssem.at[0], self.rsem.at[r], at.row(at.r_c)
        ).wait_recv()

    def start(self):
        at = self.at
        self.own().start()
        self.direct(at.r_y, 1).start()
        self.direct(at.r_c, 2).start()

    def relay(self):
        self.take(self.at.r_y)
        self.onward().start()

    def finish(self):
        at = self.at
        self.own().wait()
        self.take(at.r_c)
        self.take(at.r_yc)
        self.direct(at.r_y, 1).wait_send()
        self.direct(at.r_c, 2).wait_send()
        self.onward().wait_send()


class RowSum:
    @staticmethod
    def scratch(m, c):
        return [
            pltpu.VMEM((2, m, c), BF),
            pltpu.VMEM((m, c), BF),
            pltpu.SemaphoreType.DMA((3,)),
            pltpu.SemaphoreType.DMA((3,)),
        ]

    def __init__(self, at, grad, refs):
        self.at, self.grad = at, grad
        self.core_in, self.y_in, self.ssem, self.rsem = refs

    def to_core(self, far):
        at = self.at
        yy = 1 - at.y if far else at.y
        k = 1 if far else 0
        return remote(
            self.grad.at[yy * 2 + 1 - at.c], self.core_in.at[k], self.ssem.at[k], self.rsem.at[k],
            at.row(at.r_c),
        )

    def over_y(self):
        at = self.at
        return remote(
            self.grad.at[at.r_y], self.y_in, self.ssem.at[2], self.rsem.at[2], at.row(at.r_y)
        )

    def start(self):
        self.to_core(1).start()
        self.to_core(0).start()

    def cross(self):
        at = self.at
        self.to_core(1).wait_recv()
        self.grad[at.r_y] = (
            self.grad[at.r_y].astype(F32) + self.core_in[1].astype(F32)
        ).astype(BF)
        self.over_y().start()

    def total(self):
        at = self.at
        self.to_core(0).wait_recv()
        self.over_y().wait_recv()
        return (
            self.grad[at.r].astype(F32) + self.core_in[0].astype(F32) + self.y_in[...].astype(F32)
        )

    def finish(self):
        self.to_core(1).wait_send()
        self.to_core(0).wait_send()
        self.over_y().wait_send()


class Exchange:
    @staticmethod
    def sems(n):
        return [pltpu.SemaphoreType.DMA((n,)), pltpu.SemaphoreType.DMA((n,))]

    def __init__(self, at, mine, got, sems):
        self.at, self.mine, self.got = at, mine, got
        self.ssem, self.rsem = sems

    def send(self, i):
        at = self.at
        to = at.other(i)
        return remote(
            self.mine.at[to], self.got.at[at.j], self.ssem.at[to], self.rsem.at[at.j], at.seq(to)
        )

    def own(self):
        at = self.at
        return pltpu.make_async_copy(
            self.mine.at[at.j], self.got.at[at.j], self.ssem.at[at.j]
        )

    def start(self):
        self.own().start()

        @pl.loop(1, self.at.n)
        def _(i):
            self.send(i).start()

    def finish(self):
        at = self.at
        self.own().wait()

        @pl.loop(1, at.n)
        def _(i):
            src = at.other(i)
            remote(
                self.mine.at[src], self.got.at[src], self.ssem.at[src], self.rsem.at[src],
                at.seq(src),
            ).wait()


class SmallGather:
    @staticmethod
    def sems(n):
        return [pltpu.SemaphoreType.DMA((4,))] * 2 + [pltpu.SemaphoreType.DMA((n,))] * 2

    def __init__(self, at, mine, full, sems):
        self.at, self.mine, self.full = at, mine, full
        self.rs, self.rr, self.ss, self.sr = sems

    def beside(self, r):
        at = self.at
        return remote(
            self.mine, self.full.at[at.j, at.r], self.rs.at[r], self.rr.at[at.r], at.row(r)
        )

    def own(self):
        at = self.at
        return pltpu.make_async_copy(self.mine, self.full.at[at.j, at.r], self.rs.at[at.r])

    def onward(self, to):
        at = self.at
        return remote(
            self.full.at[at.j], self.full.at[at.j], self.ss.at[to], self.sr.at[at.j], at.seq(to)
        )

    def start(self):
        at = self.at
        self.own().start()
        for r in (at.r_y, at.r_c, at.r_yc):
            self.beside(r).start()

    def step(self):
        at = self.at
        self.own().wait()
        for r in (at.r_y, at.r_c, at.r_yc):
            remote(
                self.mine, self.full.at[at.j, r], self.rs.at[r], self.rr.at[r], at.row(r)
            ).wait()

        @pl.loop(1, at.n)
        def _(i):
            self.onward(at.other(i)).start()

    def finish(self):
        at = self.at

        @pl.loop(1, at.n)
        def _(i):
            src = at.other(i)
            remote(
                self.full.at[src], self.full.at[src], self.ss.at[src], self.sr.at[src],
                at.seq(src),
            ).wait()


class SmallSum:
    @staticmethod
    def scratch(n, w):
        q = w // 4
        return (
            [pltpu.VMEM((8, w), F32), pltpu.VMEM((4, 8, q), F32), pltpu.VMEM((8, q), F32)]
            + [pltpu.VMEM((n, 8, q), F32)]
            + [pltpu.SemaphoreType.DMA((4,))] * 2
            + [pltpu.SemaphoreType.DMA((n,))] * 2
        )

    def __init__(self, at, refs):
        self.at = at
        self.terms, self.beside_in, self.acc, self.seq_in = refs[:4]
        self.rs, self.rr, self.ss, self.sr = refs[4:]
        self.q = self.terms.shape[1] // 4

    def part(self, r):
        return self.terms.at[:, pl.ds(pl.multiple_of(r * self.q, self.q), self.q)]

    def beside(self, r):
        at = self.at
        return remote(
            self.part(r), self.beside_in.at[at.r], self.rs.at[r], self.rr.at[at.r], at.row(r)
        )

    def run(self, out):
        at = self.at
        near = (at.r_y, at.r_c, at.r_yc)
        for r in near:
            self.beside(r).start()
        self.acc[...] = self.part(at.r)[...]
        for r in near:
            remote(
                self.part(r), self.beside_in.at[r], self.rs.at[r], self.rr.at[r], at.row(r)
            ).wait()
            self.acc[...] += self.beside_in[r]

        @pl.loop(1, at.n)
        def _(i):
            to = at.other(i)
            remote(
                self.acc, self.seq_in.at[at.j], self.ss.at[to], self.sr.at[at.j], at.seq(to)
            ).start()

        out[...] = self.acc[...]

        @pl.loop(1, at.n)
        def _(i):
            src = at.other(i)
            remote(
                self.acc, self.seq_in.at[src], self.ss.at[src], self.sr.at[src], at.seq(src)
            ).wait()
            out[...] += self.seq_in[src]


class Call:
    def __init__(self, n, cid, name):
        self.n, self.cid, self.name = n, cid, name
        self.args, self.ins, self.outs, self.out_specs, self.scr = [], [], [], [], []

    def give(self, array, space=pltpu.VMEM):
        for i, known in enumerate(self.args):
            if known is array:
                return ("i", i)
        self.args.append(array)
        self.ins.append(pl.BlockSpec(memory_space=space))
        return ("i", len(self.args) - 1)

    def make(self, shape, dtype, space=pltpu.VMEM):
        self.outs.append(jax.ShapeDtypeStruct(shape, dtype))
        self.out_specs.append(pl.BlockSpec(memory_space=space))
        return ("o", len(self.outs) - 1)

    def scratch(self, items):
        at = len(self.scr)
        self.scr.extend(items)
        return [("s", at + i) for i in range(len(items))]

    def run(self, body, flops=0):
        ni, no = len(self.ins), len(self.outs)

        def kernel(*refs):
            def of(key):
                if isinstance(key, list):
                    return [of(k) for k in key]
                if isinstance(key[0], tuple):
                    return tuple(of(k) for k in key)
                kind, i = key
                return refs[i + {"i": 0, "o": ni, "s": ni + no}[kind]]

            at = Place(self.n)
            at.meet()
            body(at, of)

        return pl.pallas_call(
            kernel,
            out_shape=self.outs,
            in_specs=self.ins,
            out_specs=self.out_specs,
            scratch_shapes=self.scr,
            name=self.name,
            cost_estimate=pl.CostEstimate(
                flops=flops, bytes_accessed=1 << 24, transcendentals=0
            ),
            compiler_params=pltpu.CompilerParams(
                collective_id=self.cid, has_side_effects=True, vmem_limit_bytes=VMEM_LIMIT
            ),
        )(*self.args)


VMEM_LIMIT = 58 << 20
ANY = pltpu.VMEM
CHUNK = 512


def product(at, of, part, pairs, t):
    width, tok = at.width, part.shape[1]

    @pl.loop(0, part.shape[2] // CHUNK)
    def _(i):
        cols = pl.ds(pl.multiple_of(i * CHUNK, CHUNK), CHUNK)
        total = None
        for lhs, rhs, flip in pairs:
            left = of(lhs)[pl.ds(t * (width * tok), width * tok), :]
            if flip:
                term = dot(left, of(rhs)[cols, :], 1, 1)
            else:
                term = dot(left, of(rhs)[:, cols], 1, 0)
            total = term if total is None else total + term
        part[pl.ds(t * width, width), :, cols] = total.reshape(width, tok, CHUNK).astype(BF)


def products(at, of, part, pairs, red):
    for s in range(at.depth - 1, -1, -1):
        for t in [at.z + s, at.z - s] if s else [at.z]:

            @pl.when(jnp.logical_and(t >= 0, t < at.depth))
            def _(t=t):
                product(at, of, part, pairs, t)
                red.emit(t)


def steps(at, red, extra):
    work = extra.fill()
    for w in work[:1]:
        w()
    extra.between(1)
    red.reduce(3)
    for w in work[1:2]:
        w()
    extra.cross(0)
    for w in work[2:]:
        w()
    extra.cross(1)
    extra.between(2)
    red.reduce(2)
    extra.cross(2)
    extra.turn(0)
    extra.between(3)
    red.reduce(1)
    extra.turn(1)


def gather_all(g, between=None):
    at = g.at
    for s in range(1, at.depth):
        g.step(s)
        if between is not None:
            between(s)
    for s in range(at.depth):
        for zz in [at.z - s, at.z + s] if s else [at.z]:

            @pl.when(jnp.logical_and(zz >= 0, zz < at.depth))
            def _(zz=zz):
                g.take_side(zz)


def split_columns(src, dst, runs):
    for b, to, at, size in runs:
        dst[b, :, to : to + size] = src[:, at : at + size]


def join_columns(src, dst, runs):
    for b, to, at, size in runs:
        dst[:, at : at + size] = src[b, :, to : to + size].astype(dst.dtype)


def front_call(n, x, small, ints, weight, runs, out_w):
    tok, d = x.shape
    k, c = weight.shape[0], weight.shape[1] // n
    call = Call(n, 1, "front")
    ix = call.give(x, ANY)
    ism, iin = call.give(small), call.give(ints)
    iw = call.give(weight, ANY)
    ox = call.make((n, tok, d), BF, ANY)
    osm = call.make((n, 4) + small.shape, BF)
    oin = call.make((n,) + ints.shape, jnp.int32)
    ow = call.make((4, n, k, c), BF, ANY)
    sx = call.scratch(Gather.sems(n, ALONE))
    sp = call.scratch([pltpu.VMEM((n, k, c), BF)])
    ssm = call.scratch(SmallGather.sems(n))
    sin = call.scratch(Exchange.sems(n))
    sw = call.scratch(Columns.sems(n))
    if out_w is not None:
        io = call.give(out_w, ANY)
        oo = call.make((4,) + out_w.shape, BF, ANY)
        so = call.scratch(Rows.sems())

    def body(at, of):
        sm = SmallGather(at, of(ism), of(osm), of(ssm))
        g = Gather(at, of(ox), of(sx), ALONE)
        cols = Columns(at, of(sp)[0], of(ow), of(sw))
        spread = Spread(at, of(iin), of(oin), of(sin))
        sm.start()
        of(ox)[at.j] = of(ix)[...]
        g.start()
        spread.start()
        split_columns(of(iw), of(sp)[0], runs)
        cols.start()
        sm.step()
        if out_w is not None:
            rows = Rows(at, of(io), of(oo), of(so))
            rows.start()
        cuts = [0, n // 4, n // 2, n]

        def between(s):
            cols.step(cuts[s - 1], cuts[s])

        gather_all(g, between)
        cols.relay(0, n)
        if out_w is not None:
            rows.relay()
            rows.finish()
        cols.finish()
        g.finish()
        sm.finish()
        spread.finish()

    return call.run(body)


class Spread:
    def __init__(self, at, mine, got, sems):
        self.at, self.mine, self.got = at, mine, got
        self.ssem, self.rsem = sems

    def copy(self, to, src):
        at = self.at
        return remote(
            self.mine, self.got.at[src], self.ssem.at[to], self.rsem.at[src], at.seq(to)
        )

    def own(self):
        return pltpu.make_async_copy(self.mine, self.got.at[self.at.j], self.ssem.at[self.at.j])

    def start(self):
        self.own().start()

        @pl.loop(1, self.at.n)
        def _(i):
            self.copy(self.at.other(i), self.at.j).start()

    def finish(self):
        self.own().wait()

        @pl.loop(1, self.at.n)
        def _(i):
            p = self.at.other(i)
            self.copy(p, p).wait()


def sum_call(n, cid, name, pairs, tok, columns=(), rows=(), gathers=(), row_sums=(), col_sums=()):
    call = Call(n, cid, name)
    d = pairs[0][1].shape[0 if pairs[0][2] else 1]
    keys = []
    for lhs, rhs, flip in pairs:
        keys.append((call.give(lhs), call.give(rhs), flip))
    out = call.make((tok, d), F32)
    part = call.scratch([pltpu.VMEM((n, tok, d), BF)])
    red_s = call.scratch(Reduce.scratch(n, tok, d, SUM_CUTS))
    extra = Extras(call, n, columns, rows, gathers, row_sums, col_sums, PAIRED)

    def body(at, of):
        part_ref = of(part)[0]
        red = Reduce(at, part_ref, of(red_s), SUM_CUTS)
        extra.bind(at, of)
        extra.start()
        products(at, of, part_ref, keys, red)
        steps(at, red, extra)
        red.last(of(out))
        extra.finish()
        red.finish()

    flops = sum(2 * l.shape[0] * l.shape[1] * d for l, _, _ in pairs)
    return call.run(body, flops)


class Extras:
    def __init__(
        self, call, n, columns=(), rows=(), gathers=(), row_sums=(), col_sums=(), cuts=None
    ):
        self.n, self.cuts = n, cuts
        self.columns, self.rows, self.gathers, self.row_sums, self.col_sums = [], [], [], [], []
        for w, runs in columns:
            shape = (n, w.shape[0], w.shape[1] // n)
            self.columns.append(
                (
                    call.give(w),
                    call.make((4,) + shape, BF, ANY),
                    call.scratch([pltpu.VMEM(shape, BF)]),
                    call.scratch(Columns.sems(n)),
                    runs,
                )
            )
        for p in rows:
            self.rows.append(
                (call.give(p, ANY), call.make((4,) + p.shape, BF, ANY), call.scratch(Rows.sems()))
            )
        for p in gathers:
            self.gathers.append(
                (
                    call.give(p, ANY),
                    call.make((n,) + p.shape, BF, ANY),
                    call.scratch(Gather.sems(n, cuts)),
                )
            )
        self.n_row = n_row = 4
        for p in row_sums:
            lhs, rhs = p if isinstance(p, tuple) else (None, None)
            shape = (n_row, lhs.shape[1] // n_row, rhs.shape[1]) if lhs is not None else p.shape
            self.row_sums.append(
                (
                    (call.give(lhs), call.give(rhs)) if lhs is not None else call.give(p),
                    call.scratch([pltpu.VMEM(shape, BF)])[0],
                    call.make(shape[1:], F32),
                    call.scratch(RowSum.scratch(*shape[1:])),
                )
            )
        for p, runs in col_sums:
            lhs, rhs = p if isinstance(p, tuple) else (None, None)
            shape = (n_row, lhs.shape[1] // n_row, rhs.shape[1]) if lhs is not None else p.shape
            k, c = shape[1] // n, shape[2]
            self.col_sums.append(
                (
                    (call.give(lhs), call.give(rhs)) if lhs is not None else call.give(p),
                    call.scratch([pltpu.VMEM(shape, BF)])[0],
                    call.make((k, n * c), F32),
                    call.scratch(RowSum.scratch(*shape[1:])),
                    call.scratch([pltpu.VMEM((n, k, c), BF)] * 2),
                    call.scratch(Exchange.sems(n)),
                    runs,
                )
            )

    def bind(self, at, of):
        self.at, self.of = at, of
        self.b_columns = [
            (Columns(at, of(p)[0], of(o), of(s)), of(i), of(p)[0], runs)
            for i, o, p, s, runs in self.columns
        ]
        self.b_rows = [Rows(at, of(i), of(o), of(s)) for i, o, s in self.rows]
        self.b_gathers = [
            (Gather(at, of(o), of(s), self.cuts), of(i), of(o)) for i, o, s in self.gathers
        ]
        self.b_sums = [
            (RowSum(at, of(g), of(s)), of(o), of(i), of(g)) for i, g, o, s in self.row_sums
        ]
        self.b_cols = []
        for i, g, o, s, v, e, runs in self.col_sums:
            mine, got = of(v)
            self.b_cols.append(
                (
                    RowSum(at, of(g), of(s)),
                    mine,
                    Exchange(at, mine, got, of(e)),
                    (got, of(o), runs),
                    of(i),
                    of(g),
                )
            )

    def start(self):
        at = self.at
        for g, src, buf in self.b_gathers:
            buf[at.j] = src[...]
            g.start()
        for r in self.b_rows:
            r.start()
        for c, src, pieces, runs in self.b_columns:
            split_columns(src, pieces, runs)
            c.start()

    def fill_columns(self, k):
        rs, _, _, _, src, grad = self.b_cols[k]
        if isinstance(src, tuple):
            size = grad.shape[1]

            @pl.loop(0, grad.shape[0])
            def _(b):
                cols = pl.ds(pl.multiple_of(b * size, size), size)
                grad[b] = dot(src[0][:, cols], src[1][...], 0, 0).astype(BF)
        else:
            grad[...] = src[...]
        rs.start()

    def fill_rows(self, k):
        rs, _, src, grad = self.b_sums[k]
        if isinstance(src, tuple):

            @pl.loop(0, grad.shape[2] // CHUNK)
            def _(b):
                cols = pl.ds(pl.multiple_of(b * CHUNK, CHUNK), CHUNK)
                term = dot(src[0][...], src[1][:, cols], 0, 0)
                grad[:, :, cols] = term.reshape(grad.shape[0], grad.shape[1], CHUNK).astype(BF)
        else:
            grad[...] = src[...]
        rs.start()

    def fill(self):
        work = [functools.partial(self.fill_columns, k) for k in range(len(self.b_cols))]
        return work + [functools.partial(self.fill_rows, k) for k in range(len(self.b_sums))]

    def cross(self, k):
        every = [c[0] for c in self.b_cols] + [r[0] for r in self.b_sums]
        if k < len(every):
            every[k].cross()

    def turn(self, k):
        if k < len(self.b_cols):
            rs, mine, ex = self.b_cols[k][:3]
            mine[...] = rs.total().reshape(mine.shape).astype(BF)
            ex.start()

    def between(self, s):
        n = self.n
        cuts = [0, n // 4, n // 2, n]
        for g, _, _ in self.b_gathers:
            g.step(s)
        for c, *_ in self.b_columns:
            c.step(cuts[s - 1], cuts[s])

    def finish(self):
        at = self.at
        for g, _, _ in self.b_gathers:
            for zz in range(at.depth):
                g.take_side(zz)
            g.finish()
        for r in self.b_rows:
            r.relay()
        for c, *_ in self.b_columns:
            c.relay(0, self.n)
        for r in self.b_rows:
            r.finish()
        for c, *_ in self.b_columns:
            c.finish()
        for rs, out, *_ in self.b_sums:
            out[...] = rs.total()
            rs.finish()
        for rs, _, ex, (got, out, runs), *_ in self.b_cols:
            ex.finish()
            rs.finish()
            join_columns(got, out, runs)


def gather_call(n, cid, name, x, columns=(), rows=(), row_sums=(), col_sums=()):
    call = Call(n, cid, name)
    extra = Extras(call, n, columns, rows, [x], row_sums, col_sums, ALONE)

    def body(at, of):
        extra.bind(at, of)
        extra.start()
        for piece in extra.fill():
            piece()
        for k in range(3):
            extra.cross(k)
        for s in range(1, at.depth):
            extra.between(s)
        for k in range(2):
            extra.turn(k)
        extra.finish()

    return call.run(body)


def digit(code, i):
    return lax.rem(code // jnp.where(i == 0, 1, jnp.where(i == 1, 10, jnp.where(i == 2, 100, 1000))), 10)


def by_place(z, codes):
    return jnp.where(z == 0, codes[0], jnp.where(z == 1, codes[1], jnp.where(z == 2, codes[2], codes[3])))


def core_call(n, pair, x, gain, bias, columns, rows, gathers):
    call = Call(n, 2, "core")
    tok, d = x.shape
    c = columns[0][0].shape[1] // n
    wide = n // LINE * tok
    length = n * tok
    key = (call.give(pair[0]), call.give(pair[1]), False)
    i_x, i_gain, i_bias = call.give(x), call.give(gain), call.give(bias)
    o_hid = call.make((tok, d), F32)
    out = call.make((tok, d), F32)
    o_mid = call.make((n, tok, d), BF)
    o_acts = [call.make((length, c), BF) for _ in range(3)]
    part = call.scratch([pltpu.VMEM((n, tok, d), BF)] * 2)
    first_s = call.scratch(Reduce.scratch(n, tok, d, SUM_CUTS))
    extra = Extras(call, n, columns, rows, gathers, cuts=PAIRED)
    gat_s = call.scratch(Gather.sems(n, MLP_CUTS))
    red_s = call.scratch(Reduce.scratch(n, tok, d, MLP_SUMS))

    def body(at, of):
        first_part, part_ref = of(part)
        first = Reduce(at, first_part, of(first_s), SUM_CUTS)
        mid, hid = of(o_mid), of(o_hid)
        inner_ref, gg_ref, gu_ref = of(o_acts)
        gat = Gather(at, mid, of(gat_s), MLP_CUTS)
        red = Reduce(at, part_ref, of(red_s), MLP_SUMS)
        extra.bind(at, of)
        extra.start()
        products(at, of, first_part, [key], first)
        steps(at, first, extra)
        first.last(hid)
        hid[...] += of(i_x)[...].astype(F32)
        normed, _ = norm_stats(hid[...])
        mid[at.j] = (normed * of(i_gain)[...] + of(i_bias)[...]).astype(BF)
        gat.start()
        extra.finish()
        gat.open_wide()
        gate, up = (c[0].full for c in extra.b_columns)
        down, grad = extra.b_rows[0].full, extra.b_gathers[0][2]
        gate, up = gate.reshape(d, c), up.reshape(d, c)
        down = down.reshape(c, d)
        order = by_place(at.z, (3210, 3201, 132, 123))
        edge = jnp.logical_or(at.z == 0, at.z == at.depth - 1)

        @pl.loop(0, LINE)
        def _(i):
            t = digit(order, i)
            lo = jnp.where(edge, i + 1, jnp.where(i == 0, 1, jnp.where(i == 1, 3, 4)))
            hi = jnp.where(edge, jnp.minimum(i + 2, 4), jnp.where(i == 0, 3, 4))

            @pl.loop(lo, hi)
            def _(m):
                gat.fetch(digit(order, m))

            gat.take_side(t)
            here = pl.ds(t * at.width, at.width)
            these = pl.ds(t * wide, wide)
            tokens = mid[here].reshape(wide, d)
            gate_pre = dot(tokens, gate[...], 1, 0)
            sig = 1.0 / (1.0 + jnp.exp(-gate_pre))
            silu = gate_pre * sig
            up_pre = dot(tokens, up[...], 1, 0)
            inner_ref[these] = (silu * up_pre).astype(BF)
            g_inner = dot(grad[here].reshape(wide, d), down[...], 1, 1)
            gu_ref[these] = (g_inner * silu).astype(BF)
            gg_ref[these] = (g_inner * up_pre * sig * (1.0 + gate_pre * (1.0 - sig))).astype(BF)
            product(at, lambda k: k, part_ref, [(gg_ref, gate, True), (gu_ref, up, True)], t)
            red.emit(t)

            @pl.when(jnp.logical_and(edge, i >= 2))
            def _():
                red.pass_on(digit(order, i - 1))

        rest = by_place(at.z, (3, 32, 301, 0))

        @pl.loop(0, jnp.where(edge, 1, 3))
        def _(i):
            red.pass_on(digit(rest, i))

        red.last(of(out))
        gat.finish()
        first.finish()
        red.finish()

    return call.run(body)


def last_call(n, cid, pairs, tok, normed, known, row_sums, col_sums):
    call = Call(n, cid, "last")
    d = pairs[0][1].shape[0]
    keys = []
    for lhs, rhs, flip in pairs:
        keys.append((call.give(lhs), call.give(rhs), flip))
    i_norm, i_known = call.give(normed), call.give(known)
    out = call.make((tok, d), F32)
    o_small = call.make((8, d // 4), F32)
    part = call.scratch([pltpu.VMEM((n, tok, d), BF)])
    red_s = call.scratch(Reduce.scratch(n, tok, d, SUM_CUTS))
    s_small = call.scratch(SmallSum.scratch(n, d))
    extra = Extras(call, n, row_sums=row_sums, col_sums=col_sums)

    def body(at, of):
        part_ref = of(part)[0]
        red = Reduce(at, part_ref, of(red_s), SUM_CUTS)
        extra.bind(at, of)
        extra.start()
        products(at, of, part_ref, keys, red)
        steps(at, red, extra)
        red.last(of(out))
        small = SmallSum(at, of(s_small))
        small.terms[...] = of(i_known)[...]
        grad = of(out)[...]
        small.terms[0:1, :] = jnp.sum(grad * of(i_norm)[...], axis=0, keepdims=True)
        small.terms[1:2, :] = jnp.sum(grad, axis=0, keepdims=True)
        small.run(of(o_small))
        extra.finish()
        red.finish()

    return call.run(body)


def attention(queries, keys, values, allowed):
    scores = jnp.einsum("qhd,khd->hqk", queries, keys, preferred_element_type=F32)
    exp_weights = jnp.where(allowed[None], jnp.exp(scores), 0.0)
    denominator = jnp.sum(exp_weights, axis=-1)
    numerator = jnp.einsum(
        "hqk,khd->qhd", exp_weights.astype(BF), values, preferred_element_type=F32
    )
    return numerator / jnp.transpose(denominator)[:, :, None], denominator


def attention_back(queries, keys, values, allowed, denominator, context, g_context):
    den = jnp.transpose(denominator)
    g_numer = (g_context / den[:, :, None]).astype(BF)
    g_den = jnp.transpose(-jnp.sum(g_context * context, axis=-1) / den)
    scores = jnp.einsum("qhd,khd->hqk", queries, keys, preferred_element_type=F32)
    exp_weights = jnp.where(allowed[None], jnp.exp(scores), 0.0)
    g_values = jnp.einsum(
        "hqk,qhd->khd", exp_weights.astype(BF), g_numer, preferred_element_type=F32
    )
    g_weights = jnp.einsum("qhd,khd->hqk", g_numer, values, preferred_element_type=F32)
    g_scores = (exp_weights * (g_weights + g_den[:, :, None])).astype(BF)
    g_queries = jnp.einsum("hqk,khd->qhd", g_scores, keys, preferred_element_type=F32)
    g_keys = jnp.einsum("hqk,qhd->khd", g_scores, queries, preferred_element_type=F32)
    return g_queries, g_keys, g_values


def body(nrow, n, *args):
    (
        layer_in,
        segments,
        positions,
        attn_norm_gain,
        attn_norm_bias,
        qkv_weight,
        qkv_bias,
        out_weight,
        mlp_norm_gain,
        mlp_norm_bias,
        gate_weight,
        up_weight,
        down_weight,
        out_grad,
    ) = args
    j = lax.axis_index("seq")
    tok = layer_in.shape[1]
    length = n * tok
    k = qkv_weight.shape[0]
    f = down_weight.shape[0]
    hp = H // n
    whole_heads = out_weight.shape[0] == HD
    roomy = length * D <= 1 << 22

    if whole_heads:
        head_runs = [
            (b, (m * nrow + r) * HD, m * D + (r * n + b) * HD, HD)
            for b in range(n) for m in range(3) for r in range(nrow)
        ]
    else:
        size = hp * HD
        head_runs = [
            (b, m * size, m * D + b * size, size) for b in range(n) for m in range(3)
        ]
    ff_runs = [(b, r * f, (r * n + b) * f, f) for b in range(n) for r in range(nrow)]

    def split_heads(w):
        lead = w.shape[0]
        if whole_heads:
            w = w.reshape(lead, 3, nrow, n, HD).transpose(3, 0, 1, 2, 4)
        else:
            w = w.reshape(lead, 3, n, hp, HD).transpose(2, 0, 1, 3, 4)
        return w.reshape(n, lead, 3 * hp * HD)

    def join_heads(blocks):
        lead = blocks.shape[1]
        if whole_heads:
            w = blocks.reshape(n, lead, 3, nrow, HD).transpose(1, 2, 3, 0, 4)
        else:
            w = blocks.reshape(n, lead, 3, hp, HD).transpose(1, 2, 0, 3, 4)
        return w.reshape(lead, 3 * D)

    small = jnp.concatenate(
        [attn_norm_gain, attn_norm_bias, mlp_norm_gain, mlp_norm_bias, qkv_bias]
    )
    small = jnp.pad(small, (0, 2048 - small.shape[0])).reshape(16, 128)
    ints = jnp.concatenate([segments, positions, jnp.zeros((6, tok), jnp.int32)], 0)
    front = front_call(
        n, layer_in[0], small, ints, qkv_weight, head_runs, out_weight if whole_heads else None
    )
    x_all, small_all, ints_all, qkv_own = front[:4]
    x_all = x_all.reshape(length, D)
    qkv_own = qkv_own.reshape(D, 3 * hp * HD)
    if whole_heads:
        out_own = front[4].reshape(hp * HD, D)
    else:
        out_full = lax.all_gather(out_weight, ("row", "seq"), axis=0, tiled=True)
        out_own = lax.dynamic_slice_in_dim(out_full, j * hp * HD, hp * HD, 0)
    small_all = small_all.transpose(1, 0, 2, 3).reshape(nrow * n, 2048)
    attn_gain, attn_bias, mlp_gain, mlp_bias = (
        small_all[:, c : c + k].reshape(1, D).astype(F32) for c in (0, k, 2 * k, 3 * k)
    )
    qkv_shift = small_all[:, 4 * k : 4 * k + 3 * k].reshape(1, 3 * D)
    shift_own = lax.dynamic_index_in_dim(split_heads(qkv_shift), j, 0, keepdims=False).astype(F32)
    seg_all, pos_all = ints_all[:, 0].reshape(length), ints_all[:, 1].reshape(length)

    inputs_all = (norm_stats(x_all.astype(F32))[0] * attn_gain + attn_bias).astype(BF)
    inputs_all = lax.optimization_barrier(inputs_all)
    projected = dot(inputs_all, qkv_own, 1, 0) + shift_own
    head_split = projected.reshape(length, 3, hp, HD)
    cosine, sine_part = rotary_tables(pos_all)
    queries = (rotate(head_split[:, 0], cosine, sine_part, 1.0) / math.sqrt(HD)).astype(BF)
    keys = rotate(head_split[:, 1], cosine, sine_part, 1.0).astype(BF)
    values = head_split[:, 2].astype(BF)
    index = jnp.arange(length, dtype=jnp.int32)
    allowed = (seg_all[:, None] == seg_all[None, :]) & (index[None, :] <= index[:, None])
    context, denominator = attention(queries, keys, values, allowed)
    context_low = context.reshape(length, hp * HD).astype(BF)
    x_float = layer_in[0].astype(F32)
    grad_float = out_grad[0].astype(F32)
    ff_columns = [(gate_weight, ff_runs), (up_weight, ff_runs)]
    if roomy:
        (
            hidden_mid, g_middle, middle_all, inner_act, g_gate, g_up, _, _, down_own, grad_all,
        ) = core_call(
            n, (context_low, out_own), layer_in[0], mlp_gain, mlp_bias, ff_columns, [down_weight],
            [out_grad[0]],
        )
        down_own = down_own.reshape(nrow * f, D)
        middle_all, grad_all = middle_all.reshape(length, D), grad_all.reshape(length, D)
        normed2, inv_std2 = norm_stats(hidden_mid)
    else:
        attn_branch, gate_own, up_own, down_own = sum_call(
            n, 2, "mix_sum", [(context_low, out_own, False)], tok, columns=ff_columns,
            rows=[down_weight],
        )
        gate_own, up_own = gate_own.reshape(D, nrow * f), up_own.reshape(D, nrow * f)
        down_own = down_own.reshape(nrow * f, D)
        hidden_mid = x_float + attn_branch
        normed2, inv_std2 = norm_stats(hidden_mid)
        middle = (normed2 * mlp_gain + mlp_bias).astype(BF)
        (middle_all,) = gather_call(n, 3, "middle", middle)
        middle_all = middle_all.reshape(length, D)
        gate_pre = dot(middle_all, gate_own, 1, 0)
        up_pre = dot(middle_all, up_own, 1, 0)
        sig = jax.nn.sigmoid(gate_pre)
        silu = gate_pre * sig
        inner_act = (silu * up_pre).astype(BF)
        (grad_all,) = gather_call(n, 8, "grads", out_grad[0])
        grad_all = grad_all.reshape(length, D)
        g_inner = dot(grad_all, down_own, 1, 1)
        g_gate = (g_inner * up_pre * sig * (1.0 + gate_pre * (1.0 - sig))).astype(BF)
        g_up = (g_inner * silu).astype(BF)
        (g_middle,) = sum_call(
            n, 5, "mlp_back", [(g_gate, gate_own, True), (g_up, up_own, True)], tok
        )
    normed1, inv_std1 = norm_stats(x_float)
    if roomy:
        down_part, gate_part, up_part = (inner_act, grad_all), (middle_all, g_gate), (middle_all, g_up)
    else:
        down_part = dot(inner_act, grad_all, 0, 0).astype(BF).reshape(nrow, f, D)
        gate_part = dot(middle_all, g_gate, 0, 0).astype(BF).reshape(nrow, n * k, nrow * f)
        up_part = dot(middle_all, g_up, 0, 0).astype(BF).reshape(nrow, n * k, nrow * f)
    g_hidden = grad_float + norm_back(g_middle, normed2, inv_std2, mlp_gain)
    g_attn = g_hidden.astype(BF)
    if roomy:
        mlp_branch, g_attn_all, down_grad, gate_grad, up_grad = sum_call(
            n, 6, "mlp_sum", [(inner_act, down_own, False)], tok, gathers=[g_attn],
            row_sums=[down_part], col_sums=[(gate_part, ff_runs), (up_part, ff_runs)],
        )
    else:
        mlp_branch, down_grad = sum_call(
            n, 4, "mlp_sum", [(inner_act, down_own, False)], tok, row_sums=[down_part]
        )
        g_attn_all, gate_grad, up_grad = gather_call(
            n, 6, "hidden_back", g_attn, col_sums=[(gate_part, ff_runs), (up_part, ff_runs)]
        )
    g_attn_all = g_attn_all.reshape(length, D)
    layer_out = (hidden_mid + mlp_branch).astype(BF)

    g_context = dot(g_attn_all, out_own, 1, 1).reshape(length, hp, HD)
    g_queries, g_keys, g_values = attention_back(
        queries, keys, values, allowed, denominator, context, g_context
    )
    query_part = rotate(g_queries, cosine, sine_part, -1.0) / math.sqrt(HD)
    key_part = rotate(g_keys, cosine, sine_part, -1.0)
    g_projected = (
        jnp.stack([query_part, key_part, g_values], 1).reshape(length, 3 * hp * HD).astype(BF)
    )
    if roomy:
        qkv_part, out_part = (inputs_all, g_projected), (context_low, g_attn_all)
    else:
        qkv_part = dot(inputs_all, g_projected, 0, 0).astype(BF)
        qkv_part = qkv_part.reshape(nrow, n * k, 3 * hp * HD)
        out_part = dot(context_low, g_attn_all, 0, 0).astype(BF)
        if whole_heads:
            out_part = out_part.reshape((nrow,) + out_weight.shape)
    shift_sum = jnp.sum(g_projected.astype(F32), axis=0)
    shift_blocks = lax.dynamic_update_slice_in_dim(
        jnp.zeros((n, 1, 3 * hp * HD), F32), shift_sum[None, None], j, 0
    )
    shift_full = join_heads(shift_blocks)[0]
    known = jnp.concatenate(
        [
            jnp.zeros((2, D), F32),
            jnp.sum(g_middle * normed2, axis=0)[None],
            jnp.sum(g_middle, axis=0)[None],
            shift_full.reshape(nrow, 3, D // nrow).transpose(1, 0, 2).reshape(3, D),
            jnp.zeros((1, D), F32),
        ]
    )
    last = last_call(
        n, 7, [(g_projected, qkv_own, True)], tok, normed1, known,
        [out_part] if whole_heads else [],
        [(qkv_part, head_runs)],
    )
    if whole_heads:
        g_inputs, small_grads, out_w_grad, qkv_grad = last
    else:
        g_inputs, small_grads, qkv_grad = last
        if roomy:
            out_part = dot(*out_part, 0, 0).astype(BF)
        placed = lax.dynamic_update_slice_in_dim(
            jnp.zeros((D, D), BF), out_part, j * hp * HD, 0
        )
        out_w_grad = lax.psum_scatter(
            placed, ("row", "seq"), scatter_dimension=0, tiled=True
        ).astype(F32)
    input_grad = g_hidden + norm_back(g_inputs, normed1, inv_std1, attn_gain)
    own = lax.dynamic_slice_in_dim(small_grads, j * k, k, 1)
    shift_own_grad = lax.dynamic_slice_in_dim(small_grads[4:7].reshape(-1), j * 3 * k, 3 * k, 0)
    return (
        layer_out[None],
        input_grad[None],
        own[0],
        own[1],
        qkv_grad,
        shift_own_grad,
        out_w_grad,
        own[2],
        own[3],
        gate_grad,
        up_grad,
        down_grad,
    )


def solution(mesh):
    nrow, n = mesh.shape["row"], mesh.shape["seq"]

    def local(*args):
        return body(nrow, n, *args)

    tokens, ints = P("row", "seq", None), P("row", "seq")
    vec, mat = P(("row", "seq")), P(("row", "seq"), None)
    return jax.shard_map(
        local,
        mesh=mesh,
        in_specs=(
            tokens, ints, ints, vec, vec, mat, vec, mat, vec, vec, mat, mat, mat, tokens,
        ),
        out_specs=(tokens, tokens, vec, vec, mat, vec, mat, vec, vec, mat, mat, mat),
        check_vma=False,
    )
```

```python
import functools
import math

import jax
import jax.numpy as jnp
from jax import lax
from jax.experimental import pallas as pl
from jax.experimental.pallas import tpu as pltpu
from jax.sharding import PartitionSpec as P

D = 2048
H = 32
HD = 64
ROT = 16
EPSILON = 1e-05
BF = jnp.bfloat16
F32 = jnp.float32


def dot(a, b, ca, cb):
    return lax.dot_general(a, b, (((ca,), (cb,)), ((), ())), preferred_element_type=F32)


def norm_stats(values_in):
    average = jnp.mean(values_in, axis=-1, keepdims=True)
    centered = values_in - average
    inv_std = lax.rsqrt(jnp.mean(centered * centered, axis=-1, keepdims=True) + EPSILON)
    return (centered * inv_std, inv_std)


def norm_back(grad_in, normed, inv_std, gain_vector):
    scaled = grad_in * gain_vector
    return inv_std * (
        scaled
        - jnp.mean(scaled, axis=-1, keepdims=True)
        - normed * jnp.mean(scaled * normed, axis=-1, keepdims=True)
    )


def rotary_tables(positions):
    half_rot = ROT // 2
    frequency = 10000.0 ** (-2.0 * jnp.arange(half_rot, dtype=F32) / ROT)
    angles = positions.astype(F32)[:, None] * frequency[None, :]
    return (jnp.cos(angles)[:, None, :], jnp.sin(angles)[:, None, :])


def rotate(head_values, cosine, sine_part, direction):
    half_rot = ROT // 2
    first_half = head_values[..., :half_rot]
    second = head_values[..., half_rot:ROT]
    return jnp.concatenate(
        [
            first_half * cosine - direction * second * sine_part,
            second * cosine + direction * first_half * sine_part,
            head_values[..., ROT:],
        ],
        axis=-1,
    )


MESH = pl.DeviceIdType.MESH
LINE = 4


class Place:
    def __init__(self, n):
        self.n = n
        self.depth = LINE
        self.width = n // LINE
        self.r = lax.axis_index("row")
        self.j = lax.axis_index("seq")
        self.z = self.j // self.width
        self.x = lax.rem(self.j, self.width)
        y, c = self.r // 2, lax.rem(self.r, 2)
        self.y, self.c = y, c
        self.r_y = (1 - y) * 2 + c
        self.r_c = y * 2 + (1 - c)
        self.r_yc = (1 - y) * 2 + (1 - c)

    def inner(self, t):
        return jnp.logical_or(
            jnp.logical_and(t > self.z, self.z > 0),
            jnp.logical_and(t < self.z, self.z < self.depth - 1),
        )

    def seq(self, j):
        return (self.r, j)

    def row(self, r):
        return (r, self.j)

    def other(self, i):
        return lax.rem(self.j + i, self.n)

    def meet(self):
        barrier = pltpu.get_barrier_semaphore()
        for r in (self.r_y, self.r_c, self.r_yc):
            pl.semaphore_signal(barrier, inc=1, device_id=self.row(r), device_id_type=MESH)
        for i in range(1, self.n):
            pl.semaphore_signal(
                barrier, inc=1, device_id=self.seq(self.other(i)), device_id_type=MESH
            )
        pl.semaphore_wait(barrier, self.n + 2)


def remote(src, dst, ssem, rsem, device):
    return pltpu.make_async_remote_copy(
        src_ref=src, dst_ref=dst, send_sem=ssem, recv_sem=rsem, device_id=device,
        device_id_type=MESH,
    )


ALONE = ((1, True), (3, False), (4, False))
PAIRED = ((2, True), (6, False))
SUM_CUTS = ((2, True), (6, False))
MLP_CUTS = ((2, True), (3, False), (3, False))
MLP_SUMS = ((2, True), (3, False), (3, False))


class Gather:
    @staticmethod
    def sems(n, cuts):
        w = n // LINE
        out = []
        for _ in cuts:
            out += [
                pltpu.SemaphoreType.DMA((2, n)),
                pltpu.SemaphoreType.DMA((LINE, max(w - 1, 1))),
                pltpu.SemaphoreType.DMA((n,)),
            ]
        return out

    def __init__(self, at, buf, sems, cuts):
        self.at, self.buf = at, buf
        tok = buf.shape[1]
        self.cuts = []
        first = 0
        for i, (share, wide) in enumerate(cuts):
            rows = tok * share // 8
            self.cuts.append((pl.ds(first, rows), wide, sems[3 * i : 3 * i + 3]))
            first += rows

    def copy(self, cut, b, to, sem):
        here = self.buf.at[b, cut[0]]
        return remote(here, here, sem, cut[2][2].at[b], self.at.seq(to))

    def along(self, cut, way, b):
        at = self.at
        to = at.j + at.width if way == 0 else at.j - at.width
        return self.copy(cut, b, to, cut[2][0].at[way, b])

    def across(self, cut, zz, i):
        at = self.at
        to = at.z * at.width + lax.rem(at.x + i, at.width)
        return self.copy(cut, zz * at.width + at.x, to, cut[2][1].at[zz, i - 1])

    def take(self, cut, b):
        self.copy(cut, b, self.at.other(1), cut[2][0].at[0, 0]).wait_recv()

    def onward(self, cut, way, b):
        at = self.at

        @pl.when(at.z < at.depth - 1 if way == 0 else at.z > 0)
        def _():
            self.along(cut, way, b).start()

    def start(self):
        at = self.at
        for cut in self.cuts:
            if cut[1]:
                for i in range(1, at.width):
                    self.across(cut, at.z, i).start()
        for cut in self.cuts:
            for way in range(2):
                self.onward(cut, way, at.j)
            if not cut[1]:
                for i in range(1, at.width):
                    self.across(cut, at.z, i).start()

    def step(self, s):
        at = self.at
        for cut in self.cuts:
            if s == 1 and cut[1]:
                for i in range(1, at.width):
                    b = at.z * at.width + lax.rem(at.x + i, at.width)
                    self.take(cut, b)
                    for way in range(2):
                        self.onward(cut, way, b)
        for cut in self.cuts:
            for way in range(2):
                zz = at.z - s if way == 0 else at.z + s

                @pl.when(zz >= 0 if way == 0 else zz < at.depth)
                def _(zz=zz, way=way, cut=cut):
                    if cut[1]:
                        for i in range(at.width):
                            b = zz * at.width + lax.rem(at.x + i, at.width)
                            self.take(cut, b)
                            self.onward(cut, way, b)
                    else:
                        b = zz * at.width + at.x
                        self.take(cut, b)
                        self.onward(cut, way, b)
                        for i in range(1, at.width):
                            self.across(cut, zz, i).start()

    def fetch(self, zz):
        at = self.at
        for way in range(2):

            @pl.when(zz < at.z if way == 0 else zz > at.z)
            def _(way=way):
                for cut in self.cuts:
                    for i in range(at.width if cut[1] else 1):
                        b = zz * at.width + lax.rem(at.x + i, at.width)
                        self.take(cut, b)
                        self.onward(cut, way, b)
                    if not cut[1]:
                        for i in range(1, at.width):
                            self.across(cut, zz, i).start()

    def open_wide(self):
        at = self.at
        for cut in self.cuts:
            if cut[1]:
                for i in range(1, at.width):
                    b = at.z * at.width + lax.rem(at.x + i, at.width)
                    self.take(cut, b)
                    for way in range(2):
                        self.onward(cut, way, b)

    def take_side(self, zz):
        at = self.at
        for cut in self.cuts:
            if not cut[1]:
                for i in range(1, at.width):
                    self.take(cut, zz * at.width + lax.rem(at.x + i, at.width))

    def finish(self):
        at = self.at
        for cut in self.cuts:
            for zz in range(at.depth):
                for i in range(1, at.width):
                    if cut[1]:
                        @pl.when(at.z == zz)
                        def _(zz=zz, i=i, cut=cut):
                            self.across(cut, zz, i).wait_send()
                    else:
                        self.across(cut, zz, i).wait_send()
                for way in range(2):
                    ok = jnp.logical_and(at.z >= zz, at.z < at.depth - 1) if way == 0 else jnp.logical_and(at.z <= zz, at.z > 0)

                    @pl.when(ok)
                    def _(zz=zz, way=way, cut=cut):
                        for i in range(at.width if cut[1] else 1):
                            b = zz * at.width + lax.rem(at.x + i, at.width)
                            self.along(cut, way, b).wait_send()


class NarrowSum:
    @staticmethod
    def scratch(n, size, d):
        side = max(n // LINE - 1, 1)
        return (
            [pltpu.VMEM((LINE, side, size, d), BF), pltpu.VMEM((LINE + 1, size, d), BF)]
            + [pltpu.SemaphoreType.DMA((LINE, side))] * 2
            + [pltpu.SemaphoreType.DMA((LINE,)), pltpu.SemaphoreType.DMA((LINE + 1,))]
        )

    def __init__(self, at, part, rows, refs):
        self.at, self.part, self.rows = at, part, rows
        self.xr, self.lr, self.xs_sem, self.xr_sem, self.ls_sem, self.lr_sem = refs

    def across(self, t, i):
        at = self.at
        xx = lax.rem(at.x + i, at.width)
        return remote(
            self.part.at[t * at.width + xx, self.rows], self.xr.at[t, i - 1],
            self.xs_sem.at[t, i - 1], self.xr_sem.at[t, i - 1], at.seq(at.z * at.width + xx),
        )

    def along(self, t):
        at = self.at
        there = jnp.where(t > at.z, at.j + at.width, at.j - at.width)
        slot = jnp.where(t == at.z - 1, at.depth, t)
        return remote(
            self.part.at[t * at.width + at.x, self.rows], self.lr.at[slot],
            self.ls_sem.at[t], self.lr_sem.at[slot], at.seq(there),
        )

    def landed(self, slot):
        remote(
            self.lr.at[slot], self.lr.at[slot], self.ls_sem.at[0], self.lr_sem.at[slot],
            self.at.seq(self.at.other(1)),
        ).wait_recv()

    def emit(self, t):
        for i in range(1, self.at.width):
            self.across(t, i).start()

    def summed(self, t):
        at = self.at
        total = self.part[t * at.width + at.x, self.rows].astype(F32)
        for i in range(1, at.width):
            self.across(t, i).wait_recv()
            total = total + self.xr[t, i - 1].astype(F32)
        return total

    def pass_on(self, t):
        at = self.at
        block = (t * at.width + at.x, self.rows)
        total = self.summed(t)
        inner = at.inner(t)

        @pl.when(inner)
        def _():
            self.landed(t)
            self.part[block] = (total + self.lr[t].astype(F32)).astype(BF)

        @pl.when(jnp.logical_not(inner))
        def _():
            self.part[block] = total.astype(BF)

        self.along(t).start()

    def close(self):
        pass

    def last(self, out):
        at = self.at
        out[self.rows] = self.summed(at.z)

        @pl.when(at.z > 0)
        def _():
            self.landed(at.z)
            out[self.rows] += self.lr[at.z].astype(F32)

        @pl.when(at.z < at.depth - 1)
        def _():
            self.landed(at.depth)
            out[self.rows] += self.lr[at.depth].astype(F32)

    def finish(self):
        at = self.at
        for t in range(at.depth):
            for i in range(1, at.width):
                self.across(t, i).wait_send()

            @pl.when(at.z != t)
            def _(t=t):
                self.along(t).wait_send()


class WideSum:
    @staticmethod
    def scratch(n, size, d):
        w = n // LINE
        side = max(w - 1, 1)
        return (
            [pltpu.VMEM((side, size, d), BF), pltpu.VMEM((LINE + 1, w, size, d), BF)]
            + [pltpu.SemaphoreType.DMA((side,))] * 2
            + [pltpu.SemaphoreType.DMA((LINE, w)), pltpu.SemaphoreType.DMA((LINE + 1, w))]
        )

    def __init__(self, at, part, rows, refs):
        self.at, self.part, self.rows = at, part, rows
        self.xr, self.lr, self.xs_sem, self.xr_sem, self.ls_sem, self.lr_sem = refs

    def across(self, i):
        at = self.at
        xx = lax.rem(at.x + i, at.width)
        return remote(
            self.part.at[at.z * at.width + xx, self.rows], self.xr.at[i - 1],
            self.xs_sem.at[i - 1], self.xr_sem.at[i - 1], at.seq(at.z * at.width + xx),
        )

    def along(self, t, xx):
        at = self.at
        there = jnp.where(t > at.z, at.j + at.width, at.j - at.width)
        slot = jnp.where(t == at.z - 1, at.depth, t)
        return remote(
            self.part.at[t * at.width + xx, self.rows], self.lr.at[slot, xx],
            self.ls_sem.at[t, xx], self.lr_sem.at[slot, xx], at.seq(there),
        )

    def landed(self, slot, xx):
        remote(
            self.lr.at[slot, xx], self.lr.at[slot, xx], self.ls_sem.at[0, xx],
            self.lr_sem.at[slot, xx], self.at.seq(self.at.other(1)),
        ).wait_recv()

    def emit(self, t):
        at = self.at

        @pl.when(jnp.logical_and(t != at.z, jnp.logical_not(at.inner(t))))
        def _():
            for xx in range(at.width):
                self.along(t, xx).start()

    def pass_on(self, t):
        at = self.at

        @pl.when(at.inner(t))
        def _():
            for xx in range(at.width):
                self.landed(t, xx)
                block = (t * at.width + xx, self.rows)
                total = self.part[block].astype(F32) + self.lr[t, xx].astype(F32)
                self.part[block] = total.astype(BF)
                self.along(t, xx).start()

    def line_sum(self, xx, put):
        at = self.at
        own = self.part[at.z * at.width + xx, self.rows].astype(F32)

        @pl.when(at.z == 0)
        def _():
            self.landed(at.depth, xx)
            put(own + self.lr[at.depth, xx].astype(F32))

        @pl.when(at.z == at.depth - 1)
        def _():
            self.landed(at.z, xx)
            put(own + self.lr[at.z, xx].astype(F32))

        @pl.when(jnp.logical_and(at.z > 0, at.z < at.depth - 1))
        def _():
            self.landed(at.depth, xx)
            self.landed(at.z, xx)
            put(own + self.lr[at.depth, xx].astype(F32) + self.lr[at.z, xx].astype(F32))

    def close(self):
        at = self.at
        for i in range(1, at.width):
            xx = lax.rem(at.x + i, at.width)

            def put(total, xx=xx):
                self.part[at.z * at.width + xx, self.rows] = total.astype(BF)

            self.line_sum(xx, put)
            self.across(i).start()

    def last(self, out):
        at = self.at

        def put(total):
            out[self.rows] = total

        self.line_sum(at.x, put)
        for i in range(1, at.width):
            self.across(i).wait_recv()
            out[self.rows] += self.xr[i - 1].astype(F32)

    def finish(self):
        at = self.at
        for i in range(1, at.width):
            self.across(i).wait_send()
        for t in range(at.depth):

            @pl.when(at.z != t)
            def _(t=t):
                for xx in range(at.width):
                    self.along(t, xx).wait_send()


class Reduce:
    @staticmethod
    def scratch(n, tok, d, cuts):
        out = []
        for share, wide in cuts:
            out += (WideSum if wide else NarrowSum).scratch(n, tok * share // 8, d)
        return out

    def __init__(self, at, part, refs, cuts):
        self.at, self.cuts = at, []
        tok = part.shape[1]
        first = 0
        for i, (share, wide) in enumerate(cuts):
            rows = pl.ds(first, tok * share // 8)
            first += tok * share // 8
            self.cuts.append((WideSum if wide else NarrowSum)(at, part, rows, refs[6 * i : 6 * i + 6]))

    def emit(self, t):
        for c in self.cuts:
            c.emit(t)

    def pass_on(self, t):
        for c in self.cuts:
            c.pass_on(t)

    def reduce(self, s):
        at = self.at
        for t in (at.z + s, at.z - s):

            @pl.when(jnp.logical_and(t >= 0, t < at.depth))
            def _(t=t):
                self.pass_on(t)

    def last(self, out):
        for c in self.cuts:
            c.close()
        for c in self.cuts[::-1]:
            c.last(out)

    def finish(self):
        for c in self.cuts:
            c.finish()


class Columns:
    @staticmethod
    def sems(n):
        return [pltpu.SemaphoreType.DMA((4, n)), pltpu.SemaphoreType.DMA((4, n))]

    def __init__(self, at, pieces, full, sems):
        self.at, self.pieces, self.full = at, pieces, full
        self.ssem, self.rsem = sems

    def first(self, i):
        at = self.at
        to = at.other(i)
        return remote(
            self.pieces.at[to], self.full.at[at.r, at.j], self.ssem.at[0, to],
            self.rsem.at[at.r, at.j], at.seq(to),
        )

    def own(self):
        at = self.at
        return pltpu.make_async_copy(
            self.pieces.at[at.j], self.full.at[at.r, at.j], self.ssem.at[0, at.j]
        )

    def pass_on(self, r, js, to, k):
        return remote(
            self.full.at[r, js], self.full.at[r, js], self.ssem.at[k, js], self.rsem.at[r, js],
            self.at.row(to),
        )

    def take(self, r, js):
        self.pass_on(r, js, self.at.r_c, 0).wait_recv()

    def start(self):
        at = self.at
        self.own().start()

        @pl.loop(1, at.n)
        def _(i):
            self.first(i).start()

    def step(self, lo, hi):
        at = self.at

        @pl.loop(lo, hi)
        def _(i):
            js = lax.rem(at.j + at.n - i, at.n)

            @pl.when(i == 0)
            def _():
                self.own().wait()

            @pl.when(i > 0)
            def _():
                self.take(at.r, js)

            self.pass_on(at.r, js, at.r_y, 1).start()
            self.pass_on(at.r, js, at.r_c, 2).start()

    def relay(self, lo, hi):
        at = self.at

        @pl.loop(lo, hi)
        def _(i):
            js = lax.rem(at.j + at.n - i, at.n)
            self.take(at.r_y, js)
            self.pass_on(at.r_y, js, at.r_c, 3).start()

    def finish(self):
        at = self.at

        @pl.loop(0, at.n)
        def _(js):
            self.take(at.r_c, js)
            self.take(at.r_yc, js)
            self.pass_on(at.r, js, at.r_y, 1).wait_send()
            self.pass_on(at.r, js, at.r_c, 2).wait_send()
            self.pass_on(at.r_y, js, at.r_c, 3).wait_send()

        @pl.loop(1, at.n)
        def _(i):
            self.first(i).wait_send()


class Rows:
    @staticmethod
    def sems():
        return [pltpu.SemaphoreType.DMA((4,)), pltpu.SemaphoreType.DMA((4,))]

    def __init__(self, at, shard, full, sems):
        self.at, self.shard, self.full = at, shard, full
        self.ssem, self.rsem = sems

    def own(self):
        return pltpu.make_async_copy(self.shard, self.full.at[self.at.r], self.ssem.at[0])

    def direct(self, to, k):
        r = self.at.r
        return remote(
            self.shard, self.full.at[r], self.ssem.at[k], self.rsem.at[r], self.at.row(to)
        )

    def onward(self):
        at = self.at
        r = at.r_y
        return remote(
            self.full.at[r], self.full.at[r], self.ssem.at[3], self.rsem.at[r], at.row(at.r_c)
        )

    def take(self, r):
        at = self.at
        remote(
            self.full.at[r], self.full.at[r], self.ssem.at[0], self.rsem.at[r], at.row(at.r_c)
        ).wait_recv()

    def start(self):
        at = self.at
        self.own().start()
        self.direct(at.r_y, 1).start()
        self.direct(at.r_c, 2).start()

    def relay(self):
        self.take(self.at.r_y)
        self.onward().start()

    def finish(self):
        at = self.at
        self.own().wait()
        self.take(at.r_c)
        self.take(at.r_yc)
        self.direct(at.r_y, 1).wait_send()
        self.direct(at.r_c, 2).wait_send()
        self.onward().wait_send()


class RowSum:
    @staticmethod
    def scratch(m, c):
        return [
            pltpu.VMEM((2, m, c), BF),
            pltpu.VMEM((m, c), BF),
            pltpu.SemaphoreType.DMA((3,)),
            pltpu.SemaphoreType.DMA((3,)),
        ]

    def __init__(self, at, grad, refs):
        self.at, self.grad = at, grad
        self.core_in, self.y_in, self.ssem, self.rsem = refs

    def to_core(self, far):
        at = self.at
        yy = 1 - at.y if far else at.y
        k = 1 if far else 0
        return remote(
            self.grad.at[yy * 2 + 1 - at.c], self.core_in.at[k], self.ssem.at[k], self.rsem.at[k],
            at.row(at.r_c),
        )

    def over_y(self):
        at = self.at
        return remote(
            self.grad.at[at.r_y], self.y_in, self.ssem.at[2], self.rsem.at[2], at.row(at.r_y)
        )

    def start(self):
        self.to_core(1).start()
        self.to_core(0).start()

    def cross(self):
        at = self.at
        self.to_core(1).wait_recv()
        self.grad[at.r_y] = (
            self.grad[at.r_y].astype(F32) + self.core_in[1].astype(F32)
        ).astype(BF)
        self.over_y().start()

    def total(self):
        at = self.at
        self.to_core(0).wait_recv()
        self.over_y().wait_recv()
        return (
            self.grad[at.r].astype(F32) + self.core_in[0].astype(F32) + self.y_in[...].astype(F32)
        )

    def finish(self):
        self.to_core(1).wait_send()
        self.to_core(0).wait_send()
        self.over_y().wait_send()


class Exchange:
    @staticmethod
    def sems(n):
        return [pltpu.SemaphoreType.DMA((n,)), pltpu.SemaphoreType.DMA((n,))]

    def __init__(self, at, mine, got, sems):
        self.at, self.mine, self.got = at, mine, got
        self.ssem, self.rsem = sems

    def send(self, i):
        at = self.at
        to = at.other(i)
        return remote(
            self.mine.at[to], self.got.at[at.j], self.ssem.at[to], self.rsem.at[at.j], at.seq(to)
        )

    def own(self):
        at = self.at
        return pltpu.make_async_copy(
            self.mine.at[at.j], self.got.at[at.j], self.ssem.at[at.j]
        )

    def start(self):
        self.own().start()

        @pl.loop(1, self.at.n)
        def _(i):
            self.send(i).start()

    def finish(self):
        at = self.at
        self.own().wait()

        @pl.loop(1, at.n)
        def _(i):
            src = at.other(i)
            remote(
                self.mine.at[src], self.got.at[src], self.ssem.at[src], self.rsem.at[src],
                at.seq(src),
            ).wait()


class SmallGather:
    @staticmethod
    def sems(n):
        return [pltpu.SemaphoreType.DMA((4,))] * 2 + [pltpu.SemaphoreType.DMA((n,))] * 2

    def __init__(self, at, mine, full, sems):
        self.at, self.mine, self.full = at, mine, full
        self.rs, self.rr, self.ss, self.sr = sems

    def beside(self, r):
        at = self.at
        return remote(
            self.mine, self.full.at[at.j, at.r], self.rs.at[r], self.rr.at[at.r], at.row(r)
        )

    def own(self):
        at = self.at
        return pltpu.make_async_copy(self.mine, self.full.at[at.j, at.r], self.rs.at[at.r])

    def onward(self, to):
        at = self.at
        return remote(
            self.full.at[at.j], self.full.at[at.j], self.ss.at[to], self.sr.at[at.j], at.seq(to)
        )

    def start(self):
        at = self.at
        self.own().start()
        for r in (at.r_y, at.r_c, at.r_yc):
            self.beside(r).start()

    def step(self):
        at = self.at
        self.own().wait()
        for r in (at.r_y, at.r_c, at.r_yc):
            remote(
                self.mine, self.full.at[at.j, r], self.rs.at[r], self.rr.at[r], at.row(r)
            ).wait()

        @pl.loop(1, at.n)
        def _(i):
            self.onward(at.other(i)).start()

    def finish(self):
        at = self.at

        @pl.loop(1, at.n)
        def _(i):
            src = at.other(i)
            remote(
                self.full.at[src], self.full.at[src], self.ss.at[src], self.sr.at[src],
                at.seq(src),
            ).wait()


class SmallSum:
    @staticmethod
    def scratch(n, w):
        q = w // 4
        return (
            [pltpu.VMEM((8, w), F32), pltpu.VMEM((4, 8, q), F32), pltpu.VMEM((8, q), F32)]
            + [pltpu.VMEM((n, 8, q), F32)]
            + [pltpu.SemaphoreType.DMA((4,))] * 2
            + [pltpu.SemaphoreType.DMA((n,))] * 2
        )

    def __init__(self, at, refs):
        self.at = at
        self.terms, self.beside_in, self.acc, self.seq_in = refs[:4]
        self.rs, self.rr, self.ss, self.sr = refs[4:]
        self.q = self.terms.shape[1] // 4

    def part(self, r):
        return self.terms.at[:, pl.ds(pl.multiple_of(r * self.q, self.q), self.q)]

    def beside(self, r):
        at = self.at
        return remote(
            self.part(r), self.beside_in.at[at.r], self.rs.at[r], self.rr.at[at.r], at.row(r)
        )

    def run(self, out):
        at = self.at
        near = (at.r_y, at.r_c, at.r_yc)
        for r in near:
            self.beside(r).start()
        self.acc[...] = self.part(at.r)[...]
        for r in near:
            remote(
                self.part(r), self.beside_in.at[r], self.rs.at[r], self.rr.at[r], at.row(r)
            ).wait()
            self.acc[...] += self.beside_in[r]

        @pl.loop(1, at.n)
        def _(i):
            to = at.other(i)
            remote(
                self.acc, self.seq_in.at[at.j], self.ss.at[to], self.sr.at[at.j], at.seq(to)
            ).start()

        out[...] = self.acc[...]

        @pl.loop(1, at.n)
        def _(i):
            src = at.other(i)
            remote(
                self.acc, self.seq_in.at[src], self.ss.at[src], self.sr.at[src], at.seq(src)
            ).wait()
            out[...] += self.seq_in[src]


class Call:
    def __init__(self, n, cid, name):
        self.n, self.cid, self.name = n, cid, name
        self.args, self.ins, self.outs, self.out_specs, self.scr = [], [], [], [], []

    def give(self, array, space=pltpu.VMEM):
        if isinstance(array, Made):
            return array.key
        for i, known in enumerate(self.args):
            if known is array:
                return ("i", i)
        self.args.append(array)
        self.ins.append(pl.BlockSpec(memory_space=space))
        return ("i", len(self.args) - 1)

    def make(self, shape, dtype, space=pltpu.VMEM):
        self.outs.append(jax.ShapeDtypeStruct(shape, dtype))
        self.out_specs.append(pl.BlockSpec(memory_space=space))
        return ("o", len(self.outs) - 1)

    def scratch(self, items):
        at = len(self.scr)
        self.scr.extend(items)
        return [("s", at + i) for i in range(len(items))]

    def run(self, body, flops=0):
        ni, no = len(self.ins), len(self.outs)

        def kernel(*refs):
            def of(key):
                if isinstance(key, list):
                    return [of(k) for k in key]
                if isinstance(key[0], tuple):
                    return tuple(of(k) for k in key)
                kind, i = key
                return refs[i + {"i": 0, "o": ni, "s": ni + no}[kind]]

            at = Place(self.n)
            at.meet()
            body(at, of)

        return pl.pallas_call(
            kernel,
            out_shape=self.outs,
            in_specs=self.ins,
            out_specs=self.out_specs,
            scratch_shapes=self.scr,
            name=self.name,
            cost_estimate=pl.CostEstimate(
                flops=flops, bytes_accessed=1 << 24, transcendentals=0
            ),
            compiler_params=pltpu.CompilerParams(
                collective_id=self.cid, has_side_effects=True, vmem_limit_bytes=VMEM_LIMIT
            ),
        )(*self.args)


VMEM_LIMIT = 58 << 20
ANY = pltpu.VMEM
CHUNK = 512


def product(at, of, part, pairs, t):
    width, tok = at.width, part.shape[1]

    @pl.loop(0, part.shape[2] // CHUNK)
    def _(i):
        cols = pl.ds(pl.multiple_of(i * CHUNK, CHUNK), CHUNK)
        total = None
        for lhs, rhs, flip in pairs:
            left = of(lhs)[pl.ds(t * (width * tok), width * tok), :]
            if flip:
                term = dot(left, of(rhs)[cols, :], 1, 1)
            else:
                term = dot(left, of(rhs)[:, cols], 1, 0)
            total = term if total is None else total + term
        part[pl.ds(t * width, width), :, cols] = total.reshape(width, tok, CHUNK).astype(BF)


def products(at, of, part, pairs, red):
    for s in range(at.depth - 1, -1, -1):
        for t in [at.z + s, at.z - s] if s else [at.z]:

            @pl.when(jnp.logical_and(t >= 0, t < at.depth))
            def _(t=t):
                product(at, of, part, pairs, t)
                red.emit(t)


def steps(at, red, extra):
    work = extra.fill()
    for w in work[:1]:
        w()
    extra.between(1)
    red.reduce(3)
    for w in work[1:2]:
        w()
    extra.cross(0)
    for w in work[2:]:
        w()
    extra.cross(1)
    extra.between(2)
    red.reduce(2)
    extra.cross(2)
    extra.turn(0)
    extra.between(3)
    red.reduce(1)
    extra.turn(1)


def gather_all(g, between=None):
    at = g.at
    for s in range(1, at.depth):
        g.step(s)
        if between is not None:
            between(s)
    for s in range(at.depth):
        for zz in [at.z - s, at.z + s] if s else [at.z]:

            @pl.when(jnp.logical_and(zz >= 0, zz < at.depth))
            def _(zz=zz):
                g.take_side(zz)


def split_columns(src, dst, runs):
    for b, to, at, size in runs:
        dst[b, :, to : to + size] = src[:, at : at + size]


def join_columns(src, dst, runs):
    for b, to, at, size in runs:
        dst[:, at : at + size] = src[b, :, to : to + size].astype(dst.dtype)


def front_call(n, x, small, ints, weight, runs, out_w):
    tok, d = x.shape
    k, c = weight.shape[0], weight.shape[1] // n
    call = Call(n, 1, "front")
    ix = call.give(x, ANY)
    ism, iin = call.give(small), call.give(ints)
    iw = call.give(weight, ANY)
    ox = call.make((n, tok, d), BF, ANY)
    osm = call.make((n, 4) + small.shape, BF)
    oin = call.make((n,) + ints.shape, jnp.int32)
    ow = call.make((4, n, k, c), BF, ANY)
    sx = call.scratch(Gather.sems(n, ALONE))
    sp = call.scratch([pltpu.VMEM((n, k, c), BF)])
    ssm = call.scratch(SmallGather.sems(n))
    sin = call.scratch(Exchange.sems(n))
    sw = call.scratch(Columns.sems(n))
    if out_w is not None:
        io = call.give(out_w, ANY)
        oo = call.make((4,) + out_w.shape, BF, ANY)
        so = call.scratch(Rows.sems())

    def body(at, of):
        sm = SmallGather(at, of(ism), of(osm), of(ssm))
        g = Gather(at, of(ox), of(sx), ALONE)
        cols = Columns(at, of(sp)[0], of(ow), of(sw))
        spread = Spread(at, of(iin), of(oin), of(sin))
        sm.start()
        of(ox)[at.j] = of(ix)[...]
        g.start()
        spread.start()
        split_columns(of(iw), of(sp)[0], runs)
        cols.start()
        sm.step()
        if out_w is not None:
            rows = Rows(at, of(io), of(oo), of(so))
            rows.start()
        cuts = [0, n // 4, n // 2, n]

        def between(s):
            cols.step(cuts[s - 1], cuts[s])

        gather_all(g, between)
        cols.relay(0, n)
        if out_w is not None:
            rows.relay()
            rows.finish()
        cols.finish()
        g.finish()
        sm.finish()
        spread.finish()

    return call.run(body)


def turned(line):
    return jnp.transpose(jnp.broadcast_to(line, (128, 128)))


def rotation(ints_all, frequency, block, direction):
    lane = lax.rem(lax.broadcasted_iota(jnp.int32, (128, 128), 1), HD)
    angle = turned(ints_all[block, 1:2].astype(F32)) * frequency[0:1]
    cosine, sine = jnp.cos(angle), direction * jnp.sin(angle)
    return cosine, jnp.where(lane < ROT // 2, -sine, 0.0), jnp.where(lane < ROT // 2, 0.0, sine)


def turn_pairs(u, table):
    cosine, above, below = table
    return (
        u * cosine
        + pltpu.roll(u, 128 - ROT // 2, 1) * above
        + pltpu.roll(u, ROT // 2, 1) * below
    )


def fill_mask(at, mask, ints_all, t):
    tok = 128
    index = lax.broadcasted_iota(jnp.int32, (tok, tok), 0)
    other = lax.broadcasted_iota(jnp.int32, (tok, tok), 1)
    for b in range(at.width):
        mine = turned(ints_all[t * at.width + b, 0:1].astype(F32))
        for o in range((t + 1) * at.width):
            ok = mine == ints_all[o, 0:1].astype(F32)
            if o == t * at.width + b:
                ok = jnp.logical_and(ok, other <= index)
            fill = jnp.where(ok, 0.0, -jnp.inf)
            if o > t * at.width + b:
                fill = jnp.full((tok, tok), -jnp.inf, F32)
            mask[b * tok : (b + 1) * tok, o * tok : (o + 1) * tok] = fill


class Made:
    def __init__(self, key, shape):
        self.key, self.shape = key, shape


def attend_call(n, x, small, ints, frequency, qkv_w, head_runs, out_w):
    tok, d = x.shape
    k, c = qkv_w.shape[0], qkv_w.shape[1] // n
    hp, length, wide = H // n, n * tok, n // LINE * tok
    call = Call(n, 10, "attend")
    i_x, i_small, i_ints, i_freq = (call.give(v) for v in (x, small, ints, frequency))
    i_w, i_out = call.give(qkv_w), call.give(out_w)
    o_in = call.make((n, tok, d), BF)
    o_gains = call.make((8, d), F32)
    o_ints = call.make((n,) + ints.shape, jnp.int32)
    o_w = call.make((4, n, k, c), BF)
    o_out = call.make((4,) + out_w.shape, BF)
    o_qkv = [call.make((hp, length, HD), BF) for _ in range(3)]
    o_low = call.make((length, hp * HD), BF)
    o_ctx = call.make((length, hp * HD), F32)
    o_den = call.make((length, 128), F32)
    s_x = call.scratch([pltpu.VMEM((n, tok, d), BF)])
    s_gat = call.scratch(Gather.sems(n, ALONE))
    s_pieces = call.scratch([pltpu.VMEM((n, k, c), BF)])
    s_small = call.scratch([pltpu.VMEM((n, 4) + small.shape, F32)])
    s_shift = call.scratch([pltpu.VMEM((8, c), F32)])
    s_mask = call.scratch([pltpu.VMEM((wide, length), F32)])
    s_sg = call.scratch(SmallGather.sems(n))
    s_spread = call.scratch(Exchange.sems(n))
    s_cols = call.scratch(Columns.sems(n))
    s_rows = call.scratch(Rows.sems())

    def body(at, of):
        sm_all, xs, inputs, gains = of(s_small)[0], of(s_x)[0], of(o_in), of(o_gains)
        shift, mask, w = of(s_shift)[0], of(s_mask)[0], of(o_w)
        ints_all = of(o_ints)
        q_ref, k_ref, v_ref = of(o_qkv)
        sm = SmallGather(at, of(i_small), sm_all, of(s_sg))
        gat = Gather(at, xs, of(s_gat), ALONE)
        cols = Columns(at, of(s_pieces)[0], w, of(s_cols))
        spread = Spread(at, of(i_ints), ints_all, of(s_spread))
        out_rows = Rows(at, of(i_out), of(o_out), of(s_rows))
        sm.start()
        xs[at.j] = of(i_x)[...]
        gat.start()
        spread.start()
        split_columns(of(i_w), of(s_pieces)[0], head_runs)
        cols.start()
        sm.step()
        out_rows.start()
        gat.open_wide()
        sm.finish()
        for r in range(4):
            for b in range(n):
                lanes = slice((r * n + b) * k, (r * n + b + 1) * k)
                for i in range(4):
                    gains[i : i + 1, lanes] = sm_all[b, r, i // 2 : i // 2 + 1, i % 2 * k : (i % 2 + 1) * k]
        for m in range(3):
            for r in range(4):
                block = (m * 4 + r) * n + at.j
                owner = block // 3
                line = 2 + lax.rem(block, 3)
                shift[0:1, (m * 4 + r) * HD : (m * 4 + r + 1) * HD] = sm_all[
                    lax.rem(owner, n), owner // n, pl.ds(line, 1), 0:HD
                ]
        spread.finish()

        def norm(t):
            here = pl.ds(t * at.width, at.width)
            normed, _ = norm_stats(xs[here].reshape(wide, d).astype(F32))
            low = (normed * gains[0:1] + gains[1:2]).astype(BF)
            inputs[here] = low.reshape(at.width, tok, d)

        def project(t):
            for b in range(at.width):
                block = t * at.width + b
                these = pl.ds(block * tok, tok)
                table = rotation(ints_all, of(i_freq), block, 1.0)
                projected = dot(inputs[block], w[...].reshape(d, c), 1, 0) + shift[0:1]
                for i in range(4 * hp * HD // 256):
                    u = projected[:, i * 128 : (i + 1) * 128]
                    u = turn_pairs(u, table)
                    for e in range(2):
                        head = i * 2 + e
                        val = u[:, e * HD : (e + 1) * HD]
                        if head < hp:
                            q_ref[head, these] = (val * (1.0 / math.sqrt(HD))).astype(BF)
                        else:
                            k_ref[head - hp, these] = val.astype(BF)
                for head in range(hp):
                    first = (2 * hp + head) * HD
                    v_ref[head, these] = projected[:, first : first + HD].astype(BF)

        order = by_place(at.z, (3210, 3201, 132, 123))
        edge = jnp.logical_or(at.z == 0, at.z == at.depth - 1)

        @pl.loop(0, LINE)
        def _(i):
            t = digit(order, i)
            lo = jnp.where(edge, i + 1, jnp.where(i == 0, 1, jnp.where(i == 1, 3, 4)))
            hi = jnp.where(edge, jnp.minimum(i + 2, 4), jnp.where(i == 0, 3, 4))

            @pl.loop(lo, hi)
            def _(m):
                gat.fetch(digit(order, m))

            cols.step(jnp.where(i < 3, i * (n // 4), n), jnp.where(i < 2, (i + 1) * (n // 4), n))

            @pl.when(i == 3)
            def _():
                cols.relay(0, n)
                cols.finish()

                @pl.loop(0, 3)
                def _(m):
                    project(digit(order, m))

            gat.take_side(t)
            norm(t)

        out_rows.relay()
        project(digit(order, 3))
        for t in range(LINE):
            reach = (t + 1) * wide
            fill_mask(at, mask, ints_all, t)
            these = slice(t * wide, (t + 1) * wide)
            for head in range(hp):
                lanes = slice(head * HD, (head + 1) * HD)
                scores = dot(q_ref[head, these], k_ref[head, 0:reach], 1, 1)
                weights = jnp.exp(scores + mask[:, 0:reach])
                den = jnp.sum(weights, axis=1, keepdims=True)
                numer = dot(weights.astype(BF), v_ref[head, 0:reach], 1, 0)
                ctx = numer / den
                of(o_ctx)[these, lanes] = ctx
                of(o_low)[these, lanes] = ctx.astype(BF)
                of(o_den)[these, head : head + 1] = den
        out_rows.finish()
        gat.finish()

    return call.run(body)


class Spread:
    def __init__(self, at, mine, got, sems):
        self.at, self.mine, self.got = at, mine, got
        self.ssem, self.rsem = sems

    def copy(self, to, src):
        at = self.at
        return remote(
            self.mine, self.got.at[src], self.ssem.at[to], self.rsem.at[src], at.seq(to)
        )

    def own(self):
        return pltpu.make_async_copy(self.mine, self.got.at[self.at.j], self.ssem.at[self.at.j])

    def start(self):
        self.own().start()

        @pl.loop(1, self.at.n)
        def _(i):
            self.copy(self.at.other(i), self.at.j).start()

    def finish(self):
        self.own().wait()

        @pl.loop(1, self.at.n)
        def _(i):
            p = self.at.other(i)
            self.copy(p, p).wait()


def sum_call(n, cid, name, pairs, tok, columns=(), rows=(), gathers=(), row_sums=(), col_sums=()):
    call = Call(n, cid, name)
    d = pairs[0][1].shape[0 if pairs[0][2] else 1]
    keys = []
    for lhs, rhs, flip in pairs:
        keys.append((call.give(lhs), call.give(rhs), flip))
    out = call.make((tok, d), F32)
    part = call.scratch([pltpu.VMEM((n, tok, d), BF)])
    red_s = call.scratch(Reduce.scratch(n, tok, d, SUM_CUTS))
    extra = Extras(call, n, columns, rows, gathers, row_sums, col_sums, PAIRED)

    def body(at, of):
        part_ref = of(part)[0]
        red = Reduce(at, part_ref, of(red_s), SUM_CUTS)
        extra.bind(at, of)
        extra.start()
        products(at, of, part_ref, keys, red)
        steps(at, red, extra)
        red.last(of(out))
        extra.finish()
        red.finish()

    flops = sum(2 * l.shape[0] * l.shape[1] * d for l, _, _ in pairs)
    return call.run(body, flops)


class Extras:
    def __init__(
        self, call, n, columns=(), rows=(), gathers=(), row_sums=(), col_sums=(), cuts=None
    ):
        self.n, self.cuts = n, cuts
        self.columns, self.rows, self.gathers, self.row_sums, self.col_sums = [], [], [], [], []
        for w, runs in columns:
            shape = (n, w.shape[0], w.shape[1] // n)
            self.columns.append(
                (
                    call.give(w),
                    call.make((4,) + shape, BF, ANY),
                    call.scratch([pltpu.VMEM(shape, BF)]),
                    call.scratch(Columns.sems(n)),
                    runs,
                )
            )
        for p in rows:
            self.rows.append(
                (call.give(p, ANY), call.make((4,) + p.shape, BF, ANY), call.scratch(Rows.sems()))
            )
        for p in gathers:
            self.gathers.append(
                (
                    call.give(p, ANY),
                    call.make((n,) + p.shape, BF, ANY),
                    call.scratch(Gather.sems(n, cuts)),
                )
            )
        self.n_row = n_row = 4
        for p in row_sums:
            lhs, rhs = p if isinstance(p, tuple) else (None, None)
            shape = (n_row, lhs.shape[1] // n_row, rhs.shape[1]) if lhs is not None else p.shape
            self.row_sums.append(
                (
                    (call.give(lhs), call.give(rhs)) if lhs is not None else call.give(p),
                    call.scratch([pltpu.VMEM(shape, BF)])[0],
                    call.make(shape[1:], F32),
                    call.scratch(RowSum.scratch(*shape[1:])),
                )
            )
        for p, runs in col_sums:
            lhs, rhs = p if isinstance(p, tuple) else (None, None)
            shape = (n_row, lhs.shape[1] // n_row, rhs.shape[1]) if lhs is not None else p.shape
            k, c = shape[1] // n, shape[2]
            self.col_sums.append(
                (
                    (call.give(lhs), call.give(rhs)) if lhs is not None else call.give(p),
                    call.scratch([pltpu.VMEM(shape, BF)])[0],
                    call.make((k, n * c), F32),
                    call.scratch(RowSum.scratch(*shape[1:])),
                    call.scratch([pltpu.VMEM((n, k, c), BF)] * 2),
                    call.scratch(Exchange.sems(n)),
                    runs,
                )
            )

    def bind(self, at, of):
        self.at, self.of = at, of
        self.b_columns = [
            (Columns(at, of(p)[0], of(o), of(s)), of(i), of(p)[0], runs)
            for i, o, p, s, runs in self.columns
        ]
        self.b_rows = [Rows(at, of(i), of(o), of(s)) for i, o, s in self.rows]
        self.b_gathers = [
            (Gather(at, of(o), of(s), self.cuts), of(i), of(o)) for i, o, s in self.gathers
        ]
        self.b_sums = [
            (RowSum(at, of(g), of(s)), of(o), of(i), of(g)) for i, g, o, s in self.row_sums
        ]
        self.b_cols = []
        for i, g, o, s, v, e, runs in self.col_sums:
            mine, got = of(v)
            self.b_cols.append(
                (
                    RowSum(at, of(g), of(s)),
                    mine,
                    Exchange(at, mine, got, of(e)),
                    (got, of(o), runs),
                    of(i),
                    of(g),
                )
            )

    def start(self):
        at = self.at
        for g, src, buf in self.b_gathers:
            buf[at.j] = src[...]
            g.start()
        for r in self.b_rows:
            r.start()
        for c, src, pieces, runs in self.b_columns:
            split_columns(src, pieces, runs)
            c.start()

    def fill_columns(self, k):
        rs, _, _, _, src, grad = self.b_cols[k]
        if isinstance(src, tuple):
            size = grad.shape[1]

            @pl.loop(0, grad.shape[0])
            def _(b):
                cols = pl.ds(pl.multiple_of(b * size, size), size)
                grad[b] = dot(src[0][:, cols], src[1][...], 0, 0).astype(BF)
        else:
            grad[...] = src[...]
        rs.start()

    def fill_rows(self, k):
        rs, _, src, grad = self.b_sums[k]
        if isinstance(src, tuple):

            @pl.loop(0, grad.shape[2] // CHUNK)
            def _(b):
                cols = pl.ds(pl.multiple_of(b * CHUNK, CHUNK), CHUNK)
                term = dot(src[0][...], src[1][:, cols], 0, 0)
                grad[:, :, cols] = term.reshape(grad.shape[0], grad.shape[1], CHUNK).astype(BF)
        else:
            grad[...] = src[...]
        rs.start()

    def fill(self):
        work = [functools.partial(self.fill_columns, k) for k in range(len(self.b_cols))]
        return work + [functools.partial(self.fill_rows, k) for k in range(len(self.b_sums))]

    def cross(self, k):
        every = [c[0] for c in self.b_cols] + [r[0] for r in self.b_sums]
        if k < len(every):
            every[k].cross()

    def turn(self, k):
        if k < len(self.b_cols):
            rs, mine, ex = self.b_cols[k][:3]
            mine[...] = rs.total().reshape(mine.shape).astype(BF)
            ex.start()

    def between(self, s):
        n = self.n
        cuts = [0, n // 4, n // 2, n]
        for g, _, _ in self.b_gathers:
            g.step(s)
        for c, *_ in self.b_columns:
            c.step(cuts[s - 1], cuts[s])

    def finish(self):
        at = self.at
        for g, _, _ in self.b_gathers:
            for zz in range(at.depth):
                g.take_side(zz)
            g.finish()
        for r in self.b_rows:
            r.relay()
        for c, *_ in self.b_columns:
            c.relay(0, self.n)
        for r in self.b_rows:
            r.finish()
        for c, *_ in self.b_columns:
            c.finish()
        for rs, out, *_ in self.b_sums:
            out[...] = rs.total()
            rs.finish()
        for rs, _, ex, (got, out, runs), *_ in self.b_cols:
            ex.finish()
            rs.finish()
            join_columns(got, out, runs)


def gather_call(n, cid, name, x, columns=(), rows=(), row_sums=(), col_sums=()):
    call = Call(n, cid, name)
    extra = Extras(call, n, columns, rows, [x], row_sums, col_sums, ALONE)

    def body(at, of):
        extra.bind(at, of)
        extra.start()
        for piece in extra.fill():
            piece()
        for k in range(3):
            extra.cross(k)
        for s in range(1, at.depth):
            extra.between(s)
        for k in range(2):
            extra.turn(k)
        extra.finish()

    return call.run(body)


def digit(code, i):
    return lax.rem(code // jnp.where(i == 0, 1, jnp.where(i == 1, 10, jnp.where(i == 2, 100, 1000))), 10)


def by_place(z, codes):
    return jnp.where(z == 0, codes[0], jnp.where(z == 1, codes[1], jnp.where(z == 2, codes[2], codes[3])))


def core_call(n, pair, x, gain, bias, columns, rows, gathers):
    call = Call(n, 2, "core")
    tok, d = x.shape
    c = columns[0][0].shape[1] // n
    wide = n // LINE * tok
    length = n * tok
    key = (call.give(pair[0]), call.give(pair[1]), False)
    i_x, i_gain, i_bias = call.give(x), call.give(gain), call.give(bias)
    o_hid = call.make((tok, d), F32)
    out = call.make((tok, d), F32)
    o_mid = call.make((n, tok, d), BF)
    o_acts = [call.make((length, c), BF) for _ in range(3)]
    part = call.scratch([pltpu.VMEM((n, tok, d), BF)] * 2)
    first_s = call.scratch(Reduce.scratch(n, tok, d, SUM_CUTS))
    extra = Extras(call, n, columns, rows, gathers, cuts=PAIRED)
    gat_s = call.scratch(Gather.sems(n, MLP_CUTS))
    red_s = call.scratch(Reduce.scratch(n, tok, d, MLP_SUMS))

    def body(at, of):
        first_part, part_ref = of(part)
        first = Reduce(at, first_part, of(first_s), SUM_CUTS)
        mid, hid = of(o_mid), of(o_hid)
        inner_ref, gg_ref, gu_ref = of(o_acts)
        gat = Gather(at, mid, of(gat_s), MLP_CUTS)
        red = Reduce(at, part_ref, of(red_s), MLP_SUMS)
        extra.bind(at, of)
        extra.start()
        products(at, of, first_part, [key], first)
        steps(at, first, extra)
        first.last(hid)
        hid[...] += of(i_x)[...].astype(F32)
        normed, _ = norm_stats(hid[...])
        mid[at.j] = (normed * of(i_gain)[...] + of(i_bias)[...]).astype(BF)
        gat.start()
        extra.finish()
        gat.open_wide()
        gate, up = (c[0].full for c in extra.b_columns)
        down, grad = extra.b_rows[0].full, extra.b_gathers[0][2]
        gate, up = gate.reshape(d, c), up.reshape(d, c)
        down = down.reshape(c, d)
        order = by_place(at.z, (3210, 3201, 132, 123))
        edge = jnp.logical_or(at.z == 0, at.z == at.depth - 1)

        @pl.loop(0, LINE)
        def _(i):
            t = digit(order, i)
            lo = jnp.where(edge, i + 1, jnp.where(i == 0, 1, jnp.where(i == 1, 3, 4)))
            hi = jnp.where(edge, jnp.minimum(i + 2, 4), jnp.where(i == 0, 3, 4))

            @pl.loop(lo, hi)
            def _(m):
                gat.fetch(digit(order, m))

            gat.take_side(t)
            here = pl.ds(t * at.width, at.width)
            these = pl.ds(t * wide, wide)
            tokens = mid[here].reshape(wide, d)
            gate_pre = dot(tokens, gate[...], 1, 0)
            sig = 1.0 / (1.0 + jnp.exp(-gate_pre))
            silu = gate_pre * sig
            up_pre = dot(tokens, up[...], 1, 0)
            inner_ref[these] = (silu * up_pre).astype(BF)
            g_inner = dot(grad[here].reshape(wide, d), down[...], 1, 1)
            gu_ref[these] = (g_inner * silu).astype(BF)
            gg_ref[these] = (g_inner * up_pre * sig * (1.0 + gate_pre * (1.0 - sig))).astype(BF)
            product(at, lambda k: k, part_ref, [(gg_ref, gate, True), (gu_ref, up, True)], t)
            red.emit(t)

            @pl.when(jnp.logical_and(edge, i >= 2))
            def _():
                red.pass_on(digit(order, i - 1))

        rest = by_place(at.z, (3, 32, 301, 0))

        @pl.loop(0, jnp.where(edge, 1, 3))
        def _(i):
            red.pass_on(digit(rest, i))

        red.last(of(out))
        gat.finish()
        first.finish()
        red.finish()

    return call.run(body)


def back_call(n, g_attn, out_w, qkv_w, heads, ctx, low, den, ints, frequency, inputs, normed, known, runs):
    call = Call(n, 11, "back")
    length, d = g_attn.shape
    hp, tok, wide = H // n, length // n, length // LINE
    c = 3 * hp * HD
    i_g, i_out, i_w = call.give(g_attn), call.give(out_w), call.give(qkv_w)
    i_heads = [call.give(v) for v in heads]
    i_ctx, i_den, i_ints, i_freq = (call.give(v) for v in (ctx, den, ints, frequency))
    i_norm, i_known = call.give(normed), call.give(known)
    out = call.make((tok, d), F32)
    o_small = call.make((8, d // 4), F32)
    s_proj = call.scratch([pltpu.VMEM((length, c), BF)])[0]
    s_sum = call.scratch([pltpu.VMEM((length, c), F32)])
    s_mask = call.scratch([pltpu.VMEM((wide, length), F32)])
    part = call.scratch([pltpu.VMEM((n, tok, d), BF)])
    red_s = call.scratch(Reduce.scratch(n, tok, d, SUM_CUTS))
    s_small = call.scratch(SmallSum.scratch(n, d))
    made = Made(s_proj, (length, c))
    extra = Extras(call, n, row_sums=[(low, g_attn)], col_sums=[((inputs, made), runs)])

    def body(at, of):
        part_ref = of(part)[0]
        red = Reduce(at, part_ref, of(red_s), SUM_CUTS)
        small = SmallSum(at, of(s_small))
        proj, sums, mask = of(s_proj), of(s_sum)[0], of(s_mask)[0]
        q_ref, k_ref, v_ref = of(i_heads)
        ints_all = of(i_ints)
        extra.bind(at, of)
        extra.start()
        width = hp * HD
        sums[:, width:] = jnp.zeros((length, 2 * width), F32)
        for t in range(LINE):
            these, reach = slice(t * wide, (t + 1) * wide), (t + 1) * wide
            fill_mask(at, mask, ints_all, t)
            g_ctx = dot(of(i_g)[these], of(i_out)[...], 1, 1)
            for head in range(hp):
                lanes = slice(head * HD, (head + 1) * HD)
                g_own = g_ctx[:, lanes]
                below = of(i_den)[these, head : head + 1]
                g_num = (g_own / below).astype(BF)
                g_den = -jnp.sum(g_own * of(i_ctx)[these, lanes], axis=1, keepdims=True) / below
                query = q_ref[head, these]
                scores = dot(query, k_ref[head, 0:reach], 1, 1)
                weights = jnp.exp(scores + mask[:, 0:reach])
                g_weights = dot(g_num, v_ref[head, 0:reach], 1, 1)
                g_scores = (weights * (g_weights + g_den)).astype(BF)
                sums[these, lanes] = dot(g_scores, k_ref[head, 0:reach], 1, 0)
                lanes = slice(width + head * HD, width + (head + 1) * HD)
                sums[0:reach, lanes] += dot(g_scores, query, 0, 0)
                lanes = slice(2 * width + head * HD, 2 * width + (head + 1) * HD)
                sums[0:reach, lanes] += dot(weights.astype(BF), g_num, 0, 0)

        @pl.loop(0, n)
        def _(b):
            these = pl.ds(b * tok, tok)
            table = rotation(ints_all, of(i_freq), b, -1.0)
            for i in range(2 * width // 128):
                lanes = slice(i * 128, (i + 1) * 128)
                u = turn_pairs(sums[these, lanes], table)
                if i < width // 128:
                    u = u * (1.0 / math.sqrt(HD))
                proj[these, lanes] = u.astype(BF)
            proj[these, 2 * width :] = sums[these, 2 * width :].astype(BF)

        products(at, of, part_ref, [(s_proj, i_w, True)], red)
        small.terms[...] = of(i_known)[...]
        shift = jnp.sum(proj[...].astype(F32), axis=0, keepdims=True)
        per = d // 4
        for m in range(3):
            for r in range(4):
                own = shift[:, (m * 4 + r) * HD : (m * 4 + r + 1) * HD]
                for b in range(n):
                    flat = m * d + (r * n + b) * HD
                    row, rest = flat // (3 * per), flat % (3 * per)
                    first = row * per + rest % per
                    line = 4 + rest // per
                    small.terms[line : line + 1, first : first + HD] = jnp.where(
                        at.j == b, own, 0.0
                    )
        steps(at, red, extra)
        red.last(of(out))
        grad = of(out)[...]
        small.terms[0:1, :] = jnp.sum(grad * of(i_norm)[...], axis=0, keepdims=True)
        small.terms[1:2, :] = jnp.sum(grad, axis=0, keepdims=True)
        small.run(of(o_small))
        extra.finish()
        red.finish()

    return call.run(body)


def last_call(n, cid, pairs, tok, normed, known, row_sums, col_sums):
    call = Call(n, cid, "last")
    d = pairs[0][1].shape[0]
    keys = []
    for lhs, rhs, flip in pairs:
        keys.append((call.give(lhs), call.give(rhs), flip))
    i_norm, i_known = call.give(normed), call.give(known)
    out = call.make((tok, d), F32)
    o_small = call.make((8, d // 4), F32)
    part = call.scratch([pltpu.VMEM((n, tok, d), BF)])
    red_s = call.scratch(Reduce.scratch(n, tok, d, SUM_CUTS))
    s_small = call.scratch(SmallSum.scratch(n, d))
    extra = Extras(call, n, row_sums=row_sums, col_sums=col_sums)

    def body(at, of):
        part_ref = of(part)[0]
        red = Reduce(at, part_ref, of(red_s), SUM_CUTS)
        extra.bind(at, of)
        extra.start()
        products(at, of, part_ref, keys, red)
        steps(at, red, extra)
        red.last(of(out))
        small = SmallSum(at, of(s_small))
        small.terms[...] = of(i_known)[...]
        grad = of(out)[...]
        small.terms[0:1, :] = jnp.sum(grad * of(i_norm)[...], axis=0, keepdims=True)
        small.terms[1:2, :] = jnp.sum(grad, axis=0, keepdims=True)
        small.run(of(o_small))
        extra.finish()
        red.finish()

    return call.run(body)


def attention(queries, keys, values, allowed):
    scores = jnp.einsum("qhd,khd->hqk", queries, keys, preferred_element_type=F32)
    exp_weights = jnp.where(allowed[None], jnp.exp(scores), 0.0)
    denominator = jnp.sum(exp_weights, axis=-1)
    numerator = jnp.einsum(
        "hqk,khd->qhd", exp_weights.astype(BF), values, preferred_element_type=F32
    )
    return numerator / jnp.transpose(denominator)[:, :, None], denominator


def attention_back(queries, keys, values, allowed, denominator, context, g_context):
    den = jnp.transpose(denominator)
    g_numer = (g_context / den[:, :, None]).astype(BF)
    g_den = jnp.transpose(-jnp.sum(g_context * context, axis=-1) / den)
    scores = jnp.einsum("qhd,khd->hqk", queries, keys, preferred_element_type=F32)
    exp_weights = jnp.where(allowed[None], jnp.exp(scores), 0.0)
    g_values = jnp.einsum(
        "hqk,qhd->khd", exp_weights.astype(BF), g_numer, preferred_element_type=F32
    )
    g_weights = jnp.einsum("qhd,khd->hqk", g_numer, values, preferred_element_type=F32)
    g_scores = (exp_weights * (g_weights + g_den[:, :, None])).astype(BF)
    g_queries = jnp.einsum("hqk,khd->qhd", g_scores, keys, preferred_element_type=F32)
    g_keys = jnp.einsum("hqk,qhd->khd", g_scores, queries, preferred_element_type=F32)
    return g_queries, g_keys, g_values


def body(nrow, n, *args):
    (
        layer_in,
        segments,
        positions,
        attn_norm_gain,
        attn_norm_bias,
        qkv_weight,
        qkv_bias,
        out_weight,
        mlp_norm_gain,
        mlp_norm_bias,
        gate_weight,
        up_weight,
        down_weight,
        out_grad,
    ) = args
    j = lax.axis_index("seq")
    tok = layer_in.shape[1]
    length = n * tok
    k = qkv_weight.shape[0]
    f = down_weight.shape[0]
    hp = H // n
    whole_heads = out_weight.shape[0] == HD
    roomy = length * D <= 1 << 22 and whole_heads

    if whole_heads:
        head_runs = [
            (b, (m * nrow + r) * HD, m * D + (r * n + b) * HD, HD)
            for b in range(n) for m in range(3) for r in range(nrow)
        ]
    else:
        size = hp * HD
        head_runs = [
            (b, m * size, m * D + b * size, size) for b in range(n) for m in range(3)
        ]
    ff_runs = [(b, r * f, (r * n + b) * f, f) for b in range(n) for r in range(nrow)]

    def split_heads(w):
        lead = w.shape[0]
        if whole_heads:
            w = w.reshape(lead, 3, nrow, n, HD).transpose(3, 0, 1, 2, 4)
        else:
            w = w.reshape(lead, 3, n, hp, HD).transpose(2, 0, 1, 3, 4)
        return w.reshape(n, lead, 3 * hp * HD)

    def join_heads(blocks):
        lead = blocks.shape[1]
        if whole_heads:
            w = blocks.reshape(n, lead, 3, nrow, HD).transpose(1, 2, 3, 0, 4)
        else:
            w = blocks.reshape(n, lead, 3, hp, HD).transpose(1, 2, 0, 3, 4)
        return w.reshape(lead, 3 * D)

    if roomy:
        blank = jnp.zeros((128 - 2 * k,), F32)
        vectors = [
            attn_norm_gain, attn_norm_bias, blank, mlp_norm_gain, mlp_norm_bias, blank,
            jnp.pad(qkv_bias.astype(F32).reshape(3, HD), ((0, 3), (0, 128 - HD))).reshape(-1),
        ]
        small = jnp.concatenate([v.astype(F32) for v in vectors]).reshape(8, 128)
        ints = jnp.concatenate([segments, positions, jnp.zeros((6, tok), jnp.int32)], 0)
        half = ROT // 2
        frequency = 10000.0 ** (-2.0 * jnp.arange(half, dtype=F32) / ROT)
        frequency = jnp.concatenate([frequency, frequency, jnp.zeros((HD - ROT,), F32)])
        frequency = jnp.broadcast_to(jnp.concatenate([frequency, frequency])[None], (8, 128))
        (
            inputs_all, gains, ints_all, qkv_own, out_own, queries, keys, values, context_low,
            context, denominator,
        ) = attend_call(
            n, layer_in[0], small, ints, frequency, qkv_weight, head_runs, out_weight,
        )
        inputs_all = inputs_all.reshape(length, D)
        attn_gain, mlp_gain, mlp_bias = gains[0:1], gains[2:3], gains[3:4]
        qkv_own, out_own = qkv_own.reshape(D, 3 * hp * HD), out_own.reshape(hp * HD, D)
    else:
        small = jnp.concatenate(
            [attn_norm_gain, attn_norm_bias, mlp_norm_gain, mlp_norm_bias, qkv_bias]
        )
        small = jnp.pad(small, (0, 2048 - small.shape[0])).reshape(16, 128)
        ints = jnp.concatenate([segments, positions, jnp.zeros((6, tok), jnp.int32)], 0)
        front = front_call(
            n, layer_in[0], small, ints, qkv_weight, head_runs, out_weight if whole_heads else None
        )
        x_all, small_all, ints_all, qkv_own = front[:4]
        x_all = x_all.reshape(length, D)
        qkv_own = qkv_own.reshape(D, 3 * hp * HD)
        if whole_heads:
            out_own = front[4].reshape(hp * HD, D)
        else:
            out_full = lax.all_gather(out_weight, ("row", "seq"), axis=0, tiled=True)
            out_own = lax.dynamic_slice_in_dim(out_full, j * hp * HD, hp * HD, 0)
        small_all = small_all.transpose(1, 0, 2, 3).reshape(nrow * n, 2048)
        attn_gain, attn_bias, mlp_gain, mlp_bias = (
            small_all[:, c : c + k].reshape(1, D).astype(F32) for c in (0, k, 2 * k, 3 * k)
        )
        qkv_shift = small_all[:, 4 * k : 4 * k + 3 * k].reshape(1, 3 * D)
        shift_own = lax.dynamic_index_in_dim(split_heads(qkv_shift), j, 0, keepdims=False).astype(F32)
        seg_all, pos_all = ints_all[:, 0].reshape(length), ints_all[:, 1].reshape(length)

        inputs_all = (norm_stats(x_all.astype(F32))[0] * attn_gain + attn_bias).astype(BF)
        inputs_all = lax.optimization_barrier(inputs_all)
        projected = dot(inputs_all, qkv_own, 1, 0) + shift_own
        head_split = projected.reshape(length, 3, hp, HD)
        cosine, sine_part = rotary_tables(pos_all)
        queries = (rotate(head_split[:, 0], cosine, sine_part, 1.0) / math.sqrt(HD)).astype(BF)
        keys = rotate(head_split[:, 1], cosine, sine_part, 1.0).astype(BF)
        values = head_split[:, 2].astype(BF)
        index = jnp.arange(length, dtype=jnp.int32)
        allowed = (seg_all[:, None] == seg_all[None, :]) & (index[None, :] <= index[:, None])
        context, denominator = attention(queries, keys, values, allowed)
        context_low = context.reshape(length, hp * HD).astype(BF)
    x_float = layer_in[0].astype(F32)
    grad_float = out_grad[0].astype(F32)
    ff_columns = [(gate_weight, ff_runs), (up_weight, ff_runs)]
    if roomy:
        (
            hidden_mid, g_middle, middle_all, inner_act, g_gate, g_up, _, _, down_own, grad_all,
        ) = core_call(
            n, (context_low, out_own), layer_in[0], mlp_gain, mlp_bias, ff_columns, [down_weight],
            [out_grad[0]],
        )
        down_own = down_own.reshape(nrow * f, D)
        middle_all, grad_all = middle_all.reshape(length, D), grad_all.reshape(length, D)
        normed2, inv_std2 = norm_stats(hidden_mid)
    else:
        attn_branch, gate_own, up_own, down_own = sum_call(
            n, 2, "mix_sum", [(context_low, out_own, False)], tok, columns=ff_columns,
            rows=[down_weight],
        )
        gate_own, up_own = gate_own.reshape(D, nrow * f), up_own.reshape(D, nrow * f)
        down_own = down_own.reshape(nrow * f, D)
        hidden_mid = x_float + attn_branch
        normed2, inv_std2 = norm_stats(hidden_mid)
        middle = (normed2 * mlp_gain + mlp_bias).astype(BF)
        (middle_all,) = gather_call(n, 3, "middle", middle)
        middle_all = middle_all.reshape(length, D)
        gate_pre = dot(middle_all, gate_own, 1, 0)
        up_pre = dot(middle_all, up_own, 1, 0)
        sig = jax.nn.sigmoid(gate_pre)
        silu = gate_pre * sig
        inner_act = (silu * up_pre).astype(BF)
        (grad_all,) = gather_call(n, 8, "grads", out_grad[0])
        grad_all = grad_all.reshape(length, D)
        g_inner = dot(grad_all, down_own, 1, 1)
        g_gate = (g_inner * up_pre * sig * (1.0 + gate_pre * (1.0 - sig))).astype(BF)
        g_up = (g_inner * silu).astype(BF)
        (g_middle,) = sum_call(
            n, 5, "mlp_back", [(g_gate, gate_own, True), (g_up, up_own, True)], tok
        )
    normed1, inv_std1 = norm_stats(x_float)
    if roomy:
        down_part, gate_part, up_part = (inner_act, grad_all), (middle_all, g_gate), (middle_all, g_up)
    else:
        down_part = dot(inner_act, grad_all, 0, 0).astype(BF).reshape(nrow, f, D)
        gate_part = dot(middle_all, g_gate, 0, 0).astype(BF).reshape(nrow, n * k, nrow * f)
        up_part = dot(middle_all, g_up, 0, 0).astype(BF).reshape(nrow, n * k, nrow * f)
    g_hidden = grad_float + norm_back(g_middle, normed2, inv_std2, mlp_gain)
    g_attn = g_hidden.astype(BF)
    if roomy:
        mlp_branch, g_attn_all, down_grad, gate_grad, up_grad = sum_call(
            n, 6, "mlp_sum", [(inner_act, down_own, False)], tok, gathers=[g_attn],
            row_sums=[down_part], col_sums=[(gate_part, ff_runs), (up_part, ff_runs)],
        )
    else:
        mlp_branch, down_grad = sum_call(
            n, 4, "mlp_sum", [(inner_act, down_own, False)], tok, row_sums=[down_part]
        )
        g_attn_all, gate_grad, up_grad = gather_call(
            n, 6, "hidden_back", g_attn, col_sums=[(gate_part, ff_runs), (up_part, ff_runs)]
        )
    g_attn_all = g_attn_all.reshape(length, D)
    layer_out = (hidden_mid + mlp_branch).astype(BF)

    if roomy:
        known = jnp.concatenate(
            [
                jnp.zeros((2, D), F32),
                jnp.sum(g_middle * normed2, axis=0)[None],
                jnp.sum(g_middle, axis=0)[None],
                jnp.zeros((4, D), F32),
            ]
        )
        g_inputs, small_grads, out_w_grad, qkv_grad = back_call(
            n, g_attn_all, out_own, qkv_own, (queries, keys, values), context, context_low,
            denominator, ints_all, frequency, inputs_all, normed1, known, head_runs,
        )
    else:
        g_context = dot(g_attn_all, out_own, 1, 1).reshape(length, hp, HD)
        g_queries, g_keys, g_values = attention_back(
            queries, keys, values, allowed, denominator, context, g_context
        )
        query_part = rotate(g_queries, cosine, sine_part, -1.0) / math.sqrt(HD)
        key_part = rotate(g_keys, cosine, sine_part, -1.0)
        g_projected = (
            jnp.stack([query_part, key_part, g_values], 1).reshape(length, 3 * hp * HD).astype(BF)
        )
        qkv_part = dot(inputs_all, g_projected, 0, 0).astype(BF)
        qkv_part = qkv_part.reshape(nrow, n * k, 3 * hp * HD)
        out_part = dot(context_low, g_attn_all, 0, 0).astype(BF)
        if whole_heads:
            out_part = out_part.reshape((nrow,) + out_weight.shape)
        shift_sum = jnp.sum(g_projected.astype(F32), axis=0)
        shift_blocks = lax.dynamic_update_slice_in_dim(
            jnp.zeros((n, 1, 3 * hp * HD), F32), shift_sum[None, None], j, 0
        )
        shift_full = join_heads(shift_blocks)[0]
        known = jnp.concatenate(
            [
                jnp.zeros((2, D), F32),
                jnp.sum(g_middle * normed2, axis=0)[None],
                jnp.sum(g_middle, axis=0)[None],
                shift_full.reshape(nrow, 3, D // nrow).transpose(1, 0, 2).reshape(3, D),
                jnp.zeros((1, D), F32),
            ]
        )
        last = last_call(
            n, 7, [(g_projected, qkv_own, True)], tok, normed1, known,
            [out_part] if whole_heads else [],
            [(qkv_part, head_runs)],
        )
        if whole_heads:
            g_inputs, small_grads, out_w_grad, qkv_grad = last
        else:
            g_inputs, small_grads, qkv_grad = last
            placed = lax.dynamic_update_slice_in_dim(
                jnp.zeros((D, D), BF), out_part, j * hp * HD, 0
            )
            out_w_grad = lax.psum_scatter(
                placed, ("row", "seq"), scatter_dimension=0, tiled=True
            ).astype(F32)
    input_grad = g_hidden + norm_back(g_inputs, normed1, inv_std1, attn_gain)
    own = lax.dynamic_slice_in_dim(small_grads, j * k, k, 1)
    shift_own_grad = lax.dynamic_slice_in_dim(small_grads[4:7].reshape(-1), j * 3 * k, 3 * k, 0)
    return (
        layer_out[None],
        input_grad[None],
        own[0],
        own[1],
        qkv_grad,
        shift_own_grad,
        out_w_grad,
        own[2],
        own[3],
        gate_grad,
        up_grad,
        down_grad,
    )


def solution(mesh):
    nrow, n = mesh.shape["row"], mesh.shape["seq"]

    def local(*args):
        return body(nrow, n, *args)

    tokens, ints = P("row", "seq", None), P("row", "seq")
    vec, mat = P(("row", "seq")), P(("row", "seq"), None)
    return jax.shard_map(
        local,
        mesh=mesh,
        in_specs=(
            tokens, ints, ints, vec, vec, mat, vec, mat, vec, vec, mat, mat, mat, tokens,
        ),
        out_specs=(tokens, tokens, vec, vec, mat, vec, mat, vec, vec, mat, mat, mat),
        check_vma=False,
    )
```

```python
import functools
import math

import jax
import jax.numpy as jnp
from jax import lax
from jax.experimental import pallas as pl
from jax.experimental.pallas import tpu as pltpu
from jax.sharding import PartitionSpec as P

D = 2048
H = 32
HD = 64
ROT = 16
EPSILON = 1e-05
BF = jnp.bfloat16
F32 = jnp.float32


def dot(a, b, ca, cb):
    return lax.dot_general(a, b, (((ca,), (cb,)), ((), ())), preferred_element_type=F32)


def norm_stats(values_in):
    average = jnp.mean(values_in, axis=-1, keepdims=True)
    centered = values_in - average
    inv_std = lax.rsqrt(jnp.mean(centered * centered, axis=-1, keepdims=True) + EPSILON)
    return (centered * inv_std, inv_std)


def norm_back(grad_in, normed, inv_std, gain_vector):
    scaled = grad_in * gain_vector
    return inv_std * (
        scaled
        - jnp.mean(scaled, axis=-1, keepdims=True)
        - normed * jnp.mean(scaled * normed, axis=-1, keepdims=True)
    )


def rotary_tables(positions):
    half_rot = ROT // 2
    frequency = 10000.0 ** (-2.0 * jnp.arange(half_rot, dtype=F32) / ROT)
    angles = positions.astype(F32)[:, None] * frequency[None, :]
    return (jnp.cos(angles)[:, None, :], jnp.sin(angles)[:, None, :])


def rotate(head_values, cosine, sine_part, direction):
    half_rot = ROT // 2
    first_half = head_values[..., :half_rot]
    second = head_values[..., half_rot:ROT]
    return jnp.concatenate(
        [
            first_half * cosine - direction * second * sine_part,
            second * cosine + direction * first_half * sine_part,
            head_values[..., ROT:],
        ],
        axis=-1,
    )


MESH = pl.DeviceIdType.MESH
LINE = 4


class Place:
    def __init__(self, n):
        self.n = n
        self.depth = LINE
        self.width = n // LINE
        self.r = lax.axis_index("row")
        self.j = lax.axis_index("seq")
        self.z = self.j // self.width
        self.x = lax.rem(self.j, self.width)
        y, c = self.r // 2, lax.rem(self.r, 2)
        self.y, self.c = y, c
        self.r_y = (1 - y) * 2 + c
        self.r_c = y * 2 + (1 - c)
        self.r_yc = (1 - y) * 2 + (1 - c)

    def inner(self, t):
        return jnp.logical_or(
            jnp.logical_and(t > self.z, self.z > 0),
            jnp.logical_and(t < self.z, self.z < self.depth - 1),
        )

    def seq(self, j):
        return (self.r, j)

    def row(self, r):
        return (r, self.j)

    def other(self, i):
        return lax.rem(self.j + i, self.n)

    def meet(self):
        barrier = pltpu.get_barrier_semaphore()
        for r in (self.r_y, self.r_c, self.r_yc):
            pl.semaphore_signal(barrier, inc=1, device_id=self.row(r), device_id_type=MESH)
        for i in range(1, self.n):
            pl.semaphore_signal(
                barrier, inc=1, device_id=self.seq(self.other(i)), device_id_type=MESH
            )
        pl.semaphore_wait(barrier, self.n + 2)


def remote(src, dst, ssem, rsem, device):
    return pltpu.make_async_remote_copy(
        src_ref=src, dst_ref=dst, send_sem=ssem, recv_sem=rsem, device_id=device,
        device_id_type=MESH,
    )


ALONE = ((8, False),)
PAIRED = ((2, True), (6, False))
SUM_CUTS = ((1, True), (7, False))
CORE_SUMS = ((2, True), (6, False))
CORE_PLAN = ("c0", "g1", "c1", "r3", "c2", "y0", "c3", "y1", "g2", "r2", "y2", "y3", "g3", "r1")
SUM_PLAN = ("w0", "g1", "c0", "r3", "w1", "x0", "w2", "x1", "g2", "c1", "r2", "x2", "t0", "g3", "c2", "c3", "r1", "t1", "y0", "y1", "y2", "y3")
BACK_PLAN = ("w0", "r3", "w1", "x0", "x1", "r2", "t0", "r1")
MLP_CUTS = ((2, True), (3, False), (3, False))
MLP_SUMS = ((2, True), (3, False), (3, False))


class Gather:
    @staticmethod
    def sems(n, cuts):
        w = n // LINE
        out = []
        for _ in cuts:
            out += [
                pltpu.SemaphoreType.DMA((2, n)),
                pltpu.SemaphoreType.DMA((LINE, max(w - 1, 1))),
                pltpu.SemaphoreType.DMA((n,)),
            ]
        return out

    def __init__(self, at, buf, sems, cuts):
        self.at, self.buf = at, buf
        tok = buf.shape[1]
        self.cuts = []
        first = 0
        for i, (share, wide) in enumerate(cuts):
            rows = tok * share // 8
            self.cuts.append((pl.ds(first, rows), wide, sems[3 * i : 3 * i + 3]))
            first += rows

    def copy(self, cut, b, to, sem):
        here = self.buf.at[b, cut[0]]
        return remote(here, here, sem, cut[2][2].at[b], self.at.seq(to))

    def along(self, cut, way, b):
        at = self.at
        to = at.j + at.width if way == 0 else at.j - at.width
        return self.copy(cut, b, to, cut[2][0].at[way, b])

    def across(self, cut, zz, i):
        at = self.at
        to = at.z * at.width + lax.rem(at.x + i, at.width)
        return self.copy(cut, zz * at.width + at.x, to, cut[2][1].at[zz, i - 1])

    def take(self, cut, b):
        self.copy(cut, b, self.at.other(1), cut[2][0].at[0, 0]).wait_recv()

    def onward(self, cut, way, b):
        at = self.at

        @pl.when(at.z < at.depth - 1 if way == 0 else at.z > 0)
        def _():
            self.along(cut, way, b).start()

    def start(self):
        at = self.at
        for cut in self.cuts:
            if cut[1]:
                for i in range(1, at.width):
                    self.across(cut, at.z, i).start()
        for cut in self.cuts:
            for way in range(2):
                self.onward(cut, way, at.j)
            if not cut[1]:
                for i in range(1, at.width):
                    self.across(cut, at.z, i).start()

    def step(self, s):
        at = self.at
        for cut in self.cuts:
            if s == 1 and cut[1]:
                for i in range(1, at.width):
                    b = at.z * at.width + lax.rem(at.x + i, at.width)
                    self.take(cut, b)
                    for way in range(2):
                        self.onward(cut, way, b)
        for cut in self.cuts:
            for way in range(2):
                zz = at.z - s if way == 0 else at.z + s

                @pl.when(zz >= 0 if way == 0 else zz < at.depth)
                def _(zz=zz, way=way, cut=cut):
                    if cut[1]:
                        for i in range(at.width):
                            b = zz * at.width + lax.rem(at.x + i, at.width)
                            self.take(cut, b)
                            self.onward(cut, way, b)
                    else:
                        b = zz * at.width + at.x
                        self.take(cut, b)
                        self.onward(cut, way, b)
                        for i in range(1, at.width):
                            self.across(cut, zz, i).start()

    def fetch(self, zz):
        at = self.at
        for way in range(2):

            @pl.when(zz < at.z if way == 0 else zz > at.z)
            def _(way=way):
                for cut in self.cuts:
                    for i in range(at.width if cut[1] else 1):
                        b = zz * at.width + lax.rem(at.x + i, at.width)
                        self.take(cut, b)
                        self.onward(cut, way, b)
                    if not cut[1]:
                        for i in range(1, at.width):
                            self.across(cut, zz, i).start()

    def open_wide(self):
        at = self.at
        for cut in self.cuts:
            if cut[1]:
                for i in range(1, at.width):
                    b = at.z * at.width + lax.rem(at.x + i, at.width)
                    self.take(cut, b)
                    for way in range(2):
                        self.onward(cut, way, b)

    def take_side(self, zz):
        at = self.at
        for cut in self.cuts:
            if not cut[1]:
                for i in range(1, at.width):
                    self.take(cut, zz * at.width + lax.rem(at.x + i, at.width))

    def finish(self):
        at = self.at
        for cut in self.cuts:
            for zz in range(at.depth):
                for i in range(1, at.width):
                    if cut[1]:
                        @pl.when(at.z == zz)
                        def _(zz=zz, i=i, cut=cut):
                            self.across(cut, zz, i).wait_send()
                    else:
                        self.across(cut, zz, i).wait_send()
                for way in range(2):
                    ok = jnp.logical_and(at.z >= zz, at.z < at.depth - 1) if way == 0 else jnp.logical_and(at.z <= zz, at.z > 0)

                    @pl.when(ok)
                    def _(zz=zz, way=way, cut=cut):
                        for i in range(at.width if cut[1] else 1):
                            b = zz * at.width + lax.rem(at.x + i, at.width)
                            self.along(cut, way, b).wait_send()


class NarrowSum:
    @staticmethod
    def scratch(n, size, d):
        side = max(n // LINE - 1, 1)
        return (
            [pltpu.VMEM((LINE, side, size, d), BF), pltpu.VMEM((LINE + 1, size, d), BF)]
            + [pltpu.SemaphoreType.DMA((LINE, side))] * 2
            + [pltpu.SemaphoreType.DMA((LINE,)), pltpu.SemaphoreType.DMA((LINE + 1,))]
        )

    def __init__(self, at, part, rows, refs):
        self.at, self.part, self.rows = at, part, rows
        self.xr, self.lr, self.xs_sem, self.xr_sem, self.ls_sem, self.lr_sem = refs

    def across(self, t, i):
        at = self.at
        xx = lax.rem(at.x + i, at.width)
        return remote(
            self.part.at[t * at.width + xx, self.rows], self.xr.at[t, i - 1],
            self.xs_sem.at[t, i - 1], self.xr_sem.at[t, i - 1], at.seq(at.z * at.width + xx),
        )

    def along(self, t):
        at = self.at
        there = jnp.where(t > at.z, at.j + at.width, at.j - at.width)
        slot = jnp.where(t == at.z - 1, at.depth, t)
        return remote(
            self.part.at[t * at.width + at.x, self.rows], self.lr.at[slot],
            self.ls_sem.at[t], self.lr_sem.at[slot], at.seq(there),
        )

    def landed(self, slot):
        remote(
            self.lr.at[slot], self.lr.at[slot], self.ls_sem.at[0], self.lr_sem.at[slot],
            self.at.seq(self.at.other(1)),
        ).wait_recv()

    def emit(self, t):
        for i in range(1, self.at.width):
            self.across(t, i).start()

    def summed(self, t):
        at = self.at
        total = self.part[t * at.width + at.x, self.rows].astype(F32)
        for i in range(1, at.width):
            self.across(t, i).wait_recv()
            total = total + self.xr[t, i - 1].astype(F32)
        return total

    def pass_on(self, t):
        at = self.at
        block = (t * at.width + at.x, self.rows)
        total = self.summed(t)
        inner = at.inner(t)

        @pl.when(inner)
        def _():
            self.landed(t)
            self.part[block] = (total + self.lr[t].astype(F32)).astype(BF)

        @pl.when(jnp.logical_not(inner))
        def _():
            self.part[block] = total.astype(BF)

        self.along(t).start()

    def close(self):
        pass

    def last(self, out):
        at = self.at
        out[self.rows] = self.summed(at.z)

        @pl.when(at.z > 0)
        def _():
            self.landed(at.z)
            out[self.rows] += self.lr[at.z].astype(F32)

        @pl.when(at.z < at.depth - 1)
        def _():
            self.landed(at.depth)
            out[self.rows] += self.lr[at.depth].astype(F32)

    def finish(self):
        at = self.at
        for t in range(at.depth):
            for i in range(1, at.width):
                self.across(t, i).wait_send()

            @pl.when(at.z != t)
            def _(t=t):
                self.along(t).wait_send()


class WideSum:
    @staticmethod
    def scratch(n, size, d):
        w = n // LINE
        side = max(w - 1, 1)
        return (
            [pltpu.VMEM((side, size, d), BF), pltpu.VMEM((LINE + 1, w, size, d), BF)]
            + [pltpu.SemaphoreType.DMA((side,))] * 2
            + [pltpu.SemaphoreType.DMA((LINE, w)), pltpu.SemaphoreType.DMA((LINE + 1, w))]
        )

    def __init__(self, at, part, rows, refs):
        self.at, self.part, self.rows = at, part, rows
        self.xr, self.lr, self.xs_sem, self.xr_sem, self.ls_sem, self.lr_sem = refs

    def across(self, i):
        at = self.at
        xx = lax.rem(at.x + i, at.width)
        return remote(
            self.part.at[at.z * at.width + xx, self.rows], self.xr.at[i - 1],
            self.xs_sem.at[i - 1], self.xr_sem.at[i - 1], at.seq(at.z * at.width + xx),
        )

    def along(self, t, xx):
        at = self.at
        there = jnp.where(t > at.z, at.j + at.width, at.j - at.width)
        slot = jnp.where(t == at.z - 1, at.depth, t)
        return remote(
            self.part.at[t * at.width + xx, self.rows], self.lr.at[slot, xx],
            self.ls_sem.at[t, xx], self.lr_sem.at[slot, xx], at.seq(there),
        )

    def landed(self, slot, xx):
        remote(
            self.lr.at[slot, xx], self.lr.at[slot, xx], self.ls_sem.at[0, xx],
            self.lr_sem.at[slot, xx], self.at.seq(self.at.other(1)),
        ).wait_recv()

    def emit(self, t):
        at = self.at

        @pl.when(jnp.logical_and(t != at.z, jnp.logical_not(at.inner(t))))
        def _():
            for xx in range(at.width):
                self.along(t, xx).start()

    def pass_on(self, t):
        at = self.at

        @pl.when(at.inner(t))
        def _():
            for xx in range(at.width):
                self.landed(t, xx)
                block = (t * at.width + xx, self.rows)
                total = self.part[block].astype(F32) + self.lr[t, xx].astype(F32)
                self.part[block] = total.astype(BF)
                self.along(t, xx).start()

    def line_sum(self, xx, put):
        at = self.at
        own = self.part[at.z * at.width + xx, self.rows].astype(F32)

        @pl.when(at.z == 0)
        def _():
            self.landed(at.depth, xx)
            put(own + self.lr[at.depth, xx].astype(F32))

        @pl.when(at.z == at.depth - 1)
        def _():
            self.landed(at.z, xx)
            put(own + self.lr[at.z, xx].astype(F32))

        @pl.when(jnp.logical_and(at.z > 0, at.z < at.depth - 1))
        def _():
            self.landed(at.depth, xx)
            self.landed(at.z, xx)
            put(own + self.lr[at.depth, xx].astype(F32) + self.lr[at.z, xx].astype(F32))

    def close(self):
        at = self.at
        for i in range(1, at.width):
            xx = lax.rem(at.x + i, at.width)

            def put(total, xx=xx):
                self.part[at.z * at.width + xx, self.rows] = total.astype(BF)

            self.line_sum(xx, put)
            self.across(i).start()

    def last(self, out):
        at = self.at

        def put(total):
            out[self.rows] = total

        self.line_sum(at.x, put)
        for i in range(1, at.width):
            self.across(i).wait_recv()
            out[self.rows] += self.xr[i - 1].astype(F32)

    def finish(self):
        at = self.at
        for i in range(1, at.width):
            self.across(i).wait_send()
        for t in range(at.depth):

            @pl.when(at.z != t)
            def _(t=t):
                for xx in range(at.width):
                    self.along(t, xx).wait_send()


class Reduce:
    @staticmethod
    def scratch(n, tok, d, cuts):
        out = []
        for share, wide in cuts:
            out += (WideSum if wide else NarrowSum).scratch(n, tok * share // 8, d)
        return out

    def __init__(self, at, part, refs, cuts):
        self.at, self.cuts = at, []
        tok = part.shape[1]
        first = 0
        for i, (share, wide) in enumerate(cuts):
            rows = pl.ds(first, tok * share // 8)
            first += tok * share // 8
            self.cuts.append((WideSum if wide else NarrowSum)(at, part, rows, refs[6 * i : 6 * i + 6]))

    def emit(self, t):
        for c in self.cuts:
            c.emit(t)

    def pass_on(self, t):
        for c in self.cuts:
            c.pass_on(t)

    def reduce(self, s):
        at = self.at
        for t in (at.z + s, at.z - s):

            @pl.when(jnp.logical_and(t >= 0, t < at.depth))
            def _(t=t):
                self.pass_on(t)

    def last(self, out):
        for c in self.cuts:
            c.close()
        for c in self.cuts[::-1]:
            c.last(out)

    def finish(self):
        for c in self.cuts:
            c.finish()


class Columns:
    @staticmethod
    def sems(n):
        return [pltpu.SemaphoreType.DMA((4, n)), pltpu.SemaphoreType.DMA((4, n))]

    def __init__(self, at, pieces, full, sems):
        self.at, self.pieces, self.full = at, pieces, full
        self.ssem, self.rsem = sems

    def first(self, i):
        at = self.at
        to = at.other(i)
        return remote(
            self.pieces.at[to], self.full.at[at.r, at.j], self.ssem.at[0, to],
            self.rsem.at[at.r, at.j], at.seq(to),
        )

    def own(self):
        at = self.at
        return pltpu.make_async_copy(
            self.pieces.at[at.j], self.full.at[at.r, at.j], self.ssem.at[0, at.j]
        )

    def pass_on(self, r, js, to, k):
        return remote(
            self.full.at[r, js], self.full.at[r, js], self.ssem.at[k, js], self.rsem.at[r, js],
            self.at.row(to),
        )

    def take(self, r, js):
        self.pass_on(r, js, self.at.r_c, 0).wait_recv()

    def start(self):
        at = self.at
        self.own().start()

        @pl.loop(1, at.n)
        def _(i):
            self.first(i).start()

    def step(self, lo, hi):
        at = self.at

        @pl.loop(lo, hi)
        def _(i):
            js = lax.rem(at.j + at.n - i, at.n)

            @pl.when(i == 0)
            def _():
                self.own().wait()

            @pl.when(i > 0)
            def _():
                self.take(at.r, js)

            self.pass_on(at.r, js, at.r_y, 1).start()
            self.pass_on(at.r, js, at.r_c, 2).start()

    def relay(self, lo, hi):
        at = self.at

        @pl.loop(lo, hi)
        def _(i):
            js = lax.rem(at.j + at.n - i, at.n)
            self.take(at.r_y, js)
            self.pass_on(at.r_y, js, at.r_c, 3).start()

    def finish(self):
        at = self.at

        @pl.loop(0, at.n)
        def _(js):
            self.take(at.r_c, js)
            self.take(at.r_yc, js)
            self.pass_on(at.r, js, at.r_y, 1).wait_send()
            self.pass_on(at.r, js, at.r_c, 2).wait_send()
            self.pass_on(at.r_y, js, at.r_c, 3).wait_send()

        @pl.loop(1, at.n)
        def _(i):
            self.first(i).wait_send()


class Rows:
    @staticmethod
    def sems():
        return [pltpu.SemaphoreType.DMA((4,)), pltpu.SemaphoreType.DMA((4,))]

    def __init__(self, at, shard, full, sems):
        self.at, self.shard, self.full = at, shard, full
        self.ssem, self.rsem = sems

    def own(self):
        return pltpu.make_async_copy(self.shard, self.full.at[self.at.r], self.ssem.at[0])

    def direct(self, to, k):
        r = self.at.r
        return remote(
            self.shard, self.full.at[r], self.ssem.at[k], self.rsem.at[r], self.at.row(to)
        )

    def onward(self):
        at = self.at
        r = at.r_y
        return remote(
            self.full.at[r], self.full.at[r], self.ssem.at[3], self.rsem.at[r], at.row(at.r_c)
        )

    def take(self, r):
        at = self.at
        remote(
            self.full.at[r], self.full.at[r], self.ssem.at[0], self.rsem.at[r], at.row(at.r_c)
        ).wait_recv()

    def start(self):
        at = self.at
        self.own().start()
        self.direct(at.r_y, 1).start()
        self.direct(at.r_c, 2).start()

    def relay(self):
        self.take(self.at.r_y)
        self.onward().start()

    def finish(self):
        at = self.at
        self.own().wait()
        self.take(at.r_c)
        self.take(at.r_yc)
        self.direct(at.r_y, 1).wait_send()
        self.direct(at.r_c, 2).wait_send()
        self.onward().wait_send()


class RowSum:
    @staticmethod
    def scratch(m, c):
        return [
            pltpu.VMEM((2, m, c), BF),
            pltpu.VMEM((m, c), BF),
            pltpu.SemaphoreType.DMA((3,)),
            pltpu.SemaphoreType.DMA((3,)),
        ]

    def __init__(self, at, grad, refs):
        self.at, self.grad = at, grad
        self.core_in, self.y_in, self.ssem, self.rsem = refs

    def to_core(self, far):
        at = self.at
        yy = 1 - at.y if far else at.y
        k = 1 if far else 0
        return remote(
            self.grad.at[yy * 2 + 1 - at.c], self.core_in.at[k], self.ssem.at[k], self.rsem.at[k],
            at.row(at.r_c),
        )

    def over_y(self):
        at = self.at
        return remote(
            self.grad.at[at.r_y], self.y_in, self.ssem.at[2], self.rsem.at[2], at.row(at.r_y)
        )

    def start(self):
        self.to_core(1).start()
        self.to_core(0).start()

    def cross(self):
        at = self.at
        self.to_core(1).wait_recv()
        self.grad[at.r_y] = (
            self.grad[at.r_y].astype(F32) + self.core_in[1].astype(F32)
        ).astype(BF)
        self.over_y().start()

    def total(self):
        at = self.at
        self.to_core(0).wait_recv()
        self.over_y().wait_recv()
        return (
            self.grad[at.r].astype(F32) + self.core_in[0].astype(F32) + self.y_in[...].astype(F32)
        )

    def finish(self):
        self.to_core(1).wait_send()
        self.to_core(0).wait_send()
        self.over_y().wait_send()


class Exchange:
    @staticmethod
    def sems(n):
        return [pltpu.SemaphoreType.DMA((n,)), pltpu.SemaphoreType.DMA((n,))]

    def __init__(self, at, mine, got, sems):
        self.at, self.mine, self.got = at, mine, got
        self.ssem, self.rsem = sems

    def send(self, i):
        at = self.at
        to = at.other(i)
        return remote(
            self.mine.at[to], self.got.at[at.j], self.ssem.at[to], self.rsem.at[at.j], at.seq(to)
        )

    def own(self):
        at = self.at
        return pltpu.make_async_copy(
            self.mine.at[at.j], self.got.at[at.j], self.ssem.at[at.j]
        )

    def start(self):
        self.own().start()

        @pl.loop(1, self.at.n)
        def _(i):
            self.send(i).start()

    def finish(self):
        at = self.at
        self.own().wait()

        @pl.loop(1, at.n)
        def _(i):
            src = at.other(i)
            remote(
                self.mine.at[src], self.got.at[src], self.ssem.at[src], self.rsem.at[src],
                at.seq(src),
            ).wait()


class SmallGather:
    @staticmethod
    def sems(n):
        return [pltpu.SemaphoreType.DMA((4,))] * 2 + [pltpu.SemaphoreType.DMA((n,))] * 2

    def __init__(self, at, mine, full, sems):
        self.at, self.mine, self.full = at, mine, full
        self.rs, self.rr, self.ss, self.sr = sems

    def beside(self, r):
        at = self.at
        return remote(
            self.mine, self.full.at[at.j, at.r], self.rs.at[r], self.rr.at[at.r], at.row(r)
        )

    def own(self):
        at = self.at
        return pltpu.make_async_copy(self.mine, self.full.at[at.j, at.r], self.rs.at[at.r])

    def onward(self, to):
        at = self.at
        return remote(
            self.full.at[at.j], self.full.at[at.j], self.ss.at[to], self.sr.at[at.j], at.seq(to)
        )

    def start(self):
        at = self.at
        self.own().start()
        for r in (at.r_y, at.r_c, at.r_yc):
            self.beside(r).start()

    def step(self):
        at = self.at
        self.own().wait()
        for r in (at.r_y, at.r_c, at.r_yc):
            remote(
                self.mine, self.full.at[at.j, r], self.rs.at[r], self.rr.at[r], at.row(r)
            ).wait()

        @pl.loop(1, at.n)
        def _(i):
            self.onward(at.other(i)).start()

    def finish(self):
        at = self.at

        @pl.loop(1, at.n)
        def _(i):
            src = at.other(i)
            remote(
                self.full.at[src], self.full.at[src], self.ss.at[src], self.sr.at[src],
                at.seq(src),
            ).wait()


class SmallSum:
    @staticmethod
    def scratch(n, w):
        q = w // 4
        return (
            [pltpu.VMEM((8, w), F32), pltpu.VMEM((4, 8, q), F32), pltpu.VMEM((8, q), F32)]
            + [pltpu.VMEM((n, 8, q), F32)]
            + [pltpu.SemaphoreType.DMA((4,))] * 2
            + [pltpu.SemaphoreType.DMA((n,))] * 2
        )

    def __init__(self, at, refs):
        self.at = at
        self.terms, self.beside_in, self.acc, self.seq_in = refs[:4]
        self.rs, self.rr, self.ss, self.sr = refs[4:]
        self.q = self.terms.shape[1] // 4

    def part(self, r):
        return self.terms.at[:, pl.ds(pl.multiple_of(r * self.q, self.q), self.q)]

    def beside(self, r):
        at = self.at
        return remote(
            self.part(r), self.beside_in.at[at.r], self.rs.at[r], self.rr.at[at.r], at.row(r)
        )

    def run(self, out):
        at = self.at
        near = (at.r_y, at.r_c, at.r_yc)
        for r in near:
            self.beside(r).start()
        self.acc[...] = self.part(at.r)[...]
        for r in near:
            remote(
                self.part(r), self.beside_in.at[r], self.rs.at[r], self.rr.at[r], at.row(r)
            ).wait()
            self.acc[...] += self.beside_in[r]

        @pl.loop(1, at.n)
        def _(i):
            to = at.other(i)
            remote(
                self.acc, self.seq_in.at[at.j], self.ss.at[to], self.sr.at[at.j], at.seq(to)
            ).start()

        out[...] = self.acc[...]

        @pl.loop(1, at.n)
        def _(i):
            src = at.other(i)
            remote(
                self.acc, self.seq_in.at[src], self.ss.at[src], self.sr.at[src], at.seq(src)
            ).wait()
            out[...] += self.seq_in[src]


class Call:
    def __init__(self, n, cid, name):
        self.n, self.cid, self.name = n, cid, name
        self.args, self.ins, self.outs, self.out_specs, self.scr = [], [], [], [], []

    def give(self, array, space=pltpu.VMEM):
        if isinstance(array, Made):
            return array.key
        for i, known in enumerate(self.args):
            if known is array:
                return ("i", i)
        self.args.append(array)
        self.ins.append(pl.BlockSpec(memory_space=space))
        return ("i", len(self.args) - 1)

    def make(self, shape, dtype, space=pltpu.VMEM):
        self.outs.append(jax.ShapeDtypeStruct(shape, dtype))
        self.out_specs.append(pl.BlockSpec(memory_space=space))
        return ("o", len(self.outs) - 1)

    def scratch(self, items):
        at = len(self.scr)
        self.scr.extend(items)
        return [("s", at + i) for i in range(len(items))]

    def run(self, body, flops=0):
        ni, no = len(self.ins), len(self.outs)

        def kernel(*refs):
            def of(key):
                if isinstance(key, list):
                    return [of(k) for k in key]
                if isinstance(key[0], tuple):
                    return tuple(of(k) for k in key)
                kind, i = key
                return refs[i + {"i": 0, "o": ni, "s": ni + no}[kind]]

            at = Place(self.n)
            at.meet()
            body(at, of)

        return pl.pallas_call(
            kernel,
            out_shape=self.outs,
            in_specs=self.ins,
            out_specs=self.out_specs,
            scratch_shapes=self.scr,
            name=self.name,
            cost_estimate=pl.CostEstimate(
                flops=flops, bytes_accessed=1 << 24, transcendentals=0
            ),
            compiler_params=pltpu.CompilerParams(
                collective_id=self.cid, has_side_effects=True, vmem_limit_bytes=VMEM_LIMIT
            ),
        )(*self.args)


VMEM_LIMIT = 58 << 20
ANY = pltpu.VMEM
CHUNK = 512


def product(at, of, part, pairs, t):
    width, tok = at.width, part.shape[1]

    @pl.loop(0, part.shape[2] // CHUNK)
    def _(i):
        cols = pl.ds(pl.multiple_of(i * CHUNK, CHUNK), CHUNK)
        total = None
        for lhs, rhs, flip in pairs:
            left = of(lhs)[pl.ds(t * (width * tok), width * tok), :]
            if flip:
                term = dot(left, of(rhs)[cols, :], 1, 1)
            else:
                term = dot(left, of(rhs)[:, cols], 1, 0)
            total = term if total is None else total + term
        part[pl.ds(t * width, width), :, cols] = total.reshape(width, tok, CHUNK).astype(BF)


def products(at, of, part, pairs, red):
    for s in range(at.depth - 1, -1, -1):
        for t in [at.z + s, at.z - s] if s else [at.z]:

            @pl.when(jnp.logical_and(t >= 0, t < at.depth))
            def _(t=t):
                product(at, of, part, pairs, t)
                red.emit(t)


def steps(plan, red, extra):
    work = extra.fill()
    for word in plan:
        what, k = word[0], int(word[1])
        if what == "r":
            red.reduce(k)
        elif what == "g":
            extra.gather_step(k)
        elif what == "c":
            extra.column_step(k)
        elif what == "y":
            extra.column_relay(k)
        elif what == "w" and k < len(work):
            work[k]()
        elif what == "x":
            extra.cross(k)
        elif what == "t":
            extra.turn(k)


def gather_all(g, between=None):
    at = g.at
    for s in range(1, at.depth):
        g.step(s)
        if between is not None:
            between(s)
    for s in range(at.depth):
        for zz in [at.z - s, at.z + s] if s else [at.z]:

            @pl.when(jnp.logical_and(zz >= 0, zz < at.depth))
            def _(zz=zz):
                g.take_side(zz)


def split_columns(src, dst, runs):
    for b, to, at, size in runs:
        dst[b, :, to : to + size] = src[:, at : at + size]


def join_columns(src, dst, runs):
    for b, to, at, size in runs:
        dst[:, at : at + size] = src[b, :, to : to + size].astype(dst.dtype)


def front_call(n, x, small, ints, weight, runs, out_w):
    tok, d = x.shape
    k, c = weight.shape[0], weight.shape[1] // n
    call = Call(n, 1, "front")
    ix = call.give(x, ANY)
    ism, iin = call.give(small), call.give(ints)
    iw = call.give(weight, ANY)
    ox = call.make((n, tok, d), BF, ANY)
    osm = call.make((n, 4) + small.shape, BF)
    oin = call.make((n,) + ints.shape, jnp.int32)
    ow = call.make((4, n, k, c), BF, ANY)
    sx = call.scratch(Gather.sems(n, ALONE))
    sp = call.scratch([pltpu.VMEM((n, k, c), BF)])
    ssm = call.scratch(SmallGather.sems(n))
    sin = call.scratch(Exchange.sems(n))
    sw = call.scratch(Columns.sems(n))
    if out_w is not None:
        io = call.give(out_w, ANY)
        oo = call.make((4,) + out_w.shape, BF, ANY)
        so = call.scratch(Rows.sems())

    def body(at, of):
        sm = SmallGather(at, of(ism), of(osm), of(ssm))
        g = Gather(at, of(ox), of(sx), ALONE)
        cols = Columns(at, of(sp)[0], of(ow), of(sw))
        spread = Spread(at, of(iin), of(oin), of(sin))
        sm.start()
        of(ox)[at.j] = of(ix)[...]
        g.start()
        spread.start()
        split_columns(of(iw), of(sp)[0], runs)
        cols.start()
        sm.step()
        if out_w is not None:
            rows = Rows(at, of(io), of(oo), of(so))
            rows.start()
        cuts = [0, n // 4, n // 2, n]

        def between(s):
            cols.step(cuts[s - 1], cuts[s])

        gather_all(g, between)
        cols.relay(0, n)
        if out_w is not None:
            rows.relay()
            rows.finish()
        cols.finish()
        g.finish()
        sm.finish()
        spread.finish()

    return call.run(body)


def turned(line):
    return jnp.transpose(jnp.broadcast_to(line, (128, 128)))


def rotation(ints_all, frequency, block, direction):
    lane = lax.rem(lax.broadcasted_iota(jnp.int32, (128, 128), 1), HD)
    angle = turned(ints_all[block, 1:2].astype(F32)) * frequency[0:1]
    cosine, sine = jnp.cos(angle), direction * jnp.sin(angle)
    return cosine, jnp.where(lane < ROT // 2, -sine, 0.0), jnp.where(lane < ROT // 2, 0.0, sine)


def turn_pairs(u, table):
    cosine, above, below = table
    return (
        u * cosine
        + pltpu.roll(u, 128 - ROT // 2, 1) * above
        + pltpu.roll(u, ROT // 2, 1) * below
    )


def fill_mask(at, mask, ints_all, t):
    tok = 128
    index = lax.broadcasted_iota(jnp.int32, (tok, tok), 0)
    other = lax.broadcasted_iota(jnp.int32, (tok, tok), 1)
    for b in range(at.width):
        mine = turned(ints_all[t * at.width + b, 0:1].astype(F32))
        for o in range((t + 1) * at.width):
            ok = mine == ints_all[o, 0:1].astype(F32)
            if o == t * at.width + b:
                ok = jnp.logical_and(ok, other <= index)
            fill = jnp.where(ok, 0.0, -jnp.inf)
            if o > t * at.width + b:
                fill = jnp.full((tok, tok), -jnp.inf, F32)
            mask[b * tok : (b + 1) * tok, o * tok : (o + 1) * tok] = fill


class Made:
    def __init__(self, key, shape):
        self.key, self.shape = key, shape


def attend_call(n, x, small, ints, frequency, qkv_w, head_runs, out_w):
    tok, d = x.shape
    k, c = qkv_w.shape[0], qkv_w.shape[1] // n
    hp, length, wide = H // n, n * tok, n // LINE * tok
    call = Call(n, 10, "attend")
    i_x, i_small, i_ints, i_freq = (call.give(v) for v in (x, small, ints, frequency))
    i_w, i_out = call.give(qkv_w), call.give(out_w)
    o_in = call.make((n, tok, d), BF)
    o_gains = call.make((8, d), F32)
    o_ints = call.make((n,) + ints.shape, jnp.int32)
    o_w = call.make((4, n, k, c), BF)
    o_out = call.make((4,) + out_w.shape, BF)
    o_qkv = [call.make((hp, length, HD), BF) for _ in range(3)]
    o_low = call.make((length, hp * HD), BF)
    o_ctx = call.make((length, hp * HD), F32)
    o_den = call.make((length, 128), F32)
    s_x = call.scratch([pltpu.VMEM((n, tok, d), BF)])
    s_gat = call.scratch(Gather.sems(n, ALONE))
    s_pieces = call.scratch([pltpu.VMEM((n, k, c), BF)])
    s_small = call.scratch([pltpu.VMEM((n, 4) + small.shape, F32)])
    s_shift = call.scratch([pltpu.VMEM((8, c), F32)])
    s_mask = call.scratch([pltpu.VMEM((wide, length), F32)])
    s_sg = call.scratch(SmallGather.sems(n))
    s_spread = call.scratch(Exchange.sems(n))
    s_cols = call.scratch(Columns.sems(n))
    s_rows = call.scratch(Rows.sems())

    def body(at, of):
        sm_all, xs, inputs, gains = of(s_small)[0], of(s_x)[0], of(o_in), of(o_gains)
        shift, mask, w = of(s_shift)[0], of(s_mask)[0], of(o_w)
        ints_all = of(o_ints)
        q_ref, k_ref, v_ref = of(o_qkv)
        sm = SmallGather(at, of(i_small), sm_all, of(s_sg))
        gat = Gather(at, xs, of(s_gat), ALONE)
        cols = Columns(at, of(s_pieces)[0], w, of(s_cols))
        spread = Spread(at, of(i_ints), ints_all, of(s_spread))
        out_rows = Rows(at, of(i_out), of(o_out), of(s_rows))
        sm.start()
        xs[at.j] = of(i_x)[...]
        gat.start()
        spread.start()
        split_columns(of(i_w), of(s_pieces)[0], head_runs)
        cols.start()
        sm.step()
        out_rows.start()
        gat.open_wide()
        sm.finish()
        for r in range(4):
            for b in range(n):
                lanes = slice((r * n + b) * k, (r * n + b + 1) * k)
                for i in range(4):
                    gains[i : i + 1, lanes] = sm_all[b, r, i // 2 : i // 2 + 1, i % 2 * k : (i % 2 + 1) * k]
        for m in range(3):
            for r in range(4):
                block = (m * 4 + r) * n + at.j
                owner = block // 3
                line = 2 + lax.rem(block, 3)
                shift[0:1, (m * 4 + r) * HD : (m * 4 + r + 1) * HD] = sm_all[
                    lax.rem(owner, n), owner // n, pl.ds(line, 1), 0:HD
                ]
        spread.finish()

        def norm(t):
            here = pl.ds(t * at.width, at.width)
            normed, _ = norm_stats(xs[here].reshape(wide, d).astype(F32))
            low = (normed * gains[0:1] + gains[1:2]).astype(BF)
            inputs[here] = low.reshape(at.width, tok, d)

        def project(t):
            for b in range(at.width):
                block = t * at.width + b
                these = pl.ds(block * tok, tok)
                table = rotation(ints_all, of(i_freq), block, 1.0)
                projected = dot(inputs[block], w[...].reshape(d, c), 1, 0) + shift[0:1]
                for i in range(4 * hp * HD // 256):
                    u = projected[:, i * 128 : (i + 1) * 128]
                    u = turn_pairs(u, table)
                    for e in range(2):
                        head = i * 2 + e
                        val = u[:, e * HD : (e + 1) * HD]
                        if head < hp:
                            q_ref[head, these] = (val * (1.0 / math.sqrt(HD))).astype(BF)
                        else:
                            k_ref[head - hp, these] = val.astype(BF)
                for head in range(hp):
                    first = (2 * hp + head) * HD
                    v_ref[head, these] = projected[:, first : first + HD].astype(BF)

        order = by_place(at.z, (3210, 3201, 132, 123))
        edge = jnp.logical_or(at.z == 0, at.z == at.depth - 1)

        @pl.loop(0, LINE)
        def _(i):
            t = digit(order, i)
            lo = jnp.where(edge, i + 1, jnp.where(i == 0, 1, jnp.where(i == 1, 3, 4)))
            hi = jnp.where(edge, jnp.minimum(i + 2, 4), jnp.where(i == 0, 3, 4))

            @pl.loop(lo, hi)
            def _(m):
                gat.fetch(digit(order, m))

            cols.step(jnp.where(i < 3, i * (n // 4), n), jnp.where(i < 2, (i + 1) * (n // 4), n))

            @pl.when(i == 3)
            def _():
                cols.relay(0, n)
                cols.finish()

                @pl.loop(0, 3)
                def _(m):
                    project(digit(order, m))

            gat.take_side(t)
            norm(t)

        out_rows.relay()
        project(digit(order, 3))
        for t in range(LINE):
            reach = (t + 1) * wide
            fill_mask(at, mask, ints_all, t)
            these = slice(t * wide, (t + 1) * wide)
            for head in range(hp):
                lanes = slice(head * HD, (head + 1) * HD)
                scores = dot(q_ref[head, these], k_ref[head, 0:reach], 1, 1)
                weights = jnp.exp(scores + mask[:, 0:reach])
                den = jnp.sum(weights, axis=1, keepdims=True)
                numer = dot(weights.astype(BF), v_ref[head, 0:reach], 1, 0)
                ctx = numer / den
                of(o_ctx)[these, lanes] = ctx
                of(o_low)[these, lanes] = ctx.astype(BF)
                of(o_den)[these, head : head + 1] = den
        out_rows.finish()
        gat.finish()

    return call.run(body)


class Spread:
    def __init__(self, at, mine, got, sems):
        self.at, self.mine, self.got = at, mine, got
        self.ssem, self.rsem = sems

    def copy(self, to, src):
        at = self.at
        return remote(
            self.mine, self.got.at[src], self.ssem.at[to], self.rsem.at[src], at.seq(to)
        )

    def own(self):
        return pltpu.make_async_copy(self.mine, self.got.at[self.at.j], self.ssem.at[self.at.j])

    def start(self):
        self.own().start()

        @pl.loop(1, self.at.n)
        def _(i):
            self.copy(self.at.other(i), self.at.j).start()

    def finish(self):
        self.own().wait()

        @pl.loop(1, self.at.n)
        def _(i):
            p = self.at.other(i)
            self.copy(p, p).wait()


def sum_call(n, cid, name, pairs, tok, columns=(), rows=(), gathers=(), row_sums=(), col_sums=()):
    call = Call(n, cid, name)
    d = pairs[0][1].shape[0 if pairs[0][2] else 1]
    keys = []
    for lhs, rhs, flip in pairs:
        keys.append((call.give(lhs), call.give(rhs), flip))
    out = call.make((tok, d), F32)
    part = call.scratch([pltpu.VMEM((n, tok, d), BF)])
    red_s = call.scratch(Reduce.scratch(n, tok, d, SUM_CUTS))
    extra = Extras(call, n, columns, rows, gathers, row_sums, col_sums, PAIRED)

    def body(at, of):
        part_ref = of(part)[0]
        red = Reduce(at, part_ref, of(red_s), SUM_CUTS)
        extra.bind(at, of)
        extra.start()
        products(at, of, part_ref, keys, red)
        steps(SUM_PLAN, red, extra)
        red.last(of(out))
        extra.finish()
        red.finish()

    flops = sum(2 * l.shape[0] * l.shape[1] * d for l, _, _ in pairs)
    return call.run(body, flops)


class Extras:
    def __init__(
        self, call, n, columns=(), rows=(), gathers=(), row_sums=(), col_sums=(), cuts=None
    ):
        self.n, self.cuts = n, cuts
        self.columns, self.rows, self.gathers, self.row_sums, self.col_sums = [], [], [], [], []
        for w, runs in columns:
            shape = (n, w.shape[0], w.shape[1] // n)
            self.columns.append(
                (
                    call.give(w),
                    call.make((4,) + shape, BF, ANY),
                    call.scratch([pltpu.VMEM(shape, BF)]),
                    call.scratch(Columns.sems(n)),
                    runs,
                )
            )
        for p in rows:
            self.rows.append(
                (call.give(p, ANY), call.make((4,) + p.shape, BF, ANY), call.scratch(Rows.sems()))
            )
        for p in gathers:
            self.gathers.append(
                (
                    call.give(p, ANY),
                    call.make((n,) + p.shape, BF, ANY),
                    call.scratch(Gather.sems(n, cuts)),
                )
            )
        self.n_row = n_row = 4
        for p in row_sums:
            lhs, rhs = p if isinstance(p, tuple) else (None, None)
            shape = (n_row, lhs.shape[1] // n_row, rhs.shape[1]) if lhs is not None else p.shape
            self.row_sums.append(
                (
                    (call.give(lhs), call.give(rhs)) if lhs is not None else call.give(p),
                    call.scratch([pltpu.VMEM(shape, BF)])[0],
                    call.make(shape[1:], F32),
                    call.scratch(RowSum.scratch(*shape[1:])),
                )
            )
        for p, runs in col_sums:
            lhs, rhs = p if isinstance(p, tuple) else (None, None)
            shape = (n_row, lhs.shape[1] // n_row, rhs.shape[1]) if lhs is not None else p.shape
            k, c = shape[1] // n, shape[2]
            self.col_sums.append(
                (
                    (call.give(lhs), call.give(rhs)) if lhs is not None else call.give(p),
                    call.scratch([pltpu.VMEM(shape, BF)])[0],
                    call.make((k, n * c), F32),
                    call.scratch(RowSum.scratch(*shape[1:])),
                    call.scratch([pltpu.VMEM((n, k, c), BF)] * 2),
                    call.scratch(Exchange.sems(n)),
                    runs,
                )
            )

    def bind(self, at, of):
        self.at, self.of = at, of
        self.b_columns = [
            (Columns(at, of(p)[0], of(o), of(s)), of(i), of(p)[0], runs)
            for i, o, p, s, runs in self.columns
        ]
        self.b_rows = [Rows(at, of(i), of(o), of(s)) for i, o, s in self.rows]
        self.b_gathers = [
            (Gather(at, of(o), of(s), self.cuts), of(i), of(o)) for i, o, s in self.gathers
        ]
        self.b_sums = [
            (RowSum(at, of(g), of(s)), of(o), of(i), of(g)) for i, g, o, s in self.row_sums
        ]
        self.b_cols = []
        for i, g, o, s, v, e, runs in self.col_sums:
            mine, got = of(v)
            self.b_cols.append(
                (
                    RowSum(at, of(g), of(s)),
                    mine,
                    Exchange(at, mine, got, of(e)),
                    (got, of(o), runs),
                    of(i),
                    of(g),
                )
            )

    def start(self):
        at = self.at
        for g, src, buf in self.b_gathers:
            buf[at.j] = src[...]
            g.start()
        for r in self.b_rows:
            r.start()
        for c, src, pieces, runs in self.b_columns:
            split_columns(src, pieces, runs)
            c.start()

    def fill_columns(self, k):
        rs, _, _, _, src, grad = self.b_cols[k]
        if isinstance(src, tuple):
            size = grad.shape[1]

            @pl.loop(0, grad.shape[0])
            def _(b):
                cols = pl.ds(pl.multiple_of(b * size, size), size)
                grad[b] = dot(src[0][:, cols], src[1][...], 0, 0).astype(BF)
        else:
            grad[...] = src[...]
        rs.start()

    def fill_rows(self, k):
        rs, _, src, grad = self.b_sums[k]
        if isinstance(src, tuple):

            @pl.loop(0, grad.shape[2] // CHUNK)
            def _(b):
                cols = pl.ds(pl.multiple_of(b * CHUNK, CHUNK), CHUNK)
                term = dot(src[0][...], src[1][:, cols], 0, 0)
                grad[:, :, cols] = term.reshape(grad.shape[0], grad.shape[1], CHUNK).astype(BF)
        else:
            grad[...] = src[...]
        rs.start()

    def fill(self):
        work = [functools.partial(self.fill_columns, k) for k in range(len(self.b_cols))]
        return work + [functools.partial(self.fill_rows, k) for k in range(len(self.b_sums))]

    def cross(self, k):
        every = [c[0] for c in self.b_cols] + [r[0] for r in self.b_sums]
        if k < len(every):
            every[k].cross()

    def turn(self, k):
        if k < len(self.b_cols):
            rs, mine, ex = self.b_cols[k][:3]
            mine[...] = rs.total().reshape(mine.shape).astype(BF)
            ex.start()

    def gather_step(self, s):
        for g, _, _ in self.b_gathers:
            g.step(s)

    def column_step(self, k):
        q = self.n // 4
        for c, *_ in self.b_columns:
            c.step(k * q, (k + 1) * q)

    def column_relay(self, k):
        q = self.n // 4
        for c, *_ in self.b_columns:
            c.relay(k * q, (k + 1) * q)

    def finish(self):
        at = self.at
        for g, _, _ in self.b_gathers:
            for zz in range(at.depth):
                g.take_side(zz)
            g.finish()
        for r in self.b_rows:
            r.relay()
        for r in self.b_rows:
            r.finish()
        for c, *_ in self.b_columns:
            c.finish()
        for rs, out, *_ in self.b_sums:
            out[...] = rs.total()
            rs.finish()
        for rs, _, ex, (got, out, runs), *_ in self.b_cols:
            ex.finish()
            rs.finish()
            join_columns(got, out, runs)


def gather_call(n, cid, name, x, columns=(), rows=(), row_sums=(), col_sums=()):
    call = Call(n, cid, name)
    extra = Extras(call, n, columns, rows, [x], row_sums, col_sums, ALONE)

    def body(at, of):
        extra.bind(at, of)
        extra.start()
        for piece in extra.fill():
            piece()
        for k in range(3):
            extra.cross(k)
        for s in range(1, at.depth):
            extra.gather_step(s)
        for k in range(4):
            extra.column_step(k)
        for k in range(4):
            extra.column_relay(k)
        for k in range(2):
            extra.turn(k)
        extra.finish()

    return call.run(body)


def digit(code, i):
    return lax.rem(code // jnp.where(i == 0, 1, jnp.where(i == 1, 10, jnp.where(i == 2, 100, 1000))), 10)


def by_place(z, codes):
    return jnp.where(z == 0, codes[0], jnp.where(z == 1, codes[1], jnp.where(z == 2, codes[2], codes[3])))


def core_call(n, pair, x, gain, bias, columns, rows, gathers):
    call = Call(n, 2, "core")
    tok, d = x.shape
    c = columns[0][0].shape[1] // n
    wide = n // LINE * tok
    length = n * tok
    key = (call.give(pair[0]), call.give(pair[1]), False)
    i_x, i_gain, i_bias = call.give(x), call.give(gain), call.give(bias)
    o_hid = call.make((tok, d), F32)
    out = call.make((tok, d), F32)
    o_mid = call.make((n, tok, d), BF)
    o_acts = [call.make((length, c), BF) for _ in range(3)]
    part = call.scratch([pltpu.VMEM((n, tok, d), BF)] * 2)
    first_s = call.scratch(Reduce.scratch(n, tok, d, CORE_SUMS))
    extra = Extras(call, n, columns, rows, gathers, cuts=PAIRED)
    gat_s = call.scratch(Gather.sems(n, MLP_CUTS))
    red_s = call.scratch(Reduce.scratch(n, tok, d, MLP_SUMS))

    def body(at, of):
        first_part, part_ref = of(part)
        first = Reduce(at, first_part, of(first_s), CORE_SUMS)
        mid, hid = of(o_mid), of(o_hid)
        inner_ref, gg_ref, gu_ref = of(o_acts)
        gat = Gather(at, mid, of(gat_s), MLP_CUTS)
        red = Reduce(at, part_ref, of(red_s), MLP_SUMS)
        extra.bind(at, of)
        extra.start()
        products(at, of, first_part, [key], first)
        steps(CORE_PLAN, first, extra)
        first.last(hid)
        hid[...] += of(i_x)[...].astype(F32)
        normed, _ = norm_stats(hid[...])
        mid[at.j] = (normed * of(i_gain)[...] + of(i_bias)[...]).astype(BF)
        gat.start()
        extra.finish()
        gat.open_wide()
        gate, up = (c[0].full for c in extra.b_columns)
        down, grad = extra.b_rows[0].full, extra.b_gathers[0][2]
        gate, up = gate.reshape(d, c), up.reshape(d, c)
        down = down.reshape(c, d)
        order = by_place(at.z, (3210, 3201, 132, 123))
        edge = jnp.logical_or(at.z == 0, at.z == at.depth - 1)

        @pl.loop(0, LINE)
        def _(i):
            t = digit(order, i)
            lo = jnp.where(edge, i + 1, jnp.where(i == 0, 1, jnp.where(i == 1, 3, 4)))
            hi = jnp.where(edge, jnp.minimum(i + 2, 4), jnp.where(i == 0, 3, 4))

            @pl.loop(lo, hi)
            def _(m):
                gat.fetch(digit(order, m))

            gat.take_side(t)
            here = pl.ds(t * at.width, at.width)
            these = pl.ds(t * wide, wide)
            tokens = mid[here].reshape(wide, d)
            gate_pre = dot(tokens, gate[...], 1, 0)
            sig = 1.0 / (1.0 + jnp.exp(-gate_pre))
            silu = gate_pre * sig
            up_pre = dot(tokens, up[...], 1, 0)
            inner_ref[these] = (silu * up_pre).astype(BF)
            g_inner = dot(grad[here].reshape(wide, d), down[...], 1, 1)
            gu_ref[these] = (g_inner * silu).astype(BF)
            gg_ref[these] = (g_inner * up_pre * sig * (1.0 + gate_pre * (1.0 - sig))).astype(BF)
            product(at, lambda k: k, part_ref, [(gg_ref, gate, True), (gu_ref, up, True)], t)
            red.emit(t)

            @pl.when(jnp.logical_and(edge, i >= 2))
            def _():
                red.pass_on(digit(order, i - 1))

        rest = by_place(at.z, (3, 32, 301, 0))

        @pl.loop(0, jnp.where(edge, 1, 3))
        def _(i):
            red.pass_on(digit(rest, i))

        red.last(of(out))
        gat.finish()
        first.finish()
        red.finish()

    return call.run(body)


def back_call(n, g_attn, out_w, qkv_w, heads, ctx, low, den, ints, frequency, inputs, normed, known, runs):
    call = Call(n, 11, "back")
    length, d = g_attn.shape
    hp, tok, wide = H // n, length // n, length // LINE
    c = 3 * hp * HD
    i_g, i_out, i_w = call.give(g_attn), call.give(out_w), call.give(qkv_w)
    i_heads = [call.give(v) for v in heads]
    i_ctx, i_den, i_ints, i_freq = (call.give(v) for v in (ctx, den, ints, frequency))
    i_norm, i_known = call.give(normed), call.give(known)
    out = call.make((tok, d), F32)
    o_small = call.make((8, d // 4), F32)
    s_proj = call.scratch([pltpu.VMEM((length, c), BF)])[0]
    s_sum = call.scratch([pltpu.VMEM((length, c), F32)])
    s_mask = call.scratch([pltpu.VMEM((wide, length), F32)])
    part = call.scratch([pltpu.VMEM((n, tok, d), BF)])
    red_s = call.scratch(Reduce.scratch(n, tok, d, SUM_CUTS))
    s_small = call.scratch(SmallSum.scratch(n, d))
    made = Made(s_proj, (length, c))
    extra = Extras(call, n, row_sums=[(low, g_attn)], col_sums=[((inputs, made), runs)])

    def body(at, of):
        part_ref = of(part)[0]
        red = Reduce(at, part_ref, of(red_s), SUM_CUTS)
        small = SmallSum(at, of(s_small))
        proj, sums, mask = of(s_proj), of(s_sum)[0], of(s_mask)[0]
        q_ref, k_ref, v_ref = of(i_heads)
        ints_all = of(i_ints)
        extra.bind(at, of)
        extra.start()
        width = hp * HD
        sums[:, width:] = jnp.zeros((length, 2 * width), F32)
        for t in range(LINE):
            these, reach = slice(t * wide, (t + 1) * wide), (t + 1) * wide
            fill_mask(at, mask, ints_all, t)
            g_ctx = dot(of(i_g)[these], of(i_out)[...], 1, 1)
            for head in range(hp):
                lanes = slice(head * HD, (head + 1) * HD)
                g_own = g_ctx[:, lanes]
                below = of(i_den)[these, head : head + 1]
                g_num = (g_own / below).astype(BF)
                g_den = -jnp.sum(g_own * of(i_ctx)[these, lanes], axis=1, keepdims=True) / below
                query = q_ref[head, these]
                scores = dot(query, k_ref[head, 0:reach], 1, 1)
                weights = jnp.exp(scores + mask[:, 0:reach])
                g_weights = dot(g_num, v_ref[head, 0:reach], 1, 1)
                g_scores = (weights * (g_weights + g_den)).astype(BF)
                sums[these, lanes] = dot(g_scores, k_ref[head, 0:reach], 1, 0)
                lanes = slice(width + head * HD, width + (head + 1) * HD)
                sums[0:reach, lanes] += dot(g_scores, query, 0, 0)
                lanes = slice(2 * width + head * HD, 2 * width + (head + 1) * HD)
                sums[0:reach, lanes] += dot(weights.astype(BF), g_num, 0, 0)

        @pl.loop(0, n)
        def _(b):
            these = pl.ds(b * tok, tok)
            table = rotation(ints_all, of(i_freq), b, -1.0)
            for i in range(2 * width // 128):
                lanes = slice(i * 128, (i + 1) * 128)
                u = turn_pairs(sums[these, lanes], table)
                if i < width // 128:
                    u = u * (1.0 / math.sqrt(HD))
                proj[these, lanes] = u.astype(BF)
            proj[these, 2 * width :] = sums[these, 2 * width :].astype(BF)

        products(at, of, part_ref, [(s_proj, i_w, True)], red)
        small.terms[...] = of(i_known)[...]
        shift = jnp.sum(proj[...].astype(F32), axis=0, keepdims=True)
        per = d // 4
        for m in range(3):
            for r in range(4):
                own = shift[:, (m * 4 + r) * HD : (m * 4 + r + 1) * HD]
                for b in range(n):
                    flat = m * d + (r * n + b) * HD
                    row, rest = flat // (3 * per), flat % (3 * per)
                    first = row * per + rest % per
                    line = 4 + rest // per
                    small.terms[line : line + 1, first : first + HD] = jnp.where(
                        at.j == b, own, 0.0
                    )
        steps(BACK_PLAN, red, extra)
        red.last(of(out))
        grad = of(out)[...]
        small.terms[0:1, :] = jnp.sum(grad * of(i_norm)[...], axis=0, keepdims=True)
        small.terms[1:2, :] = jnp.sum(grad, axis=0, keepdims=True)
        small.run(of(o_small))
        extra.finish()
        red.finish()

    return call.run(body)


def last_call(n, cid, pairs, tok, normed, known, row_sums, col_sums):
    call = Call(n, cid, "last")
    d = pairs[0][1].shape[0]
    keys = []
    for lhs, rhs, flip in pairs:
        keys.append((call.give(lhs), call.give(rhs), flip))
    i_norm, i_known = call.give(normed), call.give(known)
    out = call.make((tok, d), F32)
    o_small = call.make((8, d // 4), F32)
    part = call.scratch([pltpu.VMEM((n, tok, d), BF)])
    red_s = call.scratch(Reduce.scratch(n, tok, d, SUM_CUTS))
    s_small = call.scratch(SmallSum.scratch(n, d))
    extra = Extras(call, n, row_sums=row_sums, col_sums=col_sums)

    def body(at, of):
        part_ref = of(part)[0]
        red = Reduce(at, part_ref, of(red_s), SUM_CUTS)
        extra.bind(at, of)
        extra.start()
        products(at, of, part_ref, keys, red)
        steps(BACK_PLAN, red, extra)
        red.last(of(out))
        small = SmallSum(at, of(s_small))
        small.terms[...] = of(i_known)[...]
        grad = of(out)[...]
        small.terms[0:1, :] = jnp.sum(grad * of(i_norm)[...], axis=0, keepdims=True)
        small.terms[1:2, :] = jnp.sum(grad, axis=0, keepdims=True)
        small.run(of(o_small))
        extra.finish()
        red.finish()

    return call.run(body)


def attention(queries, keys, values, allowed):
    scores = jnp.einsum("qhd,khd->hqk", queries, keys, preferred_element_type=F32)
    exp_weights = jnp.where(allowed[None], jnp.exp(scores), 0.0)
    denominator = jnp.sum(exp_weights, axis=-1)
    numerator = jnp.einsum(
        "hqk,khd->qhd", exp_weights.astype(BF), values, preferred_element_type=F32
    )
    return numerator / jnp.transpose(denominator)[:, :, None], denominator


def attention_back(queries, keys, values, allowed, denominator, context, g_context):
    den = jnp.transpose(denominator)
    g_numer = (g_context / den[:, :, None]).astype(BF)
    g_den = jnp.transpose(-jnp.sum(g_context * context, axis=-1) / den)
    scores = jnp.einsum("qhd,khd->hqk", queries, keys, preferred_element_type=F32)
    exp_weights = jnp.where(allowed[None], jnp.exp(scores), 0.0)
    g_values = jnp.einsum(
        "hqk,qhd->khd", exp_weights.astype(BF), g_numer, preferred_element_type=F32
    )
    g_weights = jnp.einsum("qhd,khd->hqk", g_numer, values, preferred_element_type=F32)
    g_scores = (exp_weights * (g_weights + g_den[:, :, None])).astype(BF)
    g_queries = jnp.einsum("hqk,khd->qhd", g_scores, keys, preferred_element_type=F32)
    g_keys = jnp.einsum("hqk,qhd->khd", g_scores, queries, preferred_element_type=F32)
    return g_queries, g_keys, g_values


def body(nrow, n, *args):
    (
        layer_in,
        segments,
        positions,
        attn_norm_gain,
        attn_norm_bias,
        qkv_weight,
        qkv_bias,
        out_weight,
        mlp_norm_gain,
        mlp_norm_bias,
        gate_weight,
        up_weight,
        down_weight,
        out_grad,
    ) = args
    j = lax.axis_index("seq")
    tok = layer_in.shape[1]
    length = n * tok
    k = qkv_weight.shape[0]
    f = down_weight.shape[0]
    hp = H // n
    whole_heads = out_weight.shape[0] == HD
    roomy = length * D <= 1 << 22 and whole_heads

    if whole_heads:
        head_runs = [
            (b, (m * nrow + r) * HD, m * D + (r * n + b) * HD, HD)
            for b in range(n) for m in range(3) for r in range(nrow)
        ]
    else:
        size = hp * HD
        head_runs = [
            (b, m * size, m * D + b * size, size) for b in range(n) for m in range(3)
        ]
    ff_runs = [(b, r * f, (r * n + b) * f, f) for b in range(n) for r in range(nrow)]

    def split_heads(w):
        lead = w.shape[0]
        if whole_heads:
            w = w.reshape(lead, 3, nrow, n, HD).transpose(3, 0, 1, 2, 4)
        else:
            w = w.reshape(lead, 3, n, hp, HD).transpose(2, 0, 1, 3, 4)
        return w.reshape(n, lead, 3 * hp * HD)

    def join_heads(blocks):
        lead = blocks.shape[1]
        if whole_heads:
            w = blocks.reshape(n, lead, 3, nrow, HD).transpose(1, 2, 3, 0, 4)
        else:
            w = blocks.reshape(n, lead, 3, hp, HD).transpose(1, 2, 0, 3, 4)
        return w.reshape(lead, 3 * D)

    if roomy:
        blank = jnp.zeros((128 - 2 * k,), F32)
        vectors = [
            attn_norm_gain, attn_norm_bias, blank, mlp_norm_gain, mlp_norm_bias, blank,
            jnp.pad(qkv_bias.astype(F32).reshape(3, HD), ((0, 3), (0, 128 - HD))).reshape(-1),
        ]
        small = jnp.concatenate([v.astype(F32) for v in vectors]).reshape(8, 128)
        ints = jnp.concatenate([segments, positions, jnp.zeros((6, tok), jnp.int32)], 0)
        half = ROT // 2
        frequency = 10000.0 ** (-2.0 * jnp.arange(half, dtype=F32) / ROT)
        frequency = jnp.concatenate([frequency, frequency, jnp.zeros((HD - ROT,), F32)])
        frequency = jnp.broadcast_to(jnp.concatenate([frequency, frequency])[None], (8, 128))
        (
            inputs_all, gains, ints_all, qkv_own, out_own, queries, keys, values, context_low,
            context, denominator,
        ) = attend_call(
            n, layer_in[0], small, ints, frequency, qkv_weight, head_runs, out_weight,
        )
        inputs_all = inputs_all.reshape(length, D)
        attn_gain, mlp_gain, mlp_bias = gains[0:1], gains[2:3], gains[3:4]
        qkv_own, out_own = qkv_own.reshape(D, 3 * hp * HD), out_own.reshape(hp * HD, D)
    else:
        small = jnp.concatenate(
            [attn_norm_gain, attn_norm_bias, mlp_norm_gain, mlp_norm_bias, qkv_bias]
        )
        small = jnp.pad(small, (0, 2048 - small.shape[0])).reshape(16, 128)
        ints = jnp.concatenate([segments, positions, jnp.zeros((6, tok), jnp.int32)], 0)
        front = front_call(
            n, layer_in[0], small, ints, qkv_weight, head_runs, out_weight if whole_heads else None
        )
        x_all, small_all, ints_all, qkv_own = front[:4]
        x_all = x_all.reshape(length, D)
        qkv_own = qkv_own.reshape(D, 3 * hp * HD)
        if whole_heads:
            out_own = front[4].reshape(hp * HD, D)
        else:
            out_full = lax.all_gather(out_weight, ("row", "seq"), axis=0, tiled=True)
            out_own = lax.dynamic_slice_in_dim(out_full, j * hp * HD, hp * HD, 0)
        small_all = small_all.transpose(1, 0, 2, 3).reshape(nrow * n, 2048)
        attn_gain, attn_bias, mlp_gain, mlp_bias = (
            small_all[:, c : c + k].reshape(1, D).astype(F32) for c in (0, k, 2 * k, 3 * k)
        )
        qkv_shift = small_all[:, 4 * k : 4 * k + 3 * k].reshape(1, 3 * D)
        shift_own = lax.dynamic_index_in_dim(split_heads(qkv_shift), j, 0, keepdims=False).astype(F32)
        seg_all, pos_all = ints_all[:, 0].reshape(length), ints_all[:, 1].reshape(length)

        inputs_all = (norm_stats(x_all.astype(F32))[0] * attn_gain + attn_bias).astype(BF)
        inputs_all = lax.optimization_barrier(inputs_all)
        projected = dot(inputs_all, qkv_own, 1, 0) + shift_own
        head_split = projected.reshape(length, 3, hp, HD)
        cosine, sine_part = rotary_tables(pos_all)
        queries = (rotate(head_split[:, 0], cosine, sine_part, 1.0) / math.sqrt(HD)).astype(BF)
        keys = rotate(head_split[:, 1], cosine, sine_part, 1.0).astype(BF)
        values = head_split[:, 2].astype(BF)
        index = jnp.arange(length, dtype=jnp.int32)
        allowed = (seg_all[:, None] == seg_all[None, :]) & (index[None, :] <= index[:, None])
        context, denominator = attention(queries, keys, values, allowed)
        context_low = context.reshape(length, hp * HD).astype(BF)
    x_float = layer_in[0].astype(F32)
    grad_float = out_grad[0].astype(F32)
    ff_columns = [(gate_weight, ff_runs), (up_weight, ff_runs)]
    if roomy:
        (
            hidden_mid, g_middle, middle_all, inner_act, g_gate, g_up, _, _, down_own, grad_all,
        ) = core_call(
            n, (context_low, out_own), layer_in[0], mlp_gain, mlp_bias, ff_columns, [down_weight],
            [out_grad[0]],
        )
        down_own = down_own.reshape(nrow * f, D)
        middle_all, grad_all = middle_all.reshape(length, D), grad_all.reshape(length, D)
        normed2, inv_std2 = norm_stats(hidden_mid)
    else:
        attn_branch, gate_own, up_own, down_own = sum_call(
            n, 2, "mix_sum", [(context_low, out_own, False)], tok, columns=ff_columns,
            rows=[down_weight],
        )
        gate_own, up_own = gate_own.reshape(D, nrow * f), up_own.reshape(D, nrow * f)
        down_own = down_own.reshape(nrow * f, D)
        hidden_mid = x_float + attn_branch
        normed2, inv_std2 = norm_stats(hidden_mid)
        middle = (normed2 * mlp_gain + mlp_bias).astype(BF)
        (middle_all,) = gather_call(n, 3, "middle", middle)
        middle_all = middle_all.reshape(length, D)
        gate_pre = dot(middle_all, gate_own, 1, 0)
        up_pre = dot(middle_all, up_own, 1, 0)
        sig = jax.nn.sigmoid(gate_pre)
        silu = gate_pre * sig
        inner_act = (silu * up_pre).astype(BF)
        (grad_all,) = gather_call(n, 8, "grads", out_grad[0])
        grad_all = grad_all.reshape(length, D)
        g_inner = dot(grad_all, down_own, 1, 1)
        g_gate = (g_inner * up_pre * sig * (1.0 + gate_pre * (1.0 - sig))).astype(BF)
        g_up = (g_inner * silu).astype(BF)
        (g_middle,) = sum_call(
            n, 5, "mlp_back", [(g_gate, gate_own, True), (g_up, up_own, True)], tok
        )
    normed1, inv_std1 = norm_stats(x_float)
    if roomy:
        down_part, gate_part, up_part = (inner_act, grad_all), (middle_all, g_gate), (middle_all, g_up)
    else:
        down_part = dot(inner_act, grad_all, 0, 0).astype(BF).reshape(nrow, f, D)
        gate_part = dot(middle_all, g_gate, 0, 0).astype(BF).reshape(nrow, n * k, nrow * f)
        up_part = dot(middle_all, g_up, 0, 0).astype(BF).reshape(nrow, n * k, nrow * f)
    g_hidden = grad_float + norm_back(g_middle, normed2, inv_std2, mlp_gain)
    g_attn = g_hidden.astype(BF)
    if roomy:
        mlp_branch, g_attn_all, down_grad, gate_grad, up_grad = sum_call(
            n, 6, "mlp_sum", [(inner_act, down_own, False)], tok, gathers=[g_attn],
            row_sums=[down_part], col_sums=[(gate_part, ff_runs), (up_part, ff_runs)],
        )
    else:
        mlp_branch, down_grad = sum_call(
            n, 4, "mlp_sum", [(inner_act, down_own, False)], tok, row_sums=[down_part]
        )
        g_attn_all, gate_grad, up_grad = gather_call(
            n, 6, "hidden_back", g_attn, col_sums=[(gate_part, ff_runs), (up_part, ff_runs)]
        )
    g_attn_all = g_attn_all.reshape(length, D)
    layer_out = (hidden_mid + mlp_branch).astype(BF)

    if roomy:
        known = jnp.concatenate(
            [
                jnp.zeros((2, D), F32),
                jnp.sum(g_middle * normed2, axis=0)[None],
                jnp.sum(g_middle, axis=0)[None],
                jnp.zeros((4, D), F32),
            ]
        )
        g_inputs, small_grads, out_w_grad, qkv_grad = back_call(
            n, g_attn_all, out_own, qkv_own, (queries, keys, values), context, context_low,
            denominator, ints_all, frequency, inputs_all, normed1, known, head_runs,
        )
    else:
        g_context = dot(g_attn_all, out_own, 1, 1).reshape(length, hp, HD)
        g_queries, g_keys, g_values = attention_back(
            queries, keys, values, allowed, denominator, context, g_context
        )
        query_part = rotate(g_queries, cosine, sine_part, -1.0) / math.sqrt(HD)
        key_part = rotate(g_keys, cosine, sine_part, -1.0)
        g_projected = (
            jnp.stack([query_part, key_part, g_values], 1).reshape(length, 3 * hp * HD).astype(BF)
        )
        qkv_part = dot(inputs_all, g_projected, 0, 0).astype(BF)
        qkv_part = qkv_part.reshape(nrow, n * k, 3 * hp * HD)
        out_part = dot(context_low, g_attn_all, 0, 0).astype(BF)
        if whole_heads:
            out_part = out_part.reshape((nrow,) + out_weight.shape)
        shift_sum = jnp.sum(g_projected.astype(F32), axis=0)
        shift_blocks = lax.dynamic_update_slice_in_dim(
            jnp.zeros((n, 1, 3 * hp * HD), F32), shift_sum[None, None], j, 0
        )
        shift_full = join_heads(shift_blocks)[0]
        known = jnp.concatenate(
            [
                jnp.zeros((2, D), F32),
                jnp.sum(g_middle * normed2, axis=0)[None],
                jnp.sum(g_middle, axis=0)[None],
                shift_full.reshape(nrow, 3, D // nrow).transpose(1, 0, 2).reshape(3, D),
                jnp.zeros((1, D), F32),
            ]
        )
        last = last_call(
            n, 7, [(g_projected, qkv_own, True)], tok, normed1, known,
            [out_part] if whole_heads else [],
            [(qkv_part, head_runs)],
        )
        if whole_heads:
            g_inputs, small_grads, out_w_grad, qkv_grad = last
        else:
            g_inputs, small_grads, qkv_grad = last
            placed = lax.dynamic_update_slice_in_dim(
                jnp.zeros((D, D), BF), out_part, j * hp * HD, 0
            )
            out_w_grad = lax.psum_scatter(
                placed, ("row", "seq"), scatter_dimension=0, tiled=True
            ).astype(F32)
    input_grad = g_hidden + norm_back(g_inputs, normed1, inv_std1, attn_gain)
    own = lax.dynamic_slice_in_dim(small_grads, j * k, k, 1)
    shift_own_grad = lax.dynamic_slice_in_dim(small_grads[4:7].reshape(-1), j * 3 * k, 3 * k, 0)
    return (
        layer_out[None],
        input_grad[None],
        own[0],
        own[1],
        qkv_grad,
        shift_own_grad,
        out_w_grad,
        own[2],
        own[3],
        gate_grad,
        up_grad,
        down_grad,
    )


def solution(mesh):
    nrow, n = mesh.shape["row"], mesh.shape["seq"]

    def local(*args):
        return body(nrow, n, *args)

    tokens, ints = P("row", "seq", None), P("row", "seq")
    vec, mat = P(("row", "seq")), P(("row", "seq"), None)
    return jax.shard_map(
        local,
        mesh=mesh,
        in_specs=(
            tokens, ints, ints, vec, vec, mat, vec, mat, vec, vec, mat, mat, mat, tokens,
        ),
        out_specs=(tokens, tokens, vec, vec, mat, vec, mat, vec, vec, mat, mat, mat),
        check_vma=False,
    )
```

```python
import functools
import math

import jax
import jax.numpy as jnp
from jax import lax
from jax.experimental import pallas as pl
from jax.experimental.pallas import tpu as pltpu
from jax.sharding import PartitionSpec as P

D = 2048
H = 32
HD = 64
ROT = 16
EPSILON = 1e-05
BF = jnp.bfloat16
F32 = jnp.float32


def dot(a, b, ca, cb):
    return lax.dot_general(a, b, (((ca,), (cb,)), ((), ())), preferred_element_type=F32)


def norm_stats(values_in):
    average = jnp.mean(values_in, axis=-1, keepdims=True)
    centered = values_in - average
    inv_std = lax.rsqrt(jnp.mean(centered * centered, axis=-1, keepdims=True) + EPSILON)
    return (centered * inv_std, inv_std)


def norm_back(grad_in, normed, inv_std, gain_vector):
    scaled = grad_in * gain_vector
    return inv_std * (
        scaled
        - jnp.mean(scaled, axis=-1, keepdims=True)
        - normed * jnp.mean(scaled * normed, axis=-1, keepdims=True)
    )


def rotary_tables(positions):
    half_rot = ROT // 2
    frequency = 10000.0 ** (-2.0 * jnp.arange(half_rot, dtype=F32) / ROT)
    angles = positions.astype(F32)[:, None] * frequency[None, :]
    return (jnp.cos(angles)[:, None, :], jnp.sin(angles)[:, None, :])


def rotate(head_values, cosine, sine_part, direction):
    half_rot = ROT // 2
    first_half = head_values[..., :half_rot]
    second = head_values[..., half_rot:ROT]
    return jnp.concatenate(
        [
            first_half * cosine - direction * second * sine_part,
            second * cosine + direction * first_half * sine_part,
            head_values[..., ROT:],
        ],
        axis=-1,
    )


MESH = pl.DeviceIdType.MESH
LINE = 4


class Place:
    def __init__(self, n):
        self.n = n
        self.depth = LINE
        self.width = n // LINE
        self.r = lax.axis_index("row")
        self.j = lax.axis_index("seq")
        self.z = self.j // self.width
        self.x = lax.rem(self.j, self.width)
        y, c = self.r // 2, lax.rem(self.r, 2)
        self.y, self.c = y, c
        self.r_y = (1 - y) * 2 + c
        self.r_c = y * 2 + (1 - c)
        self.r_yc = (1 - y) * 2 + (1 - c)

    def inner(self, t):
        return jnp.logical_or(
            jnp.logical_and(t > self.z, self.z > 0),
            jnp.logical_and(t < self.z, self.z < self.depth - 1),
        )

    def seq(self, j):
        return (self.r, j)

    def row(self, r):
        return (r, self.j)

    def other(self, i):
        return lax.rem(self.j + i, self.n)

    def meet(self):
        barrier = pltpu.get_barrier_semaphore()
        for r in (self.r_y, self.r_c, self.r_yc):
            pl.semaphore_signal(barrier, inc=1, device_id=self.row(r), device_id_type=MESH)
        for i in range(1, self.n):
            pl.semaphore_signal(
                barrier, inc=1, device_id=self.seq(self.other(i)), device_id_type=MESH
            )
        pl.semaphore_wait(barrier, self.n + 2)


def remote(src, dst, ssem, rsem, device):
    return pltpu.make_async_remote_copy(
        src_ref=src, dst_ref=dst, send_sem=ssem, recv_sem=rsem, device_id=device,
        device_id_type=MESH,
    )


ALONE = ((8, False),)
PAIRED = ((2, True), (6, False))
SUM_CUTS = ((1, True), (7, False))
CORE_SUMS = ((2, True), (6, False))
CORE_PLAN = ("c0", "g1", "c1", "r3", "c2", "y0", "c3", "y1", "g2", "r2", "y2", "y3", "g3", "r1")
SUM_PLAN = ("w0", "g1", "c0", "r3", "w1", "x0", "w2", "x1", "g2", "c1", "r2", "x2", "t0", "g3", "c2", "c3", "r1", "t1", "y0", "y1", "y2", "y3")
GATHER_PLAN = ("w0", "g1", "w1", "x0", "w2", "x1", "g2", "x2", "t0", "g3", "t1")
BACK_PLAN = ("w0", "r3", "w1", "x0", "x1", "r2", "t0", "r1")
MLP_CUTS = ((2, True), (3, False), (3, False))
MLP_SUMS = ((2, True), (3, False), (3, False))


class Gather:
    @staticmethod
    def sems(n, cuts):
        w = n // LINE
        out = []
        for _ in cuts:
            out += [
                pltpu.SemaphoreType.DMA((2, n)),
                pltpu.SemaphoreType.DMA((LINE, max(w - 1, 1))),
                pltpu.SemaphoreType.DMA((n,)),
            ]
        return out

    def __init__(self, at, buf, sems, cuts):
        self.at, self.buf = at, buf
        tok = buf.shape[1]
        self.cuts = []
        first = 0
        for i, (share, wide) in enumerate(cuts):
            rows = tok * share // 8
            self.cuts.append((pl.ds(first, rows), wide, sems[3 * i : 3 * i + 3]))
            first += rows

    def copy(self, cut, b, to, sem):
        here = self.buf.at[b, cut[0]]
        return remote(here, here, sem, cut[2][2].at[b], self.at.seq(to))

    def along(self, cut, way, b):
        at = self.at
        to = at.j + at.width if way == 0 else at.j - at.width
        return self.copy(cut, b, to, cut[2][0].at[way, b])

    def across(self, cut, zz, i):
        at = self.at
        to = at.z * at.width + lax.rem(at.x + i, at.width)
        return self.copy(cut, zz * at.width + at.x, to, cut[2][1].at[zz, i - 1])

    def take(self, cut, b):
        self.copy(cut, b, self.at.other(1), cut[2][0].at[0, 0]).wait_recv()

    def onward(self, cut, way, b):
        at = self.at

        @pl.when(at.z < at.depth - 1 if way == 0 else at.z > 0)
        def _():
            self.along(cut, way, b).start()

    def start(self):
        at = self.at
        for cut in self.cuts:
            if cut[1]:
                for i in range(1, at.width):
                    self.across(cut, at.z, i).start()
        for cut in self.cuts:
            for way in range(2):
                self.onward(cut, way, at.j)
            if not cut[1]:
                for i in range(1, at.width):
                    self.across(cut, at.z, i).start()

    def step(self, s):
        at = self.at
        for cut in self.cuts:
            if s == 1 and cut[1]:
                for i in range(1, at.width):
                    b = at.z * at.width + lax.rem(at.x + i, at.width)
                    self.take(cut, b)
                    for way in range(2):
                        self.onward(cut, way, b)
        for cut in self.cuts:
            for way in range(2):
                zz = at.z - s if way == 0 else at.z + s

                @pl.when(zz >= 0 if way == 0 else zz < at.depth)
                def _(zz=zz, way=way, cut=cut):
                    if cut[1]:
                        for i in range(at.width):
                            b = zz * at.width + lax.rem(at.x + i, at.width)
                            self.take(cut, b)
                            self.onward(cut, way, b)
                    else:
                        b = zz * at.width + at.x
                        self.take(cut, b)
                        self.onward(cut, way, b)
                        for i in range(1, at.width):
                            self.across(cut, zz, i).start()

    def fetch(self, zz):
        at = self.at
        for way in range(2):

            @pl.when(zz < at.z if way == 0 else zz > at.z)
            def _(way=way):
                for cut in self.cuts:
                    for i in range(at.width if cut[1] else 1):
                        b = zz * at.width + lax.rem(at.x + i, at.width)
                        self.take(cut, b)
                        self.onward(cut, way, b)
                    if not cut[1]:
                        for i in range(1, at.width):
                            self.across(cut, zz, i).start()

    def open_wide(self):
        at = self.at
        for cut in self.cuts:
            if cut[1]:
                for i in range(1, at.width):
                    b = at.z * at.width + lax.rem(at.x + i, at.width)
                    self.take(cut, b)
                    for way in range(2):
                        self.onward(cut, way, b)

    def take_side(self, zz):
        at = self.at
        for cut in self.cuts:
            if not cut[1]:
                for i in range(1, at.width):
                    self.take(cut, zz * at.width + lax.rem(at.x + i, at.width))

    def finish(self):
        at = self.at
        for cut in self.cuts:
            for zz in range(at.depth):
                for i in range(1, at.width):
                    if cut[1]:
                        @pl.when(at.z == zz)
                        def _(zz=zz, i=i, cut=cut):
                            self.across(cut, zz, i).wait_send()
                    else:
                        self.across(cut, zz, i).wait_send()
                for way in range(2):
                    ok = jnp.logical_and(at.z >= zz, at.z < at.depth - 1) if way == 0 else jnp.logical_and(at.z <= zz, at.z > 0)

                    @pl.when(ok)
                    def _(zz=zz, way=way, cut=cut):
                        for i in range(at.width if cut[1] else 1):
                            b = zz * at.width + lax.rem(at.x + i, at.width)
                            self.along(cut, way, b).wait_send()


class NarrowSum:
    @staticmethod
    def scratch(n, size, d):
        side = max(n // LINE - 1, 1)
        return (
            [pltpu.VMEM((LINE, side, size, d), BF), pltpu.VMEM((LINE + 1, size, d), BF)]
            + [pltpu.SemaphoreType.DMA((LINE, side))] * 2
            + [pltpu.SemaphoreType.DMA((LINE,)), pltpu.SemaphoreType.DMA((LINE + 1,))]
        )

    def __init__(self, at, part, rows, refs):
        self.at, self.part, self.rows = at, part, rows
        self.xr, self.lr, self.xs_sem, self.xr_sem, self.ls_sem, self.lr_sem = refs

    def across(self, t, i):
        at = self.at
        xx = lax.rem(at.x + i, at.width)
        return remote(
            self.part.at[t * at.width + xx, self.rows], self.xr.at[t, i - 1],
            self.xs_sem.at[t, i - 1], self.xr_sem.at[t, i - 1], at.seq(at.z * at.width + xx),
        )

    def along(self, t):
        at = self.at
        there = jnp.where(t > at.z, at.j + at.width, at.j - at.width)
        slot = jnp.where(t == at.z - 1, at.depth, t)
        return remote(
            self.part.at[t * at.width + at.x, self.rows], self.lr.at[slot],
            self.ls_sem.at[t], self.lr_sem.at[slot], at.seq(there),
        )

    def landed(self, slot):
        remote(
            self.lr.at[slot], self.lr.at[slot], self.ls_sem.at[0], self.lr_sem.at[slot],
            self.at.seq(self.at.other(1)),
        ).wait_recv()

    def emit(self, t):
        for i in range(1, self.at.width):
            self.across(t, i).start()

    def summed(self, t):
        at = self.at
        total = self.part[t * at.width + at.x, self.rows].astype(F32)
        for i in range(1, at.width):
            self.across(t, i).wait_recv()
            total = total + self.xr[t, i - 1].astype(F32)
        return total

    def pass_on(self, t):
        at = self.at
        block = (t * at.width + at.x, self.rows)
        total = self.summed(t)
        inner = at.inner(t)

        @pl.when(inner)
        def _():
            self.landed(t)
            self.part[block] = (total + self.lr[t].astype(F32)).astype(BF)

        @pl.when(jnp.logical_not(inner))
        def _():
            self.part[block] = total.astype(BF)

        self.along(t).start()

    def close(self):
        pass

    def last(self, out):
        at = self.at
        out[self.rows] = self.summed(at.z)

        @pl.when(at.z > 0)
        def _():
            self.landed(at.z)
            out[self.rows] += self.lr[at.z].astype(F32)

        @pl.when(at.z < at.depth - 1)
        def _():
            self.landed(at.depth)
            out[self.rows] += self.lr[at.depth].astype(F32)

    def finish(self):
        at = self.at
        for t in range(at.depth):
            for i in range(1, at.width):
                self.across(t, i).wait_send()

            @pl.when(at.z != t)
            def _(t=t):
                self.along(t).wait_send()


class WideSum:
    @staticmethod
    def scratch(n, size, d):
        w = n // LINE
        side = max(w - 1, 1)
        return (
            [pltpu.VMEM((side, size, d), BF), pltpu.VMEM((LINE + 1, w, size, d), BF)]
            + [pltpu.SemaphoreType.DMA((side,))] * 2
            + [pltpu.SemaphoreType.DMA((LINE, w)), pltpu.SemaphoreType.DMA((LINE + 1, w))]
        )

    def __init__(self, at, part, rows, refs):
        self.at, self.part, self.rows = at, part, rows
        self.xr, self.lr, self.xs_sem, self.xr_sem, self.ls_sem, self.lr_sem = refs

    def across(self, i):
        at = self.at
        xx = lax.rem(at.x + i, at.width)
        return remote(
            self.part.at[at.z * at.width + xx, self.rows], self.xr.at[i - 1],
            self.xs_sem.at[i - 1], self.xr_sem.at[i - 1], at.seq(at.z * at.width + xx),
        )

    def along(self, t, xx):
        at = self.at
        there = jnp.where(t > at.z, at.j + at.width, at.j - at.width)
        slot = jnp.where(t == at.z - 1, at.depth, t)
        return remote(
            self.part.at[t * at.width + xx, self.rows], self.lr.at[slot, xx],
            self.ls_sem.at[t, xx], self.lr_sem.at[slot, xx], at.seq(there),
        )

    def landed(self, slot, xx):
        remote(
            self.lr.at[slot, xx], self.lr.at[slot, xx], self.ls_sem.at[0, xx],
            self.lr_sem.at[slot, xx], self.at.seq(self.at.other(1)),
        ).wait_recv()

    def emit(self, t):
        at = self.at

        @pl.when(jnp.logical_and(t != at.z, jnp.logical_not(at.inner(t))))
        def _():
            for xx in range(at.width):
                self.along(t, xx).start()

    def pass_on(self, t):
        at = self.at

        @pl.when(at.inner(t))
        def _():
            for xx in range(at.width):
                self.landed(t, xx)
                block = (t * at.width + xx, self.rows)
                total = self.part[block].astype(F32) + self.lr[t, xx].astype(F32)
                self.part[block] = total.astype(BF)
                self.along(t, xx).start()

    def line_sum(self, xx, put):
        at = self.at
        own = self.part[at.z * at.width + xx, self.rows].astype(F32)

        @pl.when(at.z == 0)
        def _():
            self.landed(at.depth, xx)
            put(own + self.lr[at.depth, xx].astype(F32))

        @pl.when(at.z == at.depth - 1)
        def _():
            self.landed(at.z, xx)
            put(own + self.lr[at.z, xx].astype(F32))

        @pl.when(jnp.logical_and(at.z > 0, at.z < at.depth - 1))
        def _():
            self.landed(at.depth, xx)
            self.landed(at.z, xx)
            put(own + self.lr[at.depth, xx].astype(F32) + self.lr[at.z, xx].astype(F32))

    def close(self):
        at = self.at
        for i in range(1, at.width):
            xx = lax.rem(at.x + i, at.width)

            def put(total, xx=xx):
                self.part[at.z * at.width + xx, self.rows] = total.astype(BF)

            self.line_sum(xx, put)
            self.across(i).start()

    def last(self, out):
        at = self.at

        def put(total):
            out[self.rows] = total

        self.line_sum(at.x, put)
        for i in range(1, at.width):
            self.across(i).wait_recv()
            out[self.rows] += self.xr[i - 1].astype(F32)

    def finish(self):
        at = self.at
        for i in range(1, at.width):
            self.across(i).wait_send()
        for t in range(at.depth):

            @pl.when(at.z != t)
            def _(t=t):
                for xx in range(at.width):
                    self.along(t, xx).wait_send()


class Reduce:
    @staticmethod
    def scratch(n, tok, d, cuts):
        out = []
        for share, wide in cuts:
            out += (WideSum if wide else NarrowSum).scratch(n, tok * share // 8, d)
        return out

    def __init__(self, at, part, refs, cuts):
        self.at, self.cuts = at, []
        tok = part.shape[1]
        first = 0
        for i, (share, wide) in enumerate(cuts):
            rows = pl.ds(first, tok * share // 8)
            first += tok * share // 8
            self.cuts.append((WideSum if wide else NarrowSum)(at, part, rows, refs[6 * i : 6 * i + 6]))

    def emit(self, t):
        for c in self.cuts:
            c.emit(t)

    def pass_on(self, t):
        for c in self.cuts:
            c.pass_on(t)

    def reduce(self, s):
        at = self.at
        for t in (at.z + s, at.z - s):

            @pl.when(jnp.logical_and(t >= 0, t < at.depth))
            def _(t=t):
                self.pass_on(t)

    def last(self, out):
        for c in self.cuts:
            c.close()
        for c in self.cuts[::-1]:
            c.last(out)

    def finish(self):
        for c in self.cuts:
            c.finish()


class Columns:
    @staticmethod
    def sems(n):
        return [pltpu.SemaphoreType.DMA((4, n)), pltpu.SemaphoreType.DMA((4, n))]

    def __init__(self, at, pieces, full, sems):
        self.at, self.pieces, self.full = at, pieces, full
        self.ssem, self.rsem = sems

    def first(self, i):
        at = self.at
        to = at.other(i)
        return remote(
            self.pieces.at[to], self.full.at[at.r, at.j], self.ssem.at[0, to],
            self.rsem.at[at.r, at.j], at.seq(to),
        )

    def own(self):
        at = self.at
        return pltpu.make_async_copy(
            self.pieces.at[at.j], self.full.at[at.r, at.j], self.ssem.at[0, at.j]
        )

    def pass_on(self, r, js, to, k):
        return remote(
            self.full.at[r, js], self.full.at[r, js], self.ssem.at[k, js], self.rsem.at[r, js],
            self.at.row(to),
        )

    def take(self, r, js):
        self.pass_on(r, js, self.at.r_c, 0).wait_recv()

    def start(self):
        at = self.at
        self.own().start()

        @pl.loop(1, at.n)
        def _(i):
            self.first(i).start()

    def step(self, lo, hi):
        at = self.at

        @pl.loop(lo, hi)
        def _(i):
            js = lax.rem(at.j + at.n - i, at.n)

            @pl.when(i == 0)
            def _():
                self.own().wait()

            @pl.when(i > 0)
            def _():
                self.take(at.r, js)

            self.pass_on(at.r, js, at.r_y, 1).start()
            self.pass_on(at.r, js, at.r_c, 2).start()

    def relay(self, lo, hi):
        at = self.at

        @pl.loop(lo, hi)
        def _(i):
            js = lax.rem(at.j + at.n - i, at.n)
            self.take(at.r_y, js)
            self.pass_on(at.r_y, js, at.r_c, 3).start()

    def finish(self):
        at = self.at

        @pl.loop(0, at.n)
        def _(js):
            self.take(at.r_c, js)
            self.take(at.r_yc, js)
            self.pass_on(at.r, js, at.r_y, 1).wait_send()
            self.pass_on(at.r, js, at.r_c, 2).wait_send()
            self.pass_on(at.r_y, js, at.r_c, 3).wait_send()

        @pl.loop(1, at.n)
        def _(i):
            self.first(i).wait_send()


class Rows:
    @staticmethod
    def sems():
        return [pltpu.SemaphoreType.DMA((4,)), pltpu.SemaphoreType.DMA((4,))]

    def __init__(self, at, shard, full, sems):
        self.at, self.shard, self.full = at, shard, full
        self.ssem, self.rsem = sems

    def own(self):
        return pltpu.make_async_copy(self.shard, self.full.at[self.at.r], self.ssem.at[0])

    def direct(self, to, k):
        r = self.at.r
        return remote(
            self.shard, self.full.at[r], self.ssem.at[k], self.rsem.at[r], self.at.row(to)
        )

    def onward(self):
        at = self.at
        r = at.r_y
        return remote(
            self.full.at[r], self.full.at[r], self.ssem.at[3], self.rsem.at[r], at.row(at.r_c)
        )

    def take(self, r):
        at = self.at
        remote(
            self.full.at[r], self.full.at[r], self.ssem.at[0], self.rsem.at[r], at.row(at.r_c)
        ).wait_recv()

    def start(self):
        at = self.at
        self.own().start()
        self.direct(at.r_y, 1).start()
        self.direct(at.r_c, 2).start()

    def relay(self):
        self.take(self.at.r_y)
        self.onward().start()

    def finish(self):
        at = self.at
        self.own().wait()
        self.take(at.r_c)
        self.take(at.r_yc)
        self.direct(at.r_y, 1).wait_send()
        self.direct(at.r_c, 2).wait_send()
        self.onward().wait_send()


class RowSum:
    @staticmethod
    def scratch(m, c):
        return [
            pltpu.VMEM((2, m, c), BF),
            pltpu.VMEM((m, c), BF),
            pltpu.SemaphoreType.DMA((3,)),
            pltpu.SemaphoreType.DMA((3,)),
        ]

    def __init__(self, at, grad, refs):
        self.at, self.grad = at, grad
        self.core_in, self.y_in, self.ssem, self.rsem = refs

    def to_core(self, far):
        at = self.at
        yy = 1 - at.y if far else at.y
        k = 1 if far else 0
        return remote(
            self.grad.at[yy * 2 + 1 - at.c], self.core_in.at[k], self.ssem.at[k], self.rsem.at[k],
            at.row(at.r_c),
        )

    def over_y(self):
        at = self.at
        return remote(
            self.grad.at[at.r_y], self.y_in, self.ssem.at[2], self.rsem.at[2], at.row(at.r_y)
        )

    def start(self):
        self.to_core(1).start()
        self.to_core(0).start()

    def cross(self):
        at = self.at
        self.to_core(1).wait_recv()
        self.grad[at.r_y] = (
            self.grad[at.r_y].astype(F32) + self.core_in[1].astype(F32)
        ).astype(BF)
        self.over_y().start()

    def total(self):
        at = self.at
        self.to_core(0).wait_recv()
        self.over_y().wait_recv()
        return (
            self.grad[at.r].astype(F32) + self.core_in[0].astype(F32) + self.y_in[...].astype(F32)
        )

    def finish(self):
        self.to_core(1).wait_send()
        self.to_core(0).wait_send()
        self.over_y().wait_send()


class Exchange:
    @staticmethod
    def sems(n):
        return [pltpu.SemaphoreType.DMA((n,)), pltpu.SemaphoreType.DMA((n,))]

    def __init__(self, at, mine, got, sems):
        self.at, self.mine, self.got = at, mine, got
        self.ssem, self.rsem = sems

    def send(self, i):
        at = self.at
        to = at.other(i)
        return remote(
            self.mine.at[to], self.got.at[at.j], self.ssem.at[to], self.rsem.at[at.j], at.seq(to)
        )

    def own(self):
        at = self.at
        return pltpu.make_async_copy(
            self.mine.at[at.j], self.got.at[at.j], self.ssem.at[at.j]
        )

    def start(self):
        self.own().start()

        @pl.loop(1, self.at.n)
        def _(i):
            self.send(i).start()

    def finish(self):
        at = self.at
        self.own().wait()

        @pl.loop(1, at.n)
        def _(i):
            src = at.other(i)
            remote(
                self.mine.at[src], self.got.at[src], self.ssem.at[src], self.rsem.at[src],
                at.seq(src),
            ).wait()


class SmallGather:
    @staticmethod
    def sems(n):
        return [pltpu.SemaphoreType.DMA((4,))] * 2 + [pltpu.SemaphoreType.DMA((n,))] * 2

    def __init__(self, at, mine, full, sems):
        self.at, self.mine, self.full = at, mine, full
        self.rs, self.rr, self.ss, self.sr = sems

    def beside(self, r):
        at = self.at
        return remote(
            self.mine, self.full.at[at.j, at.r], self.rs.at[r], self.rr.at[at.r], at.row(r)
        )

    def own(self):
        at = self.at
        return pltpu.make_async_copy(self.mine, self.full.at[at.j, at.r], self.rs.at[at.r])

    def onward(self, to):
        at = self.at
        return remote(
            self.full.at[at.j], self.full.at[at.j], self.ss.at[to], self.sr.at[at.j], at.seq(to)
        )

    def start(self):
        at = self.at
        self.own().start()
        for r in (at.r_y, at.r_c, at.r_yc):
            self.beside(r).start()

    def step(self):
        at = self.at
        self.own().wait()
        for r in (at.r_y, at.r_c, at.r_yc):
            remote(
                self.mine, self.full.at[at.j, r], self.rs.at[r], self.rr.at[r], at.row(r)
            ).wait()

        @pl.loop(1, at.n)
        def _(i):
            self.onward(at.other(i)).start()

    def finish(self):
        at = self.at

        @pl.loop(1, at.n)
        def _(i):
            src = at.other(i)
            remote(
                self.full.at[src], self.full.at[src], self.ss.at[src], self.sr.at[src],
                at.seq(src),
            ).wait()


class SmallSum:
    @staticmethod
    def scratch(n, w):
        q = w // 4
        return (
            [pltpu.VMEM((8, w), F32), pltpu.VMEM((4, 8, q), F32), pltpu.VMEM((8, q), F32)]
            + [pltpu.VMEM((n, 8, q), F32)]
            + [pltpu.SemaphoreType.DMA((4,))] * 2
            + [pltpu.SemaphoreType.DMA((n,))] * 2
        )

    def __init__(self, at, refs):
        self.at = at
        self.terms, self.beside_in, self.acc, self.seq_in = refs[:4]
        self.rs, self.rr, self.ss, self.sr = refs[4:]
        self.q = self.terms.shape[1] // 4

    def part(self, r):
        return self.terms.at[:, pl.ds(pl.multiple_of(r * self.q, self.q), self.q)]

    def beside(self, r):
        at = self.at
        return remote(
            self.part(r), self.beside_in.at[at.r], self.rs.at[r], self.rr.at[at.r], at.row(r)
        )

    def run(self, out):
        at = self.at
        near = (at.r_y, at.r_c, at.r_yc)
        for r in near:
            self.beside(r).start()
        self.acc[...] = self.part(at.r)[...]
        for r in near:
            remote(
                self.part(r), self.beside_in.at[r], self.rs.at[r], self.rr.at[r], at.row(r)
            ).wait()
            self.acc[...] += self.beside_in[r]

        @pl.loop(1, at.n)
        def _(i):
            to = at.other(i)
            remote(
                self.acc, self.seq_in.at[at.j], self.ss.at[to], self.sr.at[at.j], at.seq(to)
            ).start()

        out[...] = self.acc[...]

        @pl.loop(1, at.n)
        def _(i):
            src = at.other(i)
            remote(
                self.acc, self.seq_in.at[src], self.ss.at[src], self.sr.at[src], at.seq(src)
            ).wait()
            out[...] += self.seq_in[src]


class Call:
    def __init__(self, n, cid, name):
        self.n, self.cid, self.name = n, cid, name
        self.args, self.ins, self.outs, self.out_specs, self.scr = [], [], [], [], []

    def give(self, array, space=pltpu.VMEM):
        if isinstance(array, Made):
            return array.key
        for i, known in enumerate(self.args):
            if known is array:
                return ("i", i)
        self.args.append(array)
        self.ins.append(pl.BlockSpec(memory_space=space))
        return ("i", len(self.args) - 1)

    def make(self, shape, dtype, space=pltpu.VMEM):
        self.outs.append(jax.ShapeDtypeStruct(shape, dtype))
        self.out_specs.append(pl.BlockSpec(memory_space=space))
        return ("o", len(self.outs) - 1)

    def scratch(self, items):
        at = len(self.scr)
        self.scr.extend(items)
        return [("s", at + i) for i in range(len(items))]

    def run(self, body, flops=0):
        ni, no = len(self.ins), len(self.outs)

        def kernel(*refs):
            def of(key):
                if isinstance(key, list):
                    return [of(k) for k in key]
                if isinstance(key[0], tuple):
                    return tuple(of(k) for k in key)
                kind, i = key
                return refs[i + {"i": 0, "o": ni, "s": ni + no}[kind]]

            at = Place(self.n)
            at.meet()
            body(at, of)

        return pl.pallas_call(
            kernel,
            out_shape=self.outs,
            in_specs=self.ins,
            out_specs=self.out_specs,
            scratch_shapes=self.scr,
            name=self.name,
            cost_estimate=pl.CostEstimate(
                flops=flops, bytes_accessed=1 << 24, transcendentals=0
            ),
            compiler_params=pltpu.CompilerParams(
                collective_id=self.cid, has_side_effects=True, vmem_limit_bytes=VMEM_LIMIT
            ),
        )(*self.args)


VMEM_LIMIT = 60 << 20
ANY = pltpu.VMEM
CHUNK = 512


def product(at, of, part, pairs, t):
    width, tok = at.width, part.shape[1]

    @pl.loop(0, part.shape[2] // CHUNK)
    def _(i):
        cols = pl.ds(pl.multiple_of(i * CHUNK, CHUNK), CHUNK)
        total = None
        for lhs, rhs, flip in pairs:
            left = of(lhs)[pl.ds(t * (width * tok), width * tok), :]
            if flip:
                term = dot(left, of(rhs)[cols, :], 1, 1)
            else:
                term = dot(left, of(rhs)[:, cols], 1, 0)
            total = term if total is None else total + term
        part[pl.ds(t * width, width), :, cols] = total.reshape(width, tok, CHUNK).astype(BF)


def products(at, of, part, pairs, red):
    for s in range(at.depth - 1, -1, -1):
        for t in [at.z + s, at.z - s] if s else [at.z]:

            @pl.when(jnp.logical_and(t >= 0, t < at.depth))
            def _(t=t):
                product(at, of, part, pairs, t)
                red.emit(t)


def steps(plan, red, extra):
    work = extra.fill()
    for word in plan:
        what, k = word[0], int(word[1])
        if what == "r":
            red.reduce(k)
        elif what == "g":
            extra.gather_step(k)
        elif what == "c":
            extra.column_step(k)
        elif what == "y":
            extra.column_relay(k)
        elif what == "w" and k < len(work):
            work[k]()
        elif what == "x":
            extra.cross(k)
        elif what == "t":
            extra.turn(k)


def gather_all(g, between=None):
    at = g.at
    for s in range(1, at.depth):
        g.step(s)
        if between is not None:
            between(s)
    for s in range(at.depth):
        for zz in [at.z - s, at.z + s] if s else [at.z]:

            @pl.when(jnp.logical_and(zz >= 0, zz < at.depth))
            def _(zz=zz):
                g.take_side(zz)


def split_columns(src, dst, runs):
    for b, to, at, size in runs:
        dst[b, :, to : to + size] = src[:, at : at + size]


def join_columns(src, dst, runs):
    for b, to, at, size in runs:
        dst[:, at : at + size] = src[b, :, to : to + size].astype(dst.dtype)


def front_call(n, x, small, ints, weight, runs, out_w):
    tok, d = x.shape
    k, c = weight.shape[0], weight.shape[1] // n
    call = Call(n, 1, "front")
    ix = call.give(x, ANY)
    ism, iin = call.give(small), call.give(ints)
    iw = call.give(weight, ANY)
    ox = call.make((n, tok, d), BF, ANY)
    osm = call.make((n, 4) + small.shape, BF)
    oin = call.make((n,) + ints.shape, jnp.int32)
    ow = call.make((4, n, k, c), BF, ANY)
    sx = call.scratch(Gather.sems(n, ALONE))
    sp = call.scratch([pltpu.VMEM((n, k, c), BF)])
    ssm = call.scratch(SmallGather.sems(n))
    sin = call.scratch(Exchange.sems(n))
    sw = call.scratch(Columns.sems(n))
    if out_w is not None:
        io = call.give(out_w, ANY)
        oo = call.make((4,) + out_w.shape, BF, ANY)
        so = call.scratch(Rows.sems())

    def body(at, of):
        sm = SmallGather(at, of(ism), of(osm), of(ssm))
        g = Gather(at, of(ox), of(sx), ALONE)
        cols = Columns(at, of(sp)[0], of(ow), of(sw))
        spread = Spread(at, of(iin), of(oin), of(sin))
        sm.start()
        of(ox)[at.j] = of(ix)[...]
        g.start()
        spread.start()
        split_columns(of(iw), of(sp)[0], runs)
        cols.start()
        sm.step()
        if out_w is not None:
            rows = Rows(at, of(io), of(oo), of(so))
            rows.start()
        cuts = [0, n // 4, n // 2, n]

        def between(s):
            cols.step(cuts[s - 1], cuts[s])

        gather_all(g, between)
        cols.relay(0, n)
        if out_w is not None:
            rows.relay()
            rows.finish()
        cols.finish()
        g.finish()
        sm.finish()
        spread.finish()

    return call.run(body)


def turned(line):
    return jnp.transpose(jnp.broadcast_to(line, (128, 128)))


def rotation(ints_all, frequency, block, direction):
    lane = lax.rem(lax.broadcasted_iota(jnp.int32, (128, 128), 1), HD)
    angle = turned(ints_all[block, 1:2].astype(F32)) * frequency[0:1]
    cosine, sine = jnp.cos(angle), direction * jnp.sin(angle)
    return cosine, jnp.where(lane < ROT // 2, -sine, 0.0), jnp.where(lane < ROT // 2, 0.0, sine)


def turn_pairs(u, table):
    cosine, above, below = table
    return (
        u * cosine
        + pltpu.roll(u, 128 - ROT // 2, 1) * above
        + pltpu.roll(u, ROT // 2, 1) * below
    )


def fill_mask(at, mask, ints_all, t):
    tok = 128
    index = lax.broadcasted_iota(jnp.int32, (tok, tok), 0)
    other = lax.broadcasted_iota(jnp.int32, (tok, tok), 1)
    for b in range(at.width):
        mine = turned(ints_all[t * at.width + b, 0:1].astype(F32))
        for o in range((t + 1) * at.width):
            ok = mine == ints_all[o, 0:1].astype(F32)
            if o == t * at.width + b:
                ok = jnp.logical_and(ok, other <= index)
            fill = jnp.where(ok, 0.0, -jnp.inf)
            if o > t * at.width + b:
                fill = jnp.full((tok, tok), -jnp.inf, F32)
            mask[b * tok : (b + 1) * tok, o * tok : (o + 1) * tok] = fill


class Made:
    def __init__(self, key, shape):
        self.key, self.shape = key, shape


def attend_call(n, x, small, ints, frequency, qkv_w, head_runs, out_w):
    tok, d = x.shape
    k, c = qkv_w.shape[0], qkv_w.shape[1] // n
    hp, length, wide = H // n, n * tok, n // LINE * tok
    call = Call(n, 10, "attend")
    i_x, i_small, i_ints, i_freq = (call.give(v) for v in (x, small, ints, frequency))
    i_w, i_out = call.give(qkv_w), call.give(out_w)
    o_in = call.make((n, tok, d), BF)
    o_gains = call.make((8, d), F32)
    o_ints = call.make((n,) + ints.shape, jnp.int32)
    o_w = call.make((4, n, k, c), BF)
    o_out = call.make((4,) + out_w.shape, BF)
    o_qkv = [call.make((hp, length, HD), BF) for _ in range(3)]
    o_low = call.make((length, hp * HD), BF)
    o_ctx = call.make((length, hp * HD), F32)
    o_den = call.make((length, 128), F32)
    s_x = call.scratch([pltpu.VMEM((n, tok, d), BF)])
    s_gat = call.scratch(Gather.sems(n, ALONE))
    s_pieces = call.scratch([pltpu.VMEM((n, k, c), BF)])
    s_small = call.scratch([pltpu.VMEM((n, 4) + small.shape, F32)])
    s_shift = call.scratch([pltpu.VMEM((8, c), F32)])
    s_mask = call.scratch([pltpu.VMEM((wide, length), F32)])
    s_sg = call.scratch(SmallGather.sems(n))
    s_spread = call.scratch(Exchange.sems(n))
    s_cols = call.scratch(Columns.sems(n))
    s_rows = call.scratch(Rows.sems())

    def body(at, of):
        sm_all, xs, inputs, gains = of(s_small)[0], of(s_x)[0], of(o_in), of(o_gains)
        shift, mask, w = of(s_shift)[0], of(s_mask)[0], of(o_w)
        ints_all = of(o_ints)
        q_ref, k_ref, v_ref = of(o_qkv)
        sm = SmallGather(at, of(i_small), sm_all, of(s_sg))
        gat = Gather(at, xs, of(s_gat), ALONE)
        cols = Columns(at, of(s_pieces)[0], w, of(s_cols))
        spread = Spread(at, of(i_ints), ints_all, of(s_spread))
        out_rows = Rows(at, of(i_out), of(o_out), of(s_rows))
        sm.start()
        xs[at.j] = of(i_x)[...]
        gat.start()
        spread.start()
        split_columns(of(i_w), of(s_pieces)[0], head_runs)
        cols.start()
        sm.step()
        out_rows.start()
        gat.open_wide()
        sm.finish()
        for r in range(4):
            for b in range(n):
                lanes = slice((r * n + b) * k, (r * n + b + 1) * k)
                for i in range(4):
                    gains[i : i + 1, lanes] = sm_all[b, r, i // 2 : i // 2 + 1, i % 2 * k : (i % 2 + 1) * k]
        for m in range(3):
            for r in range(4):
                block = (m * 4 + r) * n + at.j
                owner = block // 3
                line = 2 + lax.rem(block, 3)
                shift[0:1, (m * 4 + r) * HD : (m * 4 + r + 1) * HD] = sm_all[
                    lax.rem(owner, n), owner // n, pl.ds(line, 1), 0:HD
                ]
        spread.finish()

        def norm(t):
            here = pl.ds(t * at.width, at.width)
            normed, _ = norm_stats(xs[here].reshape(wide, d).astype(F32))
            low = (normed * gains[0:1] + gains[1:2]).astype(BF)
            inputs[here] = low.reshape(at.width, tok, d)

        def project(t):
            for b in range(at.width):
                block = t * at.width + b
                these = pl.ds(block * tok, tok)
                table = rotation(ints_all, of(i_freq), block, 1.0)
                projected = dot(inputs[block], w[...].reshape(d, c), 1, 0) + shift[0:1]
                for i in range(4 * hp * HD // 256):
                    u = projected[:, i * 128 : (i + 1) * 128]
                    u = turn_pairs(u, table)
                    for e in range(2):
                        head = i * 2 + e
                        val = u[:, e * HD : (e + 1) * HD]
                        if head < hp:
                            q_ref[head, these] = (val * (1.0 / math.sqrt(HD))).astype(BF)
                        else:
                            k_ref[head - hp, these] = val.astype(BF)
                for head in range(hp):
                    first = (2 * hp + head) * HD
                    v_ref[head, these] = projected[:, first : first + HD].astype(BF)

        order = by_place(at.z, (3210, 3201, 132, 123))
        edge = jnp.logical_or(at.z == 0, at.z == at.depth - 1)

        @pl.loop(0, LINE)
        def _(i):
            t = digit(order, i)
            lo = jnp.where(edge, i + 1, jnp.where(i == 0, 1, jnp.where(i == 1, 3, 4)))
            hi = jnp.where(edge, jnp.minimum(i + 2, 4), jnp.where(i == 0, 3, 4))

            @pl.loop(lo, hi)
            def _(m):
                gat.fetch(digit(order, m))

            cols.step(jnp.where(i < 3, i * (n // 4), n), jnp.where(i < 2, (i + 1) * (n // 4), n))

            @pl.when(i == 3)
            def _():
                cols.relay(0, n)
                cols.finish()

                @pl.loop(0, 3)
                def _(m):
                    project(digit(order, m))

            gat.take_side(t)
            norm(t)

        out_rows.relay()
        project(digit(order, 3))
        for t in range(LINE):
            reach = (t + 1) * wide
            fill_mask(at, mask, ints_all, t)
            these = slice(t * wide, (t + 1) * wide)
            for head in range(hp):
                lanes = slice(head * HD, (head + 1) * HD)
                scores = dot(q_ref[head, these], k_ref[head, 0:reach], 1, 1)
                weights = jnp.exp(scores + mask[:, 0:reach])
                den = jnp.sum(weights, axis=1, keepdims=True)
                numer = dot(weights.astype(BF), v_ref[head, 0:reach], 1, 0)
                ctx = numer / den
                of(o_ctx)[these, lanes] = ctx
                of(o_low)[these, lanes] = ctx.astype(BF)
                of(o_den)[these, head : head + 1] = den
        out_rows.finish()
        gat.finish()

    return call.run(body)


class Spread:
    def __init__(self, at, mine, got, sems):
        self.at, self.mine, self.got = at, mine, got
        self.ssem, self.rsem = sems

    def copy(self, to, src):
        at = self.at
        return remote(
            self.mine, self.got.at[src], self.ssem.at[to], self.rsem.at[src], at.seq(to)
        )

    def own(self):
        return pltpu.make_async_copy(self.mine, self.got.at[self.at.j], self.ssem.at[self.at.j])

    def start(self):
        self.own().start()

        @pl.loop(1, self.at.n)
        def _(i):
            self.copy(self.at.other(i), self.at.j).start()

    def finish(self):
        self.own().wait()

        @pl.loop(1, self.at.n)
        def _(i):
            p = self.at.other(i)
            self.copy(p, p).wait()


def sum_call(n, cid, name, pairs, tok, columns=(), rows=(), gathers=(), row_sums=(), col_sums=()):
    call = Call(n, cid, name)
    d = pairs[0][1].shape[0 if pairs[0][2] else 1]
    keys = []
    for lhs, rhs, flip in pairs:
        keys.append((call.give(lhs), call.give(rhs), flip))
    out = call.make((tok, d), F32)
    part = call.scratch([pltpu.VMEM((n, tok, d), BF)])
    red_s = call.scratch(Reduce.scratch(n, tok, d, SUM_CUTS))
    extra = Extras(call, n, columns, rows, gathers, row_sums, col_sums, PAIRED)

    def body(at, of):
        part_ref = of(part)[0]
        red = Reduce(at, part_ref, of(red_s), SUM_CUTS)
        extra.bind(at, of)
        extra.start()
        products(at, of, part_ref, keys, red)
        steps(SUM_PLAN, red, extra)
        red.last(of(out))
        extra.finish()
        red.finish()

    flops = sum(2 * l.shape[0] * l.shape[1] * d for l, _, _ in pairs)
    return call.run(body, flops)


class Extras:
    def __init__(
        self, call, n, columns=(), rows=(), gathers=(), row_sums=(), col_sums=(), cuts=None
    ):
        self.n, self.cuts = n, cuts
        self.columns, self.rows, self.gathers, self.row_sums, self.col_sums = [], [], [], [], []
        for w, runs in columns:
            shape = (n, w.shape[0], w.shape[1] // n)
            self.columns.append(
                (
                    call.give(w),
                    call.make((4,) + shape, BF, ANY),
                    call.scratch([pltpu.VMEM(shape, BF)]),
                    call.scratch(Columns.sems(n)),
                    runs,
                )
            )
        for p in rows:
            self.rows.append(
                (call.give(p, ANY), call.make((4,) + p.shape, BF, ANY), call.scratch(Rows.sems()))
            )
        for p in gathers:
            self.gathers.append(
                (
                    call.give(p, ANY),
                    call.make((n,) + p.shape, BF, ANY),
                    call.scratch(Gather.sems(n, cuts)),
                )
            )
        self.n_row = n_row = 4
        for p in row_sums:
            lhs, rhs = p if isinstance(p, tuple) else (None, None)
            shape = (n_row, lhs.shape[1] // n_row, rhs.shape[1]) if lhs is not None else p.shape
            self.row_sums.append(
                (
                    (call.give(lhs), call.give(rhs)) if lhs is not None else call.give(p),
                    call.scratch([pltpu.VMEM(shape, BF)])[0],
                    call.make(shape[1:], F32),
                    call.scratch(RowSum.scratch(*shape[1:])),
                )
            )
        for p, runs in col_sums:
            lhs, rhs = p if isinstance(p, tuple) else (None, None)
            shape = (n_row, lhs.shape[1] // n_row, rhs.shape[1]) if lhs is not None else p.shape
            k, c = shape[1] // n, shape[2]
            self.col_sums.append(
                (
                    (call.give(lhs), call.give(rhs)) if lhs is not None else call.give(p),
                    call.scratch([pltpu.VMEM(shape, BF)])[0],
                    call.make((k, n * c), F32),
                    call.scratch(RowSum.scratch(*shape[1:])),
                    call.scratch([pltpu.VMEM((n, k, c), BF)] * 2),
                    call.scratch(Exchange.sems(n)),
                    runs,
                )
            )

    def bind(self, at, of):
        self.at, self.of = at, of
        self.b_columns = [
            (Columns(at, of(p)[0], of(o), of(s)), of(i), of(p)[0], runs)
            for i, o, p, s, runs in self.columns
        ]
        self.b_rows = [Rows(at, of(i), of(o), of(s)) for i, o, s in self.rows]
        self.b_gathers = [
            (Gather(at, of(o), of(s), self.cuts), of(i), of(o)) for i, o, s in self.gathers
        ]
        self.b_sums = [
            (RowSum(at, of(g), of(s)), of(o), of(i), of(g)) for i, g, o, s in self.row_sums
        ]
        self.b_cols = []
        for i, g, o, s, v, e, runs in self.col_sums:
            mine, got = of(v)
            self.b_cols.append(
                (
                    RowSum(at, of(g), of(s)),
                    mine,
                    Exchange(at, mine, got, of(e)),
                    (got, of(o), runs),
                    of(i),
                    of(g),
                )
            )

    def start(self):
        at = self.at
        for g, src, buf in self.b_gathers:
            buf[at.j] = src[...]
            g.start()
        for r in self.b_rows:
            r.start()
        for c, src, pieces, runs in self.b_columns:
            split_columns(src, pieces, runs)
            c.start()

    def fill_columns(self, k):
        rs, _, _, _, src, grad = self.b_cols[k]
        if isinstance(src, tuple):
            size = grad.shape[1]

            @pl.loop(0, grad.shape[0])
            def _(b):
                cols = pl.ds(pl.multiple_of(b * size, size), size)
                grad[b] = dot(src[0][:, cols], src[1][...], 0, 0).astype(BF)
        else:
            grad[...] = src[...]
        rs.start()

    def fill_rows(self, k):
        rs, _, src, grad = self.b_sums[k]
        if isinstance(src, tuple):

            @pl.loop(0, grad.shape[2] // CHUNK)
            def _(b):
                cols = pl.ds(pl.multiple_of(b * CHUNK, CHUNK), CHUNK)
                term = dot(src[0][...], src[1][:, cols], 0, 0)
                grad[:, :, cols] = term.reshape(grad.shape[0], grad.shape[1], CHUNK).astype(BF)
        else:
            grad[...] = src[...]
        rs.start()

    def fill(self):
        work = [functools.partial(self.fill_columns, k) for k in range(len(self.b_cols))]
        return work + [functools.partial(self.fill_rows, k) for k in range(len(self.b_sums))]

    def cross(self, k):
        every = [c[0] for c in self.b_cols] + [r[0] for r in self.b_sums]
        if k < len(every):
            every[k].cross()

    def turn(self, k):
        if k < len(self.b_cols):
            rs, mine, ex = self.b_cols[k][:3]
            mine[...] = rs.total().reshape(mine.shape).astype(BF)
            ex.start()

    def gather_step(self, s):
        for g, _, _ in self.b_gathers:
            g.step(s)

    def column_step(self, k):
        q = self.n // 4
        for c, *_ in self.b_columns:
            c.step(k * q, (k + 1) * q)

    def column_relay(self, k):
        q = self.n // 4
        for c, *_ in self.b_columns:
            c.relay(k * q, (k + 1) * q)

    def finish(self):
        at = self.at
        for g, _, _ in self.b_gathers:
            for zz in range(at.depth):
                g.take_side(zz)
            g.finish()
        for r in self.b_rows:
            r.relay()
        for r in self.b_rows:
            r.finish()
        for c, *_ in self.b_columns:
            c.finish()
        for rs, out, *_ in self.b_sums:
            out[...] = rs.total()
            rs.finish()
        for rs, _, ex, (got, out, runs), *_ in self.b_cols:
            ex.finish()
            rs.finish()
            join_columns(got, out, runs)


def gather_call(n, cid, name, x, columns=(), rows=(), row_sums=(), col_sums=()):
    call = Call(n, cid, name)
    extra = Extras(call, n, columns, rows, [x], row_sums, col_sums, ALONE)

    def body(at, of):
        extra.bind(at, of)
        extra.start()
        steps(GATHER_PLAN, None, extra)
        extra.finish()

    return call.run(body)


def digit(code, i):
    return lax.rem(code // jnp.where(i == 0, 1, jnp.where(i == 1, 10, jnp.where(i == 2, 100, 1000))), 10)


def by_place(z, codes):
    return jnp.where(z == 0, codes[0], jnp.where(z == 1, codes[1], jnp.where(z == 2, codes[2], codes[3])))


def core_call(n, pair, x, gain, bias, columns, rows, gathers):
    call = Call(n, 2, "core")
    tok, d = x.shape
    c = columns[0][0].shape[1] // n
    wide = n // LINE * tok
    length = n * tok
    key = (call.give(pair[0]), call.give(pair[1]), False)
    i_x, i_gain, i_bias = call.give(x), call.give(gain), call.give(bias)
    o_hid = call.make((tok, d), F32)
    out = call.make((tok, d), F32)
    o_mid = call.make((n, tok, d), BF)
    o_acts = [call.make((length, c), BF) for _ in range(3)]
    part = call.scratch([pltpu.VMEM((n, tok, d), BF)] * 2)
    first_s = call.scratch(Reduce.scratch(n, tok, d, CORE_SUMS))
    extra = Extras(call, n, columns, rows, gathers, cuts=PAIRED)
    gat_s = call.scratch(Gather.sems(n, MLP_CUTS))
    red_s = call.scratch(Reduce.scratch(n, tok, d, MLP_SUMS))

    def body(at, of):
        first_part, part_ref = of(part)
        first = Reduce(at, first_part, of(first_s), CORE_SUMS)
        mid, hid = of(o_mid), of(o_hid)
        inner_ref, gg_ref, gu_ref = of(o_acts)
        gat = Gather(at, mid, of(gat_s), MLP_CUTS)
        red = Reduce(at, part_ref, of(red_s), MLP_SUMS)
        extra.bind(at, of)
        extra.start()
        products(at, of, first_part, [key], first)
        steps(CORE_PLAN, first, extra)
        first.last(hid)
        hid[...] += of(i_x)[...].astype(F32)
        normed, _ = norm_stats(hid[...])
        mid[at.j] = (normed * of(i_gain)[...] + of(i_bias)[...]).astype(BF)
        gat.start()
        extra.finish()
        gat.open_wide()
        gate, up = (c[0].full for c in extra.b_columns)
        down, grad = extra.b_rows[0].full, extra.b_gathers[0][2]
        gate, up = gate.reshape(d, c), up.reshape(d, c)
        down = down.reshape(c, d)
        order = by_place(at.z, (3210, 3201, 132, 123))
        edge = jnp.logical_or(at.z == 0, at.z == at.depth - 1)

        @pl.loop(0, LINE)
        def _(i):
            t = digit(order, i)
            lo = jnp.where(edge, i + 1, jnp.where(i == 0, 1, jnp.where(i == 1, 3, 4)))
            hi = jnp.where(edge, jnp.minimum(i + 2, 4), jnp.where(i == 0, 3, 4))

            @pl.loop(lo, hi)
            def _(m):
                gat.fetch(digit(order, m))

            gat.take_side(t)
            here = pl.ds(t * at.width, at.width)
            these = pl.ds(t * wide, wide)
            tokens = mid[here].reshape(wide, d)
            gate_pre = dot(tokens, gate[...], 1, 0)
            sig = 1.0 / (1.0 + jnp.exp(-gate_pre))
            silu = gate_pre * sig
            up_pre = dot(tokens, up[...], 1, 0)
            inner_ref[these] = (silu * up_pre).astype(BF)
            g_inner = dot(grad[here].reshape(wide, d), down[...], 1, 1)
            gu_ref[these] = (g_inner * silu).astype(BF)
            gg_ref[these] = (g_inner * up_pre * sig * (1.0 + gate_pre * (1.0 - sig))).astype(BF)
            product(at, lambda k: k, part_ref, [(gg_ref, gate, True), (gu_ref, up, True)], t)
            red.emit(t)

            @pl.when(jnp.logical_and(edge, i >= 2))
            def _():
                red.pass_on(digit(order, i - 1))

        rest = by_place(at.z, (3, 32, 301, 0))

        @pl.loop(0, jnp.where(edge, 1, 3))
        def _(i):
            red.pass_on(digit(rest, i))

        red.last(of(out))
        gat.finish()
        first.finish()
        red.finish()

    return call.run(body)


def back_call(
    n, g_attn, out_w, qkv_w, heads, ctx, low, den, ints, frequency, inputs, normed, known, runs, mlp
):
    call = Call(n, 11, "back")
    length, d = g_attn.shape
    hp, tok, wide = H // n, length // n, length // LINE
    c = 3 * hp * HD
    i_g, i_out, i_w = call.give(g_attn), call.give(out_w), call.give(qkv_w)
    i_heads = [call.give(v) for v in heads]
    i_ctx, i_den, i_ints, i_freq = (call.give(v) for v in (ctx, den, ints, frequency))
    i_norm, i_known = call.give(normed), call.give(known)
    out = call.make((tok, d), F32)
    o_small = call.make((8, d // 4), F32)
    o_mlp = call.make((tok, d), F32)
    mlp_keys = (call.give(mlp[0]), call.give(mlp[1]), False)
    mlp_s = call.scratch(Reduce.scratch(n, tok, d, SUM_CUTS))
    s_proj = call.scratch([pltpu.VMEM((length, c), BF)])[0]
    s_sum = call.scratch([pltpu.VMEM((length, c), F32)])
    s_mask = call.scratch([pltpu.VMEM((wide, length), F32)])
    part = call.scratch([pltpu.VMEM((n, tok, d), BF)])
    red_s = call.scratch(Reduce.scratch(n, tok, d, SUM_CUTS))
    s_small = call.scratch(SmallSum.scratch(n, d))
    made = Made(s_proj, (length, c))
    extra = Extras(call, n, row_sums=[(low, g_attn)], col_sums=[((inputs, made), runs)])

    def body(at, of):
        part_ref = of(part)[0]
        red = Reduce(at, part_ref, of(red_s), SUM_CUTS)
        small = SmallSum(at, of(s_small))
        proj, sums, mask = of(s_proj), of(s_sum)[0], of(s_mask)[0]
        q_ref, k_ref, v_ref = of(i_heads)
        ints_all = of(i_ints)
        extra.bind(at, of)
        extra.start()
        branch = Reduce(at, part_ref, of(mlp_s), SUM_CUTS)
        products(at, of, part_ref, [mlp_keys], branch)
        width = hp * HD
        sums[:, width:] = jnp.zeros((length, 2 * width), F32)
        for t in range(LINE):
            these, reach = slice(t * wide, (t + 1) * wide), (t + 1) * wide
            fill_mask(at, mask, ints_all, t)
            g_ctx = dot(of(i_g)[these], of(i_out)[...], 1, 1)
            for head in range(hp):
                lanes = slice(head * HD, (head + 1) * HD)
                g_own = g_ctx[:, lanes]
                below = of(i_den)[these, head : head + 1]
                g_num = (g_own / below).astype(BF)
                g_den = -jnp.sum(g_own * of(i_ctx)[these, lanes], axis=1, keepdims=True) / below
                query = q_ref[head, these]
                scores = dot(query, k_ref[head, 0:reach], 1, 1)
                weights = jnp.exp(scores + mask[:, 0:reach])
                g_weights = dot(g_num, v_ref[head, 0:reach], 1, 1)
                g_scores = (weights * (g_weights + g_den)).astype(BF)
                sums[these, lanes] = dot(g_scores, k_ref[head, 0:reach], 1, 0)
                lanes = slice(width + head * HD, width + (head + 1) * HD)
                sums[0:reach, lanes] += dot(g_scores, query, 0, 0)
                lanes = slice(2 * width + head * HD, 2 * width + (head + 1) * HD)
                sums[0:reach, lanes] += dot(weights.astype(BF), g_num, 0, 0)
            if t < LINE - 1:
                branch.reduce(LINE - 1 - t)

        @pl.loop(0, n)
        def _(b):
            these = pl.ds(b * tok, tok)
            table = rotation(ints_all, of(i_freq), b, -1.0)
            for i in range(2 * width // 128):
                lanes = slice(i * 128, (i + 1) * 128)
                u = turn_pairs(sums[these, lanes], table)
                if i < width // 128:
                    u = u * (1.0 / math.sqrt(HD))
                proj[these, lanes] = u.astype(BF)
            proj[these, 2 * width :] = sums[these, 2 * width :].astype(BF)

        branch.last(of(o_mlp))
        branch.finish()
        products(at, of, part_ref, [(s_proj, i_w, True)], red)
        small.terms[...] = of(i_known)[...]
        shift = jnp.sum(proj[...].astype(F32), axis=0, keepdims=True)
        per = d // 4
        for m in range(3):
            for r in range(4):
                own = shift[:, (m * 4 + r) * HD : (m * 4 + r + 1) * HD]
                for b in range(n):
                    flat = m * d + (r * n + b) * HD
                    row, rest = flat // (3 * per), flat % (3 * per)
                    first = row * per + rest % per
                    line = 4 + rest // per
                    small.terms[line : line + 1, first : first + HD] = jnp.where(
                        at.j == b, own, 0.0
                    )
        steps(BACK_PLAN, red, extra)
        red.last(of(out))
        grad = of(out)[...]
        small.terms[0:1, :] = jnp.sum(grad * of(i_norm)[...], axis=0, keepdims=True)
        small.terms[1:2, :] = jnp.sum(grad, axis=0, keepdims=True)
        small.run(of(o_small))
        extra.finish()
        red.finish()

    return call.run(body)


def last_call(n, cid, pairs, tok, normed, known, row_sums, col_sums):
    call = Call(n, cid, "last")
    d = pairs[0][1].shape[0]
    keys = []
    for lhs, rhs, flip in pairs:
        keys.append((call.give(lhs), call.give(rhs), flip))
    i_norm, i_known = call.give(normed), call.give(known)
    out = call.make((tok, d), F32)
    o_small = call.make((8, d // 4), F32)
    part = call.scratch([pltpu.VMEM((n, tok, d), BF)])
    red_s = call.scratch(Reduce.scratch(n, tok, d, SUM_CUTS))
    s_small = call.scratch(SmallSum.scratch(n, d))
    extra = Extras(call, n, row_sums=row_sums, col_sums=col_sums)

    def body(at, of):
        part_ref = of(part)[0]
        red = Reduce(at, part_ref, of(red_s), SUM_CUTS)
        extra.bind(at, of)
        extra.start()
        products(at, of, part_ref, keys, red)
        steps(BACK_PLAN, red, extra)
        red.last(of(out))
        small = SmallSum(at, of(s_small))
        small.terms[...] = of(i_known)[...]
        grad = of(out)[...]
        small.terms[0:1, :] = jnp.sum(grad * of(i_norm)[...], axis=0, keepdims=True)
        small.terms[1:2, :] = jnp.sum(grad, axis=0, keepdims=True)
        small.run(of(o_small))
        extra.finish()
        red.finish()

    return call.run(body)


def attention(queries, keys, values, allowed):
    scores = jnp.einsum("qhd,khd->hqk", queries, keys, preferred_element_type=F32)
    exp_weights = jnp.where(allowed[None], jnp.exp(scores), 0.0)
    denominator = jnp.sum(exp_weights, axis=-1)
    numerator = jnp.einsum(
        "hqk,khd->qhd", exp_weights.astype(BF), values, preferred_element_type=F32
    )
    return numerator / jnp.transpose(denominator)[:, :, None], denominator


def attention_back(queries, keys, values, allowed, denominator, context, g_context):
    den = jnp.transpose(denominator)
    g_numer = (g_context / den[:, :, None]).astype(BF)
    g_den = jnp.transpose(-jnp.sum(g_context * context, axis=-1) / den)
    scores = jnp.einsum("qhd,khd->hqk", queries, keys, preferred_element_type=F32)
    exp_weights = jnp.where(allowed[None], jnp.exp(scores), 0.0)
    g_values = jnp.einsum(
        "hqk,qhd->khd", exp_weights.astype(BF), g_numer, preferred_element_type=F32
    )
    g_weights = jnp.einsum("qhd,khd->hqk", g_numer, values, preferred_element_type=F32)
    g_scores = (exp_weights * (g_weights + g_den[:, :, None])).astype(BF)
    g_queries = jnp.einsum("hqk,khd->qhd", g_scores, keys, preferred_element_type=F32)
    g_keys = jnp.einsum("hqk,qhd->khd", g_scores, queries, preferred_element_type=F32)
    return g_queries, g_keys, g_values


def body(nrow, n, *args):
    (
        layer_in,
        segments,
        positions,
        attn_norm_gain,
        attn_norm_bias,
        qkv_weight,
        qkv_bias,
        out_weight,
        mlp_norm_gain,
        mlp_norm_bias,
        gate_weight,
        up_weight,
        down_weight,
        out_grad,
    ) = args
    j = lax.axis_index("seq")
    tok = layer_in.shape[1]
    length = n * tok
    k = qkv_weight.shape[0]
    f = down_weight.shape[0]
    hp = H // n
    whole_heads = out_weight.shape[0] == HD
    roomy = length * D <= 1 << 22 and whole_heads

    if whole_heads:
        head_runs = [
            (b, (m * nrow + r) * HD, m * D + (r * n + b) * HD, HD)
            for b in range(n) for m in range(3) for r in range(nrow)
        ]
    else:
        size = hp * HD
        head_runs = [
            (b, m * size, m * D + b * size, size) for b in range(n) for m in range(3)
        ]
    ff_runs = [(b, r * f, (r * n + b) * f, f) for b in range(n) for r in range(nrow)]

    def split_heads(w):
        lead = w.shape[0]
        if whole_heads:
            w = w.reshape(lead, 3, nrow, n, HD).transpose(3, 0, 1, 2, 4)
        else:
            w = w.reshape(lead, 3, n, hp, HD).transpose(2, 0, 1, 3, 4)
        return w.reshape(n, lead, 3 * hp * HD)

    def join_heads(blocks):
        lead = blocks.shape[1]
        if whole_heads:
            w = blocks.reshape(n, lead, 3, nrow, HD).transpose(1, 2, 3, 0, 4)
        else:
            w = blocks.reshape(n, lead, 3, hp, HD).transpose(1, 2, 0, 3, 4)
        return w.reshape(lead, 3 * D)

    if roomy:
        blank = jnp.zeros((128 - 2 * k,), F32)
        vectors = [
            attn_norm_gain, attn_norm_bias, blank, mlp_norm_gain, mlp_norm_bias, blank,
            jnp.pad(qkv_bias.astype(F32).reshape(3, HD), ((0, 3), (0, 128 - HD))).reshape(-1),
        ]
        small = jnp.concatenate([v.astype(F32) for v in vectors]).reshape(8, 128)
        ints = jnp.concatenate([segments, positions, jnp.zeros((6, tok), jnp.int32)], 0)
        half = ROT // 2
        frequency = 10000.0 ** (-2.0 * jnp.arange(half, dtype=F32) / ROT)
        frequency = jnp.concatenate([frequency, frequency, jnp.zeros((HD - ROT,), F32)])
        frequency = jnp.broadcast_to(jnp.concatenate([frequency, frequency])[None], (8, 128))
        (
            inputs_all, gains, ints_all, qkv_own, out_own, queries, keys, values, context_low,
            context, denominator,
        ) = attend_call(
            n, layer_in[0], small, ints, frequency, qkv_weight, head_runs, out_weight,
        )
        inputs_all = inputs_all.reshape(length, D)
        attn_gain, mlp_gain, mlp_bias = gains[0:1], gains[2:3], gains[3:4]
        qkv_own, out_own = qkv_own.reshape(D, 3 * hp * HD), out_own.reshape(hp * HD, D)
    else:
        small = jnp.concatenate(
            [attn_norm_gain, attn_norm_bias, mlp_norm_gain, mlp_norm_bias, qkv_bias]
        )
        small = jnp.pad(small, (0, 2048 - small.shape[0])).reshape(16, 128)
        ints = jnp.concatenate([segments, positions, jnp.zeros((6, tok), jnp.int32)], 0)
        front = front_call(
            n, layer_in[0], small, ints, qkv_weight, head_runs, out_weight if whole_heads else None
        )
        x_all, small_all, ints_all, qkv_own = front[:4]
        x_all = x_all.reshape(length, D)
        qkv_own = qkv_own.reshape(D, 3 * hp * HD)
        if whole_heads:
            out_own = front[4].reshape(hp * HD, D)
        else:
            out_full = lax.all_gather(out_weight, ("row", "seq"), axis=0, tiled=True)
            out_own = lax.dynamic_slice_in_dim(out_full, j * hp * HD, hp * HD, 0)
        small_all = small_all.transpose(1, 0, 2, 3).reshape(nrow * n, 2048)
        attn_gain, attn_bias, mlp_gain, mlp_bias = (
            small_all[:, c : c + k].reshape(1, D).astype(F32) for c in (0, k, 2 * k, 3 * k)
        )
        qkv_shift = small_all[:, 4 * k : 4 * k + 3 * k].reshape(1, 3 * D)
        shift_own = lax.dynamic_index_in_dim(split_heads(qkv_shift), j, 0, keepdims=False).astype(F32)
        seg_all, pos_all = ints_all[:, 0].reshape(length), ints_all[:, 1].reshape(length)

        inputs_all = (norm_stats(x_all.astype(F32))[0] * attn_gain + attn_bias).astype(BF)
        inputs_all = lax.optimization_barrier(inputs_all)
        projected = dot(inputs_all, qkv_own, 1, 0) + shift_own
        head_split = projected.reshape(length, 3, hp, HD)
        cosine, sine_part = rotary_tables(pos_all)
        queries = (rotate(head_split[:, 0], cosine, sine_part, 1.0) / math.sqrt(HD)).astype(BF)
        keys = rotate(head_split[:, 1], cosine, sine_part, 1.0).astype(BF)
        values = head_split[:, 2].astype(BF)
        index = jnp.arange(length, dtype=jnp.int32)
        allowed = (seg_all[:, None] == seg_all[None, :]) & (index[None, :] <= index[:, None])
        context, denominator = attention(queries, keys, values, allowed)
        context_low = context.reshape(length, hp * HD).astype(BF)
    x_float = layer_in[0].astype(F32)
    grad_float = out_grad[0].astype(F32)
    ff_columns = [(gate_weight, ff_runs), (up_weight, ff_runs)]
    if roomy:
        (
            hidden_mid, g_middle, middle_all, inner_act, g_gate, g_up, _, _, down_own, grad_all,
        ) = core_call(
            n, (context_low, out_own), layer_in[0], mlp_gain, mlp_bias, ff_columns, [down_weight],
            [out_grad[0]],
        )
        down_own = down_own.reshape(nrow * f, D)
        middle_all, grad_all = middle_all.reshape(length, D), grad_all.reshape(length, D)
        normed2, inv_std2 = norm_stats(hidden_mid)
    else:
        attn_branch, gate_own, up_own, down_own = sum_call(
            n, 2, "mix_sum", [(context_low, out_own, False)], tok, columns=ff_columns,
            rows=[down_weight],
        )
        gate_own, up_own = gate_own.reshape(D, nrow * f), up_own.reshape(D, nrow * f)
        down_own = down_own.reshape(nrow * f, D)
        hidden_mid = x_float + attn_branch
        normed2, inv_std2 = norm_stats(hidden_mid)
        middle = (normed2 * mlp_gain + mlp_bias).astype(BF)
        (middle_all,) = gather_call(n, 3, "middle", middle)
        middle_all = middle_all.reshape(length, D)
        gate_pre = dot(middle_all, gate_own, 1, 0)
        up_pre = dot(middle_all, up_own, 1, 0)
        sig = jax.nn.sigmoid(gate_pre)
        silu = gate_pre * sig
        inner_act = (silu * up_pre).astype(BF)
        (grad_all,) = gather_call(n, 8, "grads", out_grad[0])
        grad_all = grad_all.reshape(length, D)
        g_inner = dot(grad_all, down_own, 1, 1)
        g_gate = (g_inner * up_pre * sig * (1.0 + gate_pre * (1.0 - sig))).astype(BF)
        g_up = (g_inner * silu).astype(BF)
        (g_middle,) = sum_call(
            n, 5, "mlp_back", [(g_gate, gate_own, True), (g_up, up_own, True)], tok
        )
    normed1, inv_std1 = norm_stats(x_float)
    if roomy:
        down_part, gate_part, up_part = (inner_act, grad_all), (middle_all, g_gate), (middle_all, g_up)
    else:
        down_part = dot(inner_act, grad_all, 0, 0).astype(BF).reshape(nrow, f, D)
        gate_part = dot(middle_all, g_gate, 0, 0).astype(BF).reshape(nrow, n * k, nrow * f)
        up_part = dot(middle_all, g_up, 0, 0).astype(BF).reshape(nrow, n * k, nrow * f)
    g_hidden = grad_float + norm_back(g_middle, normed2, inv_std2, mlp_gain)
    g_attn = g_hidden.astype(BF)
    if roomy:
        g_attn_all, down_grad, gate_grad, up_grad = gather_call(
            n, 6, "hidden_back", g_attn,
            row_sums=[down_part], col_sums=[(gate_part, ff_runs), (up_part, ff_runs)],
        )
    else:
        mlp_branch, down_grad = sum_call(
            n, 4, "mlp_sum", [(inner_act, down_own, False)], tok, row_sums=[down_part]
        )
        g_attn_all, gate_grad, up_grad = gather_call(
            n, 6, "hidden_back", g_attn, col_sums=[(gate_part, ff_runs), (up_part, ff_runs)]
        )
    g_attn_all = g_attn_all.reshape(length, D)

    if roomy:
        known = jnp.concatenate(
            [
                jnp.zeros((2, D), F32),
                jnp.sum(g_middle * normed2, axis=0)[None],
                jnp.sum(g_middle, axis=0)[None],
                jnp.zeros((4, D), F32),
            ]
        )
        g_inputs, small_grads, mlp_branch, out_w_grad, qkv_grad = back_call(
            n, g_attn_all, out_own, qkv_own, (queries, keys, values), context, context_low,
            denominator, ints_all, frequency, inputs_all, normed1, known, head_runs,
            (inner_act, down_own),
        )
    else:
        g_context = dot(g_attn_all, out_own, 1, 1).reshape(length, hp, HD)
        g_queries, g_keys, g_values = attention_back(
            queries, keys, values, allowed, denominator, context, g_context
        )
        query_part = rotate(g_queries, cosine, sine_part, -1.0) / math.sqrt(HD)
        key_part = rotate(g_keys, cosine, sine_part, -1.0)
        g_projected = (
            jnp.stack([query_part, key_part, g_values], 1).reshape(length, 3 * hp * HD).astype(BF)
        )
        qkv_part = dot(inputs_all, g_projected, 0, 0).astype(BF)
        qkv_part = qkv_part.reshape(nrow, n * k, 3 * hp * HD)
        out_part = dot(context_low, g_attn_all, 0, 0).astype(BF)
        if whole_heads:
            out_part = out_part.reshape((nrow,) + out_weight.shape)
        shift_sum = jnp.sum(g_projected.astype(F32), axis=0)
        shift_blocks = lax.dynamic_update_slice_in_dim(
            jnp.zeros((n, 1, 3 * hp * HD), F32), shift_sum[None, None], j, 0
        )
        shift_full = join_heads(shift_blocks)[0]
        known = jnp.concatenate(
            [
                jnp.zeros((2, D), F32),
                jnp.sum(g_middle * normed2, axis=0)[None],
                jnp.sum(g_middle, axis=0)[None],
                shift_full.reshape(nrow, 3, D // nrow).transpose(1, 0, 2).reshape(3, D),
                jnp.zeros((1, D), F32),
            ]
        )
        last = last_call(
            n, 7, [(g_projected, qkv_own, True)], tok, normed1, known,
            [out_part] if whole_heads else [],
            [(qkv_part, head_runs)],
        )
        if whole_heads:
            g_inputs, small_grads, out_w_grad, qkv_grad = last
        else:
            g_inputs, small_grads, qkv_grad = last
            placed = lax.dynamic_update_slice_in_dim(
                jnp.zeros((D, D), BF), out_part, j * hp * HD, 0
            )
            out_w_grad = lax.psum_scatter(
                placed, ("row", "seq"), scatter_dimension=0, tiled=True
            ).astype(F32)
    layer_out = (hidden_mid + mlp_branch).astype(BF)
    input_grad = g_hidden + norm_back(g_inputs, normed1, inv_std1, attn_gain)
    own = lax.dynamic_slice_in_dim(small_grads, j * k, k, 1)
    shift_own_grad = lax.dynamic_slice_in_dim(small_grads[4:7].reshape(-1), j * 3 * k, 3 * k, 0)
    return (
        layer_out[None],
        input_grad[None],
        own[0],
        own[1],
        qkv_grad,
        shift_own_grad,
        out_w_grad,
        own[2],
        own[3],
        gate_grad,
        up_grad,
        down_grad,
    )


def solution(mesh):
    nrow, n = mesh.shape["row"], mesh.shape["seq"]

    def local(*args):
        return body(nrow, n, *args)

    tokens, ints = P("row", "seq", None), P("row", "seq")
    vec, mat = P(("row", "seq")), P(("row", "seq"), None)
    return jax.shard_map(
        local,
        mesh=mesh,
        in_specs=(
            tokens, ints, ints, vec, vec, mat, vec, mat, vec, vec, mat, mat, mat, tokens,
        ),
        out_specs=(tokens, tokens, vec, vec, mat, vec, mat, vec, vec, mat, mat, mat),
        check_vma=False,
    )
```

```python
import functools
import math

import jax
import jax.numpy as jnp
from jax import lax
from jax.experimental import pallas as pl
from jax.experimental.pallas import tpu as pltpu
from jax.sharding import PartitionSpec as P

D = 2048
H = 32
HD = 64
ROT = 16
EPSILON = 1e-05
BF = jnp.bfloat16
F32 = jnp.float32


def dot(a, b, ca, cb):
    return lax.dot_general(a, b, (((ca,), (cb,)), ((), ())), preferred_element_type=F32)


def norm_stats(values_in):
    average = jnp.mean(values_in, axis=-1, keepdims=True)
    centered = values_in - average
    inv_std = lax.rsqrt(jnp.mean(centered * centered, axis=-1, keepdims=True) + EPSILON)
    return (centered * inv_std, inv_std)


def norm_back(grad_in, normed, inv_std, gain_vector):
    scaled = grad_in * gain_vector
    return inv_std * (
        scaled
        - jnp.mean(scaled, axis=-1, keepdims=True)
        - normed * jnp.mean(scaled * normed, axis=-1, keepdims=True)
    )


def rotary_tables(positions):
    half_rot = ROT // 2
    frequency = 10000.0 ** (-2.0 * jnp.arange(half_rot, dtype=F32) / ROT)
    angles = positions.astype(F32)[:, None] * frequency[None, :]
    return (jnp.cos(angles)[:, None, :], jnp.sin(angles)[:, None, :])


def rotate(head_values, cosine, sine_part, direction):
    half_rot = ROT // 2
    first_half = head_values[..., :half_rot]
    second = head_values[..., half_rot:ROT]
    return jnp.concatenate(
        [
            first_half * cosine - direction * second * sine_part,
            second * cosine + direction * first_half * sine_part,
            head_values[..., ROT:],
        ],
        axis=-1,
    )


MESH = pl.DeviceIdType.MESH
LINE = 4


class Place:
    def __init__(self, n):
        self.n = n
        self.depth = LINE
        self.width = n // LINE
        self.r = lax.axis_index("row")
        self.j = lax.axis_index("seq")
        self.z = self.j // self.width
        self.x = lax.rem(self.j, self.width)
        y, c = self.r // 2, lax.rem(self.r, 2)
        self.y, self.c = y, c
        self.r_y = (1 - y) * 2 + c
        self.r_c = y * 2 + (1 - c)
        self.r_yc = (1 - y) * 2 + (1 - c)

    def inner(self, t):
        return jnp.logical_or(
            jnp.logical_and(t > self.z, self.z > 0),
            jnp.logical_and(t < self.z, self.z < self.depth - 1),
        )

    def seq(self, j):
        return (self.r, j)

    def row(self, r):
        return (r, self.j)

    def other(self, i):
        return lax.rem(self.j + i, self.n)

    def meet(self):
        barrier = pltpu.get_barrier_semaphore()
        for r in (self.r_y, self.r_c, self.r_yc):
            pl.semaphore_signal(barrier, inc=1, device_id=self.row(r), device_id_type=MESH)
        for i in range(1, self.n):
            pl.semaphore_signal(
                barrier, inc=1, device_id=self.seq(self.other(i)), device_id_type=MESH
            )
        pl.semaphore_wait(barrier, self.n + 2)


def remote(src, dst, ssem, rsem, device):
    return pltpu.make_async_remote_copy(
        src_ref=src, dst_ref=dst, send_sem=ssem, recv_sem=rsem, device_id=device,
        device_id_type=MESH,
    )


ALONE = ((8, False),)
PAIRED = ((2, True), (6, False))
SUM_CUTS = ((1, True), (7, False))
CORE_SUMS = ((2, True), (6, False))
CORE_PLAN = ("c0", "g1", "c1", "r3", "c2", "y0", "c3", "y1", "g2", "r2", "y2", "y3", "g3", "r1")
SUM_PLAN = ("w0", "g1", "c0", "r3", "w1", "x0", "w2", "x1", "g2", "c1", "r2", "x2", "t0", "g3", "c2", "c3", "r1", "t1", "y0", "y1", "y2", "y3")
GATHER_PLAN = ("w0", "g1", "x0", "w1", "g2", "x1", "t0", "w2", "g3", "x2", "t1")
BACK_PLAN = ("w0", "r3", "w1", "x0", "x1", "r2", "t0", "r1")
MLP_CUTS = ((2, True), (3, False), (3, False))
MLP_SUMS = ((2, True), (3, False), (3, False))


class Gather:
    @staticmethod
    def sems(n, cuts):
        w = n // LINE
        out = []
        for _ in cuts:
            out += [
                pltpu.SemaphoreType.DMA((2, n)),
                pltpu.SemaphoreType.DMA((LINE, max(w - 1, 1))),
                pltpu.SemaphoreType.DMA((n,)),
            ]
        return out

    def __init__(self, at, buf, sems, cuts):
        self.at, self.buf = at, buf
        tok = buf.shape[1]
        self.cuts = []
        first = 0
        for i, (share, wide) in enumerate(cuts):
            rows = tok * share // 8
            self.cuts.append((pl.ds(first, rows), wide, sems[3 * i : 3 * i + 3]))
            first += rows

    def copy(self, cut, b, to, sem):
        here = self.buf.at[b, cut[0]]
        return remote(here, here, sem, cut[2][2].at[b], self.at.seq(to))

    def along(self, cut, way, b):
        at = self.at
        to = at.j + at.width if way == 0 else at.j - at.width
        return self.copy(cut, b, to, cut[2][0].at[way, b])

    def across(self, cut, zz, i):
        at = self.at
        to = at.z * at.width + lax.rem(at.x + i, at.width)
        return self.copy(cut, zz * at.width + at.x, to, cut[2][1].at[zz, i - 1])

    def take(self, cut, b):
        self.copy(cut, b, self.at.other(1), cut[2][0].at[0, 0]).wait_recv()

    def onward(self, cut, way, b):
        at = self.at

        @pl.when(at.z < at.depth - 1 if way == 0 else at.z > 0)
        def _():
            self.along(cut, way, b).start()

    def start(self):
        at = self.at
        for cut in self.cuts:
            if cut[1]:
                for i in range(1, at.width):
                    self.across(cut, at.z, i).start()
        for cut in self.cuts:
            for way in range(2):
                self.onward(cut, way, at.j)
            if not cut[1]:
                for i in range(1, at.width):
                    self.across(cut, at.z, i).start()

    def step(self, s):
        at = self.at
        for cut in self.cuts:
            if s == 1 and cut[1]:
                for i in range(1, at.width):
                    b = at.z * at.width + lax.rem(at.x + i, at.width)
                    self.take(cut, b)
                    for way in range(2):
                        self.onward(cut, way, b)
        for cut in self.cuts:
            for way in range(2):
                zz = at.z - s if way == 0 else at.z + s

                @pl.when(zz >= 0 if way == 0 else zz < at.depth)
                def _(zz=zz, way=way, cut=cut):
                    if cut[1]:
                        for i in range(at.width):
                            b = zz * at.width + lax.rem(at.x + i, at.width)
                            self.take(cut, b)
                            self.onward(cut, way, b)
                    else:
                        b = zz * at.width + at.x
                        self.take(cut, b)
                        self.onward(cut, way, b)
                        for i in range(1, at.width):
                            self.across(cut, zz, i).start()

    def fetch(self, zz):
        at = self.at
        for way in range(2):

            @pl.when(zz < at.z if way == 0 else zz > at.z)
            def _(way=way):
                for cut in self.cuts:
                    for i in range(at.width if cut[1] else 1):
                        b = zz * at.width + lax.rem(at.x + i, at.width)
                        self.take(cut, b)
                        self.onward(cut, way, b)
                    if not cut[1]:
                        for i in range(1, at.width):
                            self.across(cut, zz, i).start()

    def open_wide(self):
        at = self.at
        for cut in self.cuts:
            if cut[1]:
                for i in range(1, at.width):
                    b = at.z * at.width + lax.rem(at.x + i, at.width)
                    self.take(cut, b)
                    for way in range(2):
                        self.onward(cut, way, b)

    def take_side(self, zz):
        at = self.at
        for cut in self.cuts:
            if not cut[1]:
                for i in range(1, at.width):
                    self.take(cut, zz * at.width + lax.rem(at.x + i, at.width))

    def finish(self):
        at = self.at
        for cut in self.cuts:
            for zz in range(at.depth):
                for i in range(1, at.width):
                    if cut[1]:
                        @pl.when(at.z == zz)
                        def _(zz=zz, i=i, cut=cut):
                            self.across(cut, zz, i).wait_send()
                    else:
                        self.across(cut, zz, i).wait_send()
                for way in range(2):
                    ok = jnp.logical_and(at.z >= zz, at.z < at.depth - 1) if way == 0 else jnp.logical_and(at.z <= zz, at.z > 0)

                    @pl.when(ok)
                    def _(zz=zz, way=way, cut=cut):
                        for i in range(at.width if cut[1] else 1):
                            b = zz * at.width + lax.rem(at.x + i, at.width)
                            self.along(cut, way, b).wait_send()


class NarrowSum:
    @staticmethod
    def scratch(n, size, d):
        side = max(n // LINE - 1, 1)
        return (
            [pltpu.VMEM((LINE, side, size, d), BF), pltpu.VMEM((LINE + 1, size, d), BF)]
            + [pltpu.SemaphoreType.DMA((LINE, side))] * 2
            + [pltpu.SemaphoreType.DMA((LINE,)), pltpu.SemaphoreType.DMA((LINE + 1,))]
        )

    def __init__(self, at, part, rows, refs):
        self.at, self.part, self.rows = at, part, rows
        self.xr, self.lr, self.xs_sem, self.xr_sem, self.ls_sem, self.lr_sem = refs

    def across(self, t, i):
        at = self.at
        xx = lax.rem(at.x + i, at.width)
        return remote(
            self.part.at[t * at.width + xx, self.rows], self.xr.at[t, i - 1],
            self.xs_sem.at[t, i - 1], self.xr_sem.at[t, i - 1], at.seq(at.z * at.width + xx),
        )

    def along(self, t):
        at = self.at
        there = jnp.where(t > at.z, at.j + at.width, at.j - at.width)
        slot = jnp.where(t == at.z - 1, at.depth, t)
        return remote(
            self.part.at[t * at.width + at.x, self.rows], self.lr.at[slot],
            self.ls_sem.at[t], self.lr_sem.at[slot], at.seq(there),
        )

    def landed(self, slot):
        remote(
            self.lr.at[slot], self.lr.at[slot], self.ls_sem.at[0], self.lr_sem.at[slot],
            self.at.seq(self.at.other(1)),
        ).wait_recv()

    def emit(self, t):
        for i in range(1, self.at.width):
            self.across(t, i).start()

    def summed(self, t):
        at = self.at
        total = self.part[t * at.width + at.x, self.rows].astype(F32)
        for i in range(1, at.width):
            self.across(t, i).wait_recv()
            total = total + self.xr[t, i - 1].astype(F32)
        return total

    def pass_on(self, t):
        at = self.at
        block = (t * at.width + at.x, self.rows)
        total = self.summed(t)
        inner = at.inner(t)

        @pl.when(inner)
        def _():
            self.landed(t)
            self.part[block] = (total + self.lr[t].astype(F32)).astype(BF)

        @pl.when(jnp.logical_not(inner))
        def _():
            self.part[block] = total.astype(BF)

        self.along(t).start()

    def close(self):
        pass

    def last(self, out):
        at = self.at
        out[self.rows] = self.summed(at.z)

        @pl.when(at.z > 0)
        def _():
            self.landed(at.z)
            out[self.rows] += self.lr[at.z].astype(F32)

        @pl.when(at.z < at.depth - 1)
        def _():
            self.landed(at.depth)
            out[self.rows] += self.lr[at.depth].astype(F32)

    def finish(self):
        at = self.at
        for t in range(at.depth):
            for i in range(1, at.width):
                self.across(t, i).wait_send()

            @pl.when(at.z != t)
            def _(t=t):
                self.along(t).wait_send()


class WideSum:
    @staticmethod
    def scratch(n, size, d):
        w = n // LINE
        side = max(w - 1, 1)
        return (
            [pltpu.VMEM((side, size, d), BF), pltpu.VMEM((LINE + 1, w, size, d), BF)]
            + [pltpu.SemaphoreType.DMA((side,))] * 2
            + [pltpu.SemaphoreType.DMA((LINE, w)), pltpu.SemaphoreType.DMA((LINE + 1, w))]
        )

    def __init__(self, at, part, rows, refs):
        self.at, self.part, self.rows = at, part, rows
        self.xr, self.lr, self.xs_sem, self.xr_sem, self.ls_sem, self.lr_sem = refs

    def across(self, i):
        at = self.at
        xx = lax.rem(at.x + i, at.width)
        return remote(
            self.part.at[at.z * at.width + xx, self.rows], self.xr.at[i - 1],
            self.xs_sem.at[i - 1], self.xr_sem.at[i - 1], at.seq(at.z * at.width + xx),
        )

    def along(self, t, xx):
        at = self.at
        there = jnp.where(t > at.z, at.j + at.width, at.j - at.width)
        slot = jnp.where(t == at.z - 1, at.depth, t)
        return remote(
            self.part.at[t * at.width + xx, self.rows], self.lr.at[slot, xx],
            self.ls_sem.at[t, xx], self.lr_sem.at[slot, xx], at.seq(there),
        )

    def landed(self, slot, xx):
        remote(
            self.lr.at[slot, xx], self.lr.at[slot, xx], self.ls_sem.at[0, xx],
            self.lr_sem.at[slot, xx], self.at.seq(self.at.other(1)),
        ).wait_recv()

    def emit(self, t):
        at = self.at

        @pl.when(jnp.logical_and(t != at.z, jnp.logical_not(at.inner(t))))
        def _():
            for xx in range(at.width):
                self.along(t, xx).start()

    def pass_on(self, t):
        at = self.at

        @pl.when(at.inner(t))
        def _():
            for xx in range(at.width):
                self.landed(t, xx)
                block = (t * at.width + xx, self.rows)
                total = self.part[block].astype(F32) + self.lr[t, xx].astype(F32)
                self.part[block] = total.astype(BF)
                self.along(t, xx).start()

    def line_sum(self, xx, put):
        at = self.at
        own = self.part[at.z * at.width + xx, self.rows].astype(F32)

        @pl.when(at.z == 0)
        def _():
            self.landed(at.depth, xx)
            put(own + self.lr[at.depth, xx].astype(F32))

        @pl.when(at.z == at.depth - 1)
        def _():
            self.landed(at.z, xx)
            put(own + self.lr[at.z, xx].astype(F32))

        @pl.when(jnp.logical_and(at.z > 0, at.z < at.depth - 1))
        def _():
            self.landed(at.depth, xx)
            self.landed(at.z, xx)
            put(own + self.lr[at.depth, xx].astype(F32) + self.lr[at.z, xx].astype(F32))

    def close(self):
        at = self.at
        for i in range(1, at.width):
            xx = lax.rem(at.x + i, at.width)

            def put(total, xx=xx):
                self.part[at.z * at.width + xx, self.rows] = total.astype(BF)

            self.line_sum(xx, put)
            self.across(i).start()

    def last(self, out):
        at = self.at

        def put(total):
            out[self.rows] = total

        self.line_sum(at.x, put)
        for i in range(1, at.width):
            self.across(i).wait_recv()
            out[self.rows] += self.xr[i - 1].astype(F32)

    def finish(self):
        at = self.at
        for i in range(1, at.width):
            self.across(i).wait_send()
        for t in range(at.depth):

            @pl.when(at.z != t)
            def _(t=t):
                for xx in range(at.width):
                    self.along(t, xx).wait_send()


class Reduce:
    @staticmethod
    def scratch(n, tok, d, cuts):
        out = []
        for share, wide in cuts:
            out += (WideSum if wide else NarrowSum).scratch(n, tok * share // 8, d)
        return out

    def __init__(self, at, part, refs, cuts):
        self.at, self.cuts = at, []
        tok = part.shape[1]
        first = 0
        for i, (share, wide) in enumerate(cuts):
            rows = pl.ds(first, tok * share // 8)
            first += tok * share // 8
            self.cuts.append((WideSum if wide else NarrowSum)(at, part, rows, refs[6 * i : 6 * i + 6]))

    def emit(self, t):
        for c in self.cuts:
            c.emit(t)

    def pass_on(self, t):
        for c in self.cuts:
            c.pass_on(t)

    def reduce(self, s):
        at = self.at
        for t in (at.z + s, at.z - s):

            @pl.when(jnp.logical_and(t >= 0, t < at.depth))
            def _(t=t):
                self.pass_on(t)

    def last(self, out):
        for c in self.cuts:
            c.close()
        for c in self.cuts[::-1]:
            c.last(out)

    def finish(self):
        for c in self.cuts:
            c.finish()


class Columns:
    @staticmethod
    def sems(n):
        return [pltpu.SemaphoreType.DMA((4, n)), pltpu.SemaphoreType.DMA((4, n))]

    def __init__(self, at, pieces, full, sems):
        self.at, self.pieces, self.full = at, pieces, full
        self.ssem, self.rsem = sems

    def first(self, i):
        at = self.at
        to = at.other(i)
        return remote(
            self.pieces.at[to], self.full.at[at.r, at.j], self.ssem.at[0, to],
            self.rsem.at[at.r, at.j], at.seq(to),
        )

    def own(self):
        at = self.at
        return pltpu.make_async_copy(
            self.pieces.at[at.j], self.full.at[at.r, at.j], self.ssem.at[0, at.j]
        )

    def pass_on(self, r, js, to, k):
        return remote(
            self.full.at[r, js], self.full.at[r, js], self.ssem.at[k, js], self.rsem.at[r, js],
            self.at.row(to),
        )

    def take(self, r, js):
        self.pass_on(r, js, self.at.r_c, 0).wait_recv()

    def start(self):
        at = self.at
        self.own().start()

        @pl.loop(1, at.n)
        def _(i):
            self.first(i).start()

    def step(self, lo, hi):
        at = self.at

        @pl.loop(lo, hi)
        def _(i):
            js = lax.rem(at.j + at.n - i, at.n)

            @pl.when(i == 0)
            def _():
                self.own().wait()

            @pl.when(i > 0)
            def _():
                self.take(at.r, js)

            self.pass_on(at.r, js, at.r_y, 1).start()
            self.pass_on(at.r, js, at.r_c, 2).start()

    def relay(self, lo, hi):
        at = self.at

        @pl.loop(lo, hi)
        def _(i):
            js = lax.rem(at.j + at.n - i, at.n)
            self.take(at.r_y, js)
            self.pass_on(at.r_y, js, at.r_c, 3).start()

    def finish(self):
        at = self.at

        @pl.loop(0, at.n)
        def _(js):
            self.take(at.r_c, js)
            self.take(at.r_yc, js)
            self.pass_on(at.r, js, at.r_y, 1).wait_send()
            self.pass_on(at.r, js, at.r_c, 2).wait_send()
            self.pass_on(at.r_y, js, at.r_c, 3).wait_send()

        @pl.loop(1, at.n)
        def _(i):
            self.first(i).wait_send()


class Rows:
    @staticmethod
    def sems():
        return [pltpu.SemaphoreType.DMA((4,)), pltpu.SemaphoreType.DMA((4,))]

    def __init__(self, at, shard, full, sems):
        self.at, self.shard, self.full = at, shard, full
        self.ssem, self.rsem = sems

    def own(self):
        return pltpu.make_async_copy(self.shard, self.full.at[self.at.r], self.ssem.at[0])

    def direct(self, to, k):
        r = self.at.r
        return remote(
            self.shard, self.full.at[r], self.ssem.at[k], self.rsem.at[r], self.at.row(to)
        )

    def onward(self):
        at = self.at
        r = at.r_y
        return remote(
            self.full.at[r], self.full.at[r], self.ssem.at[3], self.rsem.at[r], at.row(at.r_c)
        )

    def take(self, r):
        at = self.at
        remote(
            self.full.at[r], self.full.at[r], self.ssem.at[0], self.rsem.at[r], at.row(at.r_c)
        ).wait_recv()

    def start(self):
        at = self.at
        self.own().start()
        self.direct(at.r_y, 1).start()
        self.direct(at.r_c, 2).start()

    def relay(self):
        self.take(self.at.r_y)
        self.onward().start()

    def finish(self):
        at = self.at
        self.own().wait()
        self.take(at.r_c)
        self.take(at.r_yc)
        self.direct(at.r_y, 1).wait_send()
        self.direct(at.r_c, 2).wait_send()
        self.onward().wait_send()


class RowSum:
    @staticmethod
    def scratch(m, c):
        return [
            pltpu.VMEM((2, m, c), BF),
            pltpu.VMEM((m, c), BF),
            pltpu.SemaphoreType.DMA((3,)),
            pltpu.SemaphoreType.DMA((3,)),
        ]

    def __init__(self, at, grad, refs):
        self.at, self.grad = at, grad
        self.core_in, self.y_in, self.ssem, self.rsem = refs

    def to_core(self, far):
        at = self.at
        yy = 1 - at.y if far else at.y
        k = 1 if far else 0
        return remote(
            self.grad.at[yy * 2 + 1 - at.c], self.core_in.at[k], self.ssem.at[k], self.rsem.at[k],
            at.row(at.r_c),
        )

    def over_y(self):
        at = self.at
        return remote(
            self.grad.at[at.r_y], self.y_in, self.ssem.at[2], self.rsem.at[2], at.row(at.r_y)
        )

    def start(self):
        self.to_core(1).start()
        self.to_core(0).start()

    def cross(self):
        at = self.at
        self.to_core(1).wait_recv()
        self.grad[at.r_y] = (
            self.grad[at.r_y].astype(F32) + self.core_in[1].astype(F32)
        ).astype(BF)
        self.over_y().start()

    def total(self):
        at = self.at
        self.to_core(0).wait_recv()
        self.over_y().wait_recv()
        return (
            self.grad[at.r].astype(F32) + self.core_in[0].astype(F32) + self.y_in[...].astype(F32)
        )

    def finish(self):
        self.to_core(1).wait_send()
        self.to_core(0).wait_send()
        self.over_y().wait_send()


class Exchange:
    @staticmethod
    def sems(n):
        return [pltpu.SemaphoreType.DMA((n,)), pltpu.SemaphoreType.DMA((n,))]

    def __init__(self, at, mine, got, sems):
        self.at, self.mine, self.got = at, mine, got
        self.ssem, self.rsem = sems

    def send(self, i):
        at = self.at
        to = at.other(i)
        return remote(
            self.mine.at[to], self.got.at[at.j], self.ssem.at[to], self.rsem.at[at.j], at.seq(to)
        )

    def own(self):
        at = self.at
        return pltpu.make_async_copy(
            self.mine.at[at.j], self.got.at[at.j], self.ssem.at[at.j]
        )

    def start(self):
        self.own().start()

        @pl.loop(1, self.at.n)
        def _(i):
            self.send(i).start()

    def finish(self):
        at = self.at
        self.own().wait()

        @pl.loop(1, at.n)
        def _(i):
            src = at.other(i)
            remote(
                self.mine.at[src], self.got.at[src], self.ssem.at[src], self.rsem.at[src],
                at.seq(src),
            ).wait()


class SmallGather:
    @staticmethod
    def sems(n):
        return [pltpu.SemaphoreType.DMA((4,))] * 2 + [pltpu.SemaphoreType.DMA((n,))] * 2

    def __init__(self, at, mine, full, sems):
        self.at, self.mine, self.full = at, mine, full
        self.rs, self.rr, self.ss, self.sr = sems

    def beside(self, r):
        at = self.at
        return remote(
            self.mine, self.full.at[at.j, at.r], self.rs.at[r], self.rr.at[at.r], at.row(r)
        )

    def own(self):
        at = self.at
        return pltpu.make_async_copy(self.mine, self.full.at[at.j, at.r], self.rs.at[at.r])

    def onward(self, to):
        at = self.at
        return remote(
            self.full.at[at.j], self.full.at[at.j], self.ss.at[to], self.sr.at[at.j], at.seq(to)
        )

    def start(self):
        at = self.at
        self.own().start()
        for r in (at.r_y, at.r_c, at.r_yc):
            self.beside(r).start()

    def step(self):
        at = self.at
        self.own().wait()
        for r in (at.r_y, at.r_c, at.r_yc):
            remote(
                self.mine, self.full.at[at.j, r], self.rs.at[r], self.rr.at[r], at.row(r)
            ).wait()

        @pl.loop(1, at.n)
        def _(i):
            self.onward(at.other(i)).start()

    def finish(self):
        at = self.at

        @pl.loop(1, at.n)
        def _(i):
            src = at.other(i)
            remote(
                self.full.at[src], self.full.at[src], self.ss.at[src], self.sr.at[src],
                at.seq(src),
            ).wait()


class SmallSum:
    @staticmethod
    def scratch(n, w):
        q = w // 4
        return (
            [pltpu.VMEM((8, w), F32), pltpu.VMEM((4, 8, q), F32), pltpu.VMEM((8, q), F32)]
            + [pltpu.VMEM((n, 8, q), F32)]
            + [pltpu.SemaphoreType.DMA((4,))] * 2
            + [pltpu.SemaphoreType.DMA((n,))] * 2
        )

    def __init__(self, at, refs):
        self.at = at
        self.terms, self.beside_in, self.acc, self.seq_in = refs[:4]
        self.rs, self.rr, self.ss, self.sr = refs[4:]
        self.q = self.terms.shape[1] // 4

    def part(self, r):
        return self.terms.at[:, pl.ds(pl.multiple_of(r * self.q, self.q), self.q)]

    def beside(self, r):
        at = self.at
        return remote(
            self.part(r), self.beside_in.at[at.r], self.rs.at[r], self.rr.at[at.r], at.row(r)
        )

    def run(self, out):
        at = self.at
        near = (at.r_y, at.r_c, at.r_yc)
        for r in near:
            self.beside(r).start()
        self.acc[...] = self.part(at.r)[...]
        for r in near:
            remote(
                self.part(r), self.beside_in.at[r], self.rs.at[r], self.rr.at[r], at.row(r)
            ).wait()
            self.acc[...] += self.beside_in[r]

        @pl.loop(1, at.n)
        def _(i):
            to = at.other(i)
            remote(
                self.acc, self.seq_in.at[at.j], self.ss.at[to], self.sr.at[at.j], at.seq(to)
            ).start()

        out[...] = self.acc[...]

        @pl.loop(1, at.n)
        def _(i):
            src = at.other(i)
            remote(
                self.acc, self.seq_in.at[src], self.ss.at[src], self.sr.at[src], at.seq(src)
            ).wait()
            out[...] += self.seq_in[src]


class Call:
    def __init__(self, n, cid, name):
        self.n, self.cid, self.name = n, cid, name
        self.args, self.ins, self.outs, self.out_specs, self.scr = [], [], [], [], []

    def give(self, array, space=pltpu.VMEM):
        if isinstance(array, Made):
            return array.key
        for i, known in enumerate(self.args):
            if known is array:
                return ("i", i)
        self.args.append(array)
        self.ins.append(pl.BlockSpec(memory_space=space))
        return ("i", len(self.args) - 1)

    def make(self, shape, dtype, space=pltpu.VMEM):
        self.outs.append(jax.ShapeDtypeStruct(shape, dtype))
        self.out_specs.append(pl.BlockSpec(memory_space=space))
        return ("o", len(self.outs) - 1)

    def scratch(self, items):
        at = len(self.scr)
        self.scr.extend(items)
        return [("s", at + i) for i in range(len(items))]

    def run(self, body, flops=0):
        ni, no = len(self.ins), len(self.outs)

        def kernel(*refs):
            def of(key):
                if isinstance(key, list):
                    return [of(k) for k in key]
                if isinstance(key[0], tuple):
                    return tuple(of(k) for k in key)
                kind, i = key
                return refs[i + {"i": 0, "o": ni, "s": ni + no}[kind]]

            at = Place(self.n)
            at.meet()
            body(at, of)

        return pl.pallas_call(
            kernel,
            out_shape=self.outs,
            in_specs=self.ins,
            out_specs=self.out_specs,
            scratch_shapes=self.scr,
            name=self.name,
            cost_estimate=pl.CostEstimate(
                flops=flops, bytes_accessed=1 << 24, transcendentals=0
            ),
            compiler_params=pltpu.CompilerParams(
                collective_id=self.cid, has_side_effects=True, vmem_limit_bytes=VMEM_LIMIT
            ),
        )(*self.args)


VMEM_LIMIT = 60 << 20
ANY = pltpu.VMEM
CHUNK = 512


def product(at, of, part, pairs, t):
    width, tok = at.width, part.shape[1]

    @pl.loop(0, part.shape[2] // CHUNK)
    def _(i):
        cols = pl.ds(pl.multiple_of(i * CHUNK, CHUNK), CHUNK)
        total = None
        for lhs, rhs, flip in pairs:
            left = of(lhs)[pl.ds(t * (width * tok), width * tok), :]
            if flip:
                term = dot(left, of(rhs)[cols, :], 1, 1)
            else:
                term = dot(left, of(rhs)[:, cols], 1, 0)
            total = term if total is None else total + term
        part[pl.ds(t * width, width), :, cols] = total.reshape(width, tok, CHUNK).astype(BF)


def products(at, of, part, pairs, red):
    for s in range(at.depth - 1, -1, -1):
        for t in [at.z + s, at.z - s] if s else [at.z]:

            @pl.when(jnp.logical_and(t >= 0, t < at.depth))
            def _(t=t):
                product(at, of, part, pairs, t)
                red.emit(t)


def steps(plan, red, extra):
    work = extra.fill()
    for word in plan:
        what, k = word[0], int(word[1])
        if what == "r":
            red.reduce(k)
        elif what == "g":
            extra.gather_step(k)
        elif what == "c":
            extra.column_step(k)
        elif what == "y":
            extra.column_relay(k)
        elif what == "w" and k < len(work):
            work[k]()
        elif what == "x":
            extra.cross(k)
        elif what == "t":
            extra.turn(k)


def gather_all(g, between=None):
    at = g.at
    for s in range(1, at.depth):
        g.step(s)
        if between is not None:
            between(s)
    for s in range(at.depth):
        for zz in [at.z - s, at.z + s] if s else [at.z]:

            @pl.when(jnp.logical_and(zz >= 0, zz < at.depth))
            def _(zz=zz):
                g.take_side(zz)


def split_columns(src, dst, runs):
    for b, to, at, size in runs:
        dst[b, :, to : to + size] = src[:, at : at + size]


def join_columns(src, dst, runs):
    for b, to, at, size in runs:
        dst[:, at : at + size] = src[b, :, to : to + size].astype(dst.dtype)


def front_call(n, x, small, ints, weight, runs, out_w):
    tok, d = x.shape
    k, c = weight.shape[0], weight.shape[1] // n
    call = Call(n, 1, "front")
    ix = call.give(x, ANY)
    ism, iin = call.give(small), call.give(ints)
    iw = call.give(weight, ANY)
    ox = call.make((n, tok, d), BF, ANY)
    osm = call.make((n, 4) + small.shape, BF)
    oin = call.make((n,) + ints.shape, jnp.int32)
    ow = call.make((4, n, k, c), BF, ANY)
    sx = call.scratch(Gather.sems(n, ALONE))
    sp = call.scratch([pltpu.VMEM((n, k, c), BF)])
    ssm = call.scratch(SmallGather.sems(n))
    sin = call.scratch(Exchange.sems(n))
    sw = call.scratch(Columns.sems(n))
    if out_w is not None:
        io = call.give(out_w, ANY)
        oo = call.make((4,) + out_w.shape, BF, ANY)
        so = call.scratch(Rows.sems())

    def body(at, of):
        sm = SmallGather(at, of(ism), of(osm), of(ssm))
        g = Gather(at, of(ox), of(sx), ALONE)
        cols = Columns(at, of(sp)[0], of(ow), of(sw))
        spread = Spread(at, of(iin), of(oin), of(sin))
        sm.start()
        of(ox)[at.j] = of(ix)[...]
        g.start()
        spread.start()
        split_columns(of(iw), of(sp)[0], runs)
        cols.start()
        sm.step()
        if out_w is not None:
            rows = Rows(at, of(io), of(oo), of(so))
            rows.start()
        cuts = [0, n // 4, n // 2, n]

        def between(s):
            cols.step(cuts[s - 1], cuts[s])

        gather_all(g, between)
        cols.relay(0, n)
        if out_w is not None:
            rows.relay()
            rows.finish()
        cols.finish()
        g.finish()
        sm.finish()
        spread.finish()

    return call.run(body)


def turned(line):
    return jnp.transpose(jnp.broadcast_to(line, (128, 128)))


def rotation(ints_all, frequency, block, direction):
    lane = lax.rem(lax.broadcasted_iota(jnp.int32, (128, 128), 1), HD)
    angle = turned(ints_all[block, 1:2].astype(F32)) * frequency[0:1]
    cosine, sine = jnp.cos(angle), direction * jnp.sin(angle)
    return cosine, jnp.where(lane < ROT // 2, -sine, 0.0), jnp.where(lane < ROT // 2, 0.0, sine)


def turn_pairs(u, table):
    cosine, above, below = table
    return (
        u * cosine
        + pltpu.roll(u, 128 - ROT // 2, 1) * above
        + pltpu.roll(u, ROT // 2, 1) * below
    )


def fill_mask(at, mask, ints_all, t):
    tok = 128
    index = lax.broadcasted_iota(jnp.int32, (tok, tok), 0)
    other = lax.broadcasted_iota(jnp.int32, (tok, tok), 1)
    for b in range(at.width):
        mine = turned(ints_all[t * at.width + b, 0:1].astype(F32))
        for o in range((t + 1) * at.width):
            ok = mine == ints_all[o, 0:1].astype(F32)
            if o == t * at.width + b:
                ok = jnp.logical_and(ok, other <= index)
            fill = jnp.where(ok, 0.0, -jnp.inf)
            if o > t * at.width + b:
                fill = jnp.full((tok, tok), -jnp.inf, F32)
            mask[b * tok : (b + 1) * tok, o * tok : (o + 1) * tok] = fill


class Made:
    def __init__(self, key, shape):
        self.key, self.shape = key, shape


def attend_call(n, x, small, ints, frequency, qkv_w, head_runs, out_w):
    tok, d = x.shape
    k, c = qkv_w.shape[0], qkv_w.shape[1] // n
    hp, length, wide = H // n, n * tok, n // LINE * tok
    call = Call(n, 10, "attend")
    i_x, i_small, i_ints, i_freq = (call.give(v) for v in (x, small, ints, frequency))
    i_w, i_out = call.give(qkv_w), call.give(out_w)
    o_in = call.make((n, tok, d), BF)
    o_gains = call.make((8, d), F32)
    o_ints = call.make((n,) + ints.shape, jnp.int32)
    o_w = call.make((4, n, k, c), BF)
    o_out = call.make((4,) + out_w.shape, BF)
    o_qkv = [call.make((hp, length, HD), BF) for _ in range(3)]
    o_low = call.make((length, hp * HD), BF)
    o_ctx = call.make((length, hp * HD), F32)
    o_den = call.make((length, 128), F32)
    s_x = call.scratch([pltpu.VMEM((n, tok, d), BF)])
    s_gat = call.scratch(Gather.sems(n, ALONE))
    s_pieces = call.scratch([pltpu.VMEM((n, k, c), BF)])
    s_small = call.scratch([pltpu.VMEM((n, 4) + small.shape, F32)])
    s_shift = call.scratch([pltpu.VMEM((8, c), F32)])
    s_mask = call.scratch([pltpu.VMEM((wide, length), F32)])
    s_sg = call.scratch(SmallGather.sems(n))
    s_spread = call.scratch(Exchange.sems(n))
    s_cols = call.scratch(Columns.sems(n))
    s_rows = call.scratch(Rows.sems())

    def body(at, of):
        sm_all, xs, inputs, gains = of(s_small)[0], of(s_x)[0], of(o_in), of(o_gains)
        shift, mask, w = of(s_shift)[0], of(s_mask)[0], of(o_w)
        ints_all = of(o_ints)
        q_ref, k_ref, v_ref = of(o_qkv)
        sm = SmallGather(at, of(i_small), sm_all, of(s_sg))
        gat = Gather(at, xs, of(s_gat), ALONE)
        cols = Columns(at, of(s_pieces)[0], w, of(s_cols))
        spread = Spread(at, of(i_ints), ints_all, of(s_spread))
        out_rows = Rows(at, of(i_out), of(o_out), of(s_rows))
        sm.start()
        xs[at.j] = of(i_x)[...]
        gat.start()
        spread.start()
        split_columns(of(i_w), of(s_pieces)[0], head_runs)
        cols.start()
        sm.step()
        out_rows.start()
        gat.open_wide()
        sm.finish()
        for r in range(4):
            for b in range(n):
                lanes = slice((r * n + b) * k, (r * n + b + 1) * k)
                for i in range(4):
                    gains[i : i + 1, lanes] = sm_all[b, r, i // 2 : i // 2 + 1, i % 2 * k : (i % 2 + 1) * k]
        for m in range(3):
            for r in range(4):
                block = (m * 4 + r) * n + at.j
                owner = block // 3
                line = 2 + lax.rem(block, 3)
                shift[0:1, (m * 4 + r) * HD : (m * 4 + r + 1) * HD] = sm_all[
                    lax.rem(owner, n), owner // n, pl.ds(line, 1), 0:HD
                ]
        spread.finish()

        def norm(t):
            here = pl.ds(t * at.width, at.width)
            normed, _ = norm_stats(xs[here].reshape(wide, d).astype(F32))
            low = (normed * gains[0:1] + gains[1:2]).astype(BF)
            inputs[here] = low.reshape(at.width, tok, d)

        def project(t):
            for b in range(at.width):
                block = t * at.width + b
                these = pl.ds(block * tok, tok)
                table = rotation(ints_all, of(i_freq), block, 1.0)
                projected = dot(inputs[block], w[...].reshape(d, c), 1, 0) + shift[0:1]
                for i in range(4 * hp * HD // 256):
                    u = projected[:, i * 128 : (i + 1) * 128]
                    u = turn_pairs(u, table)
                    for e in range(2):
                        head = i * 2 + e
                        val = u[:, e * HD : (e + 1) * HD]
                        if head < hp:
                            q_ref[head, these] = (val * (1.0 / math.sqrt(HD))).astype(BF)
                        else:
                            k_ref[head - hp, these] = val.astype(BF)
                for head in range(hp):
                    first = (2 * hp + head) * HD
                    v_ref[head, these] = projected[:, first : first + HD].astype(BF)

        order = by_place(at.z, (3210, 3201, 132, 123))
        edge = jnp.logical_or(at.z == 0, at.z == at.depth - 1)

        @pl.loop(0, LINE)
        def _(i):
            t = digit(order, i)
            lo = jnp.where(edge, i + 1, jnp.where(i == 0, 1, jnp.where(i == 1, 3, 4)))
            hi = jnp.where(edge, jnp.minimum(i + 2, 4), jnp.where(i == 0, 3, 4))

            @pl.loop(lo, hi)
            def _(m):
                gat.fetch(digit(order, m))

            cols.step(jnp.where(i < 3, i * (n // 4), n), jnp.where(i < 2, (i + 1) * (n // 4), n))

            @pl.when(i == 3)
            def _():
                cols.relay(0, n)
                cols.finish()

                @pl.loop(0, 3)
                def _(m):
                    project(digit(order, m))

            gat.take_side(t)
            norm(t)

        out_rows.relay()
        project(digit(order, 3))
        for t in range(LINE):
            reach = (t + 1) * wide
            fill_mask(at, mask, ints_all, t)
            these = slice(t * wide, (t + 1) * wide)
            for head in range(hp):
                lanes = slice(head * HD, (head + 1) * HD)
                scores = dot(q_ref[head, these], k_ref[head, 0:reach], 1, 1)
                weights = jnp.exp(scores + mask[:, 0:reach])
                den = jnp.sum(weights, axis=1, keepdims=True)
                numer = dot(weights.astype(BF), v_ref[head, 0:reach], 1, 0)
                ctx = numer / den
                of(o_ctx)[these, lanes] = ctx
                of(o_low)[these, lanes] = ctx.astype(BF)
                of(o_den)[these, head : head + 1] = den
        out_rows.finish()
        gat.finish()

    return call.run(body)


class Spread:
    def __init__(self, at, mine, got, sems):
        self.at, self.mine, self.got = at, mine, got
        self.ssem, self.rsem = sems

    def copy(self, to, src):
        at = self.at
        return remote(
            self.mine, self.got.at[src], self.ssem.at[to], self.rsem.at[src], at.seq(to)
        )

    def own(self):
        return pltpu.make_async_copy(self.mine, self.got.at[self.at.j], self.ssem.at[self.at.j])

    def start(self):
        self.own().start()

        @pl.loop(1, self.at.n)
        def _(i):
            self.copy(self.at.other(i), self.at.j).start()

    def finish(self):
        self.own().wait()

        @pl.loop(1, self.at.n)
        def _(i):
            p = self.at.other(i)
            self.copy(p, p).wait()


def sum_call(n, cid, name, pairs, tok, columns=(), rows=(), gathers=(), row_sums=(), col_sums=()):
    call = Call(n, cid, name)
    d = pairs[0][1].shape[0 if pairs[0][2] else 1]
    keys = []
    for lhs, rhs, flip in pairs:
        keys.append((call.give(lhs), call.give(rhs), flip))
    out = call.make((tok, d), F32)
    part = call.scratch([pltpu.VMEM((n, tok, d), BF)])
    red_s = call.scratch(Reduce.scratch(n, tok, d, SUM_CUTS))
    extra = Extras(call, n, columns, rows, gathers, row_sums, col_sums, PAIRED)

    def body(at, of):
        part_ref = of(part)[0]
        red = Reduce(at, part_ref, of(red_s), SUM_CUTS)
        extra.bind(at, of)
        extra.start()
        products(at, of, part_ref, keys, red)
        steps(SUM_PLAN, red, extra)
        red.last(of(out))
        extra.finish()
        red.finish()

    flops = sum(2 * l.shape[0] * l.shape[1] * d for l, _, _ in pairs)
    return call.run(body, flops)


class Extras:
    def __init__(
        self, call, n, columns=(), rows=(), gathers=(), row_sums=(), col_sums=(), cuts=None
    ):
        self.n, self.cuts = n, cuts
        self.columns, self.rows, self.gathers, self.row_sums, self.col_sums = [], [], [], [], []
        for w, runs in columns:
            shape = (n, w.shape[0], w.shape[1] // n)
            self.columns.append(
                (
                    call.give(w),
                    call.make((4,) + shape, BF, ANY),
                    call.scratch([pltpu.VMEM(shape, BF)]),
                    call.scratch(Columns.sems(n)),
                    runs,
                )
            )
        for p in rows:
            self.rows.append(
                (call.give(p, ANY), call.make((4,) + p.shape, BF, ANY), call.scratch(Rows.sems()))
            )
        for p in gathers:
            self.gathers.append(
                (
                    call.give(p, ANY),
                    call.make((n,) + p.shape, BF, ANY),
                    call.scratch(Gather.sems(n, cuts)),
                )
            )
        self.n_row = n_row = 4
        for p in row_sums:
            lhs, rhs = p if isinstance(p, tuple) else (None, None)
            shape = (n_row, lhs.shape[1] // n_row, rhs.shape[1]) if lhs is not None else p.shape
            self.row_sums.append(
                (
                    (call.give(lhs), call.give(rhs)) if lhs is not None else call.give(p),
                    call.scratch([pltpu.VMEM(shape, BF)])[0],
                    call.make(shape[1:], F32),
                    call.scratch(RowSum.scratch(*shape[1:])),
                )
            )
        for p, runs in col_sums:
            lhs, rhs = p if isinstance(p, tuple) else (None, None)
            shape = (n_row, lhs.shape[1] // n_row, rhs.shape[1]) if lhs is not None else p.shape
            k, c = shape[1] // n, shape[2]
            self.col_sums.append(
                (
                    (call.give(lhs), call.give(rhs)) if lhs is not None else call.give(p),
                    call.scratch([pltpu.VMEM(shape, BF)])[0],
                    call.make((k, n * c), F32),
                    call.scratch(RowSum.scratch(*shape[1:])),
                    call.scratch([pltpu.VMEM((n, k, c), BF)] * 2),
                    call.scratch(Exchange.sems(n)),
                    runs,
                )
            )

    def bind(self, at, of):
        self.at, self.of = at, of
        self.b_columns = [
            (Columns(at, of(p)[0], of(o), of(s)), of(i), of(p)[0], runs)
            for i, o, p, s, runs in self.columns
        ]
        self.b_rows = [Rows(at, of(i), of(o), of(s)) for i, o, s in self.rows]
        self.b_gathers = [
            (Gather(at, of(o), of(s), self.cuts), of(i), of(o)) for i, o, s in self.gathers
        ]
        self.b_sums = [
            (RowSum(at, of(g), of(s)), of(o), of(i), of(g)) for i, g, o, s in self.row_sums
        ]
        self.b_cols = []
        for i, g, o, s, v, e, runs in self.col_sums:
            mine, got = of(v)
            self.b_cols.append(
                (
                    RowSum(at, of(g), of(s)),
                    mine,
                    Exchange(at, mine, got, of(e)),
                    (got, of(o), runs),
                    of(i),
                    of(g),
                )
            )

    def start(self):
        at = self.at
        for g, src, buf in self.b_gathers:
            buf[at.j] = src[...]
            g.start()
        for r in self.b_rows:
            r.start()
        for c, src, pieces, runs in self.b_columns:
            split_columns(src, pieces, runs)
            c.start()

    def fill_columns(self, k):
        rs, _, _, _, src, grad = self.b_cols[k]
        if isinstance(src, tuple):
            size = grad.shape[1]

            @pl.loop(0, grad.shape[0])
            def _(b):
                cols = pl.ds(pl.multiple_of(b * size, size), size)
                grad[b] = dot(src[0][:, cols], src[1][...], 0, 0).astype(BF)
        else:
            grad[...] = src[...]
        rs.start()

    def fill_rows(self, k):
        rs, _, src, grad = self.b_sums[k]
        if isinstance(src, tuple):

            @pl.loop(0, grad.shape[2] // CHUNK)
            def _(b):
                cols = pl.ds(pl.multiple_of(b * CHUNK, CHUNK), CHUNK)
                term = dot(src[0][...], src[1][:, cols], 0, 0)
                grad[:, :, cols] = term.reshape(grad.shape[0], grad.shape[1], CHUNK).astype(BF)
        else:
            grad[...] = src[...]
        rs.start()

    def fill(self):
        work = [functools.partial(self.fill_columns, k) for k in range(len(self.b_cols))]
        return work + [functools.partial(self.fill_rows, k) for k in range(len(self.b_sums))]

    def cross(self, k):
        every = [c[0] for c in self.b_cols] + [r[0] for r in self.b_sums]
        if k < len(every):
            every[k].cross()

    def turn(self, k):
        if k < len(self.b_cols):
            rs, mine, ex = self.b_cols[k][:3]
            mine[...] = rs.total().reshape(mine.shape).astype(BF)
            ex.start()

    def gather_step(self, s):
        for g, _, _ in self.b_gathers:
            g.step(s)

    def column_step(self, k):
        q = self.n // 4
        for c, *_ in self.b_columns:
            c.step(k * q, (k + 1) * q)

    def column_relay(self, k):
        q = self.n // 4
        for c, *_ in self.b_columns:
            c.relay(k * q, (k + 1) * q)

    def finish(self):
        at = self.at
        for g, _, _ in self.b_gathers:
            for zz in range(at.depth):
                g.take_side(zz)
            g.finish()
        for r in self.b_rows:
            r.relay()
        for r in self.b_rows:
            r.finish()
        for c, *_ in self.b_columns:
            c.finish()
        for rs, out, *_ in self.b_sums:
            out[...] = rs.total()
            rs.finish()
        for rs, _, ex, (got, out, runs), *_ in self.b_cols:
            ex.finish()
            rs.finish()
            join_columns(got, out, runs)


def gather_call(n, cid, name, x, columns=(), rows=(), row_sums=(), col_sums=()):
    call = Call(n, cid, name)
    extra = Extras(call, n, columns, rows, [x], row_sums, col_sums, ALONE)

    def body(at, of):
        extra.bind(at, of)
        extra.start()
        steps(GATHER_PLAN, None, extra)
        extra.finish()

    return call.run(body)


def digit(code, i):
    return lax.rem(code // jnp.where(i == 0, 1, jnp.where(i == 1, 10, jnp.where(i == 2, 100, 1000))), 10)


def by_place(z, codes):
    return jnp.where(z == 0, codes[0], jnp.where(z == 1, codes[1], jnp.where(z == 2, codes[2], codes[3])))


def core_call(n, pair, x, gain, bias, columns, rows, gathers):
    call = Call(n, 2, "core")
    tok, d = x.shape
    c = columns[0][0].shape[1] // n
    wide = n // LINE * tok
    length = n * tok
    key = (call.give(pair[0]), call.give(pair[1]), False)
    i_x, i_gain, i_bias = call.give(x), call.give(gain), call.give(bias)
    o_hid = call.make((tok, d), F32)
    out = call.make((tok, d), F32)
    o_mid = call.make((n, tok, d), BF)
    o_low = call.make((tok, d), BF)
    o_known = call.make((8, d), F32)
    o_acts = [call.make((length, c), BF) for _ in range(3)]
    part = call.scratch([pltpu.VMEM((n, tok, d), BF)] * 2)
    first_s = call.scratch(Reduce.scratch(n, tok, d, CORE_SUMS))
    extra = Extras(call, n, columns, rows, gathers, cuts=PAIRED)
    gat_s = call.scratch(Gather.sems(n, MLP_CUTS))
    red_s = call.scratch(Reduce.scratch(n, tok, d, MLP_SUMS))

    def body(at, of):
        first_part, part_ref = of(part)
        first = Reduce(at, first_part, of(first_s), CORE_SUMS)
        mid, hid = of(o_mid), of(o_hid)
        inner_ref, gg_ref, gu_ref = of(o_acts)
        gat = Gather(at, mid, of(gat_s), MLP_CUTS)
        red = Reduce(at, part_ref, of(red_s), MLP_SUMS)
        extra.bind(at, of)
        extra.start()
        products(at, of, first_part, [key], first)
        steps(CORE_PLAN, first, extra)
        first.last(hid)
        hid[...] += of(i_x)[...].astype(F32)
        normed, _ = norm_stats(hid[...])
        mid[at.j] = (normed * of(i_gain)[...] + of(i_bias)[...]).astype(BF)
        gat.start()
        extra.finish()
        gat.open_wide()
        gate, up = (c[0].full for c in extra.b_columns)
        down, grad = extra.b_rows[0].full, extra.b_gathers[0][2]
        gate, up = gate.reshape(d, c), up.reshape(d, c)
        down = down.reshape(c, d)
        order = by_place(at.z, (3210, 3201, 132, 123))
        edge = jnp.logical_or(at.z == 0, at.z == at.depth - 1)

        @pl.loop(0, LINE)
        def _(i):
            t = digit(order, i)
            lo = jnp.where(edge, i + 1, jnp.where(i == 0, 1, jnp.where(i == 1, 3, 4)))
            hi = jnp.where(edge, jnp.minimum(i + 2, 4), jnp.where(i == 0, 3, 4))

            @pl.loop(lo, hi)
            def _(m):
                gat.fetch(digit(order, m))

            gat.take_side(t)
            here = pl.ds(t * at.width, at.width)
            these = pl.ds(t * wide, wide)
            tokens = mid[here].reshape(wide, d)
            gate_pre = dot(tokens, gate[...], 1, 0)
            sig = 1.0 / (1.0 + jnp.exp(-gate_pre))
            silu = gate_pre * sig
            up_pre = dot(tokens, up[...], 1, 0)
            inner_ref[these] = (silu * up_pre).astype(BF)
            g_inner = dot(grad[here].reshape(wide, d), down[...], 1, 1)
            gu_ref[these] = (g_inner * silu).astype(BF)
            gg_ref[these] = (g_inner * up_pre * sig * (1.0 + gate_pre * (1.0 - sig))).astype(BF)
            product(at, lambda k: k, part_ref, [(gg_ref, gate, True), (gu_ref, up, True)], t)
            red.emit(t)

            @pl.when(jnp.logical_and(edge, i >= 2))
            def _():
                red.pass_on(digit(order, i - 1))

        rest = by_place(at.z, (3, 32, 301, 0))

        @pl.loop(0, jnp.where(edge, 1, 3))
        def _(i):
            red.pass_on(digit(rest, i))

        red.last(of(out))
        grad_in = of(out)[...]
        normed, inv_std = norm_stats(hid[...])
        of(o_known)[...] = jnp.zeros((8, d), F32)
        of(o_known)[2:3] = jnp.sum(grad_in * normed, axis=0, keepdims=True)
        of(o_known)[3:4] = jnp.sum(grad_in, axis=0, keepdims=True)
        g_hidden = extra.b_gathers[0][1][...].astype(F32) + norm_back(
            grad_in, normed, inv_std, of(i_gain)[...]
        )
        of(out)[...] = g_hidden
        of(o_low)[...] = g_hidden.astype(BF)
        gat.finish()
        first.finish()
        red.finish()

    return call.run(body)


def back_call(
    n, g_attn, out_w, qkv_w, heads, ctx, low, den, ints, frequency, inputs, normed, known, runs, mlp
):
    call = Call(n, 11, "back")
    length, d = g_attn.shape
    hp, tok, wide = H // n, length // n, length // LINE
    c = 3 * hp * HD
    i_g, i_out, i_w = call.give(g_attn), call.give(out_w), call.give(qkv_w)
    i_heads = [call.give(v) for v in heads]
    i_ctx, i_den, i_ints, i_freq = (call.give(v) for v in (ctx, den, ints, frequency))
    i_norm, i_known = call.give(normed), call.give(known)
    out = call.make((tok, d), F32)
    o_small = call.make((8, d // 4), F32)
    o_mlp = call.make((tok, d), F32)
    mlp_keys = (call.give(mlp[0]), call.give(mlp[1]), False)
    mlp_s = call.scratch(Reduce.scratch(n, tok, d, SUM_CUTS))
    s_proj = call.scratch([pltpu.VMEM((length, c), BF)])[0]
    s_sum = call.scratch([pltpu.VMEM((length, c), F32)])
    s_mask = call.scratch([pltpu.VMEM((wide, length), F32)])
    part = call.scratch([pltpu.VMEM((n, tok, d), BF)])
    red_s = call.scratch(Reduce.scratch(n, tok, d, SUM_CUTS))
    s_small = call.scratch(SmallSum.scratch(n, d))
    made = Made(s_proj, (length, c))
    extra = Extras(call, n, row_sums=[(low, g_attn)], col_sums=[((inputs, made), runs)])

    def body(at, of):
        part_ref = of(part)[0]
        red = Reduce(at, part_ref, of(red_s), SUM_CUTS)
        small = SmallSum(at, of(s_small))
        proj, sums, mask = of(s_proj), of(s_sum)[0], of(s_mask)[0]
        q_ref, k_ref, v_ref = of(i_heads)
        ints_all = of(i_ints)
        extra.bind(at, of)
        extra.start()
        branch = Reduce(at, part_ref, of(mlp_s), SUM_CUTS)
        products(at, of, part_ref, [mlp_keys], branch)
        width = hp * HD
        sums[:, width:] = jnp.zeros((length, 2 * width), F32)
        for t in range(LINE):
            these, reach = slice(t * wide, (t + 1) * wide), (t + 1) * wide
            fill_mask(at, mask, ints_all, t)
            g_ctx = dot(of(i_g)[these], of(i_out)[...], 1, 1)
            for head in range(hp):
                lanes = slice(head * HD, (head + 1) * HD)
                g_own = g_ctx[:, lanes]
                below = of(i_den)[these, head : head + 1]
                g_num = (g_own / below).astype(BF)
                g_den = -jnp.sum(g_own * of(i_ctx)[these, lanes], axis=1, keepdims=True) / below
                query = q_ref[head, these]
                scores = dot(query, k_ref[head, 0:reach], 1, 1)
                weights = jnp.exp(scores + mask[:, 0:reach])
                g_weights = dot(g_num, v_ref[head, 0:reach], 1, 1)
                g_scores = (weights * (g_weights + g_den)).astype(BF)
                sums[these, lanes] = dot(g_scores, k_ref[head, 0:reach], 1, 0)
                lanes = slice(width + head * HD, width + (head + 1) * HD)
                sums[0:reach, lanes] += dot(g_scores, query, 0, 0)
                lanes = slice(2 * width + head * HD, 2 * width + (head + 1) * HD)
                sums[0:reach, lanes] += dot(weights.astype(BF), g_num, 0, 0)
            if t < LINE - 1:
                branch.reduce(LINE - 1 - t)

        @pl.loop(0, n)
        def _(b):
            these = pl.ds(b * tok, tok)
            table = rotation(ints_all, of(i_freq), b, -1.0)
            for i in range(2 * width // 128):
                lanes = slice(i * 128, (i + 1) * 128)
                u = turn_pairs(sums[these, lanes], table)
                if i < width // 128:
                    u = u * (1.0 / math.sqrt(HD))
                proj[these, lanes] = u.astype(BF)
            proj[these, 2 * width :] = sums[these, 2 * width :].astype(BF)

        branch.last(of(o_mlp))
        branch.finish()
        products(at, of, part_ref, [(s_proj, i_w, True)], red)
        small.terms[...] = of(i_known)[...]
        shift = jnp.sum(proj[...].astype(F32), axis=0, keepdims=True)
        per = d // 4
        for m in range(3):
            for r in range(4):
                own = shift[:, (m * 4 + r) * HD : (m * 4 + r + 1) * HD]
                for b in range(n):
                    flat = m * d + (r * n + b) * HD
                    row, rest = flat // (3 * per), flat % (3 * per)
                    first = row * per + rest % per
                    line = 4 + rest // per
                    small.terms[line : line + 1, first : first + HD] = jnp.where(
                        at.j == b, own, 0.0
                    )
        steps(BACK_PLAN, red, extra)
        red.last(of(out))
        grad = of(out)[...]
        small.terms[0:1, :] = jnp.sum(grad * of(i_norm)[...], axis=0, keepdims=True)
        small.terms[1:2, :] = jnp.sum(grad, axis=0, keepdims=True)
        small.run(of(o_small))
        extra.finish()
        red.finish()

    return call.run(body)


def last_call(n, cid, pairs, tok, normed, known, row_sums, col_sums):
    call = Call(n, cid, "last")
    d = pairs[0][1].shape[0]
    keys = []
    for lhs, rhs, flip in pairs:
        keys.append((call.give(lhs), call.give(rhs), flip))
    i_norm, i_known = call.give(normed), call.give(known)
    out = call.make((tok, d), F32)
    o_small = call.make((8, d // 4), F32)
    part = call.scratch([pltpu.VMEM((n, tok, d), BF)])
    red_s = call.scratch(Reduce.scratch(n, tok, d, SUM_CUTS))
    s_small = call.scratch(SmallSum.scratch(n, d))
    extra = Extras(call, n, row_sums=row_sums, col_sums=col_sums)

    def body(at, of):
        part_ref = of(part)[0]
        red = Reduce(at, part_ref, of(red_s), SUM_CUTS)
        extra.bind(at, of)
        extra.start()
        products(at, of, part_ref, keys, red)
        steps(BACK_PLAN, red, extra)
        red.last(of(out))
        small = SmallSum(at, of(s_small))
        small.terms[...] = of(i_known)[...]
        grad = of(out)[...]
        small.terms[0:1, :] = jnp.sum(grad * of(i_norm)[...], axis=0, keepdims=True)
        small.terms[1:2, :] = jnp.sum(grad, axis=0, keepdims=True)
        small.run(of(o_small))
        extra.finish()
        red.finish()

    return call.run(body)


def attention(queries, keys, values, allowed):
    scores = jnp.einsum("qhd,khd->hqk", queries, keys, preferred_element_type=F32)
    exp_weights = jnp.where(allowed[None], jnp.exp(scores), 0.0)
    denominator = jnp.sum(exp_weights, axis=-1)
    numerator = jnp.einsum(
        "hqk,khd->qhd", exp_weights.astype(BF), values, preferred_element_type=F32
    )
    return numerator / jnp.transpose(denominator)[:, :, None], denominator


def attention_back(queries, keys, values, allowed, denominator, context, g_context):
    den = jnp.transpose(denominator)
    g_numer = (g_context / den[:, :, None]).astype(BF)
    g_den = jnp.transpose(-jnp.sum(g_context * context, axis=-1) / den)
    scores = jnp.einsum("qhd,khd->hqk", queries, keys, preferred_element_type=F32)
    exp_weights = jnp.where(allowed[None], jnp.exp(scores), 0.0)
    g_values = jnp.einsum(
        "hqk,qhd->khd", exp_weights.astype(BF), g_numer, preferred_element_type=F32
    )
    g_weights = jnp.einsum("qhd,khd->hqk", g_numer, values, preferred_element_type=F32)
    g_scores = (exp_weights * (g_weights + g_den[:, :, None])).astype(BF)
    g_queries = jnp.einsum("hqk,khd->qhd", g_scores, keys, preferred_element_type=F32)
    g_keys = jnp.einsum("hqk,qhd->khd", g_scores, queries, preferred_element_type=F32)
    return g_queries, g_keys, g_values


def body(nrow, n, *args):
    (
        layer_in,
        segments,
        positions,
        attn_norm_gain,
        attn_norm_bias,
        qkv_weight,
        qkv_bias,
        out_weight,
        mlp_norm_gain,
        mlp_norm_bias,
        gate_weight,
        up_weight,
        down_weight,
        out_grad,
    ) = args
    j = lax.axis_index("seq")
    tok = layer_in.shape[1]
    length = n * tok
    k = qkv_weight.shape[0]
    f = down_weight.shape[0]
    hp = H // n
    whole_heads = out_weight.shape[0] == HD
    roomy = length * D <= 1 << 22 and whole_heads

    if whole_heads:
        head_runs = [
            (b, (m * nrow + r) * HD, m * D + (r * n + b) * HD, HD)
            for b in range(n) for m in range(3) for r in range(nrow)
        ]
    else:
        size = hp * HD
        head_runs = [
            (b, m * size, m * D + b * size, size) for b in range(n) for m in range(3)
        ]
    ff_runs = [(b, r * f, (r * n + b) * f, f) for b in range(n) for r in range(nrow)]

    def split_heads(w):
        lead = w.shape[0]
        if whole_heads:
            w = w.reshape(lead, 3, nrow, n, HD).transpose(3, 0, 1, 2, 4)
        else:
            w = w.reshape(lead, 3, n, hp, HD).transpose(2, 0, 1, 3, 4)
        return w.reshape(n, lead, 3 * hp * HD)

    def join_heads(blocks):
        lead = blocks.shape[1]
        if whole_heads:
            w = blocks.reshape(n, lead, 3, nrow, HD).transpose(1, 2, 3, 0, 4)
        else:
            w = blocks.reshape(n, lead, 3, hp, HD).transpose(1, 2, 0, 3, 4)
        return w.reshape(lead, 3 * D)

    if roomy:
        blank = jnp.zeros((128 - 2 * k,), F32)
        vectors = [
            attn_norm_gain, attn_norm_bias, blank, mlp_norm_gain, mlp_norm_bias, blank,
            jnp.pad(qkv_bias.astype(F32).reshape(3, HD), ((0, 3), (0, 128 - HD))).reshape(-1),
        ]
        small = jnp.concatenate([v.astype(F32) for v in vectors]).reshape(8, 128)
        ints = jnp.concatenate([segments, positions, jnp.zeros((6, tok), jnp.int32)], 0)
        half = ROT // 2
        frequency = 10000.0 ** (-2.0 * jnp.arange(half, dtype=F32) / ROT)
        frequency = jnp.concatenate([frequency, frequency, jnp.zeros((HD - ROT,), F32)])
        frequency = jnp.broadcast_to(jnp.concatenate([frequency, frequency])[None], (8, 128))
        (
            inputs_all, gains, ints_all, qkv_own, out_own, queries, keys, values, context_low,
            context, denominator,
        ) = attend_call(
            n, layer_in[0], small, ints, frequency, qkv_weight, head_runs, out_weight,
        )
        inputs_all = inputs_all.reshape(length, D)
        attn_gain, mlp_gain, mlp_bias = gains[0:1], gains[2:3], gains[3:4]
        qkv_own, out_own = qkv_own.reshape(D, 3 * hp * HD), out_own.reshape(hp * HD, D)
    else:
        small = jnp.concatenate(
            [attn_norm_gain, attn_norm_bias, mlp_norm_gain, mlp_norm_bias, qkv_bias]
        )
        small = jnp.pad(small, (0, 2048 - small.shape[0])).reshape(16, 128)
        ints = jnp.concatenate([segments, positions, jnp.zeros((6, tok), jnp.int32)], 0)
        front = front_call(
            n, layer_in[0], small, ints, qkv_weight, head_runs, out_weight if whole_heads else None
        )
        x_all, small_all, ints_all, qkv_own = front[:4]
        x_all = x_all.reshape(length, D)
        qkv_own = qkv_own.reshape(D, 3 * hp * HD)
        if whole_heads:
            out_own = front[4].reshape(hp * HD, D)
        else:
            out_full = lax.all_gather(out_weight, ("row", "seq"), axis=0, tiled=True)
            out_own = lax.dynamic_slice_in_dim(out_full, j * hp * HD, hp * HD, 0)
        small_all = small_all.transpose(1, 0, 2, 3).reshape(nrow * n, 2048)
        attn_gain, attn_bias, mlp_gain, mlp_bias = (
            small_all[:, c : c + k].reshape(1, D).astype(F32) for c in (0, k, 2 * k, 3 * k)
        )
        qkv_shift = small_all[:, 4 * k : 4 * k + 3 * k].reshape(1, 3 * D)
        shift_own = lax.dynamic_index_in_dim(split_heads(qkv_shift), j, 0, keepdims=False).astype(F32)
        seg_all, pos_all = ints_all[:, 0].reshape(length), ints_all[:, 1].reshape(length)

        inputs_all = (norm_stats(x_all.astype(F32))[0] * attn_gain + attn_bias).astype(BF)
        inputs_all = lax.optimization_barrier(inputs_all)
        projected = dot(inputs_all, qkv_own, 1, 0) + shift_own
        head_split = projected.reshape(length, 3, hp, HD)
        cosine, sine_part = rotary_tables(pos_all)
        queries = (rotate(head_split[:, 0], cosine, sine_part, 1.0) / math.sqrt(HD)).astype(BF)
        keys = rotate(head_split[:, 1], cosine, sine_part, 1.0).astype(BF)
        values = head_split[:, 2].astype(BF)
        index = jnp.arange(length, dtype=jnp.int32)
        allowed = (seg_all[:, None] == seg_all[None, :]) & (index[None, :] <= index[:, None])
        context, denominator = attention(queries, keys, values, allowed)
        context_low = context.reshape(length, hp * HD).astype(BF)
    x_float = layer_in[0].astype(F32)
    grad_float = out_grad[0].astype(F32)
    ff_columns = [(gate_weight, ff_runs), (up_weight, ff_runs)]
    if roomy:
        (
            hidden_mid, g_hidden, middle_all, g_attn, known, inner_act, g_gate, g_up, _, _, down_own,
            grad_all,
        ) = core_call(
            n, (context_low, out_own), layer_in[0], mlp_gain, mlp_bias, ff_columns, [down_weight],
            [out_grad[0]],
        )
        down_own = down_own.reshape(nrow * f, D)
        middle_all, grad_all = middle_all.reshape(length, D), grad_all.reshape(length, D)
    else:
        attn_branch, gate_own, up_own, down_own = sum_call(
            n, 2, "mix_sum", [(context_low, out_own, False)], tok, columns=ff_columns,
            rows=[down_weight],
        )
        gate_own, up_own = gate_own.reshape(D, nrow * f), up_own.reshape(D, nrow * f)
        down_own = down_own.reshape(nrow * f, D)
        hidden_mid = x_float + attn_branch
        normed2, inv_std2 = norm_stats(hidden_mid)
        middle = (normed2 * mlp_gain + mlp_bias).astype(BF)
        (middle_all,) = gather_call(n, 3, "middle", middle)
        middle_all = middle_all.reshape(length, D)
        gate_pre = dot(middle_all, gate_own, 1, 0)
        up_pre = dot(middle_all, up_own, 1, 0)
        sig = jax.nn.sigmoid(gate_pre)
        silu = gate_pre * sig
        inner_act = (silu * up_pre).astype(BF)
        (grad_all,) = gather_call(n, 8, "grads", out_grad[0])
        grad_all = grad_all.reshape(length, D)
        g_inner = dot(grad_all, down_own, 1, 1)
        g_gate = (g_inner * up_pre * sig * (1.0 + gate_pre * (1.0 - sig))).astype(BF)
        g_up = (g_inner * silu).astype(BF)
        (g_middle,) = sum_call(
            n, 5, "mlp_back", [(g_gate, gate_own, True), (g_up, up_own, True)], tok
        )
    normed1, inv_std1 = norm_stats(x_float)
    if roomy:
        down_part, gate_part, up_part = (inner_act, grad_all), (middle_all, g_gate), (middle_all, g_up)
    else:
        down_part = dot(inner_act, grad_all, 0, 0).astype(BF).reshape(nrow, f, D)
        gate_part = dot(middle_all, g_gate, 0, 0).astype(BF).reshape(nrow, n * k, nrow * f)
        up_part = dot(middle_all, g_up, 0, 0).astype(BF).reshape(nrow, n * k, nrow * f)
    if not roomy:
        g_hidden = grad_float + norm_back(g_middle, normed2, inv_std2, mlp_gain)
        g_attn = g_hidden.astype(BF)
    if roomy:
        g_attn_all, down_grad, gate_grad, up_grad = gather_call(
            n, 6, "hidden_back", g_attn,
            row_sums=[down_part], col_sums=[(gate_part, ff_runs), (up_part, ff_runs)],
        )
    else:
        mlp_branch, down_grad = sum_call(
            n, 4, "mlp_sum", [(inner_act, down_own, False)], tok, row_sums=[down_part]
        )
        g_attn_all, gate_grad, up_grad = gather_call(
            n, 6, "hidden_back", g_attn, col_sums=[(gate_part, ff_runs), (up_part, ff_runs)]
        )
    g_attn_all = g_attn_all.reshape(length, D)

    if roomy:
        g_inputs, small_grads, mlp_branch, out_w_grad, qkv_grad = back_call(
            n, g_attn_all, out_own, qkv_own, (queries, keys, values), context, context_low,
            denominator, ints_all, frequency, inputs_all, normed1, known, head_runs,
            (inner_act, down_own),
        )
    else:
        g_context = dot(g_attn_all, out_own, 1, 1).reshape(length, hp, HD)
        g_queries, g_keys, g_values = attention_back(
            queries, keys, values, allowed, denominator, context, g_context
        )
        query_part = rotate(g_queries, cosine, sine_part, -1.0) / math.sqrt(HD)
        key_part = rotate(g_keys, cosine, sine_part, -1.0)
        g_projected = (
            jnp.stack([query_part, key_part, g_values], 1).reshape(length, 3 * hp * HD).astype(BF)
        )
        qkv_part = dot(inputs_all, g_projected, 0, 0).astype(BF)
        qkv_part = qkv_part.reshape(nrow, n * k, 3 * hp * HD)
        out_part = dot(context_low, g_attn_all, 0, 0).astype(BF)
        if whole_heads:
            out_part = out_part.reshape((nrow,) + out_weight.shape)
        shift_sum = jnp.sum(g_projected.astype(F32), axis=0)
        shift_blocks = lax.dynamic_update_slice_in_dim(
            jnp.zeros((n, 1, 3 * hp * HD), F32), shift_sum[None, None], j, 0
        )
        shift_full = join_heads(shift_blocks)[0]
        known = jnp.concatenate(
            [
                jnp.zeros((2, D), F32),
                jnp.sum(g_middle * normed2, axis=0)[None],
                jnp.sum(g_middle, axis=0)[None],
                shift_full.reshape(nrow, 3, D // nrow).transpose(1, 0, 2).reshape(3, D),
                jnp.zeros((1, D), F32),
            ]
        )
        last = last_call(
            n, 7, [(g_projected, qkv_own, True)], tok, normed1, known,
            [out_part] if whole_heads else [],
            [(qkv_part, head_runs)],
        )
        if whole_heads:
            g_inputs, small_grads, out_w_grad, qkv_grad = last
        else:
            g_inputs, small_grads, qkv_grad = last
            placed = lax.dynamic_update_slice_in_dim(
                jnp.zeros((D, D), BF), out_part, j * hp * HD, 0
            )
            out_w_grad = lax.psum_scatter(
                placed, ("row", "seq"), scatter_dimension=0, tiled=True
            ).astype(F32)
    layer_out = (hidden_mid + mlp_branch).astype(BF)
    input_grad = g_hidden + norm_back(g_inputs, normed1, inv_std1, attn_gain)
    own = lax.dynamic_slice_in_dim(small_grads, j * k, k, 1)
    shift_own_grad = lax.dynamic_slice_in_dim(small_grads[4:7].reshape(-1), j * 3 * k, 3 * k, 0)
    return (
        layer_out[None],
        input_grad[None],
        own[0],
        own[1],
        qkv_grad,
        shift_own_grad,
        out_w_grad,
        own[2],
        own[3],
        gate_grad,
        up_grad,
        down_grad,
    )


def solution(mesh):
    nrow, n = mesh.shape["row"], mesh.shape["seq"]

    def local(*args):
        return body(nrow, n, *args)

    tokens, ints = P("row", "seq", None), P("row", "seq")
    vec, mat = P(("row", "seq")), P(("row", "seq"), None)
    return jax.shard_map(
        local,
        mesh=mesh,
        in_specs=(
            tokens, ints, ints, vec, vec, mat, vec, mat, vec, vec, mat, mat, mat, tokens,
        ),
        out_specs=(tokens, tokens, vec, vec, mat, vec, mat, vec, vec, mat, mat, mat),
        check_vma=False,
    )
```
